128 devices in a mesh: dp: 4 (over z), expert: 32 (over x, y, core).
Axes of the slice: x: 4, y: 4, z: 4, core: 2. Of those that a mesh axis runs over, the one named last changes fastest.
Arguments:
- tokens: bfloat16 [32768, 768], P(('dp', 'expert')), may hold values from -6 to 6
- segment_ids: int32 [128, 256], P(('dp', 'expert')), may hold values from 0 to 3, never falling along the last dimension, each value on 1 to 128 neighbouring positions
- routes: int32 [32768, 2], P(('dp', 'expert')), may hold values from 0 to 32, all different within a row; in each aligned block of 256 rows (0 to 255, 256 to 511, ...) at most 24 rows name the same one
- cotangent: bfloat16 [32768, 768], P(('dp', 'expert')), may hold values from -6 to 6
- w_qkv: bfloat16 [768, 2304], replicated, may hold values from -0.21875 to 0.21875
- w_attn_out: bfloat16 [768, 768], replicated, may hold values from -0.875 to 0.875
- w_router: bfloat16 [768, 33], replicated, may hold values from -0.15625 to 0.15625
- norm_gains: float32 [2, 768], replicated, may hold values from 0.5 to 1.5
- frozen_in: bfloat16 [768, 3072], replicated, may hold values from -0.21875 to 0.21875
- frozen_out: bfloat16 [3072, 768], replicated, may hold values from -0.109375 to 0.109375
- new_in: bfloat16 [32, 768, 3072], P('expert', 'dp'), may hold values from -0.21875 to 0.21875
- new_out: bfloat16 [32, 3072, 768], P('expert', 'dp'), may hold values from -0.109375 to 0.109375
- dense_master: float32 [2392064], P(('dp', 'expert'))
- dense_first: float32 [2392064], P(('dp', 'expert'))
- dense_second: float32 [2392064], P(('dp', 'expert')), as said below
- master_in: float32 [32, 768, 3072], P('expert', 'dp'), may hold values from -0.4375 to 0.4375
- first_in: float32 [32, 768, 3072], P('expert', 'dp'), may hold values from -32 to 32
- second_in: float32 [32, 768, 3072], P('expert', 'dp'), may hold values from 28.597527 to 114.39011
- master_out: float32 [32, 3072, 768], P('expert', 'dp'), may hold values from -0.4375 to 0.4375
- first_out: float32 [32, 3072, 768], P('expert', 'dp'), may hold values from -80 to 80
- second_out: float32 [32, 3072, 768], P('expert', 'dp'), may hold values from 178.73454 to 714.9382
Outputs:
- activations: bfloat16 [32768, 768], P(('dp', 'expert'))
- input_grad: float32 [32768, 768], P(('dp', 'expert'))
- dense_master_new: float32 [2392064], P(('dp', 'expert'))
- dense_first_new: float32 [2392064], P(('dp', 'expert'))
- dense_second_new: float32 [2392064], P(('dp', 'expert'))
- dense_copy: bfloat16 [2392064], P(('dp', 'expert'))
- in_master_new: float32 [32, 768, 3072], P('expert', 'dp')
- in_first_new: float32 [32, 768, 3072], P('expert', 'dp')
- in_second_new: float32 [32, 768, 3072], P('expert', 'dp')
- in_copy: bfloat16 [32, 768, 3072], P('expert', 'dp')
- out_master_new: float32 [32, 3072, 768], P('expert', 'dp')
- out_first_new: float32 [32, 3072, 768], P('expert', 'dp')
- out_second_new: float32 [32, 3072, 768], P('expert', 'dp')
- out_copy: bfloat16 [32, 3072, 768], P('expert', 'dp')
The draws below stay inside these ranges and needn't reach their ends.
Inputs may be any that keep to these rules, and one draw needn't show every extreme that they name: `routes`: in the 256 rows of one device no expert is named by more than 24 rows, and in every draw some expert is named by exactly 24 rows of some device; a row names two different experts. `segment_ids`: ids never fall along a row; an id covers 1 to 128 positions, some id exactly that many. `dense_second`: every entry is positive.
All inputs are finite; a program needn't handle non-finite values.
Results may differ from the reference program's by a relative error of at most 0.018.
Values may be sent and summed in bfloat16 or wider, within the bound.
No kernel may reach another device: no remote copies, remote signals or barrier semaphores. Data moves between devices by JAX's collectives and lax.ppermute only.
A program may use at most 192 MiB of HBM per device.

```python
import math
import jax
import jax.numpy as jnp
import numpy as np
from jax import lax

HEADS = 12
HEAD_DIM = 64
MODEL_DIMENSION = 768
FF = 3072
TOKENS_PER_UNIT = 256
SEGS = 4
STEP = 5
NEW = 32
NEXP = 33
CAP = 24
SEQUENCE_COUNT = 128
TOKENS = 32768
PDENSE = 2392064
N_DP = 4
N_EXPERT = 32


def dense_layout(count):
    positions = jnp.arange(count)
    qkv_end = 3 * MODEL_DIMENSION * MODEL_DIMENSION
    attn_end = qkv_end + MODEL_DIMENSION * MODEL_DIMENSION
    router_end = attn_end + MODEL_DIMENSION * NEXP
    gain_end = router_end + 2 * MODEL_DIMENSION
    grad_scale = jnp.where(positions < qkv_end, 0.7 * TOKENS ** 0.5, jnp.where(positions < attn_end, 0.25 * TOKENS ** 0.5, jnp.where(positions < router_end, 6.0 * (2.0 * TOKENS / NEXP) ** 0.5, 0.8 * TOKENS ** 0.5)))
    is_gain = (positions >= router_end) & (positions < gain_end)
    return (grad_scale.astype(jnp.float32), is_gain)


def draw_dense_master(key, part):
    key = jax.random.fold_in(key, 11)
    grad_scale, is_gain = dense_layout(PDENSE)
    noise = jax.random.normal(key, (PDENSE,), jnp.float32)
    return jnp.where(is_gain, 1.0 + 0.1 * noise, 0.03 * noise).astype(jnp.float32)


def draw_dense_first(key, part):
    key = jax.random.fold_in(key, 12)
    grad_scale, is_gain = dense_layout(PDENSE)
    sign_key, size_key = jax.random.split(key)
    signs = 2.0 * jax.random.randint(sign_key, (PDENSE,), 0, 2).astype(jnp.float32) - 1.0
    sizes = jax.random.uniform(size_key, (PDENSE,), jnp.float32, 0.5, 1.5)
    return (grad_scale * signs * sizes).astype(jnp.float32)


def draw_dense_second(key, part):
    key = jax.random.fold_in(key, 13)
    grad_scale, is_gain = dense_layout(PDENSE)
    factor = jnp.exp(jax.random.uniform(key, (PDENSE,), jnp.float32, 0.0, math.log(4.0)))
    return (grad_scale * grad_scale * factor).astype(jnp.float32)


def steps_of(own_key, dims, cuts, smallest, high):
    factor_of = 1.0
    for axis_at, blocks in cuts:
        heights = jax.random.uniform(jax.random.fold_in(jax.random.fold_in(own_key, 6), axis_at), (blocks,), jnp.float32, smallest / len(cuts), high / len(cuts))
        factor_of = factor_of * jnp.repeat(jnp.exp(heights), dims[axis_at] // blocks).reshape((-1,) + (1,) * (len(dims) - 1 - axis_at))
    return factor_of


def split_up(count, total, limit, skew):
    loads = [(1 << 20) // math.isqrt(rank ** skew) + 1 for rank in range(2, count + 1)]
    surplus, counts = total - limit - (count - 1), [1] * (count - 1)
    while surplus > 0:
        free = [i for i in range(count - 1) if counts[i] < limit]
        pool, budget = sum([loads[i] for i in free]), surplus
        for i in free:
            addition = min(limit - counts[i], max(1, budget * loads[i] // pool), surplus)
            counts[i] = counts[i] + addition
            surplus = surplus - addition
    return np.array([limit] + counts)


def uneven_parts(rng, amount, total, limit, lean):
    if amount == 2:
        one = jax.random.randint(rng, (), max(1, total - limit), min(limit, total - 1) + 1)
        return jnp.stack([one, total - one])
    sizes = jnp.asarray(split_up(amount, total, limit, lean), jnp.int32)
    couples = (amount - 1) // 2
    source_of, taker = sizes[1:1 + 2 * couples:2], sizes[2:2 + 2 * couples:2]
    margin = jnp.minimum(source_of - 1, limit - taker)
    shifted = jax.random.randint(jax.random.fold_in(rng, 1), (couples,), 0, 1 << 20) % (margin + 1)
    sizes = sizes.at[1:1 + 2 * couples:2].set(source_of - shifted).at[2:2 + 2 * couples:2].set(taker + shifted)
    return sizes[jax.random.permutation(jax.random.fold_in(rng, 2), amount)]


def deal_out(rng, own, number, rows, amount, top, most, slope):
    order = jax.random.permutation(rng, amount)
    crowded, usual = load_shares(amount, rows * top, most, slope, True), load_shares(amount, rows * top, most, slope, False)
    places = jnp.arange(amount)

    def named(sizes, rotation):
        used = int((sizes > 0).sum())
        fixed = max(1, used // 4)
        passed = fixed + (places - fixed + rotation * (used - fixed)) % max(1, amount - fixed)
        return jnp.zeros((amount,), jnp.int32).at[order[jnp.where(places < fixed, places, passed)]].set(jnp.asarray(sizes, jnp.int32))

    sizes = jnp.where(number % 4 == 0, named(crowded, number // 4), named(usual, number - number // 4 - 1))
    mixed = jax.random.permutation(jax.random.fold_in(own, 3), amount)
    giver, taker = mixed[0:amount // 2 * 2:2], mixed[1:amount // 2 * 2:2]
    slack = jnp.minimum(sizes[giver] - 1, most - sizes[taker]) // 2
    slack = jnp.where((giver == order[0]) | (taker == order[0]) | (sizes[taker] == 0), 0, jnp.maximum(slack, 0))
    passed = jax.random.randint(jax.random.fold_in(own, 4), (amount // 2,), 0, 1 << 20) % (slack + 1)
    sizes = sizes.at[giver].add(-passed).at[taker].add(passed)
    items = jnp.searchsorted(jnp.cumsum(sizes), jnp.arange(rows * top), side="right").astype(jnp.int32)
    listing = items.reshape(top, rows).T
    listing = listing[jax.random.permutation(jax.random.fold_in(own, 1), rows)]
    rotation = jax.random.randint(jax.random.fold_in(own, 2), (rows, 1), 0, top)
    return jnp.take_along_axis(listing, (jnp.arange(top)[None, :] + rotation) % top, axis=1)


def load_shares(amount, total, reach, skew, full):
    portions = [(1 << 20) // math.isqrt(rank ** skew) + 1 for rank in range(1, amount + 1)]
    largest = reach if full else min(reach, max(-(-total // amount), total * portions[0] // sum(portions)))
    least = 1 if total - largest >= amount - 1 else 0
    counts, spare = [largest] + [least] * (amount - 1), total - largest - least * (amount - 1)
    while spare > 0:
        candidates = [i for i in range(1, amount) if counts[i] < largest] or [i for i in range(1, amount) if counts[i] < reach]
        mass, left = sum([portions[i] for i in candidates]), spare
        for i in candidates:
            more = min(reach - counts[i], max(1, left * portions[i] // mass), spare)
            counts[i] = counts[i] + more
            spare = spare - more
    return np.array(counts)


def normal_values(stream_key, shape, width, bound, cuts=(), held_as=jnp.bfloat16):
    gain = steps_of(stream_key, shape, cuts, -0.22, 0.18) if cuts else 1.0
    array = jax.random.normal(stream_key, shape, jnp.float32) * width * gain
    return jnp.minimum(jnp.maximum(array, -bound), bound).astype(held_as)


def setup_inputs(seed: int = 0) -> dict:
    key_list = jax.random.split(jax.random.key(seed), 22)
    tokens = normal_values(key_list[0], (TOKENS, MODEL_DIMENSION), 1.0, 6.0, ((0, 128),))
    segment_ids = jax.vmap(lambda own: jnp.searchsorted(jnp.cumsum(uneven_parts(own, SEGS, TOKENS_PER_UNIT, TOKENS_PER_UNIT // 2, 2)), jnp.arange(TOKENS_PER_UNIT), side="right"))(jax.random.split(key_list[1], SEQUENCE_COUNT)).reshape((SEQUENCE_COUNT, TOKENS_PER_UNIT)).astype(jnp.int32)
    routes_keys = jax.random.split(jax.random.fold_in(key_list[2], 1), TOKENS // TOKENS_PER_UNIT)
    routes_turns = jax.random.permutation(jax.random.fold_in(key_list[2], 3), TOKENS // TOKENS_PER_UNIT)
    routes = jax.vmap(lambda own, number: deal_out(jax.random.fold_in(key_list[2], 2), own, number, TOKENS_PER_UNIT, NEXP, 2, CAP, 2))(routes_keys, routes_turns).reshape((TOKENS, 2))
    cotangent = normal_values(key_list[3], (TOKENS, MODEL_DIMENSION), 1.0, 6.0, ((0, 128),))
    w_qkv = normal_values(key_list[4], (MODEL_DIMENSION, 3 * MODEL_DIMENSION), MODEL_DIMENSION ** -0.5, 0.21875)
    w_attn_out = normal_values(key_list[5], (MODEL_DIMENSION, MODEL_DIMENSION), (MODEL_DIMENSION // 16) ** -0.5, 0.875)
    w_router = normal_values(key_list[6], (MODEL_DIMENSION, NEXP), (2 * MODEL_DIMENSION) ** -0.5, 0.15625)
    norm_gains = jnp.clip(1.0 + 0.1 * jax.random.normal(key_list[7], (2, MODEL_DIMENSION), jnp.float32), 0.5, 1.5)
    frozen_in = normal_values(key_list[8], (MODEL_DIMENSION, FF), MODEL_DIMENSION ** -0.5, 0.21875)
    frozen_out = normal_values(key_list[9], (FF, MODEL_DIMENSION), FF ** -0.5, 0.109375)
    new_in = normal_values(key_list[10], (NEW, MODEL_DIMENSION, FF), MODEL_DIMENSION ** -0.5, 0.21875, ((0, 32), (1, 4)))
    new_out = normal_values(key_list[11], (NEW, FF, MODEL_DIMENSION), FF ** -0.5, 0.109375, ((0, 32), (1, 4)))
    dense_master = draw_dense_master(jax.random.fold_in(key_list[21], 71), 0)
    dense_first = draw_dense_first(jax.random.fold_in(key_list[21], 71), 0)
    dense_second = draw_dense_second(jax.random.fold_in(key_list[21], 71), 0)
    master_in = normal_values(key_list[15], (NEW, MODEL_DIMENSION, FF), 0.03, 0.4375, ((0, 32), (1, 4)), jnp.float32)
    first_in = normal_values(key_list[16], (NEW, MODEL_DIMENSION, FF), (0.12 * (2 * TOKENS / NEXP) ** 0.5), 32.0, ((0, 32), (1, 4)), jnp.float32)
    second_in = jnp.clip(jnp.exp(math.log(114.39011) - 1.3862944 * jax.random.uniform(key_list[17], (NEW, MODEL_DIMENSION, FF), jnp.float32) ** steps_of(key_list[17], (NEW, MODEL_DIMENSION, FF), ((0, 32), (1, 4)), -0.2, 0.2)), 28.597527, 114.39011)
    master_out = normal_values(key_list[18], (NEW, FF, MODEL_DIMENSION), 0.03, 0.4375, ((0, 32), (1, 4)), jnp.float32)
    first_out = normal_values(key_list[19], (NEW, FF, MODEL_DIMENSION), (0.3 * (2 * TOKENS / NEXP) ** 0.5), 80.0, ((0, 32), (1, 4)), jnp.float32)
    second_out = jnp.clip(jnp.exp(math.log(714.9382) - 1.3862944 * jax.random.uniform(key_list[20], (NEW, FF, MODEL_DIMENSION), jnp.float32) ** steps_of(key_list[20], (NEW, FF, MODEL_DIMENSION), ((0, 32), (1, 4)), -0.2, 0.2)), 178.73454, 714.9382)
    return dict(tokens=tokens, segment_ids=segment_ids, routes=routes, cotangent=cotangent, w_qkv=w_qkv, w_attn_out=w_attn_out, w_router=w_router, norm_gains=norm_gains, frozen_in=frozen_in, frozen_out=frozen_out, new_in=new_in, new_out=new_out, dense_master=dense_master, dense_first=dense_first, dense_second=dense_second, master_in=master_in, first_in=first_in, second_in=second_in, master_out=master_out, first_out=first_out, second_out=second_out)


highest_precision = lax.Precision.HIGHEST
norm_eps = 1e-05
learn_rate = 0.02
beta_first = 0.5
beta_second = 0.5
adam_eps = 1e-08
decay_rate = 0.1

@jax.custom_vjp
def low(v):
    return lax.optimization_barrier(v.astype(jnp.bfloat16)).astype(jnp.float32)

@jax.custom_vjp
def lowered_backward(v):
    return v

def low_keep(v):
    return (low(v), None)

def low_pass(kept, grad):
    return (grad,)

def back_keep(v):
    return (v, None)

def back_low(kept, grad):
    return (low(grad),)
low.defvjp(low_keep, low_pass)
lowered_backward.defvjp(back_keep, back_low)

def product(left, right):
    return jnp.dot(left, right, precision=highest_precision, preferred_element_type=jnp.float32)

def layer_norm(values, gain_row):
    centered = values - lax.optimization_barrier(jnp.mean(values, axis=-1, keepdims=True))
    variance = lax.optimization_barrier(jnp.mean(centered * centered, axis=-1, keepdims=True))
    return centered * lax.rsqrt(variance + norm_eps) * gain_row

def attend_sequence(packed):
    qkv_rows, segment_row = packed
    seq_length = qkv_rows.shape[0]
    queries = qkv_rows[:, :MODEL_DIMENSION].reshape(seq_length, HEADS, HEAD_DIM)
    key_rows = qkv_rows[:, MODEL_DIMENSION:2 * MODEL_DIMENSION].reshape(seq_length, HEADS, HEAD_DIM)
    value_rows = qkv_rows[:, 2 * MODEL_DIMENSION:].reshape(seq_length, HEADS, HEAD_DIM)
    scores = lowered_backward(jnp.einsum('thd,shd->hts', queries, key_rows, precision=highest_precision) * HEAD_DIM ** (-0.5))
    positions = jnp.arange(seq_length)
    allowed = (positions[:, None] >= positions[None, :]) & (segment_row[:, None] == segment_row[None, :])
    scores = jnp.where(allowed[None], scores, -1e+30)
    probs_full = jnp.exp(scores - jax.nn.logsumexp(scores, axis=-1, keepdims=True))
    mixed_out = jnp.einsum('hts,shd->thd', low(probs_full), value_rows, precision=highest_precision)
    return mixed_out.reshape(seq_length, MODEL_DIMENSION)

def expert_apply(row_block, weight_in, weight_out):
    pre_act = lowered_backward(product(row_block, weight_in))
    hidden = low(jax.nn.gelu(pre_act, approximate=False))
    return lowered_backward(low(product(hidden, weight_out)))

def expert_groups(packed):
    row_block, weight_in, weight_out = packed
    copies_in = lowered_backward(jnp.broadcast_to(weight_in, (N_DP,) + weight_in.shape))
    copies_out = lowered_backward(jnp.broadcast_to(weight_out, (N_DP,) + weight_out.shape))
    pre_act = lowered_backward(jnp.einsum('grd,gdf->grf', row_block, copies_in, precision=highest_precision))
    hidden = low(jax.nn.gelu(pre_act, approximate=False))
    return lowered_backward(low(jnp.einsum('grf,gfd->grd', hidden, copies_out, precision=highest_precision)))

def slot_numbers(route_rows):
    flat_routes = route_rows.reshape(route_rows.shape[0], -1)
    onehot = (flat_routes[..., None] == jnp.arange(NEXP, dtype=jnp.int32)).astype(jnp.int32)
    before = jnp.cumsum(onehot, axis=1) - onehot
    return lax.optimization_barrier(jnp.sum(before * onehot, axis=-1)).reshape(route_rows.shape)

def frozen_block(row_block, frozen_one, frozen_two):
    return expert_apply(row_block, frozen_one, frozen_two)

def forward(inputs, w_qkv, w_attn_out, w_router, norm_gains, new_in, new_out, frozen_one, frozen_two, segment_ids, routes):
    normed = layer_norm(inputs, norm_gains[0])
    qkv = lowered_backward(low(product(low(normed), w_qkv)))
    mixed_out = lax.map(jax.checkpoint(attend_sequence), (qkv.reshape(SEQUENCE_COUNT, TOKENS_PER_UNIT, 3 * MODEL_DIMENSION), segment_ids))
    mixed_out = lowered_backward(low(mixed_out.reshape(TOKENS, MODEL_DIMENSION)))
    middle = inputs + lowered_backward(product(mixed_out, w_attn_out))
    feedforward_input = low(layer_norm(middle, norm_gains[1]))
    logits = lowered_backward(product(feedforward_input, w_router))
    route_rows = routes.reshape(SEQUENCE_COUNT, TOKENS_PER_UNIT, 2)
    picked = (route_rows[..., None] == jnp.arange(NEXP, dtype=jnp.int32)).astype(jnp.float32)
    chosen = jnp.einsum('sle,slke->slk', logits.reshape(SEQUENCE_COUNT, TOKENS_PER_UNIT, NEXP), picked, precision=highest_precision)
    gate_values = jax.nn.softmax(chosen, axis=-1)
    places = route_rows * CAP + slot_numbers(route_rows)
    select_rows = (places[..., None] == jnp.arange(NEXP * CAP, dtype=jnp.int32)).astype(jnp.float32)
    state_buffers = lowered_backward(jnp.einsum('fjvu,fjc->fuc', select_rows, feedforward_input.reshape(SEQUENCE_COUNT, TOKENS_PER_UNIT, MODEL_DIMENSION), precision=highest_precision))
    state_buffers = state_buffers.reshape(SEQUENCE_COUNT, NEXP, CAP, MODEL_DIMENSION)
    frozen_result = jax.checkpoint(frozen_block)(state_buffers[:, 0].reshape(SEQUENCE_COUNT * CAP, MODEL_DIMENSION), frozen_one, frozen_two)
    new_rows = jnp.transpose(state_buffers[:, 1:], (1, 0, 2, 3)).reshape(NEW, N_DP, N_EXPERT * CAP, MODEL_DIMENSION)
    new_result = lax.map(jax.checkpoint(expert_groups), (new_rows, new_in, new_out))
    new_result = jnp.transpose(new_result.reshape(NEW, SEQUENCE_COUNT, CAP, MODEL_DIMENSION), (1, 0, 2, 3))
    results = jnp.concatenate([frozen_result.reshape(SEQUENCE_COUNT, 1, CAP, MODEL_DIMENSION), new_result], axis=1)
    results = results.reshape(SEQUENCE_COUNT, NEXP * CAP, MODEL_DIMENSION)
    returned = jnp.einsum('slkp,spd->slkd', select_rows, results, precision=highest_precision)
    combined = lax.optimization_barrier(jnp.sum(gate_values[..., None] * returned, axis=2))
    return middle + combined.reshape(TOKENS, MODEL_DIMENSION)

def adamw(master, first, second, grad):
    first_new = beta_first * first + (1.0 - beta_first) * grad
    second_new = beta_second * second + (1.0 - beta_second) * grad * grad
    first_hat = first_new / (1.0 - beta_first ** STEP)
    second_hat = second_new / (1.0 - beta_second ** STEP)
    master_new = master - learn_rate * (first_hat / (jnp.sqrt(second_hat) + adam_eps) + decay_rate * master)
    return (master_new, first_new, second_new, master_new.astype(jnp.bfloat16))

def reference(tokens, segment_ids, routes, cotangent, w_qkv, w_attn_out, w_router, norm_gains, frozen_in, frozen_out, new_in, new_out, dense_master, dense_first, dense_second, master_in, first_in, second_in, master_out, first_out, second_out):
    frozen_one = frozen_in.astype(jnp.float32)
    frozen_two = frozen_out.astype(jnp.float32)

    def differentiable(inputs, qkv_weight, attn_weight, router_weight, gain_rows, expert_in, expert_out):
        return forward(inputs, qkv_weight, attn_weight, router_weight, gain_rows, expert_in, expert_out, frozen_one, frozen_two, segment_ids, routes)
    outputs, pullback = jax.vjp(differentiable, tokens.astype(jnp.float32), w_qkv.astype(jnp.float32), w_attn_out.astype(jnp.float32), w_router.astype(jnp.float32), norm_gains, new_in.astype(jnp.float32), new_out.astype(jnp.float32))
    grads = pullback(cotangent.astype(jnp.float32))
    flat_grad = jnp.concatenate([grads[1].reshape(-1), grads[2].reshape(-1), grads[3].reshape(-1), grads[4].reshape(-1)])
    flat_grad = jnp.concatenate([flat_grad, jnp.zeros((PDENSE - flat_grad.shape[0],), jnp.float32)])
    dense_new = adamw(dense_master, dense_first, dense_second, flat_grad)
    in_new = adamw(master_in, first_in, second_in, grads[5])
    out_new = adamw(master_out, first_out, second_out, grads[6])
    return (outputs.astype(jnp.bfloat16), grads[0], dense_new[0], dense_new[1], dense_new[2], dense_new[3], in_new[0], in_new[1], in_new[2], in_new[3], out_new[0], out_new[1], out_new[2], out_new[3])
```

```python
import jax
import jax.numpy as jnp
from jax import lax
from jax.sharding import Mesh
from jax.sharding import PartitionSpec as P

HEAD_DIM = 64
STEP = 5


norm_eps = 1e-05
learn_rate = 0.02
beta_first = 0.5
beta_second = 0.5
adam_eps = 1e-08
decay_rate = 0.1


def layer_norm(values, gain_row):
    centered = values - jnp.mean(values, axis=-1, keepdims=True)
    variance = jnp.mean(centered * centered, axis=-1, keepdims=True)
    return centered * lax.rsqrt(variance + norm_eps) * gain_row


def norm_back(values, gain_row, upstream):
    unused, pullback = jax.vjp(layer_norm, values, gain_row)
    return pullback(upstream)


def exact_gelu(pre_act):
    return jax.nn.gelu(pre_act, approximate=False)


def split_heads(qkv_low):
    seq_length = qkv_low.shape[0]
    model_width = qkv_low.shape[1] // 3
    head_count = model_width // HEAD_DIM
    queries = qkv_low[:, :model_width].reshape(seq_length, head_count, HEAD_DIM)
    key_rows = qkv_low[:, model_width : 2 * model_width].reshape(seq_length, head_count, HEAD_DIM)
    value_rows = qkv_low[:, 2 * model_width :].reshape(seq_length, head_count, HEAD_DIM)
    return (queries, key_rows, value_rows)


def masked_scores(queries, key_rows, segment_row):
    positions = jnp.arange(segment_row.shape[0])
    allowed = (positions[:, None] >= positions[None, :]) & (
        segment_row[:, None] == segment_row[None, :]
    )
    scores = jnp.einsum(
        "thd,shd->hts", queries, key_rows, preferred_element_type=jnp.float32
    ) * HEAD_DIM ** (-0.5)
    return jnp.where(allowed[None], scores, -1e30)


def attention_forward(qkv_low, segment_row):
    queries, key_rows, value_rows = split_heads(qkv_low)
    scores = masked_scores(queries, key_rows, segment_row)
    log_totals = jax.nn.logsumexp(scores, axis=-1, keepdims=True)
    probs_low = jnp.exp(scores - log_totals).astype(jnp.bfloat16)
    mixed_out = jnp.einsum(
        "hts,shd->thd", probs_low, value_rows, preferred_element_type=jnp.float32
    )
    return (mixed_out.reshape(qkv_low.shape[0], -1).astype(jnp.bfloat16), log_totals)


def attention_backward(qkv_low, segment_row, log_totals, grad_mixed):
    queries, key_rows, value_rows = split_heads(qkv_low)
    scores = masked_scores(queries, key_rows, segment_row)
    probs_full = jnp.exp(scores - log_totals)
    grad_heads = grad_mixed.reshape(queries.shape)
    grad_probs = jnp.einsum(
        "thd,shd->hts", grad_heads, value_rows, preferred_element_type=jnp.float32
    )
    grad_values = jnp.einsum(
        "hts,thd->shd",
        probs_full.astype(jnp.bfloat16),
        grad_heads,
        preferred_element_type=jnp.float32,
    )
    row_dots = jnp.sum(probs_full * grad_probs, axis=-1, keepdims=True)
    grad_scores = (probs_full * (grad_probs - row_dots)).astype(jnp.bfloat16)
    grad_queries = jnp.einsum(
        "hts,shd->thd", grad_scores, key_rows, preferred_element_type=jnp.float32
    ) * HEAD_DIM ** (-0.5)
    grad_keys = jnp.einsum(
        "hts,thd->shd", grad_scores, queries, preferred_element_type=jnp.float32
    ) * HEAD_DIM ** (-0.5)
    seq_length = qkv_low.shape[0]
    return jnp.concatenate(
        [
            grad_queries.reshape(seq_length, -1),
            grad_keys.reshape(seq_length, -1),
            grad_values.reshape(seq_length, -1),
        ],
        axis=1,
    )


def expert_forward(row_block, weight_in, weight_out):
    pre_act = jnp.dot(row_block, weight_in, preferred_element_type=jnp.float32)
    hidden = exact_gelu(pre_act).astype(jnp.bfloat16)
    result = jnp.dot(hidden, weight_out, preferred_element_type=jnp.float32).astype(jnp.bfloat16)
    return (pre_act, result)


def expert_backward(pre_act, grad_result, weight_in, weight_out):
    grad_hidden = jnp.einsum(
        "rd,fd->rf", grad_result, weight_out, preferred_element_type=jnp.float32
    )
    hidden, gelu_pull = jax.vjp(exact_gelu, pre_act)
    grad_pre = gelu_pull(grad_hidden)[0].astype(jnp.bfloat16)
    grad_rows = jnp.einsum(
        "rf,df->rd", grad_pre, weight_in, preferred_element_type=jnp.float32
    ).astype(jnp.bfloat16)
    return (hidden.astype(jnp.bfloat16), grad_pre, grad_rows)


def adamw(master, first, second, grad):
    first_new = beta_first * first + (1.0 - beta_first) * grad
    second_new = beta_second * second + (1.0 - beta_second) * grad * grad
    first_hat = first_new / (1.0 - beta_first**STEP)
    second_hat = second_new / (1.0 - beta_second**STEP)
    master_new = master - learn_rate * (
        first_hat / (jnp.sqrt(second_hat) + adam_eps) + decay_rate * master
    )
    return (master_new, first_new, second_new, master_new.astype(jnp.bfloat16))


PLANE = ("zl", "x", "y")
DEPTH = ("zh", "zl")
ALL = ("zh", "zl", "x", "y", "c")


def swap_core(block):
    return lax.ppermute(block, "c", [(0, 1), (1, 0)])


def along_depth(block, step):
    return lax.ppermute(block, DEPTH, [(z, (z + step) % 4) for z in range(4)])


def swap_pair(block):
    return lax.ppermute(block, DEPTH, [(z, 3 - z) for z in range(4)])


def swap_low(block):
    return lax.ppermute(block, "zl", [(0, 1), (1, 0)])


def gather_weight(own_half, mate_half, kind, core, zh, zl):
    by_kind = lambda wanted: jnp.where(wanted == core, own_half, mate_half)
    own = by_kind(kind)
    from_below = along_depth(by_kind(1 - zh), 1)
    from_above = along_depth(by_kind(zh), -1)
    far_side = jnp.where(zl == 0, from_above, from_below)
    near_side = jnp.where(zl == 0, from_below, from_above)
    across = swap_pair(far_side)
    z = 2 * zh + zl
    rows = own.shape[0]
    full = jnp.zeros((4 * rows, own.shape[1]), own.dtype)
    for block, place in ((own, z), (far_side, z ^ 1), (near_side, 3 - z), (across, (3 - z) ^ 1)):
        full = lax.dynamic_update_slice(full, block, (place * rows, 0))
    return full


def reduce_weight(partial, core, kind, zh, zl):
    rows = partial.shape[0] // 4
    away = lax.dynamic_slice(partial, ((1 - zh) * 2 * rows, 0), (2 * rows, partial.shape[1]))
    kept = lax.dynamic_slice(partial, (zh * 2 * rows, 0), (2 * rows, partial.shape[1]))
    kept = kept + swap_pair(away.astype(jnp.bfloat16)).astype(jnp.float32)
    mine = lax.dynamic_slice(kept, (zl * rows, 0), (rows, kept.shape[1]))
    other = lax.dynamic_slice(kept, ((1 - zl) * rows, 0), (rows, kept.shape[1]))
    other = swap_low(other.astype(jnp.bfloat16)).astype(jnp.float32)
    stays = jnp.where(kind == core, mine, other)
    leaves = jnp.where(kind == core, other, mine)
    arrived = swap_core(leaves.astype(jnp.bfloat16)).astype(jnp.float32)
    first = jnp.where(core == 0, stays, arrived)
    second = jnp.where(core == 0, arrived, stays)
    return first, second


def scatter_axis(blocks, axis):
    here = lax.axis_index(axis)
    total = lax.dynamic_index_in_dim(blocks, here, 0, keepdims=False)
    for step in (1, 3, 2):
        there = lax.rem(here + step, 4)
        leaving = lax.dynamic_index_in_dim(blocks, there, 0, keepdims=False).astype(jnp.bfloat16)
        moves = [(i, (i + step) % 4) for i in range(4)]
        total = total + lax.ppermute(leaving, axis, moves).astype(jnp.float32)
    return total


def scatter_dense(flat, core):
    rows = flat.shape[0] // (128 * 128)
    blocks = flat.reshape(64, 2, rows, 128)
    kept = lax.dynamic_index_in_dim(blocks, core, 1, keepdims=False)
    away = lax.dynamic_index_in_dim(blocks, 1 - core, 1, keepdims=False)
    kept = kept + swap_core(away.astype(jnp.bfloat16)).astype(jnp.float32)
    kept = kept.reshape(4, 4, 4, rows, 128)
    cut = 80
    one = kept[:, :, :, :cut]
    two = kept[:, :, :, cut:]
    one = scatter_axis(jnp.moveaxis(one, 1, 0), "x")
    two = scatter_axis(jnp.moveaxis(two, 2, 0), "y")
    one = scatter_axis(jnp.moveaxis(one, 1, 0), "y")
    two = scatter_axis(jnp.moveaxis(two, 1, 0), "x")
    both = jnp.concatenate([one, two], axis=1)
    return scatter_axis(both, DEPTH).reshape(-1)


def body(
    tokens,
    segment_ids,
    routes,
    cotangent,
    w_qkv,
    w_attn_out,
    w_router,
    norm_gains,
    frozen_in,
    frozen_out,
    new_in,
    new_out,
    dense_master,
    dense_first,
    dense_second,
    master_in,
    first_in,
    second_in,
    master_out,
    first_out,
    second_out,
):
    token_count, model_width = tokens.shape
    hidden_width = frozen_in.shape[1]
    block_width = hidden_width // 8
    expert_total = w_router.shape[1]
    capacity = 3 * token_count // expert_total + 1
    core, zh, zl = (lax.axis_index(a) for a in ("c", "zh", "zl"))
    kind = zh ^ zl

    in_blocks = new_in[0].reshape(-1, 4, 2, block_width)
    in_halves = [in_blocks[:, :, h].reshape(-1, 4 * block_width) for h in range(2)]
    out_halves = [new_out[0][h * block_width : (h + 1) * block_width] for h in range(2)]
    pick = lambda halves, which: jnp.where(which == 0, halves[0], halves[1])
    in_mate = swap_core(pick(in_halves, 1 - core))
    out_mate = swap_core(pick(out_halves, 1 - core))
    half_in = gather_weight(pick(in_halves, core), in_mate, kind, core, zh, zl)
    half_out = gather_weight(pick(out_halves, core), out_mate, kind, core, zh, zl)

    inputs = tokens.astype(jnp.float32)
    attn_in = layer_norm(inputs, norm_gains[0]).astype(jnp.bfloat16)
    qkv_low = jnp.dot(attn_in, w_qkv, preferred_element_type=jnp.float32).astype(jnp.bfloat16)
    mixed_low, log_totals = attention_forward(qkv_low, segment_ids[0])
    middle = inputs + jnp.dot(mixed_low, w_attn_out, preferred_element_type=jnp.float32)
    feedforward_input = layer_norm(middle, norm_gains[1]).astype(jnp.bfloat16)
    logits = jnp.dot(feedforward_input, w_router, preferred_element_type=jnp.float32)
    expert_ids = jnp.arange(expert_total, dtype=jnp.int32)
    picked = (routes[:, :, None] == expert_ids[None, None, :]).astype(jnp.float32)
    chosen = jnp.sum(picked * logits[:, None, :], axis=-1)
    gate_values = jax.nn.softmax(chosen, axis=-1)
    flat_routes = routes.reshape(-1)
    onehot = (flat_routes[:, None] == expert_ids[None, :]).astype(jnp.int32)
    before = jnp.cumsum(onehot, axis=0) - onehot
    new_ids = flat_routes - 1
    ordered = jnp.where(
        flat_routes == 0, 0, 1 + 16 * ((new_ids & 1) ^ zh) + jnp.right_shift(new_ids, 1)
    )
    places = ordered * capacity + jnp.sum(before * onehot, axis=1)
    select_rows = (
        places[:, None] == jnp.arange(expert_total * capacity, dtype=jnp.int32)[None, :]
    ).astype(jnp.bfloat16)
    select_rows = select_rows.reshape(token_count, 2, expert_total * capacity)
    state_buffers = jnp.einsum(
        "lkp,ld->pd", select_rows, feedforward_input, preferred_element_type=jnp.float32
    ).astype(jnp.bfloat16)
    state_buffers = state_buffers.reshape(expert_total, capacity, model_width)
    upstream = cotangent.astype(jnp.float32)
    grad_pairs = (gate_values[:, :, None] * upstream[:, None, :]).astype(jnp.bfloat16)
    grad_results = jnp.einsum(
        "lkp,lkd->pd", select_rows, grad_pairs, preferred_element_type=jnp.float32
    ).astype(jnp.bfloat16)
    grad_results = grad_results.reshape(expert_total, capacity, model_width)

    exchange = lambda v: lax.all_to_all(v, PLANE, split_axis=0, concat_axis=0, tiled=True)
    received = exchange(state_buffers[1:]).reshape(-1, model_width)
    grad_received = exchange(grad_results[1:]).reshape(-1, model_width)
    row_count = received.shape[0]
    rows = jnp.concatenate([received, swap_core(received)], axis=0)
    grad_rows_in = jnp.concatenate([grad_received, swap_core(grad_received)], axis=0)

    def merge(partial):
        mate = swap_core(partial[row_count:].astype(jnp.bfloat16)).astype(jnp.float32)
        whole = (partial[:row_count] + mate).astype(jnp.bfloat16)
        return exchange(whole.reshape(-1, capacity, model_width))

    pre_act = jnp.dot(rows, half_in, preferred_element_type=jnp.float32)
    new_hidden, gelu_pull = jax.vjp(exact_gelu, pre_act)
    new_hidden = new_hidden.astype(jnp.bfloat16)
    grad_hidden = jnp.einsum("rd,fd->rf", grad_rows_in, half_out, preferred_element_type=jnp.float32)
    new_grad_pre = gelu_pull(grad_hidden)[0].astype(jnp.bfloat16)
    grad_out_half = jnp.einsum(
        "rf,rd->fd", new_hidden, grad_rows_in, preferred_element_type=jnp.float32
    )
    out_first_half, out_second_half = reduce_weight(grad_out_half, core, kind, zh, zl)
    grad_back = merge(
        jnp.einsum("rf,df->rd", new_grad_pre, half_in, preferred_element_type=jnp.float32)
    )
    sent_back = merge(jnp.dot(new_hidden, half_out, preferred_element_type=jnp.float32))
    grad_in_half = jnp.einsum("rd,rf->df", rows, new_grad_pre, preferred_element_type=jnp.float32)
    in_first_half, in_second_half = reduce_weight(grad_in_half, core, kind, zh, zl)
    grad_out_shard = jnp.concatenate([out_first_half, out_second_half], axis=0)
    grad_in_shard = jnp.stack(
        [
            in_first_half.reshape(-1, 4, block_width),
            in_second_half.reshape(-1, 4, block_width),
        ],
        axis=2,
    ).reshape(-1, hidden_width)

    frozen_pre, frozen_result = expert_forward(state_buffers[0], frozen_in, frozen_out)
    frozen_parts = expert_backward(frozen_pre, grad_results[0], frozen_in, frozen_out)

    results = jnp.concatenate([frozen_result[None], sent_back], axis=0).reshape(
        expert_total * capacity, model_width
    )
    pair_values = jnp.einsum(
        "lkp,pd->lkd", select_rows, results, preferred_element_type=jnp.float32
    )
    activations = middle + jnp.sum(gate_values[:, :, None] * pair_values, axis=1)
    grad_gates = jnp.sum(upstream[:, None, :] * pair_values, axis=-1)
    grad_chosen = gate_values * (
        grad_gates - jnp.sum(gate_values * grad_gates, axis=-1, keepdims=True)
    )
    grad_logits = jnp.sum(picked * grad_chosen[:, :, None], axis=1).astype(jnp.bfloat16)
    router_grad = jnp.einsum(
        "ld,le->de", feedforward_input, grad_logits, preferred_element_type=jnp.float32
    )
    grad_ffn = jnp.einsum("le,de->ld", grad_logits, w_router, preferred_element_type=jnp.float32)
    grad_buffers = jnp.concatenate([frozen_parts[2][None], grad_back], axis=0).reshape(
        -1, model_width
    )
    grad_ffn = grad_ffn + jnp.einsum(
        "lkp,pd->ld", select_rows, grad_buffers, preferred_element_type=jnp.float32
    )
    grad_middle_norm, gain_ffn_grad = norm_back(middle, norm_gains[1], grad_ffn)
    grad_middle = upstream + grad_middle_norm
    grad_branch = grad_middle.astype(jnp.bfloat16)
    attn_out_grad = jnp.einsum(
        "ld,le->de", mixed_low, grad_branch, preferred_element_type=jnp.float32
    )
    grad_mixed = jnp.einsum(
        "le,de->ld", grad_branch, w_attn_out, preferred_element_type=jnp.float32
    ).astype(jnp.bfloat16)
    grad_qkv = attention_backward(qkv_low, segment_ids[0], log_totals, grad_mixed).astype(
        jnp.bfloat16
    )
    qkv_grad = jnp.einsum("ld,le->de", attn_in, grad_qkv, preferred_element_type=jnp.float32)
    grad_attn_norm = jnp.einsum("le,de->ld", grad_qkv, w_qkv, preferred_element_type=jnp.float32)
    grad_input_norm, gain_attn_grad = norm_back(inputs, norm_gains[0], grad_attn_norm)
    input_grad = grad_middle + grad_input_norm
    flat_grad = jnp.concatenate(
        [
            qkv_grad.reshape(-1),
            attn_out_grad.reshape(-1),
            router_grad.reshape(-1),
            gain_attn_grad,
            gain_ffn_grad,
        ]
    )
    flat_grad = jnp.concatenate(
        [flat_grad, jnp.zeros((dense_master.shape[0] * 128 - flat_grad.shape[0],), jnp.float32)]
    )
    dense_grad = scatter_dense(flat_grad, core)
    dense_new = adamw(dense_master, dense_first, dense_second, dense_grad)
    in_new = adamw(master_in, first_in, second_in, grad_in_shard[None])
    out_new = adamw(master_out, first_out, second_out, grad_out_shard[None])
    return (activations.astype(jnp.bfloat16), input_grad) + dense_new + in_new + out_new


def solution(mesh):
    fine = Mesh(mesh.devices.reshape(2, 2, 4, 4, 2), ALL)
    tokens = P(ALL, None)
    flat = P(ALL)
    expert = P(("x", "y", "c"), DEPTH, None)
    return jax.shard_map(
        body,
        mesh=fine,
        in_specs=(tokens,) * 4 + (P(),) * 6 + (expert,) * 2 + (flat,) * 3 + (expert,) * 6,
        out_specs=(tokens,) * 2 + (flat,) * 4 + (expert,) * 8,
        check_vma=False,
    )
```

```python
import math

import jax
import jax.numpy as jnp
from jax import lax
from jax.experimental import pallas as pl
from jax.experimental.pallas import tpu as pltpu
from jax.sharding import Mesh
from jax.sharding import PartitionSpec as P

HEAD_DIM = 64
STEP = 5


norm_eps = 1e-05
learn_rate = 0.02
beta_first = 0.5
beta_second = 0.5
adam_eps = 1e-08
decay_rate = 0.1


PLANE = ("zl", "x", "y")
DEPTH = ("zh", "zl")
ALL = ("zh", "zl", "x", "y", "c")
CAP = 24
PAIRS = 6
EXTRA = 128
VMEM = pl.BlockSpec(memory_space=pltpu.VMEM)
SMEM = pl.BlockSpec(memory_space=pltpu.SMEM)
F32 = jnp.float32
LOW = jnp.bfloat16


def params(**more):
    return pltpu.CompilerParams(vmem_limit_bytes=56 * 1024 * 1024, **more)


def cost(flops, moved):
    return pl.CostEstimate(flops=int(flops), bytes_accessed=int(moved), transcendentals=0)


def mm(left, right):
    return jnp.dot(left, right, preferred_element_type=F32)


def mm_nt(left, right):
    return lax.dot_general(left, right, (((1,), (1,)), ((), ())), preferred_element_type=F32)


def mm_tn(left, right):
    return lax.dot_general(left, right, (((0,), (0,)), ((), ())), preferred_element_type=F32)


def iota(shape, axis):
    return lax.broadcasted_iota(jnp.int32, shape, axis)


def normed(values):
    centered = values - jnp.mean(values, axis=1, keepdims=True)
    scale = lax.rsqrt(jnp.mean(centered * centered, axis=1, keepdims=True) + norm_eps)
    return centered * scale, scale


def norm_backward(values, gain, upstream):
    hat, scale = normed(values)
    gain_grad = jnp.sum(upstream * hat, axis=0, keepdims=True)
    inner = upstream * gain
    mean_inner = jnp.mean(inner, axis=1, keepdims=True)
    mean_hat = jnp.mean(inner * hat, axis=1, keepdims=True)
    return scale * (inner - mean_inner - hat * mean_hat), gain_grad


def as_row(column, eye):
    return jnp.sum(jnp.where(eye, column, jnp.zeros_like(column)), axis=0, keepdims=True)


def attention_mask(segment_row):
    count = segment_row.shape[1]
    down, across = iota((count, count), 0), iota((count, count), 1)
    eye = down == across
    column = jnp.sum(jnp.where(eye, segment_row, 0), axis=1, keepdims=True)
    return (down >= across) & (column == segment_row), eye


def dense_forward_kernel(
    zh_ref, tokens, segments, routes, cotangent, w_qkv, w_out, w_router, gains,
    attn_in_o, qkv_o, mixed_o, lse_o, middle_o, ffn_o, plan_o, rows_o, grads_o, frozen_rows_o, frozen_grads_o,
):
    width = tokens.shape[1]
    count = tokens.shape[0]
    inputs = tokens[...].astype(F32)
    hat, unused = normed(inputs)
    attn_in = (hat * gains[0:1, :]).astype(LOW)
    attn_in_o[...] = attn_in
    qkv_o[...] = mm(attn_in, w_qkv[...]).astype(LOW)
    allowed, eye = attention_mask(segments[...])
    lane = iota((count, 128), 1)
    low_lanes = lane < HEAD_DIM
    lse_all = jnp.zeros((count, 128), F32)
    for pair in range(width // 128):
        at = slice(128 * pair, 128 * pair + 128)
        queries = qkv_o[:, at] * jnp.asarray(HEAD_DIM**-0.5, LOW)
        keys = qkv_o[:, width + 128 * pair : width + 128 * pair + 128]
        values = qkv_o[:, 2 * width + 128 * pair : 2 * width + 128 * pair + 128]
        outs = []
        for half in range(2):
            mine = low_lanes if half == 0 else ~low_lanes
            scores = mm_nt(jnp.where(mine, queries, jnp.zeros_like(queries)), keys)
            scores = jnp.where(allowed, scores, -1e30)
            top = jnp.max(scores, axis=1, keepdims=True)
            raised = jnp.exp(scores - top)
            total = jnp.sum(raised, axis=1, keepdims=True)
            probs = (raised * (1.0 / total)).astype(LOW)
            outs.append(mm(probs, values))
            lse_all = jnp.where(lane == 2 * pair + half, top + jnp.log(total), lse_all)
        mixed_o[:, at] = jnp.where(low_lanes, outs[0], outs[1]).astype(LOW)
    lse_o[...] = lse_all
    middle = inputs + mm(mixed_o[...], w_out[...])
    middle_o[...] = middle
    hat, unused = normed(middle)
    ffn = (hat * gains[1:2, :]).astype(LOW)
    ffn_o[...] = ffn
    logits = mm(ffn, w_router[...])
    experts = iota(logits.shape, 1)
    picks = [experts == routes[:, k : k + 1] for k in range(2)]
    chosen = [jnp.sum(jnp.where(p, logits, 0.0), axis=1, keepdims=True) for p in picks]
    top = jnp.maximum(chosen[0], chosen[1])
    raised = [jnp.exp(c - top) for c in chosen]
    gates = [r / (raised[0] + raised[1]) for r in raised]
    named = (picks[0] | picks[1]).astype(F32).astype(LOW)
    earlier = (iota((count, count), 0) > iota((count, count), 1)).astype(F32).astype(LOW)
    before = mm(earlier, named)
    zh = zh_ref[0]
    new_place, old_place = [], []
    for k in range(2):
        route = routes[:, k : k + 1]
        slot = jnp.sum(jnp.where(picks[k], before, 0.0), axis=1, keepdims=True).astype(jnp.int32)
        fresh = route - 1
        block = 16 * ((fresh & 1) ^ zh) + lax.shift_right_arithmetic(fresh, 1)
        new_place.append(jnp.where(route > 0, block * CAP + slot, -1))
        old_place.append(jnp.where(route > 0, -1, slot))
    columns = gates + [p.astype(F32) for p in new_place + old_place]
    plan = jnp.zeros((count, 128), F32)
    for i, column in enumerate(columns):
        plan = jnp.where(lane == i, column, plan)
    plan_o[...] = plan
    up = cotangent[...].astype(F32)
    scaled = [(g * up).astype(LOW) for g in gates]
    for places, size, rows_ref, grads_ref in (
        (new_place, rows_o.shape[0], rows_o, grads_o),
        (old_place, CAP, frozen_rows_o, frozen_grads_o),
    ):
        slots = iota((size, count), 0)
        spread = [(slots == as_row(p, eye)).astype(F32).astype(LOW) for p in places]
        rows_ref[...] = mm(spread[0] + spread[1], ffn).astype(LOW)
        grads_ref[...] = (mm(spread[0], scaled[0]) + mm(spread[1], scaled[1])).astype(LOW)


def dense_forward(zh, tokens, segments, routes, cotangent, w_qkv, w_out, w_router, gains):
    count, width = tokens.shape
    slots = (w_router.shape[1] - 1) * CAP
    shapes = [
        ((count, width), LOW), ((count, 3 * width), LOW), ((count, width), LOW), ((count, 128), F32),
        ((count, width), F32), ((count, width), LOW), ((count, 128), F32),
        ((slots, width), LOW), ((slots, width), LOW), ((CAP, width), LOW), ((CAP, width), LOW),
    ]
    return pl.pallas_call(
        dense_forward_kernel,
        name="dense_forward",
        out_shape=[jax.ShapeDtypeStruct(s, t) for s, t in shapes],
        in_specs=[SMEM] + [VMEM] * 8,
        out_specs=[VMEM] * len(shapes),
        compiler_params=params(),
        cost_estimate=cost(8e9, 30e6),
    )(zh, tokens, segments, routes, cotangent, w_qkv, w_out, w_router, gains)


def dense_backward_kernel(
    core_ref, plan, routes, segments, cotangent, tokens, middle, mixed, ffn, lse, qkv, attn_in,
    w_qkv, w_out, w_router, gains, back, frozen_back,
    input_grad_o, kept_o, away_o,
    flat, gqkv,
):
    count, width = tokens.shape
    expert_total = w_router.shape[1]
    up = cotangent[...].astype(F32)
    gates = [plan[:, k : k + 1] for k in range(2)]
    new_place = [plan[:, 2 + k : 3 + k].astype(jnp.int32) for k in range(2)]
    old_place = [plan[:, 4 + k : 5 + k].astype(jnp.int32) for k in range(2)]
    allowed, eye = attention_mask(segments[...])

    grad_ffn = jnp.zeros((count, width), F32)
    weighted = [jnp.zeros((count, 1), F32) for k in range(2)]
    for places, ref in ((new_place, back), (old_place, frozen_back)):
        size = ref.shape[0]
        slots = iota((count, size), 1)
        for k in range(2):
            choice = (slots == places[k]).astype(F32).astype(LOW)
            picked = mm(choice, ref[...])
            grad_ffn = grad_ffn + picked[:, :width]
            tail = picked[:, width:]
            weighted[k] = weighted[k] + jnp.sum(tail, axis=1, keepdims=True)
    both = weighted[0] + weighted[1]
    experts = iota((count, expert_total), 1)
    grad_logits = jnp.zeros((count, expert_total), F32)
    for k in range(2):
        grad_logits = jnp.where(
            experts == routes[:, k : k + 1], weighted[k] - gates[k] * both, grad_logits
        )
    grad_logits = grad_logits.astype(LOW)
    grad_ffn = grad_ffn + mm_nt(grad_logits, w_router[...])
    grad_norm, gain_ffn = norm_backward(middle[...], gains[1:2, :], grad_ffn)
    grad_middle = up + grad_norm
    grad_branch = grad_middle.astype(LOW)

    blocks = width // 128
    first_row = 3 * blocks * width
    attn_out_grad = mm_tn(mixed[...], grad_branch)
    for j in range(blocks):
        flat[pl.ds(first_row + j, width, stride=blocks), :] = attn_out_grad[:, 128 * j : 128 * j + 128]
    router_row = first_row + blocks * width
    router_rows = width * expert_total // 128
    padded_logits = jnp.concatenate(
        [grad_logits, jnp.zeros((count, 128 - expert_total), LOW)], axis=1
    )
    router_grad = mm_tn(ffn[...], padded_logits)
    feature = iota((width, 128), 0)
    lane_w = iota((width, 128), 1)
    start = feature * expert_total
    offset = start & 127
    turned = jnp.take_along_axis(router_grad, (lane_w - offset) & 127, axis=1)
    wrapped = lane_w < offset
    row_of = lax.shift_right_logical(iota((router_rows, width), 1) * expert_total, 7)
    row_here = iota((router_rows, width), 0)
    here = (row_of == row_here).astype(F32)
    after = (row_of + 1 == row_here).astype(F32)
    exact = lambda a, b: jnp.dot(a, b, precision=lax.Precision.HIGHEST, preferred_element_type=F32)
    flat[router_row : router_row + router_rows, :] = exact(
        here, jnp.where(wrapped, 0.0, turned)
    ) + exact(after, jnp.where(wrapped, turned, 0.0))
    gain_row = router_row + router_rows

    grad_mixed = mm_nt(grad_branch, w_out[...]).astype(LOW)
    lane = iota((count, 128), 1)
    low_lanes = lane < HEAD_DIM
    scale = HEAD_DIM**-0.5
    for pair in range(blocks):
        at = slice(128 * pair, 128 * pair + 128)
        queries = qkv[:, at] * jnp.asarray(scale, LOW)
        keys = qkv[:, width + 128 * pair : width + 128 * pair + 128]
        values = qkv[:, 2 * width + 128 * pair : 2 * width + 128 * pair + 128]
        grads = grad_mixed[:, at]
        grad_q = jnp.zeros((count, 128), F32)
        grad_k = jnp.zeros((count, 128), F32)
        grad_v = jnp.zeros((count, 128), F32)
        for half in range(2):
            mine = low_lanes if half == 0 else ~low_lanes
            only = lambda v: jnp.where(mine, v, jnp.zeros_like(v))
            q_half, g_half, k_half = only(queries), only(grads), only(keys)
            scores = jnp.where(allowed, mm_nt(q_half, keys), -1e30)
            head = 2 * pair + half
            probs = jnp.exp(scores - lse[:, head : head + 1])
            grad_probs = mm_nt(g_half, values)
            grad_v = grad_v + mm_tn(probs.astype(LOW), g_half)
            dots = jnp.sum(probs * grad_probs, axis=1, keepdims=True)
            grad_scores = (probs * (grad_probs - dots)).astype(LOW)
            grad_q = grad_q + mm(grad_scores, k_half)
            grad_k = grad_k + mm_tn(grad_scores, q_half)
        gqkv[:, at] = (grad_q * scale).astype(LOW)
        gqkv[:, width + 128 * pair : width + 128 * pair + 128] = grad_k.astype(LOW)
        gqkv[:, 2 * width + 128 * pair : 2 * width + 128 * pair + 128] = grad_v.astype(LOW)
    for j in range(0, 3 * blocks, 2):
        piece = mm_tn(attn_in[...], gqkv[:, 128 * j : 128 * j + 256])
        flat[pl.ds(j, width, stride=3 * blocks), :] = piece[:, :128]
        flat[pl.ds(j + 1, width, stride=3 * blocks), :] = piece[:, 128:]
    grad_attn = mm_nt(gqkv[...], w_qkv[...])
    grad_norm, gain_attn = norm_backward(tokens[...].astype(F32), gains[0:1, :], grad_attn)
    input_grad_o[...] = grad_middle + grad_norm
    for j in range(blocks):
        flat[gain_row + j : gain_row + j + 1, :] = gain_attn[:, 128 * j : 128 * j + 128]
        flat[gain_row + blocks + j : gain_row + blocks + j + 1, :] = gain_ffn[:, 128 * j : 128 * j + 128]
    last = gain_row + 2 * blocks
    flat[last:, :] = jnp.zeros((flat.shape[0] - last, 128), F32)

    rows = kept_o.shape[1]
    core = core_ref[0]

    @pl.loop(0, kept_o.shape[0])
    def move(i):
        kept_o[pl.ds(i, 1)] = flat[pl.ds((2 * i + core) * rows, rows), :][None]
        away_o[pl.ds(i, 1)] = flat[pl.ds((2 * i + 1 - core) * rows, rows), :].astype(LOW)[None]


def dense_backward(core, dense_rows, *arrays):
    count, width = arrays[4].shape
    rows = dense_rows // 128
    return pl.pallas_call(
        dense_backward_kernel,
        name="dense_backward",
        out_shape=[
            jax.ShapeDtypeStruct((count, width), F32),
            jax.ShapeDtypeStruct((64, rows, 128), F32),
            jax.ShapeDtypeStruct((64, rows, 128), LOW),
        ],
        in_specs=[SMEM] + [VMEM] * len(arrays),
        out_specs=[VMEM] * 3,
        scratch_shapes=[
            pltpu.VMEM((rows * 128 + 16, 128), F32),
            pltpu.VMEM((count, 3 * width), LOW),
        ],
        compiler_params=params(),
        cost_estimate=cost(12e9, 40e6),
    )(core, *arrays)


def combine_kernel(plan, middle, results, frozen_result, out):
    count, width = middle.shape
    total = middle[...]
    for first, ref in ((2, results), (4, frozen_result)):
        slots = iota((count, ref.shape[0]), 1)
        for k in range(2):
            place = plan[:, first + k : first + k + 1].astype(jnp.int32)
            total = total + plan[:, k : k + 1] * mm((slots == place).astype(F32).astype(LOW), ref[...])
    out[...] = total.astype(LOW)


def combine(plan, middle, results, frozen_result):
    return pl.pallas_call(
        combine_kernel,
        name="combine",
        out_shape=jax.ShapeDtypeStruct(middle.shape, LOW),
        in_specs=[VMEM] * 4,
        out_specs=VMEM,
        compiler_params=params(),
        cost_estimate=cost(2e9, 4e6),
    )(plan, middle, results, frozen_result)


def gelu_pair(pre):
    area = 0.5 + 0.5 * lax.erf(pre * (0.5**0.5))
    density = jnp.exp(-0.5 * pre * pre) * (1.0 / (2.0 * math.pi) ** 0.5)
    return pre * area, area + pre * density


def expert_up_kernel(rows, weight, hidden_o, slope_o):
    pre = mm(rows[...], weight[...])
    hidden, slope = gelu_pair(pre)
    hidden_o[...] = hidden.astype(LOW)
    slope_o[...] = slope.astype(LOW)


def expert_up(rows, weight):
    count, width = rows.shape
    hidden = weight.shape[1]
    step = 256
    wide = jax.ShapeDtypeStruct((count, hidden), LOW)
    return pl.pallas_call(
        expert_up_kernel,
        name="expert_up",
        out_shape=[wide, wide],
        grid=(count // step,),
        in_specs=[pl.BlockSpec((step, width), lambda i: (i, 0)), pl.BlockSpec((width, hidden), lambda i: (0, 0))],
        out_specs=[pl.BlockSpec((step, hidden), lambda i: (i, 0))] * 2,
        compiler_params=params(),
        cost_estimate=cost(12e9, 10e6),
    )(rows, weight)


def split_three(value):
    high = value.astype(LOW)
    rest = value - high.astype(F32)
    mid = rest.astype(LOW)
    return high, mid, (rest - mid.astype(F32)).astype(LOW)


def with_extra(rows, value):
    lane = iota((rows.shape[0], EXTRA), 1)
    extra = jnp.zeros((rows.shape[0], EXTRA), F32)
    for i, term in enumerate(split_three(value)):
        extra = jnp.where(lane == i, term.astype(F32), extra)
    return rows.astype(LOW), extra.astype(LOW)


def expert_down_kernel(grads, w_in, w_out, hidden, slope, pre_o, rows_o, value_o=None):
    grad_hidden = mm_nt(grads[...], w_out[...])
    value = jnp.sum(hidden[...].astype(F32) * grad_hidden, axis=1, keepdims=True)
    grad_pre = (grad_hidden * slope[...].astype(F32)).astype(LOW)
    pre_o[...] = grad_pre
    grad_rows = mm_nt(grad_pre, w_in[...])
    width = grad_rows.shape[1]
    if value_o is None:
        rows, extra = with_extra(grad_rows, value)
        rows_o[:, :width] = rows
        rows_o[:, width:] = extra
    else:
        rows_o[...] = grad_rows
        value_o[...] = jnp.broadcast_to(value, value_o.shape)


def expert_down(grads, w_in, w_out, hidden, slope, leaves):
    count, width = grads.shape
    wide = hidden.shape[1]
    step = 256
    block = lambda cols: pl.BlockSpec((step, cols), lambda i: (i, 0))
    whole = lambda a: pl.BlockSpec(a.shape, lambda i: (0, 0))
    if leaves:
        outs = [((count, wide), LOW), ((count, width + EXTRA), LOW)]
    else:
        outs = [((count, wide), LOW), ((count, width), F32), ((count, EXTRA), F32)]
    return pl.pallas_call(
        expert_down_kernel,
        name="expert_down_leaving" if leaves else "expert_down_staying",
        out_shape=[jax.ShapeDtypeStruct(s, t) for s, t in outs],
        grid=(count // step,),
        in_specs=[block(width), whole(w_in), whole(w_out), block(wide), block(wide)],
        out_specs=[block(s[1]) for s, t in outs],
        compiler_params=params(),
        cost_estimate=cost(6e9, 12e6),
    )(grads, w_in, w_out, hidden, slope)


def merge_kernel(rows, value, arrived, out):
    width = rows.shape[1]
    extra = jnp.sum(arrived[:, width:].astype(F32), axis=1, keepdims=True)
    low, terms = with_extra(
        rows[...] + arrived[:, :width].astype(F32), value[:, 0:1] + extra
    )
    out[:, :width] = low
    out[:, width:] = terms


def merge_rows(rows, value, arrived):
    return pl.pallas_call(
        merge_kernel,
        name="merge_rows",
        out_shape=jax.ShapeDtypeStruct(arrived.shape, LOW),
        in_specs=[VMEM] * 3,
        out_specs=VMEM,
        compiler_params=params(),
        cost_estimate=cost(1e7, 6e6),
    )(rows, value, arrived)


def frozen_kernel(rows, grads, w_in, w_out, result_o, back_o, result_sum, back_sum, value_sum):
    step = pl.program_id(0)

    @pl.when(step == 0)
    def clear():
        result_sum[...] = jnp.zeros_like(result_sum)
        back_sum[...] = jnp.zeros_like(back_sum)
        value_sum[...] = jnp.zeros_like(value_sum)

    hidden, slope = gelu_pair(mm(rows[...], w_in[...]))
    hidden = hidden.astype(LOW)
    result_sum[...] += mm(hidden, w_out[...])
    grad_hidden = mm_nt(grads[...], w_out[...])
    value_sum[...] += jnp.sum(hidden.astype(F32) * grad_hidden, axis=1, keepdims=True)
    back_sum[...] += mm_nt((grad_hidden * slope).astype(LOW), w_in[...])

    @pl.when(step == pl.num_programs(0) - 1)
    def finish():
        result_o[...] = result_sum[...].astype(LOW)
        width = back_sum.shape[1]
        low, terms = with_extra(back_sum[...], value_sum[:, 0:1])
        back_o[:, :width] = low
        back_o[:, width:] = terms


def frozen_expert(rows, grads, w_in, w_out):
    count, width = rows.shape
    wide = w_in.shape[1]
    step = 512
    small = pl.BlockSpec((count, width), lambda i: (0, 0))
    return pl.pallas_call(
        frozen_kernel,
        name="frozen_expert",
        out_shape=[
            jax.ShapeDtypeStruct((count, width), LOW),
            jax.ShapeDtypeStruct((count, width + EXTRA), LOW),
        ],
        grid=(wide // step,),
        in_specs=[
            small, small,
            pl.BlockSpec((width, step), lambda i: (0, i)),
            pl.BlockSpec((step, width), lambda i: (i, 0)),
        ],
        out_specs=[small, pl.BlockSpec((count, width + EXTRA), lambda i: (0, 0))],
        scratch_shapes=[
            pltpu.VMEM((count, width), F32),
            pltpu.VMEM((count, width), F32),
            pltpu.VMEM((count, EXTRA), F32),
        ],
        compiler_params=params(),
        cost_estimate=cost(4e9, 10e6),
    )(rows, grads, w_in, w_out)


def stage(name, position, sources, groups, outs):
    counts = [len(s) for s in sources]

    def kernel(position_ref, *refs):
        ins, out_refs = refs[: sum(counts)], refs[sum(counts) :]
        for source, cut, axis, rows, out, to in groups:
            first = sum(counts[:source])
            arrays = ins[first : first + counts[source]]
            for step in range(4):
                place = (position_ref[axis] + step) & 3
                index = [slice(None)] * len(arrays[0].shape)
                index[cut] = place
                index[-2] = slice(*rows)
                total = arrays[0][tuple(index)].astype(F32)
                for more in arrays[1:]:
                    total = total + more[tuple(index)].astype(F32)
                target = out_refs[4 * out + step]
                spot = [slice(None)] * len(target.shape)
                spot[-2] = slice(*to)
                target[tuple(spot)] = total.astype(target.dtype)

    flat = [a for s in sources for a in s]
    shapes = [
        jax.ShapeDtypeStruct(shape, LOW if step else F32) for shape in outs for step in range(4)
    ]
    moved = sum(a.size * a.dtype.itemsize for a in flat) * 2
    results = pl.pallas_call(
        kernel,
        name=name,
        out_shape=shapes,
        in_specs=[SMEM] + [VMEM] * len(flat),
        out_specs=[VMEM] * len(shapes),
        compiler_params=params(),
        cost_estimate=cost(1e7, moved),
    )(position, *flat)
    return [results[4 * i : 4 * i + 4] for i in range(len(outs))]


def send_around(blocks, axis):
    return [blocks[0]] + [
        lax.ppermute(blocks[step], axis, [(i, (i + step) % 4) for i in range(4)]) for step in (1, 3, 2)
    ]


def scatter_dense(kept, away, position):
    rows = kept.shape[1]
    cut = rows // 32 * 16 + 16
    rest = rows - cut
    cube = (4, 4, 4, rows, 128)
    arrived = swap_core(away)
    one, two = stage(
        "scatter_first", position, [[kept.reshape(cube), arrived.reshape(cube)]],
        [(0, 1, 1, (0, cut), 0, (0, cut)), (0, 2, 2, (cut, rows), 1, (0, rest))],
        [(4, 4, cut, 128), (4, 4, rest, 128)],
    )
    one, two = send_around(one, "x"), send_around(two, "y")
    one, two = stage(
        "scatter_second", position, [one, two],
        [(0, 1, 2, (0, cut), 0, (0, cut)), (1, 1, 1, (0, rest), 1, (0, rest))],
        [(4, cut, 128), (4, rest, 128)],
    )
    one, two = send_around(one, "y"), send_around(two, "x")
    (both,) = stage(
        "scatter_third", position, [one, two],
        [(0, 0, 0, (0, cut), 0, (0, cut)), (1, 0, 0, (0, rest), 0, (cut, rows))],
        [(rows, 128)],
    )
    return send_around(both, DEPTH)


def adamw_values(master, first, second, grad):
    first_new = beta_first * first + (1.0 - beta_first) * grad
    second_new = beta_second * second + (1.0 - beta_second) * grad * grad
    first_hat = first_new * (1.0 / (1.0 - beta_first**STEP))
    second_hat = second_new * (1.0 / (1.0 - beta_second**STEP))
    master_new = master - learn_rate * (
        first_hat / (jnp.sqrt(second_hat) + adam_eps) + decay_rate * master
    )
    return master_new, first_new, second_new, master_new.astype(LOW)


def dense_update_kernel(master, first, second, *refs):
    terms, outs = refs[:4], refs[4:]
    grad = terms[0][...]
    for term in terms[1:]:
        grad = grad + term[...].astype(F32)
    for out, value in zip(outs, adamw_values(master[...], first[...], second[...], grad)):
        out[...] = value


def dense_update(master, first, second, terms):
    shape = terms[0].shape
    results = pl.pallas_call(
        dense_update_kernel,
        name="dense_update",
        out_shape=[jax.ShapeDtypeStruct(shape, t) for t in (F32, F32, F32, LOW)],
        in_specs=[VMEM] * 7,
        out_specs=[VMEM] * 4,
        compiler_params=params(),
        cost_estimate=cost(1e6, 1e6),
    )(*(a.reshape(shape) for a in (master, first, second)), *terms)
    return tuple(r.reshape(master.shape) for r in results)


def expert_update(core, master, first, second, stays, arrived, axis):
    rows, columns = master.shape[1:]
    if axis == 1:
        blocks, width = 4, columns // 4
        half = (rows, width // 2)
    else:
        blocks, width = 3, columns // 3
        half = (rows // 2, width)

    def kernel(core_ref, master, first, second, stays, arrived, *outs):
        near, far = stays[...], arrived[...].astype(F32)
        swapped = core_ref[0] == 1
        grad = jnp.concatenate(
            [jnp.where(swapped, far, near), jnp.where(swapped, near, far)], axis=axis
        )
        values = adamw_values(master[0], first[0], second[0], grad)
        for out, value in zip(outs, values):
            out[0] = value

    wide = pl.BlockSpec((1, rows, width), lambda i: (0, 0, i))
    slim = pl.BlockSpec(half, lambda i: (0, i))
    return tuple(
        pl.pallas_call(
            kernel,
            name="update_in" if axis == 1 else "update_out",
            out_shape=[jax.ShapeDtypeStruct(master.shape, t) for t in (F32, F32, F32, LOW)],
            grid=(blocks,),
            in_specs=[SMEM, wide, wide, wide, slim, slim],
            out_specs=[wide] * 4,
            compiler_params=params(),
            cost_estimate=cost(2e7, 18e6),
        )(core, master, first, second, stays, arrived)
    )


def swap_core(block):
    return lax.ppermute(block, "c", [(0, 1), (1, 0)])


def along_depth(block, step):
    return lax.ppermute(block, DEPTH, [(z, (z + step) % 4) for z in range(4)])


def swap_pair(block):
    return lax.ppermute(block, DEPTH, [(z, 3 - z) for z in range(4)])


def swap_low(block):
    return lax.ppermute(block, "zl", [(0, 1), (1, 0)])


def gather_weight(own_half, mate_half, kind, core, zh, zl):
    by_kind = lambda wanted: jnp.where(wanted == core, own_half, mate_half)
    own = by_kind(kind)
    from_below = along_depth(by_kind(1 - zh), 1)
    from_above = along_depth(by_kind(zh), -1)
    far_side = jnp.where(zl == 0, from_above, from_below)
    near_side = jnp.where(zl == 0, from_below, from_above)
    across = swap_pair(far_side)
    z = 2 * zh + zl
    rows = own.shape[0]
    full = jnp.zeros((4 * rows, own.shape[1]), own.dtype)
    for block, place in ((own, z), (far_side, z ^ 1), (near_side, 3 - z), (across, (3 - z) ^ 1)):
        full = lax.dynamic_update_slice(full, block, (place * rows, 0))
    return full


def reduce_weight(partial, core, kind, zh, zl):
    rows = partial.shape[0] // 4
    away = lax.dynamic_slice(partial, ((1 - zh) * 2 * rows, 0), (2 * rows, partial.shape[1]))
    kept = lax.dynamic_slice(partial, (zh * 2 * rows, 0), (2 * rows, partial.shape[1]))
    kept = kept + swap_pair(away.astype(LOW)).astype(F32)
    mine = lax.dynamic_slice(kept, (zl * rows, 0), (rows, kept.shape[1]))
    other = lax.dynamic_slice(kept, ((1 - zl) * rows, 0), (rows, kept.shape[1]))
    other = swap_low(other.astype(LOW)).astype(F32)
    stays = jnp.where(kind == core, mine, other)
    leaves = jnp.where(kind == core, other, mine)
    return stays, swap_core(leaves.astype(LOW))


def body(
    tokens,
    segment_ids,
    routes,
    cotangent,
    w_qkv,
    w_attn_out,
    w_router,
    norm_gains,
    frozen_in,
    frozen_out,
    new_in,
    new_out,
    dense_master,
    dense_first,
    dense_second,
    master_in,
    first_in,
    second_in,
    master_out,
    first_out,
    second_out,
):
    model_width = tokens.shape[1]
    block_width = frozen_in.shape[1] // 8
    core, zh, zl = (lax.axis_index(a) for a in ("c", "zh", "zl"))
    kind = zh ^ zl
    core_word = core.astype(jnp.int32).reshape(1)
    position = jnp.stack([2 * zh + zl, lax.axis_index("x"), lax.axis_index("y")]).astype(jnp.int32)

    in_blocks = new_in[0].reshape(-1, 4, 2, block_width)
    in_halves = [in_blocks[:, :, h].reshape(-1, 4 * block_width) for h in range(2)]
    out_halves = [new_out[0][h * block_width : (h + 1) * block_width] for h in range(2)]
    pick = lambda halves, which: jnp.where(which == 0, halves[0], halves[1])
    in_mate = swap_core(pick(in_halves, 1 - core))
    out_mate = swap_core(pick(out_halves, 1 - core))
    half_in = gather_weight(pick(in_halves, core), in_mate, kind, core, zh, zl)
    half_out = gather_weight(pick(out_halves, core), out_mate, kind, core, zh, zl)

    (
        attn_in, qkv_low, mixed_low, lse, middle, ffn_in, plan, rows_sent, grads_sent, frozen_rows, frozen_grads,
    ) = dense_forward(
        zh.astype(jnp.int32).reshape(1), tokens, segment_ids, routes, cotangent, w_qkv, w_attn_out, w_router, norm_gains
    )

    def exchange(rows):
        cut = rows.reshape(-1, CAP, rows.shape[1])
        cut = lax.all_to_all(cut, PLANE, split_axis=0, concat_axis=0, tiled=True)
        return cut.reshape(rows.shape)

    rows_own = exchange(rows_sent)
    rows_mate = swap_core(rows_own)
    grads_own = exchange(grads_sent)
    grads_mate = swap_core(grads_own)
    hidden_own, slope_own = expert_up(rows_own, half_in)
    hidden_mate, slope_mate = expert_up(rows_mate, half_in)
    grad_out_half = mm_tn(hidden_own, grads_own) + mm_tn(hidden_mate, grads_mate)
    out_stays, out_arrived = reduce_weight(grad_out_half, core, kind, zh, zl)
    pre_mate, back_mate = expert_down(grads_mate, half_in, half_out, hidden_mate, slope_mate, True)
    pre_own, back_own, value_own = expert_down(
        grads_own, half_in, half_out, hidden_own, slope_own, False
    )
    back = exchange(merge_rows(back_own, value_own, swap_core(back_mate)))
    grad_in_half = mm_tn(rows_own, pre_own) + mm_tn(rows_mate, pre_mate)
    in_stays, in_arrived = reduce_weight(grad_in_half, core, kind, zh, zl)
    result_mate = swap_core(mm(hidden_mate, half_out).astype(LOW))
    result = exchange((mm(hidden_own, half_out) + result_mate.astype(F32)).astype(LOW))

    frozen_result, frozen_back = frozen_expert(frozen_rows, frozen_grads, frozen_in, frozen_out)
    input_grad, kept, away = dense_backward(
        core_word, dense_master.shape[0], plan, routes, segment_ids, cotangent, tokens, middle, mixed_low, ffn_in, lse,
        qkv_low, attn_in, w_qkv, w_attn_out, w_router, norm_gains, back, frozen_back,
    )
    activations = combine(plan, middle, result, frozen_result)
    dense_new = dense_update(
        dense_master, dense_first, dense_second, scatter_dense(kept, away, position)
    )
    in_new = expert_update(core_word, master_in, first_in, second_in, in_stays, in_arrived, 1)
    out_new = expert_update(core_word, master_out, first_out, second_out, out_stays, out_arrived, 0)
    return (activations, input_grad) + dense_new + in_new + out_new


def solution(mesh):
    fine = Mesh(mesh.devices.reshape(2, 2, 4, 4, 2), ALL)
    tokens = P(ALL, None)
    flat = P(ALL)
    expert = P(("x", "y", "c"), DEPTH, None)
    return jax.shard_map(
        body,
        mesh=fine,
        in_specs=(tokens,) * 4 + (P(),) * 6 + (expert,) * 2 + (flat,) * 3 + (expert,) * 6,
        out_specs=(tokens,) * 2 + (flat,) * 4 + (expert,) * 8,
        check_vma=False,
    )
```

```python
import math

import jax
import jax.numpy as jnp
from jax import lax
from jax.experimental import pallas as pl
from jax.experimental.pallas import tpu as pltpu
from jax.sharding import Mesh
from jax.sharding import PartitionSpec as P

HEAD_DIM = 64
STEP = 5


norm_eps = 1e-05
learn_rate = 0.02
beta_first = 0.5
beta_second = 0.5
adam_eps = 1e-08
decay_rate = 0.1


PLANE = ("zl", "x", "y")
DEPTH = ("zh", "zl")
ALL = ("zh", "zl", "x", "y", "c")
CAP = 24
PAIRS = 6
EXTRA = 128
VMEM = pl.BlockSpec(memory_space=pltpu.VMEM)
SMEM = pl.BlockSpec(memory_space=pltpu.SMEM)
F32 = jnp.float32
LOW = jnp.bfloat16


def params(**more):
    return pltpu.CompilerParams(vmem_limit_bytes=56 * 1024 * 1024, **more)


def ordered(kernel, count, after, **call):
    extra = len(after)

    def inner(*refs):
        return kernel(*refs[:count], *refs[count + extra :])

    call["in_specs"] = list(call["in_specs"]) + [pl.BlockSpec(memory_space=pl.ANY)] * extra
    made = pl.pallas_call(inner, **call)
    return lambda *arrays: made(*arrays, *after)


def cost(flops, moved):
    return pl.CostEstimate(flops=int(flops), bytes_accessed=int(moved), transcendentals=0)


def mm(left, right):
    return jnp.dot(left, right, preferred_element_type=F32)


def mm_nt(left, right):
    return lax.dot_general(left, right, (((1,), (1,)), ((), ())), preferred_element_type=F32)


def mm_tn(left, right):
    return lax.dot_general(left, right, (((0,), (0,)), ((), ())), preferred_element_type=F32)


def iota(shape, axis):
    return lax.broadcasted_iota(jnp.int32, shape, axis)


def normed(values):
    centered = values - jnp.mean(values, axis=1, keepdims=True)
    scale = lax.rsqrt(jnp.mean(centered * centered, axis=1, keepdims=True) + norm_eps)
    return centered * scale, scale


def norm_backward(values, gain, upstream):
    hat, scale = normed(values)
    gain_grad = jnp.sum(upstream * hat, axis=0, keepdims=True)
    inner = upstream * gain
    mean_inner = jnp.mean(inner, axis=1, keepdims=True)
    mean_hat = jnp.mean(inner * hat, axis=1, keepdims=True)
    return scale * (inner - mean_inner - hat * mean_hat), gain_grad


def as_column(row, eye):
    return jnp.sum(jnp.where(eye, row, jnp.zeros_like(row)), axis=1, keepdims=True)


def as_row(column, eye):
    return jnp.sum(jnp.where(eye, column, jnp.zeros_like(column)), axis=0, keepdims=True)


def attention_mask(segment_row):
    count = segment_row.shape[1]
    down, across = iota((count, count), 0), iota((count, count), 1)
    eye = down == across
    column = jnp.sum(jnp.where(eye, segment_row, 0), axis=1, keepdims=True)
    return (down >= across) & (column == segment_row), eye


def dense_forward_kernel(
    zh_ref, tokens, segments, routes, cotangent, w_qkv, w_out, w_router, gains,
    attn_in_o, qkv_o, mixed_o, lse_o, middle_o, ffn_o, plan_o, rows_o, grads_o, frozen_rows_o, frozen_grads_o,
):
    width = tokens.shape[1]
    count = tokens.shape[0]
    inputs = tokens[...].astype(F32)
    hat, unused = normed(inputs)
    attn_in = (hat * gains[0:1, :]).astype(LOW)
    attn_in_o[...] = attn_in
    qkv_o[...] = mm(attn_in, w_qkv[...]).astype(LOW)
    allowed, eye = attention_mask(segments[...])
    lane = iota((count, 128), 1)
    low_lanes = lane < HEAD_DIM
    lse_all = jnp.zeros((count, 128), F32)
    for pair in range(width // 128):
        at = slice(128 * pair, 128 * pair + 128)
        queries = qkv_o[:, at] * jnp.asarray(HEAD_DIM**-0.5, LOW)
        keys = qkv_o[:, width + 128 * pair : width + 128 * pair + 128]
        values = qkv_o[:, 2 * width + 128 * pair : 2 * width + 128 * pair + 128]
        outs = []
        for half in range(2):
            mine = low_lanes if half == 0 else ~low_lanes
            scores = mm_nt(jnp.where(mine, queries, jnp.zeros_like(queries)), keys)
            scores = jnp.where(allowed, scores, -1e30)
            top = jnp.max(scores, axis=1, keepdims=True)
            raised = jnp.exp(scores - top)
            total = jnp.sum(raised, axis=1, keepdims=True)
            probs = (raised * (1.0 / total)).astype(LOW)
            outs.append(mm(probs, values))
            lse_all = jnp.where(lane == 2 * pair + half, top + jnp.log(total), lse_all)
        mixed_o[:, at] = jnp.where(low_lanes, outs[0], outs[1]).astype(LOW)
    lse_o[...] = lse_all
    middle = inputs + mm(mixed_o[...], w_out[...])
    middle_o[...] = middle
    hat, unused = normed(middle)
    ffn = (hat * gains[1:2, :]).astype(LOW)
    ffn_o[...] = ffn
    logits = mm_nt(ffn, w_router[...])
    experts = iota(logits.shape, 1)
    lists = [as_column(routes[k : k + 1, :], eye) for k in range(2)]
    picks = [experts == column for column in lists]
    chosen = [jnp.sum(jnp.where(p, logits, 0.0), axis=1, keepdims=True) for p in picks]
    top = jnp.maximum(chosen[0], chosen[1])
    raised = [jnp.exp(c - top) for c in chosen]
    gates = [r / (raised[0] + raised[1]) for r in raised]
    named = (picks[0] | picks[1]).astype(F32).astype(LOW)
    earlier = (iota((count, count), 0) > iota((count, count), 1)).astype(F32).astype(LOW)
    before = mm(earlier, named)
    zh = zh_ref[0]
    new_place, old_place = [], []
    for k in range(2):
        route = lists[k]
        slot = jnp.sum(jnp.where(picks[k], before, 0.0), axis=1, keepdims=True).astype(jnp.int32)
        fresh = route - 1
        block = 16 * ((fresh & 1) ^ zh) + lax.shift_right_arithmetic(fresh, 1)
        new_place.append(jnp.where(route > 0, block * CAP + slot, -1))
        old_place.append(jnp.where(route > 0, -1, slot))
    columns = gates + [p.astype(F32) for p in new_place + old_place]
    plan = jnp.zeros((count, 128), F32)
    for i, column in enumerate(columns):
        plan = jnp.where(lane == i, column, plan)
    plan_o[...] = plan
    up = cotangent[...].astype(F32)
    scaled = [(g * up).astype(LOW) for g in gates]
    for places, size, rows_ref, grads_ref in (
        (new_place, rows_o.shape[0], rows_o, grads_o),
        (old_place, CAP, frozen_rows_o, frozen_grads_o),
    ):
        slots = iota((size, count), 0)
        spread = [(slots == as_row(p, eye)).astype(F32).astype(LOW) for p in places]
        rows_ref[...] = mm(spread[0] + spread[1], ffn).astype(LOW)
        grads_ref[...] = (mm(spread[0], scaled[0]) + mm(spread[1], scaled[1])).astype(LOW)


def dense_forward(after, zh, tokens, segments, routes, cotangent, w_qkv, w_out, w_router, gains):
    count, width = tokens.shape
    slots = (w_router.shape[0] - 1) * CAP
    shapes = [
        ((count, width), LOW), ((count, 3 * width), LOW), ((count, width), LOW), ((count, 128), F32),
        ((count, width), F32), ((count, width), LOW), ((count, 128), F32),
        ((slots, width), LOW), ((slots, width), LOW), ((CAP, width), LOW), ((CAP, width), LOW),
    ]
    return ordered(
        dense_forward_kernel, 9, after,
        name="dense_forward",
        out_shape=[jax.ShapeDtypeStruct(s, t) for s, t in shapes],
        in_specs=[SMEM] + [VMEM] * 8,
        out_specs=[VMEM] * len(shapes),
        compiler_params=params(),
        cost_estimate=cost(8e9, 30e6),
    )(zh, tokens, segments, routes, cotangent, w_qkv, w_out, w_router, gains)


def dense_backward_kernel(
    core_ref, plan, routes, segments, cotangent, tokens, middle, mixed, ffn, lse, qkv, attn_in,
    w_qkv, w_out, w_router, gains, back, frozen_back,
    input_grad_o, kept_o, away_o,
    flat, gqkv,
):
    count, width = tokens.shape
    expert_total = w_router.shape[0]
    up = cotangent[...].astype(F32)
    gates = [plan[:, k : k + 1] for k in range(2)]
    new_place = [plan[:, 2 + k : 3 + k].astype(jnp.int32) for k in range(2)]
    old_place = [plan[:, 4 + k : 5 + k].astype(jnp.int32) for k in range(2)]
    allowed, eye = attention_mask(segments[...])

    grad_ffn = jnp.zeros((count, width), F32)
    weighted = [jnp.zeros((count, 1), F32) for k in range(2)]
    for places, ref in ((new_place, back), (old_place, frozen_back)):
        size = ref.shape[0]
        slots = iota((count, size), 1)
        for k in range(2):
            choice = (slots == places[k]).astype(F32).astype(LOW)
            picked = mm(choice, ref[...])
            grad_ffn = grad_ffn + picked[:, :width]
            tail = picked[:, width:]
            weighted[k] = weighted[k] + jnp.sum(tail, axis=1, keepdims=True)
    both = weighted[0] + weighted[1]
    experts = iota((count, expert_total), 1)
    grad_logits = jnp.zeros((count, expert_total), F32)
    for k in range(2):
        grad_logits = jnp.where(
            experts == as_column(routes[k : k + 1, :], eye), weighted[k] - gates[k] * both, grad_logits
        )
    grad_logits = grad_logits.astype(LOW)
    grad_ffn = grad_ffn + mm(grad_logits, w_router[...])
    grad_norm, gain_ffn = norm_backward(middle[...], gains[1:2, :], grad_ffn)
    grad_middle = up + grad_norm
    grad_branch = grad_middle.astype(LOW)

    blocks = width // 128
    first_row = 3 * blocks * width
    attn_out_grad = mm_tn(mixed[...], grad_branch)
    for j in range(blocks):
        flat[pl.ds(first_row + j, width, stride=blocks), :] = attn_out_grad[:, 128 * j : 128 * j + 128]
    router_row = first_row + blocks * width
    router_rows = width * expert_total // 128
    padded_logits = jnp.concatenate(
        [grad_logits, jnp.zeros((count, 128 - expert_total), LOW)], axis=1
    )
    router_grad = mm_tn(ffn[...], padded_logits)
    feature = iota((width, 128), 0)
    lane_w = iota((width, 128), 1)
    start = feature * expert_total
    offset = start & 127
    turned = jnp.take_along_axis(router_grad, (lane_w - offset) & 127, axis=1)
    wrapped = lane_w < offset
    row_of = lax.shift_right_logical(iota((router_rows, width), 1) * expert_total, 7)
    row_here = iota((router_rows, width), 0)
    here = (row_of == row_here).astype(F32)
    after = (row_of + 1 == row_here).astype(F32)
    exact = lambda a, b: jnp.dot(a, b, precision=lax.Precision.HIGHEST, preferred_element_type=F32)
    flat[router_row : router_row + router_rows, :] = exact(
        here, jnp.where(wrapped, 0.0, turned)
    ) + exact(after, jnp.where(wrapped, turned, 0.0))
    gain_row = router_row + router_rows

    grad_mixed = mm_nt(grad_branch, w_out[...]).astype(LOW)
    lane = iota((count, 128), 1)
    low_lanes = lane < HEAD_DIM
    scale = HEAD_DIM**-0.5
    for pair in range(blocks):
        at = slice(128 * pair, 128 * pair + 128)
        queries = qkv[:, at] * jnp.asarray(scale, LOW)
        keys = qkv[:, width + 128 * pair : width + 128 * pair + 128]
        values = qkv[:, 2 * width + 128 * pair : 2 * width + 128 * pair + 128]
        grads = grad_mixed[:, at]
        grad_q = jnp.zeros((count, 128), F32)
        grad_k = jnp.zeros((count, 128), F32)
        grad_v = jnp.zeros((count, 128), F32)
        for half in range(2):
            mine = low_lanes if half == 0 else ~low_lanes
            only = lambda v: jnp.where(mine, v, jnp.zeros_like(v))
            q_half, g_half, k_half = only(queries), only(grads), only(keys)
            scores = jnp.where(allowed, mm_nt(q_half, keys), -1e30)
            head = 2 * pair + half
            probs = jnp.exp(scores - lse[:, head : head + 1])
            grad_probs = mm_nt(g_half, values)
            grad_v = grad_v + mm_tn(probs.astype(LOW), g_half)
            dots = jnp.sum(probs * grad_probs, axis=1, keepdims=True)
            grad_scores = (probs * (grad_probs - dots)).astype(LOW)
            grad_q = grad_q + mm(grad_scores, k_half)
            grad_k = grad_k + mm_tn(grad_scores, q_half)
        gqkv[:, at] = (grad_q * scale).astype(LOW)
        gqkv[:, width + 128 * pair : width + 128 * pair + 128] = grad_k.astype(LOW)
        gqkv[:, 2 * width + 128 * pair : 2 * width + 128 * pair + 128] = grad_v.astype(LOW)
    for j in range(0, 3 * blocks, 2):
        piece = mm_tn(attn_in[...], gqkv[:, 128 * j : 128 * j + 256])
        flat[pl.ds(j, width, stride=3 * blocks), :] = piece[:, :128]
        flat[pl.ds(j + 1, width, stride=3 * blocks), :] = piece[:, 128:]
    grad_attn = mm_nt(gqkv[...], w_qkv[...])
    grad_norm, gain_attn = norm_backward(tokens[...].astype(F32), gains[0:1, :], grad_attn)
    input_grad_o[...] = grad_middle + grad_norm
    for j in range(blocks):
        flat[gain_row + j : gain_row + j + 1, :] = gain_attn[:, 128 * j : 128 * j + 128]
        flat[gain_row + blocks + j : gain_row + blocks + j + 1, :] = gain_ffn[:, 128 * j : 128 * j + 128]
    last = gain_row + 2 * blocks
    flat[last:, :] = jnp.zeros((flat.shape[0] - last, 128), F32)

    core = core_ref[0]
    rows = flat.shape[0] // 128
    padded = kept_o.shape[1]

    @pl.loop(0, kept_o.shape[0])
    def move(i):
        kept_o[pl.ds(i, 1)] = flat[pl.ds((2 * i + core) * rows, padded), :][None]
        away_o[pl.ds(i, 1)] = flat[pl.ds((2 * i + 1 - core) * rows, padded), :].astype(LOW)[None]


def dense_backward(after, core, dense_rows, *arrays):
    count, width = arrays[4].shape
    rows = dense_rows // 128
    padded = (rows + 31) // 32 * 32
    return ordered(
        dense_backward_kernel, 1 + len(arrays), after,
        name="dense_backward",
        out_shape=[
            jax.ShapeDtypeStruct((count, width), F32),
            jax.ShapeDtypeStruct((64, padded, 128), F32),
            jax.ShapeDtypeStruct((64, padded, 128), LOW),
        ],
        in_specs=[SMEM] + [VMEM] * len(arrays),
        out_specs=[VMEM] * 3,
        scratch_shapes=[
            pltpu.VMEM((rows * 128 + padded - rows, 128), F32),
            pltpu.VMEM((count, 3 * width), LOW),
        ],
        compiler_params=params(),
        cost_estimate=cost(12e9, 40e6),
    )(core, *arrays)


def combine_kernel(plan, middle, results, frozen_result, out):
    count, width = middle.shape
    total = middle[...]
    for first, ref in ((2, results), (4, frozen_result)):
        slots = iota((count, ref.shape[0]), 1)
        for k in range(2):
            place = plan[:, first + k : first + k + 1].astype(jnp.int32)
            total = total + plan[:, k : k + 1] * mm((slots == place).astype(F32).astype(LOW), ref[...])
    out[...] = total.astype(LOW)


def combine(after, plan, middle, results, frozen_result):
    return ordered(
        combine_kernel, 4, after,
        name="combine",
        out_shape=jax.ShapeDtypeStruct(middle.shape, LOW),
        in_specs=[VMEM] * 4,
        out_specs=VMEM,
        compiler_params=params(),
        cost_estimate=cost(2e9, 4e6),
    )(plan, middle, results, frozen_result)


def gelu_pair(pre):
    area = 0.5 + 0.5 * lax.erf(pre * (0.5**0.5))
    density = jnp.exp(-0.5 * pre * pre) * (1.0 / (2.0 * math.pi) ** 0.5)
    return pre * area, area + pre * density


def shift_weight(home, pieces, full, sems):
    keep, mate, below, above, across = pieces
    z, own_kind = home[0], home[1]
    rows = keep.shape[0]
    spot = lambda step: full.at[pl.ds(pl.multiple_of(((z + step) & 3) * rows, 64), rows), :]

    @pl.when(own_kind == 1)
    def from_keep():
        pltpu.make_async_copy(keep, spot(0), sems.at[0]).start()

    @pl.when(own_kind == 0)
    def from_mate():
        pltpu.make_async_copy(mate, spot(0), sems.at[0]).start()

    copies = [
        pltpu.make_async_copy(piece, spot(step), sems.at[1 + i])
        for i, (piece, step) in enumerate(((below, 3), (above, 1), (across, 2)))
    ]
    for copy in copies:
        copy.start()
    return [pltpu.make_async_copy(keep, spot(0), sems.at[0])] + copies


HBM = pl.BlockSpec(memory_space=pl.ANY)


def expert_up_kernel(home, rows, keep, mate, below, above, across, hidden_o, slope_o, weight, sems):
    @pl.when(pl.program_id(0) == 0)
    def load():
        for copy in shift_weight(home, (keep, mate, below, above, across), weight, sems):
            copy.wait()

    pre = mm(rows[...], weight[...])
    hidden, slope = gelu_pair(pre)
    hidden_o[...] = hidden.astype(LOW)
    slope_o[...] = slope.astype(LOW)


def expert_up(after, home, rows, pieces):
    count, width = rows.shape
    hidden = pieces[0].shape[1]
    step = 256
    wide = jax.ShapeDtypeStruct((count, hidden), LOW)
    return ordered(
        expert_up_kernel, 7, after,
        name="expert_up",
        out_shape=[wide, wide],
        grid=(count // step,),
        in_specs=[SMEM, pl.BlockSpec((step, width), lambda i: (i, 0))] + [HBM] * 5,
        out_specs=[pl.BlockSpec((step, hidden), lambda i: (i, 0))] * 2,
        scratch_shapes=[pltpu.VMEM((width, hidden), LOW), pltpu.SemaphoreType.DMA((4,))],
        compiler_params=params(),
        cost_estimate=cost(12e9, 10e6),
    )(home, rows, *pieces)


def split_three(value):
    high = value.astype(LOW)
    rest = value - high.astype(F32)
    mid = rest.astype(LOW)
    return high, mid, (rest - mid.astype(F32)).astype(LOW)


def with_extra(rows, value):
    lane = iota((rows.shape[0], EXTRA), 1)
    extra = jnp.zeros((rows.shape[0], EXTRA), F32)
    for i, term in enumerate(split_three(value)):
        extra = jnp.where(lane == i, term.astype(F32), extra)
    return rows.astype(LOW), extra.astype(LOW)


def expert_down_kernel(home, grads, hidden, slope, *refs):
    in_pieces, out_pieces = refs[:5], refs[5:10]
    outs, (w_in, w_out, in_sems, out_sems) = refs[10:-4], refs[-4:]

    @pl.when(pl.program_id(0) == 0)
    def load():
        copies = shift_weight(home, out_pieces, w_out, out_sems)
        copies = copies + shift_weight(home, in_pieces, w_in, in_sems)
        for copy in copies:
            copy.wait()

    grad_hidden = mm_nt(grads[...], w_out[...])
    value = jnp.sum(hidden[...].astype(F32) * grad_hidden, axis=1, keepdims=True)
    grad_pre = (grad_hidden * slope[...].astype(F32)).astype(LOW)
    outs[0][...] = grad_pre
    grad_rows = mm_nt(grad_pre, w_in[...])
    width = grad_rows.shape[1]
    if len(outs) == 2:
        rows, extra = with_extra(grad_rows, value)
        outs[1][:, :width] = rows
        outs[1][:, width:] = extra
    else:
        outs[1][...] = grad_rows
        outs[2][...] = jnp.broadcast_to(value, outs[2].shape)


def expert_down(after, home, grads, hidden, slope, in_pieces, out_pieces, leaves):
    count, width = grads.shape
    wide = hidden.shape[1]
    step = 256
    block = lambda cols: pl.BlockSpec((step, cols), lambda i: (i, 0))
    if leaves:
        outs = [((count, wide), LOW), ((count, width + EXTRA), LOW)]
    else:
        outs = [((count, wide), LOW), ((count, width), F32), ((count, EXTRA), F32)]
    return ordered(
        expert_down_kernel, 14, after,
        name="expert_down_leaving" if leaves else "expert_down_staying",
        out_shape=[jax.ShapeDtypeStruct(s, t) for s, t in outs],
        grid=(count // step,),
        in_specs=[SMEM, block(width), block(wide), block(wide)] + [HBM] * 10,
        out_specs=[block(s[1]) for s, t in outs],
        scratch_shapes=[
            pltpu.VMEM((width, wide), LOW),
            pltpu.VMEM((wide, width), LOW),
            pltpu.SemaphoreType.DMA((4,)),
            pltpu.SemaphoreType.DMA((4,)),
        ],
        compiler_params=params(),
        cost_estimate=cost(12e9, 12e6),
    )(home, grads, hidden, slope, *in_pieces, *out_pieces)


def expert_result_kernel(home, hidden, *refs):
    pieces, more, (out, weight, sems) = refs[:5], refs[5:-3], refs[-3:]

    @pl.when(pl.program_id(0) == 0)
    def load():
        for copy in shift_weight(home, pieces, weight, sems):
            copy.wait()

    total = mm(hidden[...], weight[...])
    for term in more:
        total = total + term[...].astype(F32)
    out[...] = total.astype(LOW)


def expert_result(after, home, hidden, pieces, arrived=()):
    count, wide = hidden.shape
    width = pieces[0].shape[1]
    step = 256
    block = lambda cols: pl.BlockSpec((step, cols), lambda i: (i, 0))
    return ordered(
        expert_result_kernel, 7 + len(arrived), after,
        name="expert_result",
        out_shape=jax.ShapeDtypeStruct((count, width), LOW),
        grid=(count // step,),
        in_specs=[SMEM, block(wide)] + [HBM] * 5 + [block(width)] * len(arrived),
        out_specs=block(width),
        scratch_shapes=[pltpu.VMEM((wide, width), LOW), pltpu.SemaphoreType.DMA((4,))],
        compiler_params=params(),
        cost_estimate=cost(6e9, 6e6),
    )(home, hidden, *pieces, *arrived)


def weight_grad_kernel(half_ref, left_own, left_mate, right_own, right_mate, out):
    total = mm_tn(left_own[...], right_own[...]) + mm_tn(left_mate[...], right_mate[...])
    out[...] = total.astype(out.dtype)


def weight_grad(after, name, half, lefts, rights, left_step, right_step, kind):
    rows, left_width = lefts[0].shape
    right_width = rights[0].shape[1]
    steps = left_width // 2 // left_step
    left = pl.BlockSpec((rows, left_step), lambda i, j, half: (0, half[0] * steps + i))
    right = pl.BlockSpec((rows, right_step), lambda i, j, half: (0, j))

    def inner(half_ref, a, b, c, d, *refs):
        weight_grad_kernel(half_ref, a, b, c, d, refs[-1])

    return pl.pallas_call(
        inner,
        name=name,
        out_shape=jax.ShapeDtypeStruct((left_width // 2, right_width), kind),
        grid_spec=pltpu.PrefetchScalarGridSpec(
            num_scalar_prefetch=1,
            grid=(steps, right_width // right_step),
            in_specs=[left, left, right, right] + [HBM] * len(after),
            out_specs=pl.BlockSpec((left_step, right_step), lambda i, j, half: (i, j)),
        ),
        compiler_params=params(),
        cost_estimate=cost(6e9, 6e6),
    )(half, *lefts, *rights, *after)


def cut_weights_kernel(home, new_in, new_out, in_keep, in_send, out_keep, out_send, sems):
    core = home[2]
    cols = in_keep.shape[1] // 4
    rows = out_keep.shape[0]
    copies = []
    for kept, target_in, target_out in ((True, in_keep, out_keep), (False, in_send, out_send)):
        half = core if kept else 1 - core
        for block in range(4):
            start = pl.multiple_of((2 * block + half) * cols, 128)
            copies.append(
                (new_in.at[0, :, pl.ds(start, cols)], target_in.at[:, block * cols : (block + 1) * cols])
            )
        copies.append((new_out.at[0, pl.ds(pl.multiple_of(half * rows, 64), rows), :], target_out))
    made = [pltpu.make_async_copy(a, b, sems.at[i]) for i, (a, b) in enumerate(copies)]
    for copy in made:
        copy.start()
    for copy in made:
        copy.wait()


def cut_weights(after, home, new_in, new_out):
    halves = [(new_in.shape[1], new_in.shape[2] // 2)] * 2 + [(new_out.shape[1] // 2, new_out.shape[2])] * 2
    return ordered(
        cut_weights_kernel, 3, after,
        name="cut_weights",
        out_shape=[jax.ShapeDtypeStruct(h, LOW) for h in halves],
        in_specs=[SMEM, HBM, HBM],
        out_specs=[HBM] * 4,
        scratch_shapes=[pltpu.SemaphoreType.DMA((10,))],
        compiler_params=params(),
        cost_estimate=cost(1e5, 4e6),
    )(home, new_in, new_out)


def choose(after, name, flag, pairs):
    count = len(pairs)

    def kernel(flag_ref, *refs):
        ins, outs, sems = refs[: 2 * count], refs[2 * count : -1], refs[-1]
        each = len(outs) // count

        def move(straight):
            made = []
            for i in range(count):
                for j in range(each):
                    source = ins[2 * i + (j if straight else 1 - j)]
                    made.append(pltpu.make_async_copy(source, outs[each * i + j], sems.at[each * i + j]))
            for copy in made:
                copy.start()
            for copy in made:
                copy.wait()

        pl.when(flag_ref[0] == 1)(lambda: move(True))
        pl.when(flag_ref[0] == 0)(lambda: move(False))

    each = 2 if name == "choose_both" else 1
    shapes = [jax.ShapeDtypeStruct(p[0].shape, p[0].dtype) for p in pairs for j in range(each)]
    return ordered(
        kernel, 1 + 2 * count, after,
        name=name,
        out_shape=shapes,
        in_specs=[SMEM] + [HBM] * (2 * count),
        out_specs=[HBM] * len(shapes),
        scratch_shapes=[pltpu.SemaphoreType.DMA((each * count,))],
        compiler_params=params(),
        cost_estimate=cost(1e5, 4e6),
    )(flag, *[a for p in pairs for a in p])


def reduce_first(after, low, kept, arrived):
    rows, columns = kept.shape[0] // 2, kept.shape[1]

    def kernel(low_ref, kept, arrived, mine, other):
        for out, which in ((mine, low_ref[0]), (other, 1 - low_ref[0])):
            at = pl.ds(pl.multiple_of(which * rows, 64), rows)
            out[...] = (kept[at, :] + arrived[at, :].astype(F32)).astype(out.dtype)

    return ordered(
        kernel, 3, after,
        name="reduce_first",
        out_shape=[jax.ShapeDtypeStruct((rows, columns), t) for t in (F32, LOW)],
        in_specs=[SMEM, VMEM, VMEM],
        out_specs=[VMEM] * 2,
        compiler_params=params(),
        cost_estimate=cost(1e6, 6e6),
    )(low, kept, arrived)


def reduce_second(after, same, mine, other):
    def kernel(same_ref, mine, other, stays, leaves):
        straight = same_ref[0] == 1
        near, far = mine[...], other[...].astype(F32)
        stays[...] = jnp.where(straight, near, far)
        leaves[...] = jnp.where(straight, far, near).astype(LOW)

    return ordered(
        kernel, 3, after,
        name="reduce_second",
        out_shape=[jax.ShapeDtypeStruct(mine.shape, t) for t in (F32, LOW)],
        in_specs=[SMEM, VMEM, VMEM],
        out_specs=[VMEM] * 2,
        compiler_params=params(),
        cost_estimate=cost(1e6, 6e6),
    )(same, mine, other)


def merge_kernel(rows, value, arrived, out):
    width = rows.shape[1]
    extra = jnp.sum(arrived[:, width:].astype(F32), axis=1, keepdims=True)
    low, terms = with_extra(
        rows[...] + arrived[:, :width].astype(F32), value[:, 0:1] + extra
    )
    out[:, :width] = low
    out[:, width:] = terms


def merge_rows(after, rows, value, arrived):
    return ordered(
        merge_kernel, 3, after,
        name="merge_rows",
        out_shape=jax.ShapeDtypeStruct(arrived.shape, LOW),
        in_specs=[VMEM] * 3,
        out_specs=VMEM,
        compiler_params=params(),
        cost_estimate=cost(1e7, 6e6),
    )(rows, value, arrived)


def frozen_kernel(rows, grads, w_in, w_out, result_o, back_o, result_sum, back_sum, value_sum):
    step = pl.program_id(0)

    @pl.when(step == 0)
    def clear():
        result_sum[...] = jnp.zeros_like(result_sum)
        back_sum[...] = jnp.zeros_like(back_sum)
        value_sum[...] = jnp.zeros_like(value_sum)

    hidden, slope = gelu_pair(mm(rows[...], w_in[...]))
    hidden = hidden.astype(LOW)
    result_sum[...] += mm(hidden, w_out[...])
    grad_hidden = mm_nt(grads[...], w_out[...])
    value_sum[...] += jnp.sum(hidden.astype(F32) * grad_hidden, axis=1, keepdims=True)
    back_sum[...] += mm_nt((grad_hidden * slope).astype(LOW), w_in[...])

    @pl.when(step == pl.num_programs(0) - 1)
    def finish():
        result_o[...] = result_sum[...].astype(LOW)
        width = back_sum.shape[1]
        low, terms = with_extra(back_sum[...], value_sum[:, 0:1])
        back_o[:, :width] = low
        back_o[:, width:] = terms


def frozen_expert(after, rows, grads, w_in, w_out):
    count, width = rows.shape
    wide = w_in.shape[1]
    step = 512
    small = pl.BlockSpec((count, width), lambda i: (0, 0))
    return ordered(
        frozen_kernel, 4, after,
        name="frozen_expert",
        out_shape=[
            jax.ShapeDtypeStruct((count, width), LOW),
            jax.ShapeDtypeStruct((count, width + EXTRA), LOW),
        ],
        grid=(wide // step,),
        in_specs=[
            small, small,
            pl.BlockSpec((width, step), lambda i: (0, i)),
            pl.BlockSpec((step, width), lambda i: (i, 0)),
        ],
        out_specs=[small, pl.BlockSpec((count, width + EXTRA), lambda i: (0, 0))],
        scratch_shapes=[
            pltpu.VMEM((count, width), F32),
            pltpu.VMEM((count, width), F32),
            pltpu.VMEM((count, EXTRA), F32),
        ],
        compiler_params=params(),
        cost_estimate=cost(4e9, 10e6),
    )(rows, grads, w_in, w_out)


def stage(after, name, position, sources, groups, outs):
    counts = [len(s) for s in sources]

    def kernel(position_ref, *refs):
        ins, out_refs = refs[: sum(counts)], refs[sum(counts) :]
        for source, cut, axis, rows, out, to in groups:
            first = sum(counts[:source])
            arrays = ins[first : first + counts[source]]
            for step in range(4):
                place = (position_ref[axis] + step) & 3
                index = [slice(None)] * len(arrays[0].shape)
                index[cut] = place
                index[-2] = slice(*rows)
                total = arrays[0][tuple(index)].astype(F32)
                for more in arrays[1:]:
                    total = total + more[tuple(index)].astype(F32)
                target = out_refs[4 * out + step]
                spot = [slice(None)] * len(target.shape)
                spot[-2] = slice(*to)
                target[tuple(spot)] = total.astype(target.dtype)

    flat = [a for s in sources for a in s]
    shapes = [
        jax.ShapeDtypeStruct(shape, LOW if step else F32) for shape in outs for step in range(4)
    ]
    moved = sum(a.size * a.dtype.itemsize for a in flat) * 2
    results = ordered(
        kernel, 1 + len(flat), after,
        name=name,
        out_shape=shapes,
        in_specs=[SMEM] + [VMEM] * len(flat),
        out_specs=[VMEM] * len(shapes),
        compiler_params=params(),
        cost_estimate=cost(1e7, moved),
    )(position, *flat)
    return [results[4 * i : 4 * i + 4] for i in range(len(outs))]


def send_around(blocks, axis):
    return [blocks[0]] + [
        lax.ppermute(blocks[step], axis, [(i, (i + step) % 4) for i in range(4)]) for step in (1, 3, 2)
    ]


def adamw_values(master, first, second, grad):
    first_new = beta_first * first + (1.0 - beta_first) * grad
    second_new = beta_second * second + (1.0 - beta_second) * grad * grad
    first_hat = first_new * (1.0 / (1.0 - beta_first**STEP))
    second_hat = second_new * (1.0 / (1.0 - beta_second**STEP))
    master_new = master - learn_rate * (
        first_hat / (jnp.sqrt(second_hat) + adam_eps) + decay_rate * master
    )
    return master_new, first_new, second_new, master_new.astype(LOW)


def dense_update_kernel(master, first, second, *refs):
    terms, outs = refs[:4], refs[4:]
    rows = master.shape[0]
    grad = terms[0][:rows]
    for term in terms[1:]:
        grad = grad + term[:rows].astype(F32)
    for out, value in zip(outs, adamw_values(master[...], first[...], second[...], grad)):
        out[...] = value


def dense_update(after, master, first, second, terms):
    shape = (master.shape[0] // 128, 128)
    results = ordered(
        dense_update_kernel, 7, after,
        name="dense_update",
        out_shape=[jax.ShapeDtypeStruct(shape, t) for t in (F32, F32, F32, LOW)],
        in_specs=[VMEM] * 7,
        out_specs=[VMEM] * 4,
        compiler_params=params(),
        cost_estimate=cost(1e6, 1e6),
    )(*(a.reshape(shape) for a in (master, first, second)), *terms)
    return tuple(r.reshape(master.shape) for r in results)


def expert_update(after, core, master, first, second, stays, arrived, axis):
    rows, columns = master.shape[1:]
    if axis == 1:
        blocks, width = 4, columns // 4
        half = (rows, width // 2)
    else:
        blocks, width = 3, columns // 3
        half = (rows // 2, width)

    def kernel(core_ref, master, first, second, stays, arrived, *outs):
        near, far = stays[...], arrived[...].astype(F32)
        swapped = core_ref[0] == 1
        grad = jnp.concatenate(
            [jnp.where(swapped, far, near), jnp.where(swapped, near, far)], axis=axis
        )
        values = adamw_values(master[0], first[0], second[0], grad)
        for out, value in zip(outs, values):
            out[0] = value

    wide = pl.BlockSpec((1, rows, width), lambda i: (0, 0, i))
    slim = pl.BlockSpec(half, lambda i: (0, i))
    return tuple(
        ordered(
        kernel, 6, after,
            name="update_in" if axis == 1 else "update_out",
            out_shape=[jax.ShapeDtypeStruct(master.shape, t) for t in (F32, F32, F32, LOW)],
            grid=(blocks,),
            in_specs=[SMEM, wide, wide, wide, slim, slim],
            out_specs=[wide] * 4,
            compiler_params=params(),
            cost_estimate=cost(2e7, 18e6),
        )(core, master, first, second, stays, arrived)
    )


def swap_core(block):
    return lax.ppermute(block, "c", [(0, 1), (1, 0)])


def along_depth(block, step):
    return lax.ppermute(block, DEPTH, [(z, (z + step) % 4) for z in range(4)])


def swap_pair(block):
    return lax.ppermute(block, DEPTH, [(z, 3 - z) for z in range(4)])


def swap_low(block):
    return lax.ppermute(block, "zl", [(0, 1), (1, 0)])


def exchange(rows):
    cut = rows.reshape(-1, CAP, rows.shape[1])
    cut = lax.all_to_all(cut, PLANE, split_axis=0, concat_axis=0, tiled=True)
    return cut.reshape(rows.shape)


def word(*values):
    return jnp.stack([jnp.asarray(v, jnp.int32) for v in values])


def body(
    tokens,
    segment_ids,
    routes,
    cotangent,
    w_qkv,
    w_attn_out,
    w_router,
    norm_gains,
    frozen_in,
    frozen_out,
    new_in,
    new_out,
    dense_master,
    dense_first,
    dense_second,
    master_in,
    first_in,
    second_in,
    master_out,
    first_out,
    second_out,
):
    core, zh, zl = (lax.axis_index(a) for a in ("c", "zh", "zl"))
    z = 2 * zh + zl
    kind = zh ^ zl
    same = jnp.where(kind == core, 1, 0)
    home = word(z, same, core)
    position = word(z, lax.axis_index("x"), lax.axis_index("y"))
    core_word, low_word, same_word = word(core), word(zl), word(same)
    routes = routes.T
    w_router = w_router.T

    in_keep, in_send, out_keep, out_send = cut_weights((), home, new_in, new_out)
    in_mate, out_mate = swap_core(in_send), swap_core(out_send)

    (
        attn_in, qkv_low, mixed_low, lse, middle, ffn_in, plan, rows_sent, grads_sent, frozen_rows, frozen_grads,
    ) = dense_forward(
        (in_send,), word(zh), tokens, segment_ids, routes, cotangent, w_qkv, w_attn_out, w_router, norm_gains
    )
    in_up, in_down, out_up, out_down = choose(
        (plan,), "choose_both", word(core != zh), [(in_keep, in_mate), (out_keep, out_mate)]
    )
    in_below, in_above = along_depth(in_up, 1), along_depth(in_down, -1)
    out_below, out_above = along_depth(out_up, 1), along_depth(out_down, -1)
    rows_own = exchange(rows_sent)
    grads_own = exchange(grads_sent)
    rows_mate, grads_mate = swap_core(rows_own), swap_core(grads_own)

    frozen_result, frozen_back = frozen_expert((in_up,), frozen_rows, frozen_grads, frozen_in, frozen_out)
    in_across = swap_pair(choose((frozen_back,), "choose_in", low_word, [(in_below, in_above)])[0])
    out_across = swap_pair(choose((in_across,), "choose_out", low_word, [(out_below, out_above)])[0])
    in_pieces = (in_keep, in_mate, in_below, in_above, in_across)
    out_pieces = (out_keep, out_mate, out_below, out_above, out_across)

    hidden_own, slope_own = expert_up((), home, rows_own, in_pieces)
    hidden_mate, slope_mate = expert_up((hidden_own,), home, rows_mate, in_pieces)
    hiddens, grads, rows = (hidden_own, hidden_mate), (grads_own, grads_mate), (rows_own, rows_mate)
    keep_half, away_half = word(zh), word(1 - zh)
    out_away = weight_grad((), "grad_out_leaving", away_half, hiddens, grads, 256, 768, LOW)
    out_arrived = swap_pair(out_away)
    pre_mate, back_mate = expert_down(
        (out_away,), home, grads_mate, hidden_mate, slope_mate, in_pieces, out_pieces, True
    )
    pre_own, back_own, value_own = expert_down(
        (back_mate,), home, grads_own, hidden_own, slope_own, in_pieces, out_pieces, False
    )
    merged = merge_rows((), back_own, value_own, swap_core(back_mate))
    back = exchange(merged)
    pres = (pre_own, pre_mate)
    in_away = weight_grad((merged,), "grad_in_leaving", away_half, rows, pres, 384, 512, LOW)
    in_arrived = swap_pair(in_away)
    result_mate = expert_result((in_away,), home, hidden_mate, out_pieces)
    result_arrived = swap_core(result_mate)
    out_kept = weight_grad((result_mate,), "grad_out_staying", keep_half, hiddens, grads, 256, 768, F32)
    in_kept = weight_grad((out_kept,), "grad_in_staying", keep_half, rows, pres, 384, 512, F32)
    out_mine, out_other = reduce_first((in_kept,), low_word, out_kept, out_arrived)
    out_other = swap_low(out_other)

    input_grad, kept, away = dense_backward(
        (out_mine,), core_word, dense_master.shape[0], plan, routes, segment_ids, cotangent, tokens, middle,
        mixed_low, ffn_in, lse, qkv_low, attn_in, w_qkv, w_attn_out, w_router, norm_gains, back, frozen_back,
    )
    arrived = swap_core(away)
    in_mine, in_other = reduce_first((kept,), low_word, in_kept, in_arrived)
    in_other = swap_low(in_other)
    out_stays, out_leaves = reduce_second((in_mine,), same_word, out_mine, out_other)
    out_mate_grad = swap_core(out_leaves)

    padded = kept.shape[1]
    cut = rest = padded // 2
    cube = (4, 4, 4, padded, 128)
    one, two = stage(
        (out_stays,), "scatter_first", position, [[kept.reshape(cube), arrived.reshape(cube)]],
        [(0, 1, 1, (0, cut), 0, (0, cut)), (0, 2, 2, (cut, padded), 1, (0, rest))],
        [(4, 4, cut, 128), (4, 4, rest, 128)],
    )
    first_done = one[0]
    one, two = send_around(one, "x"), send_around(two, "y")
    result = expert_result((first_done,), home, hidden_own, out_pieces, (result_arrived,))
    result_back = exchange(result)
    out_new = expert_update(
        (result,), core_word, master_out, first_out, second_out, out_stays, out_mate_grad, 0
    )
    one, two = stage(
        (out_new[0],), "scatter_second", position, [one, two],
        [(0, 1, 2, (0, cut), 0, (0, cut)), (1, 1, 1, (0, rest), 1, (0, rest))],
        [(4, cut, 128), (4, rest, 128)],
    )
    second_done = one[0]
    one, two = send_around(one, "y"), send_around(two, "x")
    in_stays, in_leaves = reduce_second((second_done,), same_word, in_mine, in_other)
    in_mate_grad = swap_core(in_leaves)
    (both,) = stage(
        (in_stays,), "scatter_third", position, [one, two],
        [(0, 0, 0, (0, cut), 0, (0, cut)), (1, 0, 0, (0, rest), 0, (cut, padded))],
        [(padded, 128)],
    )
    third_done = both[0]
    both = send_around(both, DEPTH)
    in_new = expert_update(
        (third_done,), core_word, master_in, first_in, second_in, in_stays, in_mate_grad, 1
    )
    activations = combine((in_new[0],), plan, middle, result_back, frozen_result)
    dense_new = dense_update((activations,), dense_master, dense_first, dense_second, both)
    return (activations, input_grad) + dense_new + in_new + out_new


def solution(mesh):
    fine = Mesh(mesh.devices.reshape(2, 2, 4, 4, 2), ALL)
    tokens = P(ALL, None)
    flat = P(ALL)
    expert = P(("x", "y", "c"), DEPTH, None)
    return jax.shard_map(
        body,
        mesh=fine,
        in_specs=(tokens,) * 4 + (P(),) * 6 + (expert,) * 2 + (flat,) * 3 + (expert,) * 6,
        out_specs=(tokens,) * 2 + (flat,) * 4 + (expert,) * 8,
        check_vma=False,
    )
```

```python
import math

import jax
import jax.numpy as jnp
from jax import lax
from jax.experimental import pallas as pl
from jax.experimental.pallas import tpu as pltpu
from jax.sharding import Mesh
from jax.sharding import PartitionSpec as P

HEAD_DIM = 64
STEP = 5


norm_eps = 1e-05
learn_rate = 0.02
beta_first = 0.5
beta_second = 0.5
adam_eps = 1e-08
decay_rate = 0.1


PLANE = ("zl", "x", "y")
DEPTH = ("zh", "zl")
ALL = ("zh", "zl", "x", "y", "c")
CAP = 24
PAIRS = 6
EXTRA = 128
VMEM = pl.BlockSpec(memory_space=pltpu.VMEM)
SMEM = pl.BlockSpec(memory_space=pltpu.SMEM)
F32 = jnp.float32
LOW = jnp.bfloat16


def params(**more):
    return pltpu.CompilerParams(vmem_limit_bytes=56 * 1024 * 1024, **more)


def ordered(kernel, count, after, **call):
    extra = len(after)

    def inner(*refs):
        return kernel(*refs[:count], *refs[count + extra :])

    call["in_specs"] = list(call["in_specs"]) + [pl.BlockSpec(memory_space=pl.ANY)] * extra
    made = pl.pallas_call(inner, **call)
    return lambda *arrays: made(*arrays, *after)


def cost(flops, moved):
    return pl.CostEstimate(flops=int(flops), bytes_accessed=int(moved), transcendentals=0)


def mm(left, right):
    return jnp.dot(left, right, preferred_element_type=F32)


def mm_nt(left, right):
    return lax.dot_general(left, right, (((1,), (1,)), ((), ())), preferred_element_type=F32)


def mm_tn(left, right):
    return lax.dot_general(left, right, (((0,), (0,)), ((), ())), preferred_element_type=F32)


def iota(shape, axis):
    return lax.broadcasted_iota(jnp.int32, shape, axis)


def normed(values):
    centered = values - jnp.mean(values, axis=1, keepdims=True)
    scale = lax.rsqrt(jnp.mean(centered * centered, axis=1, keepdims=True) + norm_eps)
    return centered * scale, scale


def norm_backward(values, gain, upstream):
    hat, scale = normed(values)
    gain_grad = jnp.sum(upstream * hat, axis=0, keepdims=True)
    inner = upstream * gain
    mean_inner = jnp.mean(inner, axis=1, keepdims=True)
    mean_hat = jnp.mean(inner * hat, axis=1, keepdims=True)
    return scale * (inner - mean_inner - hat * mean_hat), gain_grad


def as_column(row, eye):
    return jnp.sum(jnp.where(eye, row, jnp.zeros_like(row)), axis=1, keepdims=True)


def as_row(column, eye):
    return jnp.sum(jnp.where(eye, column, jnp.zeros_like(column)), axis=0, keepdims=True)


def attention_mask(segment_row):
    count = segment_row.shape[1]
    down, across = iota((count, count), 0), iota((count, count), 1)
    eye = down == across
    column = jnp.sum(jnp.where(eye, segment_row, 0), axis=1, keepdims=True)
    return (down >= across) & (column == segment_row), eye


def dense_forward_kernel(
    zh_ref, tokens, segments, routes, cotangent, w_qkv, w_out, w_router, gains,
    attn_in_o, qkv_o, mixed_o, lse_o, middle_o, ffn_o, plan_o, rows_o, grads_o, frozen_rows_o, frozen_grads_o,
):
    width = tokens.shape[1]
    count = tokens.shape[0]
    inputs = tokens[...].astype(F32)
    hat, unused = normed(inputs)
    attn_in = (hat * gains[0:1, :]).astype(LOW)
    attn_in_o[...] = attn_in
    qkv_o[...] = mm(attn_in, w_qkv[...]).astype(LOW)
    allowed, eye = attention_mask(segments[...])
    lane = iota((count, 128), 1)
    low_lanes = lane < HEAD_DIM
    lse_all = jnp.zeros((count, 128), F32)
    for pair in range(width // 128):
        at = slice(128 * pair, 128 * pair + 128)
        queries = qkv_o[:, at] * jnp.asarray(HEAD_DIM**-0.5, LOW)
        keys = qkv_o[:, width + 128 * pair : width + 128 * pair + 128]
        values = qkv_o[:, 2 * width + 128 * pair : 2 * width + 128 * pair + 128]
        outs = []
        for half in range(2):
            mine = low_lanes if half == 0 else ~low_lanes
            scores = mm_nt(jnp.where(mine, queries, jnp.zeros_like(queries)), keys)
            scores = jnp.where(allowed, scores, -1e30)
            top = jnp.max(scores, axis=1, keepdims=True)
            raised = jnp.exp(scores - top)
            total = jnp.sum(raised, axis=1, keepdims=True)
            probs = (raised * (1.0 / total)).astype(LOW)
            outs.append(mm(probs, values))
            lse_all = jnp.where(lane == 2 * pair + half, top + jnp.log(total), lse_all)
        mixed_o[:, at] = jnp.where(low_lanes, outs[0], outs[1]).astype(LOW)
    lse_o[...] = lse_all
    middle = inputs + mm(mixed_o[...], w_out[...])
    middle_o[...] = middle
    hat, unused = normed(middle)
    ffn = (hat * gains[1:2, :]).astype(LOW)
    ffn_o[...] = ffn
    logits = mm_nt(ffn, w_router[...])
    experts = iota(logits.shape, 1)
    lists = [as_column(routes[k : k + 1, :], eye) for k in range(2)]
    picks = [experts == column for column in lists]
    chosen = [jnp.sum(jnp.where(p, logits, 0.0), axis=1, keepdims=True) for p in picks]
    top = jnp.maximum(chosen[0], chosen[1])
    raised = [jnp.exp(c - top) for c in chosen]
    gates = [r / (raised[0] + raised[1]) for r in raised]
    named = (picks[0] | picks[1]).astype(F32).astype(LOW)
    earlier = (iota((count, count), 0) > iota((count, count), 1)).astype(F32).astype(LOW)
    before = mm(earlier, named)
    zh = zh_ref[0]
    new_place, old_place = [], []
    for k in range(2):
        route = lists[k]
        slot = jnp.sum(jnp.where(picks[k], before, 0.0), axis=1, keepdims=True).astype(jnp.int32)
        fresh = route - 1
        block = 16 * ((fresh & 1) ^ zh) + lax.shift_right_arithmetic(fresh, 1)
        new_place.append(jnp.where(route > 0, block * CAP + slot, -1))
        old_place.append(jnp.where(route > 0, -1, slot))
    columns = gates + [p.astype(F32) for p in new_place + old_place]
    plan = jnp.zeros((count, 128), F32)
    for i, column in enumerate(columns):
        plan = jnp.where(lane == i, column, plan)
    plan_o[...] = plan
    up = cotangent[...].astype(F32)
    scaled = [(g * up).astype(LOW) for g in gates]
    for places, size, rows_ref, grads_ref in (
        (new_place, rows_o.shape[0], rows_o, grads_o),
        (old_place, CAP, frozen_rows_o, frozen_grads_o),
    ):
        slots = iota((size, count), 0)
        spread = [(slots == as_row(p, eye)).astype(F32).astype(LOW) for p in places]
        rows_ref[...] = mm(spread[0] + spread[1], ffn).astype(LOW)
        grads_ref[...] = (mm(spread[0], scaled[0]) + mm(spread[1], scaled[1])).astype(LOW)


def dense_forward(after, zh, tokens, segments, routes, cotangent, w_qkv, w_out, w_router, gains):
    count, width = tokens.shape
    slots = (w_router.shape[0] - 1) * CAP
    shapes = [
        ((count, width), LOW), ((count, 3 * width), LOW), ((count, width), LOW), ((count, 128), F32),
        ((count, width), F32), ((count, width), LOW), ((count, 128), F32),
        ((slots, width), LOW), ((slots, width), LOW), ((CAP, width), LOW), ((CAP, width), LOW),
    ]
    return ordered(
        dense_forward_kernel, 9, after,
        name="dense_forward",
        out_shape=[jax.ShapeDtypeStruct(s, t) for s, t in shapes],
        in_specs=[SMEM] + [VMEM] * 8,
        out_specs=[VMEM] * len(shapes),
        compiler_params=params(),
        cost_estimate=cost(8e9, 30e6),
    )(zh, tokens, segments, routes, cotangent, w_qkv, w_out, w_router, gains)


def dense_backward_kernel(
    core_ref, plan, routes, segments, cotangent, tokens, middle, mixed, ffn, lse, qkv, attn_in,
    w_qkv, w_out, w_router, gains, back, frozen_back,
    input_grad_o, kept_o, away_o,
    flat, gqkv,
):
    count, width = tokens.shape
    expert_total = w_router.shape[0]
    up = cotangent[...].astype(F32)
    gates = [plan[:, k : k + 1] for k in range(2)]
    new_place = [plan[:, 2 + k : 3 + k].astype(jnp.int32) for k in range(2)]
    old_place = [plan[:, 4 + k : 5 + k].astype(jnp.int32) for k in range(2)]
    allowed, eye = attention_mask(segments[...])

    grad_ffn = jnp.zeros((count, width), F32)
    weighted = [jnp.zeros((count, 1), F32) for k in range(2)]
    for places, ref in ((new_place, back), (old_place, frozen_back)):
        size = ref.shape[0]
        slots = iota((count, size), 1)
        for k in range(2):
            choice = (slots == places[k]).astype(F32).astype(LOW)
            picked = mm(choice, ref[...])
            grad_ffn = grad_ffn + picked[:, :width]
            tail = picked[:, width:]
            weighted[k] = weighted[k] + jnp.sum(tail, axis=1, keepdims=True)
    both = weighted[0] + weighted[1]
    experts = iota((count, expert_total), 1)
    grad_logits = jnp.zeros((count, expert_total), F32)
    for k in range(2):
        grad_logits = jnp.where(
            experts == as_column(routes[k : k + 1, :], eye), weighted[k] - gates[k] * both, grad_logits
        )
    grad_logits = grad_logits.astype(LOW)
    grad_ffn = grad_ffn + mm(grad_logits, w_router[...])
    grad_norm, gain_ffn = norm_backward(middle[...], gains[1:2, :], grad_ffn)
    grad_middle = up + grad_norm
    grad_branch = grad_middle.astype(LOW)

    blocks = width // 128
    first_row = 3 * blocks * width
    attn_out_grad = mm_tn(mixed[...], grad_branch)
    for j in range(blocks):
        flat[pl.ds(first_row + j, width, stride=blocks), :] = attn_out_grad[:, 128 * j : 128 * j + 128]
    router_row = first_row + blocks * width
    router_rows = width * expert_total // 128
    padded_logits = jnp.concatenate(
        [grad_logits, jnp.zeros((count, 128 - expert_total), LOW)], axis=1
    )
    router_grad = mm_tn(ffn[...], padded_logits)
    feature = iota((width, 128), 0)
    lane_w = iota((width, 128), 1)
    start = feature * expert_total
    offset = start & 127
    turned = jnp.take_along_axis(router_grad, (lane_w - offset) & 127, axis=1)
    wrapped = lane_w < offset
    row_of = lax.shift_right_logical(iota((router_rows, width), 1) * expert_total, 7)
    row_here = iota((router_rows, width), 0)
    here = (row_of == row_here).astype(F32)
    after = (row_of + 1 == row_here).astype(F32)
    exact = lambda a, b: jnp.dot(a, b, precision=lax.Precision.HIGHEST, preferred_element_type=F32)
    flat[router_row : router_row + router_rows, :] = exact(
        here, jnp.where(wrapped, 0.0, turned)
    ) + exact(after, jnp.where(wrapped, turned, 0.0))
    gain_row = router_row + router_rows

    grad_mixed = mm_nt(grad_branch, w_out[...]).astype(LOW)
    lane = iota((count, 128), 1)
    low_lanes = lane < HEAD_DIM
    scale = HEAD_DIM**-0.5
    for pair in range(blocks):
        at = slice(128 * pair, 128 * pair + 128)
        queries = qkv[:, at] * jnp.asarray(scale, LOW)
        keys = qkv[:, width + 128 * pair : width + 128 * pair + 128]
        values = qkv[:, 2 * width + 128 * pair : 2 * width + 128 * pair + 128]
        grads = grad_mixed[:, at]
        grad_q = jnp.zeros((count, 128), F32)
        grad_k = jnp.zeros((count, 128), F32)
        grad_v = jnp.zeros((count, 128), F32)
        for half in range(2):
            mine = low_lanes if half == 0 else ~low_lanes
            only = lambda v: jnp.where(mine, v, jnp.zeros_like(v))
            q_half, g_half, k_half = only(queries), only(grads), only(keys)
            scores = jnp.where(allowed, mm_nt(q_half, keys), -1e30)
            head = 2 * pair + half
            probs = jnp.exp(scores - lse[:, head : head + 1])
            grad_probs = mm_nt(g_half, values)
            grad_v = grad_v + mm_tn(probs.astype(LOW), g_half)
            dots = jnp.sum(probs * grad_probs, axis=1, keepdims=True)
            grad_scores = (probs * (grad_probs - dots)).astype(LOW)
            grad_q = grad_q + mm(grad_scores, k_half)
            grad_k = grad_k + mm_tn(grad_scores, q_half)
        gqkv[:, at] = (grad_q * scale).astype(LOW)
        gqkv[:, width + 128 * pair : width + 128 * pair + 128] = grad_k.astype(LOW)
        gqkv[:, 2 * width + 128 * pair : 2 * width + 128 * pair + 128] = grad_v.astype(LOW)
    for j in range(0, 3 * blocks, 2):
        piece = mm_tn(attn_in[...], gqkv[:, 128 * j : 128 * j + 256])
        flat[pl.ds(j, width, stride=3 * blocks), :] = piece[:, :128]
        flat[pl.ds(j + 1, width, stride=3 * blocks), :] = piece[:, 128:]
    grad_attn = mm_nt(gqkv[...], w_qkv[...])
    grad_norm, gain_attn = norm_backward(tokens[...].astype(F32), gains[0:1, :], grad_attn)
    input_grad_o[...] = grad_middle + grad_norm
    for j in range(blocks):
        flat[gain_row + j : gain_row + j + 1, :] = gain_attn[:, 128 * j : 128 * j + 128]
        flat[gain_row + blocks + j : gain_row + blocks + j + 1, :] = gain_ffn[:, 128 * j : 128 * j + 128]
    last = gain_row + 2 * blocks
    flat[last:, :] = jnp.zeros((flat.shape[0] - last, 128), F32)

    core = core_ref[0]
    rows = flat.shape[0] // 128
    padded = kept_o.shape[1]

    @pl.loop(0, kept_o.shape[0])
    def move(i):
        kept_o[pl.ds(i, 1)] = flat[pl.ds((2 * i + core) * rows, padded), :].astype(LOW)[None]
        away_o[pl.ds(i, 1)] = flat[pl.ds((2 * i + 1 - core) * rows, padded), :].astype(LOW)[None]


def dense_backward(after, core, dense_rows, *arrays):
    count, width = arrays[4].shape
    rows = dense_rows // 128
    padded = (rows + 31) // 32 * 32
    return ordered(
        dense_backward_kernel, 1 + len(arrays), after,
        name="dense_backward",
        out_shape=[
            jax.ShapeDtypeStruct((count, width), F32),
            jax.ShapeDtypeStruct((64, padded, 128), LOW),
            jax.ShapeDtypeStruct((64, padded, 128), LOW),
        ],
        in_specs=[SMEM] + [VMEM] * len(arrays),
        out_specs=[VMEM] * 3,
        scratch_shapes=[
            pltpu.VMEM((rows * 128 + padded - rows, 128), F32),
            pltpu.VMEM((count, 3 * width), LOW),
        ],
        compiler_params=params(),
        cost_estimate=cost(12e9, 40e6),
    )(core, *arrays)


def combine_kernel(plan, middle, results, frozen_result, out):
    count, width = middle.shape
    total = middle[...]
    for first, ref in ((2, results), (4, frozen_result)):
        slots = iota((count, ref.shape[0]), 1)
        for k in range(2):
            place = plan[:, first + k : first + k + 1].astype(jnp.int32)
            total = total + plan[:, k : k + 1] * mm((slots == place).astype(F32).astype(LOW), ref[...])
    out[...] = total.astype(LOW)


def combine(after, plan, middle, results, frozen_result):
    return ordered(
        combine_kernel, 4, after,
        name="combine",
        out_shape=jax.ShapeDtypeStruct(middle.shape, LOW),
        in_specs=[VMEM] * 4,
        out_specs=VMEM,
        compiler_params=params(),
        cost_estimate=cost(200e9, 4e6),
    )(plan, middle, results, frozen_result)


def gelu_pair(pre):
    area = 0.5 + 0.5 * lax.erf(pre * (0.5**0.5))
    density = jnp.exp(-0.5 * pre * pre) * (1.0 / (2.0 * math.pi) ** 0.5)
    return pre * area, area + pre * density


def shift_weight(home, pieces, full, sems):
    keep, mate, below, above, across = pieces
    z, own_kind = home[0], home[1]
    rows = keep.shape[0]
    spot = lambda step: full.at[pl.ds(pl.multiple_of(((z + step) & 3) * rows, 64), rows), :]

    @pl.when(own_kind == 1)
    def from_keep():
        pltpu.make_async_copy(keep, spot(0), sems.at[0]).start()

    @pl.when(own_kind == 0)
    def from_mate():
        pltpu.make_async_copy(mate, spot(0), sems.at[0]).start()

    copies = [
        pltpu.make_async_copy(piece, spot(step), sems.at[1 + i])
        for i, (piece, step) in enumerate(((below, 3), (above, 1), (across, 2)))
    ]
    for copy in copies:
        copy.start()
    return [pltpu.make_async_copy(keep, spot(0), sems.at[0])] + copies


HBM = pl.BlockSpec(memory_space=pl.ANY)


def expert_up_kernel(home, rows, keep, mate, below, above, across, hidden_o, slope_o, weight, sems):
    @pl.when(pl.program_id(0) == 0)
    def load():
        for copy in shift_weight(home, (keep, mate, below, above, across), weight, sems):
            copy.wait()

    pre = mm(rows[...], weight[...])
    hidden, slope = gelu_pair(pre)
    hidden_o[...] = hidden.astype(LOW)
    slope_o[...] = slope.astype(LOW)


def expert_up(after, home, rows, pieces):
    count, width = rows.shape
    hidden = pieces[0].shape[1]
    step = 256
    wide = jax.ShapeDtypeStruct((count, hidden), LOW)
    return ordered(
        expert_up_kernel, 7, after,
        name="expert_up",
        out_shape=[wide, wide],
        grid=(count // step,),
        in_specs=[SMEM, pl.BlockSpec((step, width), lambda i: (i, 0))] + [HBM] * 5,
        out_specs=[pl.BlockSpec((step, hidden), lambda i: (i, 0))] * 2,
        scratch_shapes=[pltpu.VMEM((width, hidden), LOW), pltpu.SemaphoreType.DMA((4,))],
        compiler_params=params(),
        cost_estimate=cost(12e9, 10e6),
    )(home, rows, *pieces)


def split_three(value):
    high = value.astype(LOW)
    rest = value - high.astype(F32)
    mid = rest.astype(LOW)
    return high, mid, (rest - mid.astype(F32)).astype(LOW)


def with_extra(rows, value):
    lane = iota((rows.shape[0], EXTRA), 1)
    extra = jnp.zeros((rows.shape[0], EXTRA), F32)
    for i, term in enumerate(split_three(value)):
        extra = jnp.where(lane == i, term.astype(F32), extra)
    return rows.astype(LOW), extra.astype(LOW)


def expert_down_kernel(home, grads, hidden, slope, *refs):
    in_pieces, out_pieces = refs[:5], refs[5:10]
    outs, (w_in, w_out, in_sems, out_sems) = refs[10:-4], refs[-4:]

    @pl.when(pl.program_id(0) == 0)
    def load():
        copies = shift_weight(home, out_pieces, w_out, out_sems)
        copies = copies + shift_weight(home, in_pieces, w_in, in_sems)
        for copy in copies:
            copy.wait()

    grad_hidden = mm_nt(grads[...], w_out[...])
    value = jnp.sum(hidden[...].astype(F32) * grad_hidden, axis=1, keepdims=True)
    grad_pre = (grad_hidden * slope[...].astype(F32)).astype(LOW)
    outs[0][...] = grad_pre
    grad_rows = mm_nt(grad_pre, w_in[...])
    width = grad_rows.shape[1]
    if len(outs) == 2:
        rows, extra = with_extra(grad_rows, value)
        outs[1][:, :width] = rows
        outs[1][:, width:] = extra
    else:
        outs[1][...] = grad_rows
        outs[2][...] = jnp.broadcast_to(value, outs[2].shape)


def expert_down(after, home, grads, hidden, slope, in_pieces, out_pieces, leaves):
    count, width = grads.shape
    wide = hidden.shape[1]
    step = 256
    block = lambda cols: pl.BlockSpec((step, cols), lambda i: (i, 0))
    if leaves:
        outs = [((count, wide), LOW), ((count, width + EXTRA), LOW)]
    else:
        outs = [((count, wide), LOW), ((count, width), F32), ((count, EXTRA), F32)]
    return ordered(
        expert_down_kernel, 14, after,
        name="expert_down_leaving" if leaves else "expert_down_staying",
        out_shape=[jax.ShapeDtypeStruct(s, t) for s, t in outs],
        grid=(count // step,),
        in_specs=[SMEM, block(width), block(wide), block(wide)] + [HBM] * 10,
        out_specs=[block(s[1]) for s, t in outs],
        scratch_shapes=[
            pltpu.VMEM((width, wide), LOW),
            pltpu.VMEM((wide, width), LOW),
            pltpu.SemaphoreType.DMA((4,)),
            pltpu.SemaphoreType.DMA((4,)),
        ],
        compiler_params=params(),
        cost_estimate=cost(12e9, 12e6),
    )(home, grads, hidden, slope, *in_pieces, *out_pieces)


def expert_result_kernel(home, hidden, *refs):
    pieces, more, (out, weight, sems) = refs[:5], refs[5:-3], refs[-3:]

    @pl.when(pl.program_id(0) == 0)
    def load():
        for copy in shift_weight(home, pieces, weight, sems):
            copy.wait()

    total = mm(hidden[...], weight[...])
    for term in more:
        total = total + term[...].astype(F32)
    out[...] = total.astype(LOW)


def expert_result(after, home, hidden, pieces, arrived=()):
    count, wide = hidden.shape
    width = pieces[0].shape[1]
    step = 256
    block = lambda cols: pl.BlockSpec((step, cols), lambda i: (i, 0))
    return ordered(
        expert_result_kernel, 7 + len(arrived), after,
        name="expert_result",
        out_shape=jax.ShapeDtypeStruct((count, width), LOW),
        grid=(count // step,),
        in_specs=[SMEM, block(wide)] + [HBM] * 5 + [block(width)] * len(arrived),
        out_specs=block(width),
        scratch_shapes=[pltpu.VMEM((wide, width), LOW), pltpu.SemaphoreType.DMA((4,))],
        compiler_params=params(),
        cost_estimate=cost(6e9, 6e6),
    )(home, hidden, *pieces, *arrived)


def weight_grad_kernel(half_ref, left_own, left_mate, right_own, right_mate, out):
    total = mm_tn(left_own[...], right_own[...]) + mm_tn(left_mate[...], right_mate[...])
    out[...] = total.astype(out.dtype)


def weight_grad(after, name, half, lefts, rights, left_step, right_step, kind):
    rows, left_width = lefts[0].shape
    right_width = rights[0].shape[1]
    steps = left_width // 2 // left_step
    left = pl.BlockSpec((rows, left_step), lambda i, j, half: (0, half[0] * steps + i))
    right = pl.BlockSpec((rows, right_step), lambda i, j, half: (0, j))

    def inner(half_ref, a, b, c, d, *refs):
        weight_grad_kernel(half_ref, a, b, c, d, refs[-1])

    return pl.pallas_call(
        inner,
        name=name,
        out_shape=jax.ShapeDtypeStruct((left_width // 2, right_width), kind),
        grid_spec=pltpu.PrefetchScalarGridSpec(
            num_scalar_prefetch=1,
            grid=(steps, right_width // right_step),
            in_specs=[left, left, right, right] + [HBM] * len(after),
            out_specs=pl.BlockSpec((left_step, right_step), lambda i, j, half: (i, j)),
        ),
        compiler_params=params(),
        cost_estimate=cost(6e9, 6e6),
    )(half, *lefts, *rights, *after)


def cut_weights_kernel(home, new_in, new_out, in_keep, in_send, out_keep, out_send):
    core = home[2]
    cols = in_keep.shape[1] // 4
    rows = out_keep.shape[0]
    for half, to_in, to_out in ((core, in_keep, out_keep), (1 - core, in_send, out_send)):
        for block in range(4):
            start = pl.multiple_of((2 * block + half) * cols, 128)
            to_in[:, block * cols : (block + 1) * cols] = new_in[0, :, pl.ds(start, cols)]
        to_out[...] = new_out[0, pl.ds(pl.multiple_of(half * rows, 64), rows), :]


def cut_weights(after, home, new_in, new_out):
    halves = [(new_in.shape[1], new_in.shape[2] // 2)] * 2 + [(new_out.shape[1] // 2, new_out.shape[2])] * 2
    return ordered(
        cut_weights_kernel, 3, after,
        name="cut_weights",
        out_shape=[jax.ShapeDtypeStruct(h, LOW) for h in halves],
        in_specs=[SMEM, VMEM, VMEM],
        out_specs=[VMEM] * 4,
        compiler_params=params(),
        cost_estimate=cost(1e5, 5e6),
    )(home, new_in, new_out)


def choose(after, name, flag, pairs, both):
    count = len(pairs)
    each = 2 if both else 1

    def kernel(flag_ref, *refs):
        straight = flag_ref[0] == 1
        for i in range(count):
            first, second = refs[2 * i][...], refs[2 * i + 1][...]
            outs = refs[2 * count + each * i : 2 * count + each * i + each]
            outs[0][...] = jnp.where(straight, first, second)
            if both:
                outs[1][...] = jnp.where(straight, second, first)

    shapes = [jax.ShapeDtypeStruct(p[0].shape, p[0].dtype) for p in pairs for j in range(each)]
    return ordered(
        kernel, 1 + 2 * count, after,
        name=name,
        out_shape=shapes,
        in_specs=[SMEM] + [VMEM] * (2 * count),
        out_specs=[VMEM] * len(shapes),
        compiler_params=params(),
        cost_estimate=cost(1e5, 4e6),
    )(flag, *[a for p in pairs for a in p])


def reduce_first(after, low, kept, arrived):
    rows, columns = kept.shape[0] // 2, kept.shape[1]

    def kernel(low_ref, kept, arrived, mine, other):
        for out, which in ((mine, low_ref[0]), (other, 1 - low_ref[0])):
            at = pl.ds(pl.multiple_of(which * rows, 64), rows)
            out[...] = (kept[at, :] + arrived[at, :].astype(F32)).astype(out.dtype)

    return ordered(
        kernel, 3, after,
        name="reduce_first",
        out_shape=[jax.ShapeDtypeStruct((rows, columns), t) for t in (F32, LOW)],
        in_specs=[SMEM, VMEM, VMEM],
        out_specs=[VMEM] * 2,
        compiler_params=params(),
        cost_estimate=cost(1e6, 6e6),
    )(low, kept, arrived)


def reduce_second(after, same, mine, other):
    def kernel(same_ref, mine, other, stays, leaves):
        straight = same_ref[0] == 1
        near, far = mine[...], other[...].astype(F32)
        stays[...] = jnp.where(straight, near, far)
        leaves[...] = jnp.where(straight, far, near).astype(LOW)

    return ordered(
        kernel, 3, after,
        name="reduce_second",
        out_shape=[jax.ShapeDtypeStruct(mine.shape, t) for t in (F32, LOW)],
        in_specs=[SMEM, VMEM, VMEM],
        out_specs=[VMEM] * 2,
        compiler_params=params(),
        cost_estimate=cost(1e6, 6e6),
    )(same, mine, other)


def merge_kernel(rows, value, arrived, out):
    width = rows.shape[1]
    extra = jnp.sum(arrived[:, width:].astype(F32), axis=1, keepdims=True)
    low, terms = with_extra(
        rows[...] + arrived[:, :width].astype(F32), value[:, 0:1] + extra
    )
    out[:, :width] = low
    out[:, width:] = terms


def merge_rows(after, rows, value, arrived):
    return ordered(
        merge_kernel, 3, after,
        name="merge_rows",
        out_shape=jax.ShapeDtypeStruct(arrived.shape, LOW),
        in_specs=[VMEM] * 3,
        out_specs=VMEM,
        compiler_params=params(),
        cost_estimate=cost(1e7, 6e6),
    )(rows, value, arrived)


def frozen_kernel(rows, grads, w_in, w_out, result_o, back_o, result_sum, back_sum, value_sum):
    step = pl.program_id(0)

    @pl.when(step == 0)
    def clear():
        result_sum[...] = jnp.zeros_like(result_sum)
        back_sum[...] = jnp.zeros_like(back_sum)
        value_sum[...] = jnp.zeros_like(value_sum)

    hidden, slope = gelu_pair(mm(rows[...], w_in[...]))
    hidden = hidden.astype(LOW)
    result_sum[...] += mm(hidden, w_out[...])
    grad_hidden = mm_nt(grads[...], w_out[...])
    value_sum[...] += jnp.sum(hidden.astype(F32) * grad_hidden, axis=1, keepdims=True)
    back_sum[...] += mm_nt((grad_hidden * slope).astype(LOW), w_in[...])

    @pl.when(step == pl.num_programs(0) - 1)
    def finish():
        result_o[...] = result_sum[...].astype(LOW)
        width = back_sum.shape[1]
        low, terms = with_extra(back_sum[...], value_sum[:, 0:1])
        back_o[:, :width] = low
        back_o[:, width:] = terms


def frozen_expert(after, rows, grads, w_in, w_out):
    count, width = rows.shape
    wide = w_in.shape[1]
    step = 512
    small = pl.BlockSpec((count, width), lambda i: (0, 0))
    return ordered(
        frozen_kernel, 4, after,
        name="frozen_expert",
        out_shape=[
            jax.ShapeDtypeStruct((count, width), LOW),
            jax.ShapeDtypeStruct((count, width + EXTRA), LOW),
        ],
        grid=(wide // step,),
        in_specs=[
            small, small,
            pl.BlockSpec((width, step), lambda i: (0, i)),
            pl.BlockSpec((step, width), lambda i: (i, 0)),
        ],
        out_specs=[small, pl.BlockSpec((count, width + EXTRA), lambda i: (0, 0))],
        scratch_shapes=[
            pltpu.VMEM((count, width), F32),
            pltpu.VMEM((count, width), F32),
            pltpu.VMEM((count, EXTRA), F32),
        ],
        compiler_params=params(),
        cost_estimate=cost(4e9, 10e6),
    )(rows, grads, w_in, w_out)


def add_kernel(near, far, out):
    out[...] = (near[...].astype(F32) + far[...].astype(F32)).astype(out.dtype)


def add_halves(after, near, far):
    step = 16
    block = pl.BlockSpec((step,) + near.shape[1:], lambda i: (i, 0, 0))
    return ordered(
        add_kernel, 2, after,
        name="add_halves",
        out_shape=jax.ShapeDtypeStruct(near.shape, LOW),
        grid=(near.shape[0] // step,),
        in_specs=[block] * 2,
        out_specs=block,
        compiler_params=params(),
        cost_estimate=cost(1e6, 8e6),
    )(near, far)


def adamw_values(master, first, second, grad):
    first_new = beta_first * first + (1.0 - beta_first) * grad
    second_new = beta_second * second + (1.0 - beta_second) * grad * grad
    first_hat = first_new * (1.0 / (1.0 - beta_first**STEP))
    second_hat = second_new * (1.0 / (1.0 - beta_second**STEP))
    master_new = master - learn_rate * (
        first_hat / (jnp.sqrt(second_hat) + adam_eps) + decay_rate * master
    )
    return master_new, first_new, second_new, master_new.astype(LOW)


def dense_update_kernel(master, first, second, terms, *outs):
    rows = master.shape[0]
    grad = jnp.sum(terms[...].astype(F32), axis=0)[:rows]
    for out, value in zip(outs, adamw_values(master[...], first[...], second[...], grad)):
        out[...] = value


def dense_update(after, master, first, second, terms):
    shape = (master.shape[0] // 128, 128)
    results = ordered(
        dense_update_kernel, 4, after,
        name="dense_update",
        out_shape=[jax.ShapeDtypeStruct(shape, t) for t in (F32, F32, F32, LOW)],
        in_specs=[VMEM] * 4,
        out_specs=[VMEM] * 4,
        compiler_params=params(),
        cost_estimate=cost(1e6, 4e6),
    )(*(a.reshape(shape) for a in (master, first, second)), terms)
    return tuple(r.reshape(master.shape) for r in results)


def expert_update(after, core, master, first, second, stays, arrived, axis):
    rows, columns = master.shape[1:]
    if axis == 1:
        blocks, width = 4, columns // 4
        half = (rows, width // 2)
    else:
        blocks, width = 3, columns // 3
        half = (rows // 2, width)

    def kernel(core_ref, master, first, second, stays, arrived, *outs):
        near, far = stays[...], arrived[...].astype(F32)
        swapped = core_ref[0] == 1
        grad = jnp.concatenate(
            [jnp.where(swapped, far, near), jnp.where(swapped, near, far)], axis=axis
        )
        values = adamw_values(master[0], first[0], second[0], grad)
        for out, value in zip(outs, values):
            out[0] = value

    wide = pl.BlockSpec((1, rows, width), lambda i: (0, 0, i))
    slim = pl.BlockSpec(half, lambda i: (0, i))
    return tuple(
        ordered(
        kernel, 6, after,
            name="update_in" if axis == 1 else "update_out",
            out_shape=[jax.ShapeDtypeStruct(master.shape, t) for t in (F32, F32, F32, LOW)],
            grid=(blocks,),
            in_specs=[SMEM, wide, wide, wide, slim, slim],
            out_specs=[wide] * 4,
            compiler_params=params(),
            cost_estimate=cost(2e7, 18e6),
        )(core, master, first, second, stays, arrived)
    )


def swap_core(block):
    return lax.ppermute(block, "c", [(0, 1), (1, 0)])


def along_depth(block, step):
    return lax.ppermute(block, DEPTH, [(z, (z + step) % 4) for z in range(4)])


def swap_pair(block):
    return lax.ppermute(block, DEPTH, [(z, 3 - z) for z in range(4)])


def swap_low(block):
    return lax.ppermute(block, "zl", [(0, 1), (1, 0)])


def exchange(rows):
    cut = rows.reshape(-1, CAP, rows.shape[1])
    cut = lax.all_to_all(cut, PLANE, split_axis=0, concat_axis=0, tiled=True)
    return cut.reshape(rows.shape)


def word(*values):
    return jnp.stack([jnp.asarray(v, jnp.int32) for v in values])


def body(
    tokens,
    segment_ids,
    routes,
    cotangent,
    w_qkv,
    w_attn_out,
    w_router,
    norm_gains,
    frozen_in,
    frozen_out,
    new_in,
    new_out,
    dense_master,
    dense_first,
    dense_second,
    master_in,
    first_in,
    second_in,
    master_out,
    first_out,
    second_out,
):
    core, zh, zl = (lax.axis_index(a) for a in ("c", "zh", "zl"))
    z = 2 * zh + zl
    kind = zh ^ zl
    same = jnp.where(kind == core, 1, 0)
    home = word(z, same, core)
    core_word, low_word, same_word = word(core), word(zl), word(same)
    routes = routes.T
    w_router = w_router.T

    in_keep, in_send, out_keep, out_send = cut_weights((), home, new_in, new_out)
    in_mate, out_mate = swap_core(in_send), swap_core(out_send)

    in_up, in_down, out_up, out_down = choose(
        (), "choose_both", word(core != zh), [(in_keep, in_mate), (out_keep, out_mate)], True
    )
    (
        attn_in, qkv_low, mixed_low, lse, middle, ffn_in, plan, rows_sent, grads_sent, frozen_rows, frozen_grads,
    ) = dense_forward(
        (in_up,), word(zh), tokens, segment_ids, routes, cotangent, w_qkv, w_attn_out, w_router, norm_gains
    )
    in_below, in_above = along_depth(in_up, 1), along_depth(in_down, -1)
    out_below, out_above = along_depth(out_up, 1), along_depth(out_down, -1)
    rows_own = exchange(rows_sent)
    grads_own = exchange(grads_sent)
    rows_mate, grads_mate = swap_core(rows_own), swap_core(grads_own)

    frozen_result, frozen_back = frozen_expert((in_up,), frozen_rows, frozen_grads, frozen_in, frozen_out)
    in_far = choose((frozen_back,), "choose_in", low_word, [(in_below, in_above)], False)[0]
    in_across = swap_pair(in_far)
    out_across = swap_pair(choose((in_far,), "choose_out", low_word, [(out_below, out_above)], False)[0])
    in_pieces = (in_keep, in_mate, in_below, in_above, in_across)
    out_pieces = (out_keep, out_mate, out_below, out_above, out_across)

    hidden_own, slope_own = expert_up((), home, rows_own, in_pieces)
    hidden_mate, slope_mate = expert_up((hidden_own,), home, rows_mate, in_pieces)
    hiddens, grads, rows = (hidden_own, hidden_mate), (grads_own, grads_mate), (rows_own, rows_mate)
    keep_half, away_half = word(zh), word(1 - zh)
    result_mate = expert_result((hidden_mate,), home, hidden_mate, out_pieces)
    result_arrived = swap_core(result_mate)
    out_away = weight_grad((result_mate,), "grad_out_leaving", away_half, hiddens, grads, 256, 768, LOW)
    out_arrived = swap_pair(out_away)
    pre_mate, back_mate = expert_down(
        (out_away,), home, grads_mate, hidden_mate, slope_mate, in_pieces, out_pieces, True
    )
    pre_own, back_own, value_own = expert_down(
        (back_mate,), home, grads_own, hidden_own, slope_own, in_pieces, out_pieces, False
    )
    merged = merge_rows((), back_own, value_own, swap_core(back_mate))
    back = exchange(merged)
    pres = (pre_own, pre_mate)
    in_away = weight_grad((merged,), "grad_in_leaving", away_half, rows, pres, 384, 512, LOW)
    in_arrived = swap_pair(in_away)
    result = expert_result((in_away,), home, hidden_own, out_pieces, (result_arrived,))
    result_back = exchange(result)
    out_kept = weight_grad((result,), "grad_out_staying", keep_half, hiddens, grads, 256, 768, F32)
    in_kept = weight_grad((out_kept,), "grad_in_staying", keep_half, rows, pres, 384, 512, F32)
    out_mine, out_other = reduce_first((in_kept,), low_word, out_kept, out_arrived)
    out_other = swap_low(out_other)

    input_grad, kept, away = dense_backward(
        (out_mine, in_arrived), core_word, dense_master.shape[0], plan, routes, segment_ids, cotangent, tokens, middle,
        mixed_low, ffn_in, lse, qkv_low, attn_in, w_qkv, w_attn_out, w_router, norm_gains, back, frozen_back,
    )
    arrived = swap_core(away)
    activations = combine((kept,), plan, middle, result_back, frozen_result)
    summed = add_halves((activations,), kept, arrived)
    terms = lax.all_to_all(summed, ("zh", "zl", "x", "y"), split_axis=0, concat_axis=0, tiled=True)
    in_mine, in_other = reduce_first((summed,), low_word, in_kept, in_arrived)
    in_other = swap_low(in_other)
    out_stays, out_leaves = reduce_second((in_mine,), same_word, out_mine, out_other)
    out_mate_grad = swap_core(out_leaves)
    out_new = expert_update(
        (out_stays,), core_word, master_out, first_out, second_out, out_stays, out_mate_grad, 0
    )
    in_stays, in_leaves = reduce_second((out_new[0],), same_word, in_mine, in_other)
    in_mate_grad = swap_core(in_leaves)
    in_new = expert_update(
        (in_stays,), core_word, master_in, first_in, second_in, in_stays, in_mate_grad, 1
    )
    dense_new = dense_update((in_new[0],), dense_master, dense_first, dense_second, terms)
    return (activations, input_grad) + dense_new + in_new + out_new


def solution(mesh):
    fine = Mesh(mesh.devices.reshape(2, 2, 4, 4, 2), ALL)
    tokens = P(ALL, None)
    flat = P(ALL)
    expert = P(("x", "y", "c"), DEPTH, None)
    return jax.shard_map(
        body,
        mesh=fine,
        in_specs=(tokens,) * 4 + (P(),) * 6 + (expert,) * 2 + (flat,) * 3 + (expert,) * 6,
        out_specs=(tokens,) * 2 + (flat,) * 4 + (expert,) * 8,
        check_vma=False,
    )
```

```python
import math

import jax
import jax.numpy as jnp
from jax import lax
from jax.experimental import pallas as pl
from jax.experimental.pallas import tpu as pltpu
from jax.sharding import Mesh
from jax.sharding import PartitionSpec as P

HEAD_DIM = 64
STEP = 5


norm_eps = 1e-05
learn_rate = 0.02
beta_first = 0.5
beta_second = 0.5
adam_eps = 1e-08
decay_rate = 0.1


PLANE = ("zl", "x", "y")
DEPTH = ("zh", "zl")
ALL = ("zh", "zl", "x", "y", "c")
CAP = 24
PAIRS = 6
EXTRA = 128
VMEM = pl.BlockSpec(memory_space=pltpu.VMEM)
SMEM = pl.BlockSpec(memory_space=pltpu.SMEM)
F32 = jnp.float32
LOW = jnp.bfloat16


def params(**more):
    return pltpu.CompilerParams(vmem_limit_bytes=56 * 1024 * 1024, **more)


def ordered(kernel, count, after, **call):
    extra = len(after)

    def inner(*refs):
        return kernel(*refs[:count], *refs[count + extra :])

    call["in_specs"] = list(call["in_specs"]) + [pl.BlockSpec(memory_space=pl.ANY)] * extra
    made = pl.pallas_call(inner, **call)
    return lambda *arrays: made(*arrays, *after)


def cost(flops, moved):
    return pl.CostEstimate(flops=int(flops), bytes_accessed=int(moved), transcendentals=0)


def mm(left, right):
    return jnp.dot(left, right, preferred_element_type=F32)


def mm_nt(left, right):
    return lax.dot_general(left, right, (((1,), (1,)), ((), ())), preferred_element_type=F32)


def mm_tn(left, right):
    return lax.dot_general(left, right, (((0,), (0,)), ((), ())), preferred_element_type=F32)


def iota(shape, axis):
    return lax.broadcasted_iota(jnp.int32, shape, axis)


def normed(values):
    centered = values - jnp.mean(values, axis=1, keepdims=True)
    scale = lax.rsqrt(jnp.mean(centered * centered, axis=1, keepdims=True) + norm_eps)
    return centered * scale, scale


def norm_backward(values, gain, upstream):
    hat, scale = normed(values)
    gain_grad = jnp.sum(upstream * hat, axis=0, keepdims=True)
    inner = upstream * gain
    mean_inner = jnp.mean(inner, axis=1, keepdims=True)
    mean_hat = jnp.mean(inner * hat, axis=1, keepdims=True)
    return scale * (inner - mean_inner - hat * mean_hat), gain_grad


def as_column(row, eye):
    return jnp.sum(jnp.where(eye, row, jnp.zeros_like(row)), axis=1, keepdims=True)


def as_row(column, eye):
    return jnp.sum(jnp.where(eye, column, jnp.zeros_like(column)), axis=0, keepdims=True)


def attention_mask(segment_row):
    count = segment_row.shape[1]
    down, across = iota((count, count), 0), iota((count, count), 1)
    eye = down == across
    column = jnp.sum(jnp.where(eye, segment_row, 0), axis=1, keepdims=True)
    return (down >= across) & (column == segment_row), eye


def dense_forward_kernel(
    zh_ref, tokens, segments, routes, w_qkv, w_out, w_router, gains,
    attn_in_o, qkv_o, mixed_o, lse_o, middle_o, ffn_o, plan_o, rows_o, frozen_rows_o,
):
    width = tokens.shape[1]
    count = tokens.shape[0]
    inputs = tokens[...].astype(F32)
    hat, unused = normed(inputs)
    attn_in = (hat * gains[0:1, :]).astype(LOW)
    attn_in_o[...] = attn_in
    qkv_o[...] = mm(attn_in, w_qkv[...]).astype(LOW)
    allowed, eye = attention_mask(segments[...])
    lane = iota((count, 128), 1)
    low_lanes = lane < HEAD_DIM
    lse_all = jnp.zeros((count, 128), F32)
    for pair in range(width // 128):
        at = slice(128 * pair, 128 * pair + 128)
        queries = qkv_o[:, at] * jnp.asarray(HEAD_DIM**-0.5, LOW)
        keys = qkv_o[:, width + 128 * pair : width + 128 * pair + 128]
        values = qkv_o[:, 2 * width + 128 * pair : 2 * width + 128 * pair + 128]
        outs = []
        for half in range(2):
            mine = low_lanes if half == 0 else ~low_lanes
            scores = mm_nt(jnp.where(mine, queries, jnp.zeros_like(queries)), keys)
            scores = jnp.where(allowed, scores, -1e30)
            top = jnp.max(scores, axis=1, keepdims=True)
            raised = jnp.exp(scores - top)
            total = jnp.sum(raised, axis=1, keepdims=True)
            probs = (raised * (1.0 / total)).astype(LOW)
            outs.append(mm(probs, values))
            lse_all = jnp.where(lane == 2 * pair + half, top + jnp.log(total), lse_all)
        mixed_o[:, at] = jnp.where(low_lanes, outs[0], outs[1]).astype(LOW)
    lse_o[...] = lse_all
    middle = inputs + mm(mixed_o[...], w_out[...])
    middle_o[...] = middle
    hat, unused = normed(middle)
    ffn = (hat * gains[1:2, :]).astype(LOW)
    ffn_o[...] = ffn
    logits = mm_nt(ffn, w_router[...])
    experts = iota(logits.shape, 1)
    lists = [as_column(routes[k : k + 1, :], eye) for k in range(2)]
    picks = [experts == column for column in lists]
    chosen = [jnp.sum(jnp.where(p, logits, 0.0), axis=1, keepdims=True) for p in picks]
    top = jnp.maximum(chosen[0], chosen[1])
    raised = [jnp.exp(c - top) for c in chosen]
    gates = [r / (raised[0] + raised[1]) for r in raised]
    named = (picks[0] | picks[1]).astype(F32).astype(LOW)
    earlier = (iota((count, count), 0) > iota((count, count), 1)).astype(F32).astype(LOW)
    before = mm(earlier, named)
    zh = zh_ref[0]
    new_place, old_place = [], []
    for k in range(2):
        route = lists[k]
        slot = jnp.sum(jnp.where(picks[k], before, 0.0), axis=1, keepdims=True).astype(jnp.int32)
        fresh = route - 1
        block = 16 * ((fresh & 1) ^ zh) + lax.shift_right_arithmetic(fresh, 1)
        new_place.append(jnp.where(route > 0, block * CAP + slot, -1))
        old_place.append(jnp.where(route > 0, -1, slot))
    columns = gates + [p.astype(F32) for p in new_place + old_place]
    plan = jnp.zeros((count, 128), F32)
    for i, column in enumerate(columns):
        plan = jnp.where(lane == i, column, plan)
    plan_o[...] = plan
    for places, rows_ref in ((new_place, rows_o), (old_place, frozen_rows_o)):
        slots = iota((rows_ref.shape[0], count), 0)
        spread = [(slots == as_row(p, eye)).astype(F32).astype(LOW) for p in places]
        rows_ref[...] = mm(spread[0] + spread[1], ffn).astype(LOW)


def spread_grads_kernel(plan, cotangent, grads_o, frozen_grads_o):
    count = plan.shape[0]
    eye = iota((count, count), 0) == iota((count, count), 1)
    up = cotangent[...].astype(F32)
    scaled = [(plan[:, k : k + 1] * up).astype(LOW) for k in range(2)]
    for first, ref in ((2, grads_o), (4, frozen_grads_o)):
        slots = iota((ref.shape[0], count), 0)
        total = 0.0
        for k in range(2):
            place = as_row(plan[:, first + k : first + k + 1], eye).astype(jnp.int32)
            total = total + mm((slots == place).astype(F32).astype(LOW), scaled[k])
        ref[...] = total.astype(LOW)


def spread_grads(after, plan, cotangent, slots):
    width = cotangent.shape[1]
    return ordered(
        spread_grads_kernel, 2, after,
        name="spread_grads",
        out_shape=[jax.ShapeDtypeStruct((n, width), LOW) for n in (slots, CAP)],
        in_specs=[VMEM] * 2,
        out_specs=[VMEM] * 2,
        compiler_params=params(),
        cost_estimate=cost(2e9, 2e6),
    )(plan, cotangent)


def dense_forward(after, zh, tokens, segments, routes, w_qkv, w_out, w_router, gains):
    count, width = tokens.shape
    slots = (w_router.shape[0] - 1) * CAP
    shapes = [
        ((count, width), LOW), ((count, 3 * width), LOW), ((count, width), LOW), ((count, 128), F32),
        ((count, width), F32), ((count, width), LOW), ((count, 128), F32),
        ((slots, width), LOW), ((CAP, width), LOW),
    ]
    return ordered(
        dense_forward_kernel, 8, after,
        name="dense_forward",
        out_shape=[jax.ShapeDtypeStruct(s, t) for s, t in shapes],
        in_specs=[SMEM] + [VMEM] * 7,
        out_specs=[VMEM] * len(shapes),
        compiler_params=params(),
        cost_estimate=cost(8e9, 30e6),
    )(zh, tokens, segments, routes, w_qkv, w_out, w_router, gains)


def dense_backward_kernel(
    core_ref, plan, routes, segments, cotangent, tokens, middle, mixed, ffn, lse, qkv, attn_in,
    w_qkv, w_out, w_router, gains, back, frozen_back,
    input_grad_o, kept_o, away_o,
    flat, gqkv,
):
    count, width = tokens.shape
    expert_total = w_router.shape[0]
    up = cotangent[...].astype(F32)
    gates = [plan[:, k : k + 1] for k in range(2)]
    new_place = [plan[:, 2 + k : 3 + k].astype(jnp.int32) for k in range(2)]
    old_place = [plan[:, 4 + k : 5 + k].astype(jnp.int32) for k in range(2)]
    allowed, eye = attention_mask(segments[...])

    grad_ffn = jnp.zeros((count, width), F32)
    weighted = [jnp.zeros((count, 1), F32) for k in range(2)]
    for places, ref in ((new_place, back), (old_place, frozen_back)):
        size = ref.shape[0]
        slots = iota((count, size), 1)
        for k in range(2):
            choice = (slots == places[k]).astype(F32).astype(LOW)
            picked = mm(choice, ref[...])
            grad_ffn = grad_ffn + picked[:, :width]
            tail = picked[:, width:]
            weighted[k] = weighted[k] + jnp.sum(tail, axis=1, keepdims=True)
    both = weighted[0] + weighted[1]
    experts = iota((count, expert_total), 1)
    grad_logits = jnp.zeros((count, expert_total), F32)
    for k in range(2):
        grad_logits = jnp.where(
            experts == as_column(routes[k : k + 1, :], eye), weighted[k] - gates[k] * both, grad_logits
        )
    grad_logits = grad_logits.astype(LOW)
    grad_ffn = grad_ffn + mm(grad_logits, w_router[...])
    grad_norm, gain_ffn = norm_backward(middle[...], gains[1:2, :], grad_ffn)
    grad_middle = up + grad_norm
    grad_branch = grad_middle.astype(LOW)

    blocks = width // 128
    first_row = 3 * blocks * width
    attn_out_grad = mm_tn(mixed[...], grad_branch)
    for j in range(blocks):
        flat[pl.ds(first_row + j, width, stride=blocks), :] = attn_out_grad[:, 128 * j : 128 * j + 128]
    router_row = first_row + blocks * width
    router_rows = width * expert_total // 128
    padded_logits = jnp.concatenate(
        [grad_logits, jnp.zeros((count, 128 - expert_total), LOW)], axis=1
    )
    router_grad = mm_tn(ffn[...], padded_logits)
    feature = iota((width, 128), 0)
    lane_w = iota((width, 128), 1)
    start = feature * expert_total
    offset = start & 127
    turned = jnp.take_along_axis(router_grad, (lane_w - offset) & 127, axis=1)
    wrapped = lane_w < offset
    row_of = lax.shift_right_logical(iota((router_rows, width), 1) * expert_total, 7)
    row_here = iota((router_rows, width), 0)
    here = (row_of == row_here).astype(F32)
    after = (row_of + 1 == row_here).astype(F32)
    exact = lambda a, b: jnp.dot(a, b, precision=lax.Precision.HIGHEST, preferred_element_type=F32)
    flat[router_row : router_row + router_rows, :] = exact(
        here, jnp.where(wrapped, 0.0, turned)
    ) + exact(after, jnp.where(wrapped, turned, 0.0))
    gain_row = router_row + router_rows

    grad_mixed = mm_nt(grad_branch, w_out[...]).astype(LOW)
    lane = iota((count, 128), 1)
    low_lanes = lane < HEAD_DIM
    scale = HEAD_DIM**-0.5
    for pair in range(blocks):
        at = slice(128 * pair, 128 * pair + 128)
        queries = qkv[:, at] * jnp.asarray(scale, LOW)
        keys = qkv[:, width + 128 * pair : width + 128 * pair + 128]
        values = qkv[:, 2 * width + 128 * pair : 2 * width + 128 * pair + 128]
        grads = grad_mixed[:, at]
        grad_q = jnp.zeros((count, 128), F32)
        grad_k = jnp.zeros((count, 128), F32)
        grad_v = jnp.zeros((count, 128), F32)
        for half in range(2):
            mine = low_lanes if half == 0 else ~low_lanes
            only = lambda v: jnp.where(mine, v, jnp.zeros_like(v))
            q_half, g_half, k_half = only(queries), only(grads), only(keys)
            scores = jnp.where(allowed, mm_nt(q_half, keys), -1e30)
            head = 2 * pair + half
            probs = jnp.exp(scores - lse[:, head : head + 1])
            grad_probs = mm_nt(g_half, values)
            grad_v = grad_v + mm_tn(probs.astype(LOW), g_half)
            dots = jnp.sum(probs * grad_probs, axis=1, keepdims=True)
            grad_scores = (probs * (grad_probs - dots)).astype(LOW)
            grad_q = grad_q + mm(grad_scores, k_half)
            grad_k = grad_k + mm_tn(grad_scores, q_half)
        gqkv[:, at] = (grad_q * scale).astype(LOW)
        gqkv[:, width + 128 * pair : width + 128 * pair + 128] = grad_k.astype(LOW)
        gqkv[:, 2 * width + 128 * pair : 2 * width + 128 * pair + 128] = grad_v.astype(LOW)
    for j in range(0, 3 * blocks, 2):
        piece = mm_tn(attn_in[...], gqkv[:, 128 * j : 128 * j + 256])
        flat[pl.ds(j, width, stride=3 * blocks), :] = piece[:, :128]
        flat[pl.ds(j + 1, width, stride=3 * blocks), :] = piece[:, 128:]
    grad_attn = mm_nt(gqkv[...], w_qkv[...])
    grad_norm, gain_attn = norm_backward(tokens[...].astype(F32), gains[0:1, :], grad_attn)
    input_grad_o[...] = grad_middle + grad_norm
    for j in range(blocks):
        flat[gain_row + j : gain_row + j + 1, :] = gain_attn[:, 128 * j : 128 * j + 128]
        flat[gain_row + blocks + j : gain_row + blocks + j + 1, :] = gain_ffn[:, 128 * j : 128 * j + 128]
    last = gain_row + 2 * blocks
    flat[last:, :] = jnp.zeros((flat.shape[0] - last, 128), F32)

    core = core_ref[0]
    rows = flat.shape[0] // 128
    padded = kept_o.shape[1]

    @pl.loop(0, kept_o.shape[0])
    def move(i):
        kept_o[pl.ds(i, 1)] = flat[pl.ds((2 * i + core) * rows, padded), :].astype(LOW)[None]
        away_o[pl.ds(i, 1)] = flat[pl.ds((2 * i + 1 - core) * rows, padded), :].astype(LOW)[None]


def dense_backward(after, core, dense_rows, *arrays):
    count, width = arrays[4].shape
    rows = dense_rows // 128
    padded = (rows + 31) // 32 * 32
    return ordered(
        dense_backward_kernel, 1 + len(arrays), after,
        name="dense_backward",
        out_shape=[
            jax.ShapeDtypeStruct((count, width), F32),
            jax.ShapeDtypeStruct((64, padded, 128), LOW),
            jax.ShapeDtypeStruct((64, padded, 128), LOW),
        ],
        in_specs=[SMEM] + [VMEM] * len(arrays),
        out_specs=[VMEM] * 3,
        scratch_shapes=[
            pltpu.VMEM((rows * 128 + padded - rows, 128), F32),
            pltpu.VMEM((count, 3 * width), LOW),
        ],
        compiler_params=params(),
        cost_estimate=cost(12e9, 40e6),
    )(core, *arrays)


def combine_kernel(plan, middle, results, frozen_result, out):
    count, width = middle.shape
    total = middle[...]
    for first, ref in ((2, results), (4, frozen_result)):
        slots = iota((count, ref.shape[0]), 1)
        for k in range(2):
            place = plan[:, first + k : first + k + 1].astype(jnp.int32)
            total = total + plan[:, k : k + 1] * mm((slots == place).astype(F32).astype(LOW), ref[...])
    out[...] = total.astype(LOW)


def combine(after, plan, middle, results, frozen_result):
    return ordered(
        combine_kernel, 4, after,
        name="combine",
        out_shape=jax.ShapeDtypeStruct(middle.shape, LOW),
        in_specs=[VMEM] * 4,
        out_specs=VMEM,
        compiler_params=params(),
        cost_estimate=cost(200e9, 4e6),
    )(plan, middle, results, frozen_result)


def gelu_pair(pre):
    area = 0.5 + 0.5 * lax.erf(pre * (0.5**0.5))
    density = jnp.exp(-0.5 * pre * pre) * (1.0 / (2.0 * math.pi) ** 0.5)
    return pre * area, area + pre * density


HBM = pl.BlockSpec(memory_space=pl.ANY)


def half_of(shard, half, by_rows):
    if by_rows:
        rows = shard.shape[1] // 2
        return shard[0, pl.ds(pl.multiple_of(half * rows, 64), rows), :]
    cols = shard.shape[2] // 8
    starts = [pl.multiple_of((2 * block + half) * cols, 128) for block in range(4)]
    return jnp.concatenate([shard[0, :, pl.ds(start, cols)] for start in starts], axis=1)


def pack_weight(after, name, home, local, near, across, by_rows):
    def kernel(home_ref, local, near, across, out):
        half = 1 - home_ref[2]

        @pl.when(home_ref[1] == 1)
        def same():
            out[0] = half_of(local, half, by_rows)
            out[1] = half_of(near, half, by_rows)

        @pl.when(home_ref[1] == 0)
        def other():
            out[0] = half_of(near, half, by_rows)
            out[1] = half_of(across, half, by_rows)

    rows, cols = local.shape[1:]
    shape = (2, rows // 2, cols) if by_rows else (2, rows, cols // 2)
    return ordered(
        kernel, 4, after,
        name=name,
        out_shape=jax.ShapeDtypeStruct(shape, LOW),
        in_specs=[SMEM] + [VMEM] * 3,
        out_specs=VMEM,
        compiler_params=params(),
        cost_estimate=cost(1e5, 5e6),
    )(home, local, near, across)


def build_weight(after, name, home, local, near, across, arrived, by_rows):
    def kernel(home_ref, local, near, across, arrived, out):
        z, half = home_ref[0], home_ref[2]
        rows = arrived.shape[1]
        spot = lambda step: pl.ds(pl.multiple_of(((z + step) & 3) * rows, 64), rows)

        @pl.when(home_ref[1] == 1)
        def same():
            out[spot(0), :] = half_of(local, half, by_rows)
            out[spot(3), :] = half_of(near, half, by_rows)
            out[spot(1), :] = arrived[0]
            out[spot(2), :] = arrived[1]

        @pl.when(home_ref[1] == 0)
        def other():
            out[spot(1), :] = half_of(near, half, by_rows)
            out[spot(2), :] = half_of(across, half, by_rows)
            out[spot(0), :] = arrived[0]
            out[spot(3), :] = arrived[1]

    rows, cols = arrived.shape[1:]
    return ordered(
        kernel, 5, after,
        name=name,
        out_shape=jax.ShapeDtypeStruct((4 * rows, cols), LOW),
        in_specs=[SMEM] + [VMEM] * 4,
        out_specs=VMEM,
        compiler_params=params(),
        cost_estimate=cost(1e5, 8e6),
    )(home, local, near, across, arrived)


def expert_up_kernel(rows, weight, hidden_o, slope_o):
    pre = mm(rows[...], weight[...])
    hidden, slope = gelu_pair(pre)
    hidden_o[...] = hidden.astype(LOW)
    slope_o[...] = slope.astype(LOW)


def expert_up(after, rows, weight):
    count, width = rows.shape
    hidden = weight.shape[1]
    step = 256
    wide = jax.ShapeDtypeStruct((count, hidden), LOW)
    return ordered(
        expert_up_kernel, 2, after,
        name="expert_up",
        out_shape=[wide, wide],
        grid=(count // step,),
        in_specs=[pl.BlockSpec((step, width), lambda i: (i, 0)), pl.BlockSpec((width, hidden), lambda i: (0, 0))],
        out_specs=[pl.BlockSpec((step, hidden), lambda i: (i, 0))] * 2,
        compiler_params=params(),
        cost_estimate=cost(6e9, 8e6),
    )(rows, weight)


def split_three(value):
    high = value.astype(LOW)
    rest = value - high.astype(F32)
    mid = rest.astype(LOW)
    return high, mid, (rest - mid.astype(F32)).astype(LOW)


def with_extra(rows, value):
    lane = iota((rows.shape[0], EXTRA), 1)
    extra = jnp.zeros((rows.shape[0], EXTRA), F32)
    for i, term in enumerate(split_three(value)):
        extra = jnp.where(lane == i, term.astype(F32), extra)
    return rows.astype(LOW), extra.astype(LOW)


def merge_kernel(rows, arrived, grads, result, out):
    width = rows.shape[1]
    value = jnp.sum(grads[...].astype(F32) * result[...].astype(F32), axis=1, keepdims=True)
    low, terms = with_extra(rows[...] + arrived[...].astype(F32), value)
    out[:, :width] = low
    out[:, width:] = terms


def merge_rows(after, rows, arrived, grads, result):
    count, width = rows.shape
    step = 256
    block = lambda cols: pl.BlockSpec((step, cols), lambda i: (i, 0))
    return ordered(
        merge_kernel, 4, after,
        name="merge_rows",
        out_shape=jax.ShapeDtypeStruct((count, width + EXTRA), LOW),
        grid=(count // step,),
        in_specs=[block(width)] * 4,
        out_specs=block(width + EXTRA),
        compiler_params=params(),
        cost_estimate=cost(1e7, 7e6),
    )(rows, arrived, grads, result)


def reduce_first(after, planes, partial, arrived):
    rows, columns = partial.shape[0] // 4, partial.shape[1]

    def kernel(planes, kept, arrived, *refs):
        mine, other = refs[-2:]
        for out, which in ((mine, planes[1]), (other, 1 - planes[1])):
            at = pl.ds(pl.multiple_of(which * rows, 64), rows)
            out[...] = (kept[at, :] + arrived[at, :].astype(F32)).astype(out.dtype)

    return pl.pallas_call(
        kernel,
        name="reduce_first",
        out_shape=[jax.ShapeDtypeStruct((rows, columns), t) for t in (F32, LOW)],
        grid_spec=pltpu.PrefetchScalarGridSpec(
            num_scalar_prefetch=1,
            grid=(1,),
            in_specs=[
                pl.BlockSpec((2 * rows, columns), lambda i, planes: (planes[0], 0)),
                pl.BlockSpec((2 * rows, columns), lambda i, planes: (0, 0)),
            ] + [HBM] * len(after),
            out_specs=[pl.BlockSpec((rows, columns), lambda i, planes: (0, 0))] * 2,
        ),
        compiler_params=params(),
        cost_estimate=cost(1e6, 6e6),
    )(planes, partial, arrived, *after)


def reduce_second(after, same, mine, other):
    def kernel(same_ref, mine, other, stays, leaves):
        straight = same_ref[0] == 1
        near, far = mine[...], other[...].astype(F32)
        stays[...] = jnp.where(straight, near, far)
        leaves[...] = jnp.where(straight, far, near).astype(LOW)

    return ordered(
        kernel, 3, after,
        name="reduce_second",
        out_shape=[jax.ShapeDtypeStruct(mine.shape, t) for t in (F32, LOW)],
        in_specs=[SMEM, VMEM, VMEM],
        out_specs=[VMEM] * 2,
        compiler_params=params(),
        cost_estimate=cost(1e6, 6e6),
    )(same, mine, other)


def frozen_kernel(rows, grads, w_in, w_out, result_o, back_o, result_sum, back_sum, value_sum):
    step = pl.program_id(0)

    @pl.when(step == 0)
    def clear():
        result_sum[...] = jnp.zeros_like(result_sum)
        back_sum[...] = jnp.zeros_like(back_sum)
        value_sum[...] = jnp.zeros_like(value_sum)

    hidden, slope = gelu_pair(mm(rows[...], w_in[...]))
    hidden = hidden.astype(LOW)
    result_sum[...] += mm(hidden, w_out[...])
    grad_hidden = mm_nt(grads[...], w_out[...])
    value_sum[...] += jnp.sum(hidden.astype(F32) * grad_hidden, axis=1, keepdims=True)
    back_sum[...] += mm_nt((grad_hidden * slope).astype(LOW), w_in[...])

    @pl.when(step == pl.num_programs(0) - 1)
    def finish():
        result_o[...] = result_sum[...].astype(LOW)
        width = back_sum.shape[1]
        low, terms = with_extra(back_sum[...], value_sum[:, 0:1])
        back_o[:, :width] = low
        back_o[:, width:] = terms


def frozen_expert(after, rows, grads, w_in, w_out):
    count, width = rows.shape
    wide = w_in.shape[1]
    step = 512
    small = pl.BlockSpec((count, width), lambda i: (0, 0))
    return ordered(
        frozen_kernel, 4, after,
        name="frozen_expert",
        out_shape=[
            jax.ShapeDtypeStruct((count, width), LOW),
            jax.ShapeDtypeStruct((count, width + EXTRA), LOW),
        ],
        grid=(wide // step,),
        in_specs=[
            small, small,
            pl.BlockSpec((width, step), lambda i: (0, i)),
            pl.BlockSpec((step, width), lambda i: (i, 0)),
        ],
        out_specs=[small, pl.BlockSpec((count, width + EXTRA), lambda i: (0, 0))],
        scratch_shapes=[
            pltpu.VMEM((count, width), F32),
            pltpu.VMEM((count, width), F32),
            pltpu.VMEM((count, EXTRA), F32),
        ],
        compiler_params=params(),
        cost_estimate=cost(4e9, 10e6),
    )(rows, grads, w_in, w_out)


def add_kernel(near, far, out):
    out[...] = (near[...].astype(F32) + far[...].astype(F32)).astype(out.dtype)


def add_halves(after, near, far):
    step = 16
    block = pl.BlockSpec((step,) + near.shape[1:], lambda i: (i, 0, 0))
    return ordered(
        add_kernel, 2, after,
        name="add_halves",
        out_shape=jax.ShapeDtypeStruct(near.shape, LOW),
        grid=(near.shape[0] // step,),
        in_specs=[block] * 2,
        out_specs=block,
        compiler_params=params(),
        cost_estimate=cost(1e6, 8e6),
    )(near, far)


def adamw_values(master, first, second, grad):
    first_new = beta_first * first + (1.0 - beta_first) * grad
    second_new = beta_second * second + (1.0 - beta_second) * grad * grad
    first_hat = first_new * (1.0 / (1.0 - beta_first**STEP))
    second_hat = second_new * (1.0 / (1.0 - beta_second**STEP))
    master_new = master - learn_rate * (
        first_hat / (jnp.sqrt(second_hat) + adam_eps) + decay_rate * master
    )
    return master_new, first_new, second_new, master_new.astype(LOW)


def dense_update_kernel(master, first, second, terms, *outs):
    rows = master.shape[0]
    grad = jnp.sum(terms[...].astype(F32), axis=0)[:rows]
    for out, value in zip(outs, adamw_values(master[...], first[...], second[...], grad)):
        out[...] = value


def dense_update(after, master, first, second, terms):
    shape = (master.shape[0] // 128, 128)
    results = ordered(
        dense_update_kernel, 4, after,
        name="dense_update",
        out_shape=[jax.ShapeDtypeStruct(shape, t) for t in (F32, F32, F32, LOW)],
        in_specs=[VMEM] * 4,
        out_specs=[VMEM] * 4,
        compiler_params=params(),
        cost_estimate=cost(1e6, 4e6),
    )(*(a.reshape(shape) for a in (master, first, second)), terms)
    return tuple(r.reshape(master.shape) for r in results)


def expert_update(after, core, master, first, second, stays, arrived, axis):
    rows, columns = master.shape[1:]
    if axis == 1:
        blocks, width = 4, columns // 4
        half = (rows, width // 2)
    else:
        blocks, width = 3, columns // 3
        half = (rows // 2, width)

    def kernel(core_ref, master, first, second, stays, arrived, *outs):
        near, far = stays[...], arrived[...].astype(F32)
        swapped = core_ref[0] == 1
        grad = jnp.concatenate(
            [jnp.where(swapped, far, near), jnp.where(swapped, near, far)], axis=axis
        )
        values = adamw_values(master[0], first[0], second[0], grad)
        for out, value in zip(outs, values):
            out[0] = value

    wide = pl.BlockSpec((1, rows, width), lambda i: (0, 0, i))
    slim = pl.BlockSpec(half, lambda i: (0, i))
    return tuple(
        ordered(
        kernel, 6, after,
            name="update_in" if axis == 1 else "update_out",
            out_shape=[jax.ShapeDtypeStruct(master.shape, t) for t in (F32, F32, F32, LOW)],
            grid=(blocks,),
            in_specs=[SMEM, wide, wide, wide, slim, slim],
            out_specs=[wide] * 4,
            compiler_params=params(),
            cost_estimate=cost(2e7, 18e6),
        )(core, master, first, second, stays, arrived)
    )


def swap_core(block):
    return lax.ppermute(block, "c", [(0, 1), (1, 0)])


KINDS = (0, 1, 1, 0)


def to_neighbours(shard):
    moves = []
    for z, kind in enumerate(KINDS):
        moves.append(((z - 1) % 4 * 2 + kind, z * 2 + kind))
        moves.append(((z + 1) % 4 * 2 + kind, z * 2 + 1 - kind))
    return lax.ppermute(shard, DEPTH + ("c",), moves)


def to_opposite(shard):
    moves = []
    for z, kind in enumerate(KINDS):
        source = kind if z % 2 else 1 - kind
        moves.append((z * 2 + source, (3 - z) * 2 + 1 - kind))
    return lax.ppermute(shard, DEPTH + ("c",), moves)


def swap_pair(block):
    return lax.ppermute(block, DEPTH, [(z, 3 - z) for z in range(4)])


def swap_low(block):
    return lax.ppermute(block, "zl", [(0, 1), (1, 0)])


def exchange(rows):
    cut = rows.reshape(-1, CAP, rows.shape[1])
    cut = lax.all_to_all(cut, PLANE, split_axis=0, concat_axis=0, tiled=True)
    return cut.reshape(rows.shape)


def word(*values):
    return jnp.stack([jnp.asarray(v, jnp.int32) for v in values])


def body(
    tokens,
    segment_ids,
    routes,
    cotangent,
    w_qkv,
    w_attn_out,
    w_router,
    norm_gains,
    frozen_in,
    frozen_out,
    new_in,
    new_out,
    dense_master,
    dense_first,
    dense_second,
    master_in,
    first_in,
    second_in,
    master_out,
    first_out,
    second_out,
):
    core, zh, zl = (lax.axis_index(a) for a in ("c", "zh", "zl"))
    z = 2 * zh + zl
    kind = zh ^ zl
    same = jnp.where(kind == core, 1, 0)
    home = word(z, same, core)
    core_word, same_word = word(core), word(same)
    routes = routes.T
    w_router = w_router.T

    in_near, out_near = to_neighbours(new_in), to_neighbours(new_out)
    (
        attn_in, qkv_low, mixed_low, lse, middle, ffn_in, plan, rows_sent, frozen_rows,
    ) = dense_forward(
        (), word(zh), tokens, segment_ids, routes, w_qkv, w_attn_out, w_router, norm_gains
    )
    rows_own = exchange(rows_sent)
    grads_sent, frozen_grads = spread_grads((), plan, cotangent, rows_sent.shape[0])
    grads_own = exchange(grads_sent)
    rows_mate, grads_mate = swap_core(rows_own), swap_core(grads_own)
    frozen_result, frozen_back = frozen_expert((), frozen_rows, frozen_grads, frozen_in, frozen_out)
    in_far = lax.optimization_barrier((in_near, plan))[0]
    out_far = lax.optimization_barrier((out_near, plan))[0]
    in_across, out_across = to_opposite(in_far), to_opposite(out_far)
    in_sent = pack_weight((frozen_back,), "pack_in", home, new_in, in_near, in_across, False)
    out_sent = pack_weight((in_sent,), "pack_out", home, new_out, out_near, out_across, True)
    half_in = build_weight(
        (out_sent,), "build_in", home, new_in, in_near, in_across, swap_core(in_sent), False
    )
    hidden_own, slope_own = expert_up((), rows_own, half_in)
    half_out = build_weight(
        (hidden_own,), "build_out", home, new_out, out_near, out_across, swap_core(out_sent), True
    )
    hidden_mate, slope_mate = expert_up((half_out,), rows_mate, half_in)

    result_arrived = swap_core(mm(hidden_mate, half_out).astype(LOW))
    result = (mm(hidden_own, half_out) + result_arrived.astype(F32)).astype(LOW)
    pre_of = lambda grads, slope: (mm_nt(grads, half_out) * slope.astype(F32)).astype(LOW)
    pre_mate, pre_own = pre_of(grads_mate, slope_mate), pre_of(grads_own, slope_own)
    back_arrived = swap_core(mm_nt(pre_mate, half_in).astype(LOW))
    merged = merge_rows((), mm_nt(pre_own, half_in), back_arrived, grads_own, result)
    back = exchange(merged)
    result_back = exchange(result)
    grad_out = mm_tn(hidden_own, grads_own) + mm_tn(hidden_mate, grads_mate)
    grad_in = mm_tn(rows_own, pre_own) + mm_tn(rows_mate, pre_mate)

    def leaving(partial):
        rows = partial.shape[0] // 2
        away = lax.dynamic_slice(partial, ((1 - zh) * rows, 0), (rows, partial.shape[1]))
        return swap_pair(away.astype(LOW))

    out_arrived, in_arrived = leaving(grad_out), leaving(grad_in)
    planes = word(zh, zl)
    out_mine, out_other = reduce_first((merged,), planes, grad_out, out_arrived)
    out_other = swap_low(out_other)

    input_grad, kept, away = dense_backward(
        (out_mine,), core_word, dense_master.shape[0], plan, routes, segment_ids, cotangent, tokens, middle,
        mixed_low, ffn_in, lse, qkv_low, attn_in, w_qkv, w_attn_out, w_router, norm_gains, back, frozen_back,
    )
    arrived = swap_core(away)
    in_mine, in_other = reduce_first((kept,), planes, grad_in, in_arrived)
    in_other = swap_low(in_other)
    activations = combine((in_mine,), plan, middle, result_back, frozen_result)
    summed = add_halves((activations, out_other), kept, arrived)
    terms = lax.all_to_all(summed, ("zh", "zl", "x", "y"), split_axis=0, concat_axis=0, tiled=True)
    out_stays, out_leaves = reduce_second((summed,), same_word, out_mine, out_other)
    out_mate_grad = swap_core(out_leaves)
    out_new = expert_update(
        (out_stays,), core_word, master_out, first_out, second_out, out_stays, out_mate_grad, 0
    )
    in_stays, in_leaves = reduce_second((out_new[0],), same_word, in_mine, in_other)
    in_mate_grad = swap_core(in_leaves)
    in_new = expert_update(
        (in_stays,), core_word, master_in, first_in, second_in, in_stays, in_mate_grad, 1
    )
    dense_new = dense_update((in_new[0],), dense_master, dense_first, dense_second, terms)
    return (activations, input_grad) + dense_new + in_new + out_new


def solution(mesh):
    fine = Mesh(mesh.devices.reshape(2, 2, 4, 4, 2), ALL)
    tokens = P(ALL, None)
    flat = P(ALL)
    expert = P(("x", "y", "c"), DEPTH, None)
    return jax.shard_map(
        body,
        mesh=fine,
        in_specs=(tokens,) * 4 + (P(),) * 6 + (expert,) * 2 + (flat,) * 3 + (expert,) * 6,
        out_specs=(tokens,) * 2 + (flat,) * 4 + (expert,) * 8,
        check_vma=False,
    )
```

```python
import math

import jax
import jax.numpy as jnp
from jax import lax
from jax.experimental import pallas as pl
from jax.experimental.pallas import tpu as pltpu
from jax.sharding import Mesh
from jax.sharding import PartitionSpec as P

HEAD_DIM = 64
STEP = 5


norm_eps = 1e-05
learn_rate = 0.02
beta_first = 0.5
beta_second = 0.5
adam_eps = 1e-08
decay_rate = 0.1


PLANE = ("zl", "x", "y")
DEPTH = ("zh", "zl")
ALL = ("zh", "zl", "x", "y", "c")
CAP = 24
PAIRS = 6
EXTRA = 128
VMEM = pl.BlockSpec(memory_space=pltpu.VMEM)
SMEM = pl.BlockSpec(memory_space=pltpu.SMEM)
F32 = jnp.float32
LOW = jnp.bfloat16


def params(**more):
    return pltpu.CompilerParams(vmem_limit_bytes=56 * 1024 * 1024, **more)


def ordered(kernel, count, after, **call):
    extra = len(after)

    def inner(*refs):
        return kernel(*refs[:count], *refs[count + extra :])

    call["in_specs"] = list(call["in_specs"]) + [pl.BlockSpec(memory_space=pl.ANY)] * extra
    made = pl.pallas_call(inner, **call)
    return lambda *arrays: made(*arrays, *after)


def cost(flops, moved):
    return pl.CostEstimate(flops=int(flops), bytes_accessed=int(moved), transcendentals=0)


def mm(left, right):
    return jnp.dot(left, right, preferred_element_type=F32)


def mm_nt(left, right):
    return lax.dot_general(left, right, (((1,), (1,)), ((), ())), preferred_element_type=F32)


def mm_tn(left, right):
    return lax.dot_general(left, right, (((0,), (0,)), ((), ())), preferred_element_type=F32)


def iota(shape, axis):
    return lax.broadcasted_iota(jnp.int32, shape, axis)


def normed(values):
    centered = values - jnp.mean(values, axis=1, keepdims=True)
    scale = lax.rsqrt(jnp.mean(centered * centered, axis=1, keepdims=True) + norm_eps)
    return centered * scale, scale


def norm_backward(values, gain, upstream):
    hat, scale = normed(values)
    gain_grad = jnp.sum(upstream * hat, axis=0, keepdims=True)
    inner = upstream * gain
    mean_inner = jnp.mean(inner, axis=1, keepdims=True)
    mean_hat = jnp.mean(inner * hat, axis=1, keepdims=True)
    return scale * (inner - mean_inner - hat * mean_hat), gain_grad


def as_column(row, eye):
    return jnp.sum(jnp.where(eye, row, jnp.zeros_like(row)), axis=1, keepdims=True)


def as_row(column, eye):
    return jnp.sum(jnp.where(eye, column, jnp.zeros_like(column)), axis=0, keepdims=True)


def attention_mask(segment_row):
    count = segment_row.shape[1]
    down, across = iota((count, count), 0), iota((count, count), 1)
    eye = down == across
    column = jnp.sum(jnp.where(eye, segment_row, 0), axis=1, keepdims=True)
    return (down >= across) & (column == segment_row), eye


def dense_forward_kernel(
    zh_ref, tokens, segments, routes, cotangent, w_qkv, w_out, w_router, gains,
    attn_in_o, qkv_o, mixed_o, lse_o, middle_o, ffn_o, plan_o, sent_o, frozen_sent_o,
):
    width = tokens.shape[1]
    count = tokens.shape[0]
    inputs = tokens[...].astype(F32)
    hat, unused = normed(inputs)
    attn_in = (hat * gains[0:1, :]).astype(LOW)
    attn_in_o[...] = attn_in
    qkv_o[...] = mm(attn_in, w_qkv[...]).astype(LOW)
    allowed, eye = attention_mask(segments[...])
    lane = iota((count, 128), 1)
    low_lanes = lane < HEAD_DIM
    lse_all = jnp.zeros((count, 128), F32)
    for pair in range(width // 128):
        at = slice(128 * pair, 128 * pair + 128)
        queries = qkv_o[:, at] * jnp.asarray(HEAD_DIM**-0.5, LOW)
        keys = qkv_o[:, width + 128 * pair : width + 128 * pair + 128]
        values = qkv_o[:, 2 * width + 128 * pair : 2 * width + 128 * pair + 128]
        outs = []
        for half in range(2):
            mine = low_lanes if half == 0 else ~low_lanes
            scores = mm_nt(jnp.where(mine, queries, jnp.zeros_like(queries)), keys)
            scores = jnp.where(allowed, scores, -1e30)
            top = jnp.max(scores, axis=1, keepdims=True)
            raised = jnp.exp(scores - top)
            total = jnp.sum(raised, axis=1, keepdims=True)
            probs = (raised * (1.0 / total)).astype(LOW)
            outs.append(mm(probs, values))
            lse_all = jnp.where(lane == 2 * pair + half, top + jnp.log(total), lse_all)
        mixed_o[:, at] = jnp.where(low_lanes, outs[0], outs[1]).astype(LOW)
    lse_o[...] = lse_all
    middle = inputs + mm(mixed_o[...], w_out[...])
    middle_o[...] = middle
    hat, unused = normed(middle)
    ffn = (hat * gains[1:2, :]).astype(LOW)
    ffn_o[...] = ffn
    logits = mm_nt(ffn, w_router[...])
    experts = iota(logits.shape, 1)
    lists = [as_column(routes[k : k + 1, :], eye) for k in range(2)]
    picks = [experts == column for column in lists]
    chosen = [jnp.sum(jnp.where(p, logits, 0.0), axis=1, keepdims=True) for p in picks]
    top = jnp.maximum(chosen[0], chosen[1])
    raised = [jnp.exp(c - top) for c in chosen]
    gates = [r / (raised[0] + raised[1]) for r in raised]
    named = (picks[0] | picks[1]).astype(F32).astype(LOW)
    earlier = (iota((count, count), 0) > iota((count, count), 1)).astype(F32).astype(LOW)
    before = mm(earlier, named)
    zh = zh_ref[0]
    new_place, old_place = [], []
    for k in range(2):
        route = lists[k]
        slot = jnp.sum(jnp.where(picks[k], before, 0.0), axis=1, keepdims=True).astype(jnp.int32)
        fresh = route - 1
        block = 16 * ((fresh & 1) ^ zh) + lax.shift_right_arithmetic(fresh, 1)
        new_place.append(jnp.where(route > 0, block * CAP + slot, -1))
        old_place.append(jnp.where(route > 0, -1, slot))
    columns = gates + [p.astype(F32) for p in new_place + old_place]
    plan = jnp.zeros((count, 128), F32)
    for i, column in enumerate(columns):
        plan = jnp.where(lane == i, column, plan)
    plan_o[...] = plan
    up = cotangent[...].astype(F32)
    scaled = [(g * up).astype(LOW) for g in gates]
    for places, ref in ((new_place, sent_o), (old_place, frozen_sent_o)):
        slots = iota((ref.shape[0], count), 0)
        spread = [(slots == as_row(p, eye)).astype(F32).astype(LOW) for p in places]
        ref[:, :width] = mm(spread[0] + spread[1], ffn).astype(LOW)
        ref[:, width:] = (mm(spread[0], scaled[0]) + mm(spread[1], scaled[1])).astype(LOW)


def dense_forward(after, zh, tokens, segments, routes, cotangent, w_qkv, w_out, w_router, gains):
    count, width = tokens.shape
    slots = (w_router.shape[0] - 1) * CAP
    shapes = [
        ((count, width), LOW), ((count, 3 * width), LOW), ((count, width), LOW), ((count, 128), F32),
        ((count, width), F32), ((count, width), LOW), ((count, 128), F32),
        ((slots, 2 * width), LOW), ((CAP, 2 * width), LOW),
    ]
    return ordered(
        dense_forward_kernel, 9, after,
        name="dense_forward",
        out_shape=[jax.ShapeDtypeStruct(s, t) for s, t in shapes],
        in_specs=[SMEM] + [VMEM] * 8,
        out_specs=[VMEM] * len(shapes),
        compiler_params=params(),
        cost_estimate=cost(8e9, 30e6),
    )(zh, tokens, segments, routes, cotangent, w_qkv, w_out, w_router, gains)


def dense_backward_kernel(
    core_ref, plan, routes, segments, cotangent, tokens, middle, mixed, ffn, lse, qkv, attn_in,
    w_qkv, w_out, w_router, gains, back, frozen_back,
    input_grad_o, kept_o, away_o,
    flat, gqkv,
):
    count, width = tokens.shape
    expert_total = w_router.shape[0]
    up = cotangent[...].astype(F32)
    gates = [plan[:, k : k + 1] for k in range(2)]
    new_place = [plan[:, 2 + k : 3 + k].astype(jnp.int32) for k in range(2)]
    old_place = [plan[:, 4 + k : 5 + k].astype(jnp.int32) for k in range(2)]
    allowed, eye = attention_mask(segments[...])

    grad_ffn = jnp.zeros((count, width), F32)
    weighted = [jnp.zeros((count, 1), F32) for k in range(2)]
    for places, ref in ((new_place, back), (old_place, frozen_back)):
        size = ref.shape[0]
        slots = iota((count, size), 1)
        for k in range(2):
            choice = (slots == places[k]).astype(F32).astype(LOW)
            picked = mm(choice, ref[...])
            grad_ffn = grad_ffn + picked[:, :width]
            tail = picked[:, width:]
            weighted[k] = weighted[k] + jnp.sum(tail, axis=1, keepdims=True)
    both = weighted[0] + weighted[1]
    experts = iota((count, expert_total), 1)
    grad_logits = jnp.zeros((count, expert_total), F32)
    for k in range(2):
        grad_logits = jnp.where(
            experts == as_column(routes[k : k + 1, :], eye), weighted[k] - gates[k] * both, grad_logits
        )
    grad_logits = grad_logits.astype(LOW)
    grad_ffn = grad_ffn + mm(grad_logits, w_router[...])
    grad_norm, gain_ffn = norm_backward(middle[...], gains[1:2, :], grad_ffn)
    grad_middle = up + grad_norm
    grad_branch = grad_middle.astype(LOW)

    blocks = width // 128
    first_row = 3 * blocks * width
    attn_out_grad = mm_tn(mixed[...], grad_branch)
    for j in range(blocks):
        flat[pl.ds(first_row + j, width, stride=blocks), :] = attn_out_grad[:, 128 * j : 128 * j + 128]
    router_row = first_row + blocks * width
    router_rows = width * expert_total // 128
    padded_logits = jnp.concatenate(
        [grad_logits, jnp.zeros((count, 128 - expert_total), LOW)], axis=1
    )
    router_grad = mm_tn(ffn[...], padded_logits)
    feature = iota((width, 128), 0)
    lane_w = iota((width, 128), 1)
    start = feature * expert_total
    offset = start & 127
    turned = jnp.take_along_axis(router_grad, (lane_w - offset) & 127, axis=1)
    wrapped = lane_w < offset
    row_of = lax.shift_right_logical(iota((router_rows, width), 1) * expert_total, 7)
    row_here = iota((router_rows, width), 0)
    here = (row_of == row_here).astype(F32)
    after = (row_of + 1 == row_here).astype(F32)
    exact = lambda a, b: jnp.dot(a, b, precision=lax.Precision.HIGHEST, preferred_element_type=F32)
    flat[router_row : router_row + router_rows, :] = exact(
        here, jnp.where(wrapped, 0.0, turned)
    ) + exact(after, jnp.where(wrapped, turned, 0.0))
    gain_row = router_row + router_rows

    grad_mixed = mm_nt(grad_branch, w_out[...]).astype(LOW)
    lane = iota((count, 128), 1)
    low_lanes = lane < HEAD_DIM
    scale = HEAD_DIM**-0.5
    for pair in range(blocks):
        at = slice(128 * pair, 128 * pair + 128)
        queries = qkv[:, at] * jnp.asarray(scale, LOW)
        keys = qkv[:, width + 128 * pair : width + 128 * pair + 128]
        values = qkv[:, 2 * width + 128 * pair : 2 * width + 128 * pair + 128]
        grads = grad_mixed[:, at]
        grad_q = jnp.zeros((count, 128), F32)
        grad_k = jnp.zeros((count, 128), F32)
        grad_v = jnp.zeros((count, 128), F32)
        for half in range(2):
            mine = low_lanes if half == 0 else ~low_lanes
            only = lambda v: jnp.where(mine, v, jnp.zeros_like(v))
            q_half, g_half, k_half = only(queries), only(grads), only(keys)
            scores = jnp.where(allowed, mm_nt(q_half, keys), -1e30)
            head = 2 * pair + half
            probs = jnp.exp(scores - lse[:, head : head + 1])
            grad_probs = mm_nt(g_half, values)
            grad_v = grad_v + mm_tn(probs.astype(LOW), g_half)
            dots = jnp.sum(probs * grad_probs, axis=1, keepdims=True)
            grad_scores = (probs * (grad_probs - dots)).astype(LOW)
            grad_q = grad_q + mm(grad_scores, k_half)
            grad_k = grad_k + mm_tn(grad_scores, q_half)
        gqkv[:, at] = (grad_q * scale).astype(LOW)
        gqkv[:, width + 128 * pair : width + 128 * pair + 128] = grad_k.astype(LOW)
        gqkv[:, 2 * width + 128 * pair : 2 * width + 128 * pair + 128] = grad_v.astype(LOW)
    for j in range(0, 3 * blocks, 2):
        piece = mm_tn(attn_in[...], gqkv[:, 128 * j : 128 * j + 256])
        flat[pl.ds(j, width, stride=3 * blocks), :] = piece[:, :128]
        flat[pl.ds(j + 1, width, stride=3 * blocks), :] = piece[:, 128:]
    grad_attn = mm_nt(gqkv[...], w_qkv[...])
    grad_norm, gain_attn = norm_backward(tokens[...].astype(F32), gains[0:1, :], grad_attn)
    input_grad_o[...] = grad_middle + grad_norm
    for j in range(blocks):
        flat[gain_row + j : gain_row + j + 1, :] = gain_attn[:, 128 * j : 128 * j + 128]
        flat[gain_row + blocks + j : gain_row + blocks + j + 1, :] = gain_ffn[:, 128 * j : 128 * j + 128]
    last = gain_row + 2 * blocks
    flat[last:, :] = jnp.zeros((flat.shape[0] - last, 128), F32)

    core = core_ref[0]
    rows = flat.shape[0] // 128
    padded = kept_o.shape[1]

    @pl.loop(0, kept_o.shape[0])
    def move(i):
        kept_o[pl.ds(i, 1)] = flat[pl.ds((2 * i + core) * rows, padded), :].astype(LOW)[None]
        away_o[pl.ds(i, 1)] = flat[pl.ds((2 * i + 1 - core) * rows, padded), :].astype(LOW)[None]


def dense_backward(after, core, dense_rows, *arrays):
    count, width = arrays[4].shape
    rows = dense_rows // 128
    padded = (rows + 31) // 32 * 32
    return ordered(
        dense_backward_kernel, 1 + len(arrays), after,
        name="dense_backward",
        out_shape=[
            jax.ShapeDtypeStruct((count, width), F32),
            jax.ShapeDtypeStruct((64, padded, 128), LOW),
            jax.ShapeDtypeStruct((64, padded, 128), LOW),
        ],
        in_specs=[SMEM] + [VMEM] * len(arrays),
        out_specs=[VMEM] * 3,
        scratch_shapes=[
            pltpu.VMEM((rows * 128 + padded - rows, 128), F32),
            pltpu.VMEM((count, 3 * width), LOW),
        ],
        compiler_params=params(),
        cost_estimate=cost(12e9, 40e6),
    )(core, *arrays)


def combine_kernel(plan, middle, results, frozen_result, out):
    count, width = middle.shape
    total = middle[...]
    for first, ref in ((2, results), (4, frozen_result)):
        slots = iota((count, ref.shape[0]), 1)
        for k in range(2):
            place = plan[:, first + k : first + k + 1].astype(jnp.int32)
            total = total + plan[:, k : k + 1] * mm((slots == place).astype(F32).astype(LOW), ref[...])
    out[...] = total.astype(LOW)


def combine(after, plan, middle, results, frozen_result):
    return ordered(
        combine_kernel, 4, after,
        name="combine",
        out_shape=jax.ShapeDtypeStruct(middle.shape, LOW),
        in_specs=[VMEM] * 4,
        out_specs=VMEM,
        compiler_params=params(),
        cost_estimate=cost(200e9, 4e6),
    )(plan, middle, results, frozen_result)


def gelu_pair(pre):
    area = 0.5 + 0.5 * lax.erf(pre * (0.5**0.5))
    density = jnp.exp(-0.5 * pre * pre) * (1.0 / (2.0 * math.pi) ** 0.5)
    return pre * area, area + pre * density


HBM = pl.BlockSpec(memory_space=pl.ANY)


def build_weight(after, name, home, sources, by_rows):
    rows, cols = sources[0].shape[1:]

    def kernel(home_ref, local, near, across, local_mate, near_mate, across_mate, out, sems):
        z, half = home_ref[0], home_ref[2]

        def move(blocks):
            copies = []
            for step, shard in enumerate(blocks):
                if by_rows:
                    start = pl.multiple_of(half * (rows // 2), 64)
                    place = pl.ds(pl.multiple_of(((z + step) & 3) * (rows // 2), 64), rows // 2)
                    copies.append((shard.at[0, pl.ds(start, rows // 2), :], out.at[place, :]))
                else:
                    place = pl.ds(pl.multiple_of(((z + step) & 3) * rows, 64), rows)
                    for block in range(4):
                        start = pl.multiple_of((2 * block + half) * (cols // 8), 128)
                        to = slice(block * (cols // 8), (block + 1) * (cols // 8))
                        copies.append((shard.at[0, :, pl.ds(start, cols // 8)], out.at[place, to]))
            made = [pltpu.make_async_copy(a, b, sems.at[i]) for i, (a, b) in enumerate(copies)]
            for copy in made:
                copy.start()
            for copy in made:
                copy.wait()

        pl.when(home_ref[1] == 1)(lambda: move((local, near_mate, across_mate, near)))
        pl.when(home_ref[1] == 0)(lambda: move((local_mate, near, across, near_mate)))

    shape = (2 * rows, cols) if by_rows else (4 * rows, cols // 2)
    return ordered(
        kernel, 7, after,
        name=name,
        out_shape=jax.ShapeDtypeStruct(shape, LOW),
        in_specs=[SMEM] + [HBM] * 6,
        out_specs=VMEM,
        scratch_shapes=[pltpu.SemaphoreType.DMA((16,))],
        compiler_params=params(),
        cost_estimate=cost(1e5, 8e6),
    )(home, *sources)


def expert_up_kernel(rows, weight, hidden_o, slope_o):
    pre = mm(rows[...], weight[...])
    hidden, slope = gelu_pair(pre)
    hidden_o[...] = hidden.astype(LOW)
    slope_o[...] = slope.astype(LOW)


def expert_up(after, rows, weight):
    count, width = rows.shape[0], weight.shape[0]
    hidden = weight.shape[1]
    step = 256
    wide = jax.ShapeDtypeStruct((count, hidden), LOW)
    return ordered(
        expert_up_kernel, 2, after,
        name="expert_up",
        out_shape=[wide, wide],
        grid=(count // step,),
        in_specs=[pl.BlockSpec((step, width), lambda i: (i, 0)), pl.BlockSpec((width, hidden), lambda i: (0, 0))],
        out_specs=[pl.BlockSpec((step, hidden), lambda i: (i, 0))] * 2,
        compiler_params=params(),
        cost_estimate=cost(6e9, 8e6),
    )(rows, weight)


def split_three(value):
    high = lax.reduce_precision(value, 8, 7)
    mid = lax.reduce_precision(value - high, 8, 7)
    return high, mid, value - high - mid


def extra_terms(value):
    lane = iota((value.shape[0], EXTRA), 1)
    extra = jnp.zeros((value.shape[0], EXTRA), F32)
    for i, term in enumerate(split_three(value)):
        extra = jnp.where(lane == i, term, extra)
    return extra.astype(LOW)


def reduce_first(after, planes, partial, arrived):
    rows, columns = partial.shape[0] // 4, partial.shape[1]

    def kernel(planes, kept, arrived, *refs):
        mine, other = refs[-2:]
        for out, which in ((mine, planes[1]), (other, 1 - planes[1])):
            at = pl.ds(pl.multiple_of(which * rows, 64), rows)
            out[...] = (kept[at, :] + arrived[at, :].astype(F32)).astype(out.dtype)

    return pl.pallas_call(
        kernel,
        name="reduce_first",
        out_shape=[jax.ShapeDtypeStruct((rows, columns), t) for t in (F32, LOW)],
        grid_spec=pltpu.PrefetchScalarGridSpec(
            num_scalar_prefetch=1,
            grid=(1,),
            in_specs=[
                pl.BlockSpec((2 * rows, columns), lambda i, planes: (planes[0], 0)),
                pl.BlockSpec((2 * rows, columns), lambda i, planes: (0, 0)),
            ] + [HBM] * len(after),
            out_specs=[pl.BlockSpec((rows, columns), lambda i, planes: (0, 0))] * 2,
        ),
        compiler_params=params(),
        cost_estimate=cost(1e6, 6e6),
    )(planes, partial, arrived, *after)


def reduce_second(after, same, mine, other):
    def kernel(same_ref, mine, other, stays, leaves):
        straight = same_ref[0] == 1
        near, far = mine[...], other[...].astype(F32)
        stays[...] = jnp.where(straight, near, far)
        leaves[...] = jnp.where(straight, far, near).astype(LOW)

    return ordered(
        kernel, 3, after,
        name="reduce_second",
        out_shape=[jax.ShapeDtypeStruct(mine.shape, t) for t in (F32, LOW)],
        in_specs=[SMEM, VMEM, VMEM],
        out_specs=[VMEM] * 2,
        compiler_params=params(),
        cost_estimate=cost(1e6, 6e6),
    )(same, mine, other)


def frozen_kernel(rows, grads, w_in, w_out, result_o, back_o, result_sum, back_sum, value_sum):
    step = pl.program_id(0)

    @pl.when(step == 0)
    def clear():
        result_sum[...] = jnp.zeros_like(result_sum)
        back_sum[...] = jnp.zeros_like(back_sum)
        value_sum[...] = jnp.zeros_like(value_sum)

    hidden, slope = gelu_pair(mm(rows[...], w_in[...]))
    hidden = hidden.astype(LOW)
    result_sum[...] += mm(hidden, w_out[...])
    grad_hidden = mm_nt(grads[...], w_out[...])
    value_sum[...] += jnp.sum(hidden.astype(F32) * grad_hidden, axis=1, keepdims=True)
    back_sum[...] += mm_nt((grad_hidden * slope).astype(LOW), w_in[...])

    @pl.when(step == pl.num_programs(0) - 1)
    def finish():
        result_o[...] = result_sum[...].astype(LOW)
        width = back_sum.shape[1]
        back_o[:, :width] = back_sum[...].astype(LOW)
        back_o[:, width:] = extra_terms(value_sum[:, 0:1])


def frozen_expert(after, sent, w_in, w_out):
    count, width = sent.shape[0], w_in.shape[0]
    wide = w_in.shape[1]
    step = 512
    small = pl.BlockSpec((count, width), lambda i: (0, 0))
    return ordered(
        frozen_kernel, 4, after,
        name="frozen_expert",
        out_shape=[
            jax.ShapeDtypeStruct((count, width), LOW),
            jax.ShapeDtypeStruct((count, width + EXTRA), LOW),
        ],
        grid=(wide // step,),
        in_specs=[
            small, pl.BlockSpec((count, width), lambda i: (0, 1)),
            pl.BlockSpec((width, step), lambda i: (0, i)),
            pl.BlockSpec((step, width), lambda i: (i, 0)),
        ],
        out_specs=[small, pl.BlockSpec((count, width + EXTRA), lambda i: (0, 0))],
        scratch_shapes=[
            pltpu.VMEM((count, width), F32),
            pltpu.VMEM((count, width), F32),
            pltpu.VMEM((count, EXTRA), F32),
        ],
        compiler_params=params(),
        cost_estimate=cost(4e9, 10e6),
    )(sent, sent, w_in, w_out)


def adamw_values(master, first, second, grad):
    first_new = beta_first * first + (1.0 - beta_first) * grad
    second_new = beta_second * second + (1.0 - beta_second) * grad * grad
    first_hat = first_new * (1.0 / (1.0 - beta_first**STEP))
    second_hat = second_new * (1.0 / (1.0 - beta_second**STEP))
    master_new = master - learn_rate * (
        first_hat / (jnp.sqrt(second_hat) + adam_eps) + decay_rate * master
    )
    return master_new, first_new, second_new, master_new.astype(LOW)


def dense_update_kernel(master, first, second, terms, *outs):
    rows = master.shape[0]
    grad = jnp.sum(terms[...].astype(F32), axis=0)[:rows]
    for out, value in zip(outs, adamw_values(master[...], first[...], second[...], grad)):
        out[...] = value


def dense_update(after, master, first, second, terms):
    shape = (master.shape[0] // 128, 128)
    results = ordered(
        dense_update_kernel, 4, after,
        name="dense_update",
        out_shape=[jax.ShapeDtypeStruct(shape, t) for t in (F32, F32, F32, LOW)],
        in_specs=[VMEM] * 4,
        out_specs=[VMEM] * 4,
        compiler_params=params(),
        cost_estimate=cost(1e6, 4e6),
    )(*(a.reshape(shape) for a in (master, first, second)), terms)
    return tuple(r.reshape(master.shape) for r in results)


def expert_update(after, core, master, first, second, stays, arrived, axis):
    rows, columns = master.shape[1:]
    if axis == 1:
        blocks, width = 4, columns // 4
        half = (rows, width // 2)
    else:
        blocks, width = 3, columns // 3
        half = (rows // 2, width)

    def kernel(core_ref, master, first, second, stays, arrived, *outs):
        near, far = stays[...], arrived[...].astype(F32)
        swapped = core_ref[0] == 1
        grad = jnp.concatenate(
            [jnp.where(swapped, far, near), jnp.where(swapped, near, far)], axis=axis
        )
        values = adamw_values(master[0], first[0], second[0], grad)
        for out, value in zip(outs, values):
            out[0] = value

    wide = pl.BlockSpec((1, rows, width), lambda i: (0, 0, i))
    slim = pl.BlockSpec(half, lambda i: (0, i))
    return tuple(
        ordered(
        kernel, 6, after,
            name="update_in" if axis == 1 else "update_out",
            out_shape=[jax.ShapeDtypeStruct(master.shape, t) for t in (F32, F32, F32, LOW)],
            grid=(blocks,),
            in_specs=[SMEM, wide, wide, wide, slim, slim],
            out_specs=[wide] * 4,
            compiler_params=params(),
            cost_estimate=cost(2e7, 18e6),
        )(core, master, first, second, stays, arrived)
    )


def swap_core(block):
    return lax.ppermute(block, "c", [(0, 1), (1, 0)])


KINDS = (0, 1, 1, 0)


def to_neighbours(shard):
    moves = []
    for z, kind in enumerate(KINDS):
        moves.append(((z - 1) % 4 * 2 + kind, z * 2 + kind))
        moves.append(((z + 1) % 4 * 2 + kind, z * 2 + 1 - kind))
    return lax.ppermute(shard, DEPTH + ("c",), moves)


def to_opposite(shard):
    moves = []
    for z, kind in enumerate(KINDS):
        source = kind if z % 2 else 1 - kind
        moves.append((z * 2 + source, (3 - z) * 2 + 1 - kind))
    return lax.ppermute(shard, DEPTH + ("c",), moves)


def swap_pair(block):
    return lax.ppermute(block, DEPTH, [(z, 3 - z) for z in range(4)])


def swap_low(block):
    return lax.ppermute(block, "zl", [(0, 1), (1, 0)])


def exchange(rows):
    cut = rows.reshape(-1, CAP, rows.shape[1])
    cut = lax.all_to_all(cut, PLANE, split_axis=0, concat_axis=0, tiled=True)
    return cut.reshape(rows.shape)


def tie(array, *others):
    return lax.optimization_barrier((array,) + others)[0]


def word(*values):
    return jnp.stack([jnp.asarray(v, jnp.int32) for v in values])


def body(
    tokens,
    segment_ids,
    routes,
    cotangent,
    w_qkv,
    w_attn_out,
    w_router,
    norm_gains,
    frozen_in,
    frozen_out,
    new_in,
    new_out,
    dense_master,
    dense_first,
    dense_second,
    master_in,
    first_in,
    second_in,
    master_out,
    first_out,
    second_out,
):
    core, zh, zl = (lax.axis_index(a) for a in ("c", "zh", "zl"))
    z = 2 * zh + zl
    kind = zh ^ zl
    same = jnp.where(kind == core, 1, 0)
    home = word(z, same, core)
    core_word, same_word = word(core), word(same)
    routes = routes.T
    w_router = w_router.T

    in_near, out_near = to_neighbours(new_in), to_neighbours(new_out)
    attn_in, qkv_low, mixed_low, lse, middle, ffn_in, plan, sent, frozen_sent = dense_forward(
        (), word(zh), tokens, segment_ids, routes, cotangent, w_qkv, w_attn_out, w_router, norm_gains
    )
    received = exchange(sent)
    in_across = to_opposite(tie(in_near, plan))
    out_across = to_opposite(tie(out_near, plan))
    frozen_result, frozen_back = frozen_expert((), frozen_sent, frozen_in, frozen_out)
    in_shards, out_shards = (new_in, in_near, in_across), (new_out, out_near, out_across)
    in_shards = in_shards + tuple(swap_core(tie(s, plan)) for s in in_shards)
    out_shards = out_shards + tuple(swap_core(tie(s, plan)) for s in out_shards)
    half_in = build_weight((frozen_back,), "build_in", home, in_shards, False)
    half_out = build_weight((half_in,), "build_out", home, out_shards, True)
    received = tie(received, frozen_back)
    received_mate = swap_core(received)
    width = tokens.shape[1]
    rows_own, rows_mate = received[:, :width], received_mate[:, :width]
    grads_own, grads_mate = received[:, width:], received_mate[:, width:]

    hidden_own, slope_own = expert_up((), received, half_in)
    hidden_mate, slope_mate = expert_up((hidden_own,), received_mate, half_in)
    pre_of = lambda grads, slope: (mm_nt(grads, half_out) * slope.astype(F32)).astype(LOW)
    pre_mate = pre_of(grads_mate, slope_mate)
    back_arrived = swap_core(mm_nt(pre_mate, half_in).astype(LOW))
    result_arrived = swap_core(mm(hidden_mate, half_out).astype(LOW))
    pre_own = pre_of(grads_own, slope_own)
    result = (mm(hidden_own, half_out) + result_arrived.astype(F32)).astype(LOW)
    back = (mm_nt(pre_own, half_in) + back_arrived.astype(F32)).astype(LOW)
    value = jnp.sum(grads_own.astype(F32) * result.astype(F32), axis=1, keepdims=True)
    merged = jnp.concatenate([back, extra_terms(value)], axis=1)
    back = exchange(merged)
    result_back = exchange(result)
    grad_out = mm_tn(hidden_own, grads_own) + mm_tn(hidden_mate, grads_mate)
    grad_in = mm_tn(rows_own, pre_own) + mm_tn(rows_mate, pre_mate)

    def leaving(partial):
        rows = partial.shape[0] // 2
        away = lax.dynamic_slice(partial, ((1 - zh) * rows, 0), (rows, partial.shape[1]))
        return swap_pair(away.astype(LOW))

    out_arrived, in_arrived = leaving(grad_out), leaving(grad_in)
    planes = word(zh, zl)
    out_mine, out_other = reduce_first((merged,), planes, grad_out, out_arrived)
    out_other = swap_low(out_other)

    input_grad, kept, away = dense_backward(
        (out_mine,), core_word, dense_master.shape[0], plan, routes, segment_ids, cotangent, tokens, middle,
        mixed_low, ffn_in, lse, qkv_low, attn_in, w_qkv, w_attn_out, w_router, norm_gains, back, frozen_back,
    )
    arrived = swap_core(away)
    in_mine, in_other = reduce_first((kept,), planes, grad_in, in_arrived)
    in_other = swap_low(in_other)
    activations = combine((in_mine,), plan, middle, result_back, frozen_result)
    kept = tie(kept, activations, out_other)
    summed = (kept.astype(F32) + arrived.astype(F32)).astype(LOW)
    terms = lax.all_to_all(summed, ("zh", "zl", "x", "y"), split_axis=0, concat_axis=0, tiled=True)
    out_stays, out_leaves = reduce_second((summed,), same_word, out_mine, out_other)
    out_mate_grad = swap_core(out_leaves)
    in_stays, in_leaves = reduce_second((out_stays,), same_word, in_mine, in_other)
    in_mate_grad = swap_core(in_leaves)
    out_new = expert_update(
        (in_stays,), core_word, master_out, first_out, second_out, out_stays, out_mate_grad, 0
    )
    in_new = expert_update(
        (out_new[0],), core_word, master_in, first_in, second_in, in_stays, in_mate_grad, 1
    )
    dense_new = dense_update((in_new[0],), dense_master, dense_first, dense_second, terms)
    return (activations, input_grad) + dense_new + in_new + out_new


def solution(mesh):
    fine = Mesh(mesh.devices.reshape(2, 2, 4, 4, 2), ALL)
    tokens = P(ALL, None)
    flat = P(ALL)
    expert = P(("x", "y", "c"), DEPTH, None)
    return jax.shard_map(
        body,
        mesh=fine,
        in_specs=(tokens,) * 4 + (P(),) * 6 + (expert,) * 2 + (flat,) * 3 + (expert,) * 6,
        out_specs=(tokens,) * 2 + (flat,) * 4 + (expert,) * 8,
        check_vma=False,
    )
```

```python
import math

import jax
import jax.numpy as jnp
from jax import lax
from jax.experimental import pallas as pl
from jax.experimental.pallas import tpu as pltpu
from jax.sharding import Mesh
from jax.sharding import PartitionSpec as P

HEAD_DIM = 64
STEP = 5


norm_eps = 1e-05
learn_rate = 0.02
beta_first = 0.5
beta_second = 0.5
adam_eps = 1e-08
decay_rate = 0.1


PLANE = ("zl", "x", "y")
DEPTH = ("zh", "zl")
ALL = ("zh", "zl", "x", "y", "c")
CAP = 24
PAIRS = 6
EXTRA = 128
VMEM = pl.BlockSpec(memory_space=pltpu.VMEM)
SMEM = pl.BlockSpec(memory_space=pltpu.SMEM)
F32 = jnp.float32
LOW = jnp.bfloat16


def params(**more):
    return pltpu.CompilerParams(vmem_limit_bytes=56 * 1024 * 1024, **more)


def ordered(kernel, count, after, **call):
    extra = len(after)

    def inner(*refs):
        return kernel(*refs[:count], *refs[count + extra :])

    call["in_specs"] = list(call["in_specs"]) + [pl.BlockSpec(memory_space=pl.ANY)] * extra
    made = pl.pallas_call(inner, **call)
    return lambda *arrays: made(*arrays, *after)


def cost(flops, moved):
    return pl.CostEstimate(flops=int(flops), bytes_accessed=int(moved), transcendentals=0)


def mm(left, right):
    return jnp.dot(left, right, preferred_element_type=F32)


def mm_nt(left, right):
    return lax.dot_general(left, right, (((1,), (1,)), ((), ())), preferred_element_type=F32)


def mm_tn(left, right):
    return lax.dot_general(left, right, (((0,), (0,)), ((), ())), preferred_element_type=F32)


def iota(shape, axis):
    return lax.broadcasted_iota(jnp.int32, shape, axis)


def normed(values):
    centered = values - jnp.mean(values, axis=1, keepdims=True)
    scale = lax.rsqrt(jnp.mean(centered * centered, axis=1, keepdims=True) + norm_eps)
    return centered * scale, scale


def norm_backward(values, gain, upstream):
    hat, scale = normed(values)
    gain_grad = jnp.sum(upstream * hat, axis=0, keepdims=True)
    inner = upstream * gain
    mean_inner = jnp.mean(inner, axis=1, keepdims=True)
    mean_hat = jnp.mean(inner * hat, axis=1, keepdims=True)
    return scale * (inner - mean_inner - hat * mean_hat), gain_grad


def as_column(row, eye):
    return jnp.sum(jnp.where(eye, row, jnp.zeros_like(row)), axis=1, keepdims=True)


def as_row(column, eye):
    return jnp.sum(jnp.where(eye, column, jnp.zeros_like(column)), axis=0, keepdims=True)


def attention_mask(segment_row):
    count = segment_row.shape[1]
    down, across = iota((count, count), 0), iota((count, count), 1)
    eye = down == across
    column = jnp.sum(jnp.where(eye, segment_row, 0), axis=1, keepdims=True)
    return (down >= across) & (column == segment_row), eye


def dense_forward_kernel(
    zh_ref, tokens, segments, routes, cotangent, w_qkv, w_out, w_router, gains,
    attn_in_o, qkv_o, mixed_o, lse_o, middle_o, ffn_o, plan_o, sent_o, frozen_sent_o,
):
    width = tokens.shape[1]
    count = tokens.shape[0]
    inputs = tokens[...].astype(F32)
    hat, unused = normed(inputs)
    attn_in = (hat * gains[0:1, :]).astype(LOW)
    attn_in_o[...] = attn_in
    qkv_o[...] = mm(attn_in, w_qkv[...]).astype(LOW)
    allowed, eye = attention_mask(segments[...])
    lane = iota((count, 128), 1)
    low_lanes = lane < HEAD_DIM
    lse_all = jnp.zeros((count, 128), F32)
    for pair in range(width // 128):
        at = slice(128 * pair, 128 * pair + 128)
        queries = qkv_o[:, at] * jnp.asarray(HEAD_DIM**-0.5, LOW)
        keys = qkv_o[:, width + 128 * pair : width + 128 * pair + 128]
        values = qkv_o[:, 2 * width + 128 * pair : 2 * width + 128 * pair + 128]
        outs = []
        for half in range(2):
            mine = low_lanes if half == 0 else ~low_lanes
            scores = mm_nt(jnp.where(mine, queries, jnp.zeros_like(queries)), keys)
            scores = jnp.where(allowed, scores, -1e30)
            top = jnp.max(scores, axis=1, keepdims=True)
            raised = jnp.exp(scores - top)
            total = jnp.sum(raised, axis=1, keepdims=True)
            probs = (raised * (1.0 / total)).astype(LOW)
            outs.append(mm(probs, values))
            lse_all = jnp.where(lane == 2 * pair + half, top + jnp.log(total), lse_all)
        mixed_o[:, at] = jnp.where(low_lanes, outs[0], outs[1]).astype(LOW)
    lse_o[...] = lse_all
    middle = inputs + mm(mixed_o[...], w_out[...])
    middle_o[...] = middle
    hat, unused = normed(middle)
    ffn = (hat * gains[1:2, :]).astype(LOW)
    ffn_o[...] = ffn
    logits = mm_nt(ffn, w_router[...])
    experts = iota(logits.shape, 1)
    lists = [as_column(routes[k : k + 1, :], eye) for k in range(2)]
    picks = [experts == column for column in lists]
    chosen = [jnp.sum(jnp.where(p, logits, 0.0), axis=1, keepdims=True) for p in picks]
    top = jnp.maximum(chosen[0], chosen[1])
    raised = [jnp.exp(c - top) for c in chosen]
    gates = [r / (raised[0] + raised[1]) for r in raised]
    named = (picks[0] | picks[1]).astype(F32).astype(LOW)
    earlier = (iota((count, count), 0) > iota((count, count), 1)).astype(F32).astype(LOW)
    before = mm(earlier, named)
    zh = zh_ref[0]
    new_place, old_place = [], []
    for k in range(2):
        route = lists[k]
        slot = jnp.sum(jnp.where(picks[k], before, 0.0), axis=1, keepdims=True).astype(jnp.int32)
        fresh = route - 1
        block = 16 * ((fresh & 1) ^ zh) + lax.shift_right_arithmetic(fresh, 1)
        new_place.append(jnp.where(route > 0, block * CAP + slot, -1))
        old_place.append(jnp.where(route > 0, -1, slot))
    columns = gates + [p.astype(F32) for p in new_place + old_place]
    plan = jnp.zeros((count, 128), F32)
    for i, column in enumerate(columns):
        plan = jnp.where(lane == i, column, plan)
    plan_o[...] = plan
    up = cotangent[...].astype(F32)
    scaled = [(g * up).astype(LOW) for g in gates]
    for places, ref in ((new_place, sent_o), (old_place, frozen_sent_o)):
        slots = iota((ref.shape[0], count), 0)
        spread = [(slots == as_row(p, eye)).astype(F32).astype(LOW) for p in places]
        ref[:, :width] = mm(spread[0] + spread[1], ffn).astype(LOW)
        ref[:, width:] = (mm(spread[0], scaled[0]) + mm(spread[1], scaled[1])).astype(LOW)


def dense_forward(after, zh, tokens, segments, routes, cotangent, w_qkv, w_out, w_router, gains):
    count, width = tokens.shape
    slots = (w_router.shape[0] - 1) * CAP
    shapes = [
        ((count, width), LOW), ((count, 3 * width), LOW), ((count, width), LOW), ((count, 128), F32),
        ((count, width), F32), ((count, width), LOW), ((count, 128), F32),
        ((slots, 2 * width), LOW), ((CAP, 2 * width), LOW),
    ]
    return ordered(
        dense_forward_kernel, 9, after,
        name="dense_forward",
        out_shape=[jax.ShapeDtypeStruct(s, t) for s, t in shapes],
        in_specs=[SMEM] + [VMEM] * 8,
        out_specs=[VMEM] * len(shapes),
        compiler_params=params(),
        cost_estimate=cost(8e9, 30e6),
    )(zh, tokens, segments, routes, cotangent, w_qkv, w_out, w_router, gains)


def dense_backward_kernel(
    core_ref, plan, routes, segments, cotangent, tokens, middle, mixed, ffn, lse, qkv, attn_in,
    w_qkv, w_out, w_router, gains, back, frozen_back,
    input_grad_o, kept_o, away_o,
    flat, gqkv,
):
    count, width = tokens.shape
    expert_total = w_router.shape[0]
    up = cotangent[...].astype(F32)
    gates = [plan[:, k : k + 1] for k in range(2)]
    new_place = [plan[:, 2 + k : 3 + k].astype(jnp.int32) for k in range(2)]
    old_place = [plan[:, 4 + k : 5 + k].astype(jnp.int32) for k in range(2)]
    allowed, eye = attention_mask(segments[...])

    grad_ffn = jnp.zeros((count, width), F32)
    weighted = [jnp.zeros((count, 1), F32) for k in range(2)]
    for places, ref in ((new_place, back), (old_place, frozen_back)):
        size = ref.shape[0]
        slots = iota((count, size), 1)
        for k in range(2):
            choice = (slots == places[k]).astype(F32).astype(LOW)
            picked = mm(choice, ref[...])
            grad_ffn = grad_ffn + picked[:, :width]
            tail = picked[:, width:]
            weighted[k] = weighted[k] + jnp.sum(tail, axis=1, keepdims=True)
    both = weighted[0] + weighted[1]
    experts = iota((count, expert_total), 1)
    grad_logits = jnp.zeros((count, expert_total), F32)
    for k in range(2):
        grad_logits = jnp.where(
            experts == as_column(routes[k : k + 1, :], eye), weighted[k] - gates[k] * both, grad_logits
        )
    grad_logits = grad_logits.astype(LOW)
    grad_ffn = grad_ffn + mm(grad_logits, w_router[...])
    grad_norm, gain_ffn = norm_backward(middle[...], gains[1:2, :], grad_ffn)
    grad_middle = up + grad_norm
    grad_branch = grad_middle.astype(LOW)

    blocks = width // 128
    first_row = 3 * blocks * width
    attn_out_grad = mm_tn(mixed[...], grad_branch)
    for j in range(blocks):
        flat[pl.ds(first_row + j, width, stride=blocks), :] = attn_out_grad[:, 128 * j : 128 * j + 128]
    router_row = first_row + blocks * width
    router_rows = width * expert_total // 128
    padded_logits = jnp.concatenate(
        [grad_logits, jnp.zeros((count, 128 - expert_total), LOW)], axis=1
    )
    router_grad = mm_tn(ffn[...], padded_logits)
    feature = iota((width, 128), 0)
    lane_w = iota((width, 128), 1)
    start = feature * expert_total
    offset = start & 127
    turned = jnp.take_along_axis(router_grad, (lane_w - offset) & 127, axis=1)
    wrapped = lane_w < offset
    row_of = lax.shift_right_logical(iota((router_rows, width), 1) * expert_total, 7)
    row_here = iota((router_rows, width), 0)
    here = (row_of == row_here).astype(F32)
    after = (row_of + 1 == row_here).astype(F32)
    exact = lambda a, b: jnp.dot(a, b, precision=lax.Precision.HIGHEST, preferred_element_type=F32)
    flat[router_row : router_row + router_rows, :] = exact(
        here, jnp.where(wrapped, 0.0, turned)
    ) + exact(after, jnp.where(wrapped, turned, 0.0))
    gain_row = router_row + router_rows

    grad_mixed = mm_nt(grad_branch, w_out[...]).astype(LOW)
    lane = iota((count, 128), 1)
    low_lanes = lane < HEAD_DIM
    scale = HEAD_DIM**-0.5
    for pair in range(blocks):
        at = slice(128 * pair, 128 * pair + 128)
        queries = qkv[:, at] * jnp.asarray(scale, LOW)
        keys = qkv[:, width + 128 * pair : width + 128 * pair + 128]
        values = qkv[:, 2 * width + 128 * pair : 2 * width + 128 * pair + 128]
        grads = grad_mixed[:, at]
        grad_q = jnp.zeros((count, 128), F32)
        grad_k = jnp.zeros((count, 128), F32)
        grad_v = jnp.zeros((count, 128), F32)
        for half in range(2):
            mine = low_lanes if half == 0 else ~low_lanes
            only = lambda v: jnp.where(mine, v, jnp.zeros_like(v))
            q_half, g_half, k_half = only(queries), only(grads), only(keys)
            scores = jnp.where(allowed, mm_nt(q_half, keys), -1e30)
            head = 2 * pair + half
            probs = jnp.exp(scores - lse[:, head : head + 1])
            grad_probs = mm_nt(g_half, values)
            grad_v = grad_v + mm_tn(probs.astype(LOW), g_half)
            dots = jnp.sum(probs * grad_probs, axis=1, keepdims=True)
            grad_scores = (probs * (grad_probs - dots)).astype(LOW)
            grad_q = grad_q + mm(grad_scores, k_half)
            grad_k = grad_k + mm_tn(grad_scores, q_half)
        gqkv[:, at] = (grad_q * scale).astype(LOW)
        gqkv[:, width + 128 * pair : width + 128 * pair + 128] = grad_k.astype(LOW)
        gqkv[:, 2 * width + 128 * pair : 2 * width + 128 * pair + 128] = grad_v.astype(LOW)
    for j in range(0, 3 * blocks, 2):
        piece = mm_tn(attn_in[...], gqkv[:, 128 * j : 128 * j + 256])
        flat[pl.ds(j, width, stride=3 * blocks), :] = piece[:, :128]
        flat[pl.ds(j + 1, width, stride=3 * blocks), :] = piece[:, 128:]
    grad_attn = mm_nt(gqkv[...], w_qkv[...])
    grad_norm, gain_attn = norm_backward(tokens[...].astype(F32), gains[0:1, :], grad_attn)
    input_grad_o[...] = grad_middle + grad_norm
    for j in range(blocks):
        flat[gain_row + j : gain_row + j + 1, :] = gain_attn[:, 128 * j : 128 * j + 128]
        flat[gain_row + blocks + j : gain_row + blocks + j + 1, :] = gain_ffn[:, 128 * j : 128 * j + 128]
    last = gain_row + 2 * blocks
    flat[last:, :] = jnp.zeros((flat.shape[0] - last, 128), F32)

    core = core_ref[0]
    rows = flat.shape[0] // 128
    padded = kept_o.shape[1]

    @pl.loop(0, kept_o.shape[0])
    def move(i):
        kept_o[pl.ds(i, 1)] = flat[pl.ds((2 * i + core) * rows, padded), :].astype(LOW)[None]
        away_o[pl.ds(i, 1)] = flat[pl.ds((2 * i + 1 - core) * rows, padded), :].astype(LOW)[None]


def dense_backward(after, core, dense_rows, *arrays):
    count, width = arrays[4].shape
    rows = dense_rows // 128
    padded = (rows + 31) // 32 * 32
    return ordered(
        dense_backward_kernel, 1 + len(arrays), after,
        name="dense_backward",
        out_shape=[
            jax.ShapeDtypeStruct((count, width), F32),
            jax.ShapeDtypeStruct((64, padded, 128), LOW),
            jax.ShapeDtypeStruct((64, padded, 128), LOW),
        ],
        in_specs=[SMEM] + [VMEM] * len(arrays),
        out_specs=[VMEM] * 3,
        scratch_shapes=[
            pltpu.VMEM((rows * 128 + padded - rows, 128), F32),
            pltpu.VMEM((count, 3 * width), LOW),
        ],
        compiler_params=params(),
        cost_estimate=cost(12e9, 40e6),
    )(core, *arrays)


def combine_kernel(plan, middle, results, frozen_result, out):
    count, width = middle.shape
    total = middle[...]
    for first, ref in ((2, results), (4, frozen_result)):
        slots = iota((count, ref.shape[0]), 1)
        for k in range(2):
            place = plan[:, first + k : first + k + 1].astype(jnp.int32)
            total = total + plan[:, k : k + 1] * mm((slots == place).astype(F32).astype(LOW), ref[...])
    out[...] = total.astype(LOW)


def combine(after, plan, middle, results, frozen_result):
    return ordered(
        combine_kernel, 4, after,
        name="combine",
        out_shape=jax.ShapeDtypeStruct(middle.shape, LOW),
        in_specs=[VMEM] * 4,
        out_specs=VMEM,
        compiler_params=params(),
        cost_estimate=cost(200e9, 4e6),
    )(plan, middle, results, frozen_result)


def gelu_pair(pre):
    area = 0.5 + 0.5 * lax.erf(pre * (0.5**0.5))
    density = jnp.exp(-0.5 * pre * pre) * (1.0 / (2.0 * math.pi) ** 0.5)
    return pre * area, area + pre * density


HBM = pl.BlockSpec(memory_space=pl.ANY)


def build_weight(after, name, home, sources, by_rows):
    rows, cols = sources[0].shape[1:]

    def kernel(home_ref, local, near, across, local_mate, near_mate, across_mate, out, sems):
        z, half = home_ref[0], home_ref[2]

        def move(blocks):
            copies = []
            for step, shard in enumerate(blocks):
                if by_rows:
                    start = pl.multiple_of(half * (rows // 2), 64)
                    place = pl.ds(pl.multiple_of(((z + step) & 3) * (rows // 2), 64), rows // 2)
                    copies.append((shard.at[0, pl.ds(start, rows // 2), :], out.at[place, :]))
                else:
                    place = pl.ds(pl.multiple_of(((z + step) & 3) * rows, 64), rows)
                    for block in range(4):
                        start = pl.multiple_of((2 * block + half) * (cols // 8), 128)
                        to = slice(block * (cols // 8), (block + 1) * (cols // 8))
                        copies.append((shard.at[0, :, pl.ds(start, cols // 8)], out.at[place, to]))
            made = [pltpu.make_async_copy(a, b, sems.at[i]) for i, (a, b) in enumerate(copies)]
            for copy in made:
                copy.start()
            for copy in made:
                copy.wait()

        pl.when(home_ref[1] == 1)(lambda: move((local, near_mate, across_mate, near)))
        pl.when(home_ref[1] == 0)(lambda: move((local_mate, near, across, near_mate)))

    shape = (2 * rows, cols) if by_rows else (4 * rows, cols // 2)
    return ordered(
        kernel, 7, after,
        name=name,
        out_shape=jax.ShapeDtypeStruct(shape, LOW),
        in_specs=[SMEM] + [HBM] * 6,
        out_specs=VMEM,
        scratch_shapes=[pltpu.SemaphoreType.DMA((16,))],
        compiler_params=params(),
        cost_estimate=cost(1e5, 8e6),
    )(home, *sources)


def expert_up_kernel(rows, weight, hidden_o, slope_o):
    pre = mm(rows[...], weight[...])
    hidden, slope = gelu_pair(pre)
    hidden_o[...] = hidden.astype(LOW)
    slope_o[...] = slope.astype(LOW)


def expert_up(after, rows, weight):
    count, width = rows.shape[0], weight.shape[0]
    hidden = weight.shape[1]
    step = 256
    wide = jax.ShapeDtypeStruct((count, hidden), LOW)
    return ordered(
        expert_up_kernel, 2, after,
        name="expert_up",
        out_shape=[wide, wide],
        grid=(count // step,),
        in_specs=[pl.BlockSpec((step, width), lambda i: (i, 0)), pl.BlockSpec((width, hidden), lambda i: (0, 0))],
        out_specs=[pl.BlockSpec((step, hidden), lambda i: (i, 0))] * 2,
        compiler_params=params(),
        cost_estimate=cost(6e9, 8e6),
    )(rows, weight)


def split_three(value):
    high = lax.reduce_precision(value, 8, 7)
    mid = lax.reduce_precision(value - high, 8, 7)
    return high, mid, value - high - mid


def extra_terms(value):
    lane = iota((value.shape[0], EXTRA), 1)
    extra = jnp.zeros((value.shape[0], EXTRA), F32)
    for i, term in enumerate(split_three(value)):
        extra = jnp.where(lane == i, term, extra)
    return extra.astype(LOW)


def reduce_first(after, planes, partial, arrived):
    rows, columns = partial.shape[0] // 4, partial.shape[1]

    def kernel(planes, kept, arrived, *refs):
        mine, other = refs[-2:]
        for out, which in ((mine, planes[1]), (other, 1 - planes[1])):
            at = pl.ds(pl.multiple_of(which * rows, 64), rows)
            out[...] = (kept[at, :] + arrived[at, :].astype(F32)).astype(out.dtype)

    return pl.pallas_call(
        kernel,
        name="reduce_first",
        out_shape=[jax.ShapeDtypeStruct((rows, columns), t) for t in (F32, LOW)],
        grid_spec=pltpu.PrefetchScalarGridSpec(
            num_scalar_prefetch=1,
            grid=(1,),
            in_specs=[
                pl.BlockSpec((2 * rows, columns), lambda i, planes: (planes[0], 0)),
                pl.BlockSpec((2 * rows, columns), lambda i, planes: (0, 0)),
            ] + [HBM] * len(after),
            out_specs=[pl.BlockSpec((rows, columns), lambda i, planes: (0, 0))] * 2,
        ),
        compiler_params=params(),
        cost_estimate=cost(1e6, 6e6),
    )(planes, partial, arrived, *after)


def reduce_second(after, same, mine, other):
    def kernel(same_ref, mine, other, stays, leaves):
        straight = same_ref[0] == 1
        near, far = mine[...], other[...].astype(F32)
        stays[...] = jnp.where(straight, near, far)
        leaves[...] = jnp.where(straight, far, near).astype(LOW)

    return ordered(
        kernel, 3, after,
        name="reduce_second",
        out_shape=[jax.ShapeDtypeStruct(mine.shape, t) for t in (F32, LOW)],
        in_specs=[SMEM, VMEM, VMEM],
        out_specs=[VMEM] * 2,
        compiler_params=params(),
        cost_estimate=cost(1e6, 6e6),
    )(same, mine, other)


def frozen_kernel(rows, grads, w_in, w_out, result_o, back_o, result_sum, back_sum, value_sum):
    step = pl.program_id(0)

    @pl.when(step == 0)
    def clear():
        result_sum[...] = jnp.zeros_like(result_sum)
        back_sum[...] = jnp.zeros_like(back_sum)
        value_sum[...] = jnp.zeros_like(value_sum)

    hidden, slope = gelu_pair(mm(rows[...], w_in[...]))
    hidden = hidden.astype(LOW)
    result_sum[...] += mm(hidden, w_out[...])
    grad_hidden = mm_nt(grads[...], w_out[...])
    value_sum[...] += jnp.sum(hidden.astype(F32) * grad_hidden, axis=1, keepdims=True)
    back_sum[...] += mm_nt((grad_hidden * slope).astype(LOW), w_in[...])

    @pl.when(step == pl.num_programs(0) - 1)
    def finish():
        result_o[...] = result_sum[...].astype(LOW)
        width = back_sum.shape[1]
        back_o[:, :width] = back_sum[...].astype(LOW)
        back_o[:, width:] = extra_terms(value_sum[:, 0:1])


def frozen_expert(after, sent, w_in, w_out):
    count, width = sent.shape[0], w_in.shape[0]
    wide = w_in.shape[1]
    step = 512
    small = pl.BlockSpec((count, width), lambda i: (0, 0))
    return ordered(
        frozen_kernel, 4, after,
        name="frozen_expert",
        out_shape=[
            jax.ShapeDtypeStruct((count, width), LOW),
            jax.ShapeDtypeStruct((count, width + EXTRA), LOW),
        ],
        grid=(wide // step,),
        in_specs=[
            small, pl.BlockSpec((count, width), lambda i: (0, 1)),
            pl.BlockSpec((width, step), lambda i: (0, i)),
            pl.BlockSpec((step, width), lambda i: (i, 0)),
        ],
        out_specs=[small, pl.BlockSpec((count, width + EXTRA), lambda i: (0, 0))],
        scratch_shapes=[
            pltpu.VMEM((count, width), F32),
            pltpu.VMEM((count, width), F32),
            pltpu.VMEM((count, EXTRA), F32),
        ],
        compiler_params=params(),
        cost_estimate=cost(4e9, 10e6),
    )(sent, sent, w_in, w_out)


def adamw_values(master, first, second, grad):
    first_new = beta_first * first + (1.0 - beta_first) * grad
    second_new = beta_second * second + (1.0 - beta_second) * grad * grad
    first_hat = first_new * (1.0 / (1.0 - beta_first**STEP))
    second_hat = second_new * (1.0 / (1.0 - beta_second**STEP))
    master_new = master - learn_rate * (
        first_hat / (jnp.sqrt(second_hat) + adam_eps) + decay_rate * master
    )
    return master_new, first_new, second_new, master_new.astype(LOW)


def dense_update_kernel(master, first, second, terms, *outs):
    rows = master.shape[0]
    grad = jnp.sum(terms[...].astype(F32), axis=0)[:rows]
    for out, value in zip(outs, adamw_values(master[...], first[...], second[...], grad)):
        out[...] = value


def dense_update(after, master, first, second, terms):
    shape = (master.shape[0] // 128, 128)
    results = ordered(
        dense_update_kernel, 4, after,
        name="dense_update",
        out_shape=[jax.ShapeDtypeStruct(shape, t) for t in (F32, F32, F32, LOW)],
        in_specs=[VMEM] * 4,
        out_specs=[VMEM] * 4,
        compiler_params=params(),
        cost_estimate=cost(1e6, 4e6),
    )(*(a.reshape(shape) for a in (master, first, second)), terms)
    return tuple(r.reshape(master.shape) for r in results)


def expert_update(after, core, master, first, second, stays, arrived, axis):
    rows, columns = master.shape[1:]
    if axis == 1:
        blocks, width = 4, columns // 4
        half = (rows, width // 2)
    else:
        blocks, width = 3, columns // 3
        half = (rows // 2, width)

    def kernel(core_ref, master, first, second, stays, arrived, *outs):
        near, far = stays[...], arrived[...].astype(F32)
        swapped = core_ref[0] == 1
        grad = jnp.concatenate(
            [jnp.where(swapped, far, near), jnp.where(swapped, near, far)], axis=axis
        )
        values = adamw_values(master[0], first[0], second[0], grad)
        for out, value in zip(outs, values):
            out[0] = value

    wide = pl.BlockSpec((1, rows, width), lambda i: (0, 0, i))
    slim = pl.BlockSpec(half, lambda i: (0, i))
    return tuple(
        ordered(
        kernel, 6, after,
            name="update_in" if axis == 1 else "update_out",
            out_shape=[jax.ShapeDtypeStruct(master.shape, t) for t in (F32, F32, F32, LOW)],
            grid=(blocks,),
            in_specs=[SMEM, wide, wide, wide, slim, slim],
            out_specs=[wide] * 4,
            compiler_params=params(),
            cost_estimate=cost(2e7, 18e6),
        )(core, master, first, second, stays, arrived)
    )


def swap_core(block):
    return lax.ppermute(block, "c", [(0, 1), (1, 0)])


KINDS = (0, 1, 1, 0)


def to_neighbours(shard):
    moves = []
    for z, kind in enumerate(KINDS):
        moves.append(((z - 1) % 4 * 2 + kind, z * 2 + kind))
        moves.append(((z + 1) % 4 * 2 + kind, z * 2 + 1 - kind))
    return lax.ppermute(shard, DEPTH + ("c",), moves)


def to_opposite(shard):
    moves = []
    for z, kind in enumerate(KINDS):
        source = kind if z % 2 else 1 - kind
        moves.append((z * 2 + source, (3 - z) * 2 + 1 - kind))
    return lax.ppermute(shard, DEPTH + ("c",), moves)


def swap_pair(block):
    return lax.ppermute(block, DEPTH, [(z, 3 - z) for z in range(4)])


def swap_low(block):
    return lax.ppermute(block, "zl", [(0, 1), (1, 0)])


def exchange(rows):
    cut = rows.reshape(-1, CAP, rows.shape[1])
    cut = lax.all_to_all(cut, PLANE, split_axis=0, concat_axis=0, tiled=True)
    return cut.reshape(rows.shape)


def tie(array, *others):
    return lax.optimization_barrier((array,) + others)[0]


def word(*values):
    return jnp.stack([jnp.asarray(v, jnp.int32) for v in values])


def body(
    tokens,
    segment_ids,
    routes,
    cotangent,
    w_qkv,
    w_attn_out,
    w_router,
    norm_gains,
    frozen_in,
    frozen_out,
    new_in,
    new_out,
    dense_master,
    dense_first,
    dense_second,
    master_in,
    first_in,
    second_in,
    master_out,
    first_out,
    second_out,
):
    core, zh, zl = (lax.axis_index(a) for a in ("c", "zh", "zl"))
    z = 2 * zh + zl
    kind = zh ^ zl
    same = jnp.where(kind == core, 1, 0)
    home = word(z, same, core)
    core_word, same_word = word(core), word(same)
    routes = routes.T
    w_router = w_router.T

    in_near, out_near = to_neighbours(new_in), to_neighbours(new_out)
    attn_in, qkv_low, mixed_low, lse, middle, ffn_in, plan, sent, frozen_sent = dense_forward(
        (), word(zh), tokens, segment_ids, routes, cotangent, w_qkv, w_attn_out, w_router, norm_gains
    )
    received = exchange(sent)
    in_across = to_opposite(tie(in_near, plan))
    frozen_result, frozen_back = frozen_expert((in_near,), frozen_sent, frozen_in, frozen_out)
    out_across = to_opposite(tie(out_near, frozen_back))
    in_shards, out_shards = (new_in, in_near, in_across), (new_out, out_near, out_across)
    in_shards = in_shards + tuple(swap_core(s) for s in (new_in, tie(in_near, plan), in_across))
    out_shards = out_shards + tuple(swap_core(s) for s in (new_out, tie(out_near, frozen_back), out_across))
    half_in = build_weight((frozen_back,), "build_in", home, in_shards, False)
    half_out = build_weight((half_in,), "build_out", home, out_shards, True)
    received = tie(received, frozen_back)
    received_mate = swap_core(received)
    width = tokens.shape[1]
    rows_own, rows_mate = received[:, :width], received_mate[:, :width]
    grads_own, grads_mate = received[:, width:], received_mate[:, width:]

    hidden_own, slope_own = expert_up((), received, half_in)
    hidden_mate, slope_mate = expert_up((hidden_own,), received_mate, half_in)
    pre_of = lambda grads, slope: (mm_nt(grads, half_out) * slope.astype(F32)).astype(LOW)
    pre_mate = pre_of(grads_mate, slope_mate)
    back_arrived = swap_core(mm_nt(pre_mate, half_in).astype(LOW))
    result_arrived = swap_core(mm(hidden_mate, half_out).astype(LOW))
    pre_own = pre_of(grads_own, slope_own)
    result = (mm(hidden_own, half_out) + result_arrived.astype(F32)).astype(LOW)
    back = (mm_nt(pre_own, half_in) + back_arrived.astype(F32)).astype(LOW)
    value = jnp.sum(grads_own.astype(F32) * result.astype(F32), axis=1, keepdims=True)
    merged = jnp.concatenate([back, extra_terms(value)], axis=1)
    back = exchange(merged)
    grad_out = mm_tn(hidden_own, grads_own) + mm_tn(hidden_mate, grads_mate)
    grad_in = mm_tn(rows_own, pre_own) + mm_tn(rows_mate, pre_mate)

    def leaving(partial):
        rows = partial.shape[0] // 2
        away = lax.dynamic_slice(partial, ((1 - zh) * rows, 0), (rows, partial.shape[1]))
        return swap_pair(away.astype(LOW))

    out_arrived, in_arrived = leaving(grad_out), leaving(grad_in)
    planes = word(zh, zl)
    out_mine, out_other = reduce_first((merged,), planes, grad_out, out_arrived)
    out_other = swap_low(out_other)
    result_back = exchange(tie(result, out_mine))

    input_grad, kept, away = dense_backward(
        (out_mine,), core_word, dense_master.shape[0], plan, routes, segment_ids, cotangent, tokens, middle,
        mixed_low, ffn_in, lse, qkv_low, attn_in, w_qkv, w_attn_out, w_router, norm_gains, back, frozen_back,
    )
    arrived = swap_core(away)
    in_mine, in_other = reduce_first((kept,), planes, grad_in, in_arrived)
    in_other = swap_low(in_other)
    activations = combine((in_mine,), plan, middle, result_back, frozen_result)
    kept = tie(kept, activations, out_other, in_other)
    summed = (kept.astype(F32) + arrived.astype(F32)).astype(LOW)
    terms = lax.all_to_all(summed, ("zh", "zl", "x", "y"), split_axis=0, concat_axis=0, tiled=True)
    out_stays, out_leaves = reduce_second((summed,), same_word, out_mine, out_other)
    out_mate_grad = swap_core(out_leaves)
    in_stays, in_leaves = reduce_second((out_stays,), same_word, in_mine, in_other)
    in_mate_grad = swap_core(in_leaves)
    out_new = expert_update(
        (in_stays,), core_word, master_out, first_out, second_out, out_stays, out_mate_grad, 0
    )
    in_new = expert_update(
        (out_new[0],), core_word, master_in, first_in, second_in, in_stays, in_mate_grad, 1
    )
    dense_new = dense_update((in_new[0],), dense_master, dense_first, dense_second, terms)
    return (activations, input_grad) + dense_new + in_new + out_new


def solution(mesh):
    fine = Mesh(mesh.devices.reshape(2, 2, 4, 4, 2), ALL)
    tokens = P(ALL, None)
    flat = P(ALL)
    expert = P(("x", "y", "c"), DEPTH, None)
    return jax.shard_map(
        body,
        mesh=fine,
        in_specs=(tokens,) * 4 + (P(),) * 6 + (expert,) * 2 + (flat,) * 3 + (expert,) * 6,
        out_specs=(tokens,) * 2 + (flat,) * 4 + (expert,) * 8,
        check_vma=False,
    )
```

```python
import math

import jax
import jax.numpy as jnp
from jax import lax
from jax.experimental import pallas as pl
from jax.experimental.pallas import tpu as pltpu
from jax.sharding import Mesh
from jax.sharding import PartitionSpec as P

HEAD_DIM = 64
STEP = 5


norm_eps = 1e-05
learn_rate = 0.02
beta_first = 0.5
beta_second = 0.5
adam_eps = 1e-08
decay_rate = 0.1


PLANE = ("zl", "x", "y")
DEPTH = ("zh", "zl")
ALL = ("zh", "zl", "x", "y", "c")
CAP = 24
PAIRS = 6
EXTRA = 128
VMEM = pl.BlockSpec(memory_space=pltpu.VMEM)
SMEM = pl.BlockSpec(memory_space=pltpu.SMEM)
F32 = jnp.float32
LOW = jnp.bfloat16


def params(**more):
    return pltpu.CompilerParams(vmem_limit_bytes=56 * 1024 * 1024, **more)


def ordered(kernel, count, after, **call):
    extra = len(after)

    def inner(*refs):
        return kernel(*refs[:count], *refs[count + extra :])

    call["in_specs"] = list(call["in_specs"]) + [pl.BlockSpec(memory_space=pl.ANY)] * extra
    made = pl.pallas_call(inner, **call)
    return lambda *arrays: made(*arrays, *after)


def cost(flops, moved):
    return pl.CostEstimate(flops=int(flops), bytes_accessed=int(moved), transcendentals=0)


def mm(left, right):
    return jnp.dot(left, right, preferred_element_type=F32)


def mm_nt(left, right):
    return lax.dot_general(left, right, (((1,), (1,)), ((), ())), preferred_element_type=F32)


def mm_tn(left, right):
    return lax.dot_general(left, right, (((0,), (0,)), ((), ())), preferred_element_type=F32)


def iota(shape, axis):
    return lax.broadcasted_iota(jnp.int32, shape, axis)


def normed(values):
    centered = values - jnp.mean(values, axis=1, keepdims=True)
    scale = lax.rsqrt(jnp.mean(centered * centered, axis=1, keepdims=True) + norm_eps)
    return centered * scale, scale


def norm_backward(values, gain, upstream):
    hat, scale = normed(values)
    gain_grad = jnp.sum(upstream * hat, axis=0, keepdims=True)
    inner = upstream * gain
    mean_inner = jnp.mean(inner, axis=1, keepdims=True)
    mean_hat = jnp.mean(inner * hat, axis=1, keepdims=True)
    return scale * (inner - mean_inner - hat * mean_hat), gain_grad


def as_column(row, eye):
    return jnp.sum(jnp.where(eye, row, jnp.zeros_like(row)), axis=1, keepdims=True)


def as_row(column, eye):
    return jnp.sum(jnp.where(eye, column, jnp.zeros_like(column)), axis=0, keepdims=True)


def attention_mask(segment_row):
    count = segment_row.shape[1]
    down, across = iota((count, count), 0), iota((count, count), 1)
    eye = down == across
    column = jnp.sum(jnp.where(eye, segment_row, 0), axis=1, keepdims=True)
    return (down >= across) & (column == segment_row), eye


def dense_forward_kernel(
    zh_ref, tokens, segments, routes, cotangent, w_qkv, w_out, w_router, gains,
    attn_in_o, qkv_o, mixed_o, lse_o, middle_o, ffn_o, plan_o, sent_o, frozen_sent_o,
):
    width = tokens.shape[1]
    count = tokens.shape[0]
    inputs = tokens[...].astype(F32)
    hat, unused = normed(inputs)
    attn_in = (hat * gains[0:1, :]).astype(LOW)
    attn_in_o[...] = attn_in
    qkv_o[...] = mm(attn_in, w_qkv[...]).astype(LOW)
    allowed, eye = attention_mask(segments[...])
    lane = iota((count, 128), 1)
    low_lanes = lane < HEAD_DIM
    lse_all = jnp.zeros((count, 128), F32)
    for pair in range(width // 128):
        at = slice(128 * pair, 128 * pair + 128)
        queries = qkv_o[:, at] * jnp.asarray(HEAD_DIM**-0.5, LOW)
        keys = qkv_o[:, width + 128 * pair : width + 128 * pair + 128]
        values = qkv_o[:, 2 * width + 128 * pair : 2 * width + 128 * pair + 128]
        outs = []
        for half in range(2):
            mine = low_lanes if half == 0 else ~low_lanes
            scores = mm_nt(jnp.where(mine, queries, jnp.zeros_like(queries)), keys)
            scores = jnp.where(allowed, scores, -1e30)
            top = jnp.max(scores, axis=1, keepdims=True)
            raised = jnp.exp(scores - top)
            total = jnp.sum(raised, axis=1, keepdims=True)
            probs = (raised * (1.0 / total)).astype(LOW)
            outs.append(mm(probs, values))
            lse_all = jnp.where(lane == 2 * pair + half, top + jnp.log(total), lse_all)
        mixed_o[:, at] = jnp.where(low_lanes, outs[0], outs[1]).astype(LOW)
    lse_o[...] = lse_all
    middle = inputs + mm(mixed_o[...], w_out[...])
    middle_o[...] = middle
    hat, unused = normed(middle)
    ffn = (hat * gains[1:2, :]).astype(LOW)
    ffn_o[...] = ffn
    logits = mm_nt(ffn, w_router[...])
    experts = iota(logits.shape, 1)
    lists = [as_column(routes[k : k + 1, :], eye) for k in range(2)]
    picks = [experts == column for column in lists]
    chosen = [jnp.sum(jnp.where(p, logits, 0.0), axis=1, keepdims=True) for p in picks]
    top = jnp.maximum(chosen[0], chosen[1])
    raised = [jnp.exp(c - top) for c in chosen]
    gates = [r / (raised[0] + raised[1]) for r in raised]
    named = (picks[0] | picks[1]).astype(F32).astype(LOW)
    earlier = (iota((count, count), 0) > iota((count, count), 1)).astype(F32).astype(LOW)
    before = mm(earlier, named)
    zh = zh_ref[0]
    new_place, old_place = [], []
    for k in range(2):
        route = lists[k]
        slot = jnp.sum(jnp.where(picks[k], before, 0.0), axis=1, keepdims=True).astype(jnp.int32)
        fresh = route - 1
        block = 16 * ((fresh & 1) ^ zh) + lax.shift_right_arithmetic(fresh, 1)
        new_place.append(jnp.where(route > 0, block * CAP + slot, -1))
        old_place.append(jnp.where(route > 0, -1, slot))
    columns = gates + [p.astype(F32) for p in new_place + old_place]
    plan = jnp.zeros((count, 128), F32)
    for i, column in enumerate(columns):
        plan = jnp.where(lane == i, column, plan)
    plan_o[...] = plan
    up = cotangent[...].astype(F32)
    scaled = [(g * up).astype(LOW) for g in gates]
    for places, ref in ((new_place, sent_o), (old_place, frozen_sent_o)):
        slots = iota((ref.shape[0], count), 0)
        spread = [(slots == as_row(p, eye)).astype(F32).astype(LOW) for p in places]
        ref[:, :width] = mm(spread[0] + spread[1], ffn).astype(LOW)
        ref[:, width:] = (mm(spread[0], scaled[0]) + mm(spread[1], scaled[1])).astype(LOW)


def dense_forward(after, zh, tokens, segments, routes, cotangent, w_qkv, w_out, w_router, gains):
    count, width = tokens.shape
    slots = (w_router.shape[0] - 1) * CAP
    shapes = [
        ((count, width), LOW), ((count, 3 * width), LOW), ((count, width), LOW), ((count, 128), F32),
        ((count, width), F32), ((count, width), LOW), ((count, 128), F32),
        ((slots, 2 * width), LOW), ((CAP, 2 * width), LOW),
    ]
    return ordered(
        dense_forward_kernel, 9, after,
        name="dense_forward",
        out_shape=[jax.ShapeDtypeStruct(s, t) for s, t in shapes],
        in_specs=[SMEM] + [VMEM] * 8,
        out_specs=[VMEM] * len(shapes),
        compiler_params=params(),
        cost_estimate=cost(8e9, 30e6),
    )(zh, tokens, segments, routes, cotangent, w_qkv, w_out, w_router, gains)


def dense_backward_kernel(
    core_ref, plan, routes, segments, cotangent, tokens, middle, mixed, ffn, lse, qkv, attn_in,
    w_qkv, w_out, w_router, gains, back, frozen_back,
    input_grad_o, kept_o, away_o,
    flat, gqkv,
):
    count, width = tokens.shape
    expert_total = w_router.shape[0]
    up = cotangent[...].astype(F32)
    gates = [plan[:, k : k + 1] for k in range(2)]
    new_place = [plan[:, 2 + k : 3 + k].astype(jnp.int32) for k in range(2)]
    old_place = [plan[:, 4 + k : 5 + k].astype(jnp.int32) for k in range(2)]
    allowed, eye = attention_mask(segments[...])

    grad_ffn = jnp.zeros((count, width), F32)
    weighted = [jnp.zeros((count, 1), F32) for k in range(2)]
    for places, ref in ((new_place, back), (old_place, frozen_back)):
        size = ref.shape[0]
        slots = iota((count, size), 1)
        for k in range(2):
            choice = (slots == places[k]).astype(F32).astype(LOW)
            picked = mm(choice, ref[...])
            grad_ffn = grad_ffn + picked[:, :width]
            tail = picked[:, width:]
            weighted[k] = weighted[k] + jnp.sum(tail, axis=1, keepdims=True)
    both = weighted[0] + weighted[1]
    experts = iota((count, expert_total), 1)
    grad_logits = jnp.zeros((count, expert_total), F32)
    for k in range(2):
        grad_logits = jnp.where(
            experts == as_column(routes[k : k + 1, :], eye), weighted[k] - gates[k] * both, grad_logits
        )
    grad_logits = grad_logits.astype(LOW)
    grad_ffn = grad_ffn + mm(grad_logits, w_router[...])
    grad_norm, gain_ffn = norm_backward(middle[...], gains[1:2, :], grad_ffn)
    grad_middle = up + grad_norm
    grad_branch = grad_middle.astype(LOW)

    blocks = width // 128
    first_row = 3 * blocks * width
    attn_out_grad = mm_tn(mixed[...], grad_branch)
    for j in range(blocks):
        flat[pl.ds(first_row + j, width, stride=blocks), :] = attn_out_grad[:, 128 * j : 128 * j + 128]
    router_row = first_row + blocks * width
    router_rows = width * expert_total // 128
    padded_logits = jnp.concatenate(
        [grad_logits, jnp.zeros((count, 128 - expert_total), LOW)], axis=1
    )
    router_grad = mm_tn(ffn[...], padded_logits)
    feature = iota((width, 128), 0)
    lane_w = iota((width, 128), 1)
    start = feature * expert_total
    offset = start & 127
    turned = jnp.take_along_axis(router_grad, (lane_w - offset) & 127, axis=1)
    wrapped = lane_w < offset
    row_of = lax.shift_right_logical(iota((router_rows, width), 1) * expert_total, 7)
    row_here = iota((router_rows, width), 0)
    here = (row_of == row_here).astype(F32)
    after = (row_of + 1 == row_here).astype(F32)
    exact = lambda a, b: jnp.dot(a, b, precision=lax.Precision.HIGHEST, preferred_element_type=F32)
    flat[router_row : router_row + router_rows, :] = exact(
        here, jnp.where(wrapped, 0.0, turned)
    ) + exact(after, jnp.where(wrapped, turned, 0.0))
    gain_row = router_row + router_rows

    grad_mixed = mm_nt(grad_branch, w_out[...]).astype(LOW)
    lane = iota((count, 128), 1)
    low_lanes = lane < HEAD_DIM
    scale = HEAD_DIM**-0.5
    for pair in range(blocks):
        at = slice(128 * pair, 128 * pair + 128)
        queries = qkv[:, at] * jnp.asarray(scale, LOW)
        keys = qkv[:, width + 128 * pair : width + 128 * pair + 128]
        values = qkv[:, 2 * width + 128 * pair : 2 * width + 128 * pair + 128]
        grads = grad_mixed[:, at]
        grad_q = jnp.zeros((count, 128), F32)
        grad_k = jnp.zeros((count, 128), F32)
        grad_v = jnp.zeros((count, 128), F32)
        for half in range(2):
            mine = low_lanes if half == 0 else ~low_lanes
            only = lambda v: jnp.where(mine, v, jnp.zeros_like(v))
            q_half, g_half, k_half = only(queries), only(grads), only(keys)
            scores = jnp.where(allowed, mm_nt(q_half, keys), -1e30)
            head = 2 * pair + half
            probs = jnp.exp(scores - lse[:, head : head + 1])
            grad_probs = mm_nt(g_half, values)
            grad_v = grad_v + mm_tn(probs.astype(LOW), g_half)
            dots = jnp.sum(probs * grad_probs, axis=1, keepdims=True)
            grad_scores = (probs * (grad_probs - dots)).astype(LOW)
            grad_q = grad_q + mm(grad_scores, k_half)
            grad_k = grad_k + mm_tn(grad_scores, q_half)
        gqkv[:, at] = (grad_q * scale).astype(LOW)
        gqkv[:, width + 128 * pair : width + 128 * pair + 128] = grad_k.astype(LOW)
        gqkv[:, 2 * width + 128 * pair : 2 * width + 128 * pair + 128] = grad_v.astype(LOW)
    for j in range(0, 3 * blocks, 2):
        piece = mm_tn(attn_in[...], gqkv[:, 128 * j : 128 * j + 256])
        flat[pl.ds(j, width, stride=3 * blocks), :] = piece[:, :128]
        flat[pl.ds(j + 1, width, stride=3 * blocks), :] = piece[:, 128:]
    grad_attn = mm_nt(gqkv[...], w_qkv[...])
    grad_norm, gain_attn = norm_backward(tokens[...].astype(F32), gains[0:1, :], grad_attn)
    input_grad_o[...] = grad_middle + grad_norm
    for j in range(blocks):
        flat[gain_row + j : gain_row + j + 1, :] = gain_attn[:, 128 * j : 128 * j + 128]
        flat[gain_row + blocks + j : gain_row + blocks + j + 1, :] = gain_ffn[:, 128 * j : 128 * j + 128]
    last = gain_row + 2 * blocks
    flat[last:, :] = jnp.zeros((flat.shape[0] - last, 128), F32)

    core = core_ref[0]
    rows = flat.shape[0] // 128
    padded = kept_o.shape[1]

    @pl.loop(0, kept_o.shape[0])
    def move(i):
        kept_o[pl.ds(i, 1)] = flat[pl.ds((2 * i + core) * rows, padded), :].astype(LOW)[None]
        away_o[pl.ds(i, 1)] = flat[pl.ds((2 * i + 1 - core) * rows, padded), :].astype(LOW)[None]


def dense_backward(after, core, dense_rows, *arrays):
    count, width = arrays[4].shape
    rows = dense_rows // 128
    padded = (rows + 31) // 32 * 32
    return ordered(
        dense_backward_kernel, 1 + len(arrays), after,
        name="dense_backward",
        out_shape=[
            jax.ShapeDtypeStruct((count, width), F32),
            jax.ShapeDtypeStruct((64, padded, 128), LOW),
            jax.ShapeDtypeStruct((64, padded, 128), LOW),
        ],
        in_specs=[SMEM] + [VMEM] * len(arrays),
        out_specs=[VMEM] * 3,
        scratch_shapes=[
            pltpu.VMEM((rows * 128 + padded - rows, 128), F32),
            pltpu.VMEM((count, 3 * width), LOW),
        ],
        compiler_params=params(),
        cost_estimate=cost(12e9, 40e6),
    )(core, *arrays)


def combine_kernel(plan, middle, results, frozen_result, out):
    count, width = middle.shape
    total = middle[...]
    for first, ref in ((2, results), (4, frozen_result)):
        slots = iota((count, ref.shape[0]), 1)
        for k in range(2):
            place = plan[:, first + k : first + k + 1].astype(jnp.int32)
            total = total + plan[:, k : k + 1] * mm((slots == place).astype(F32).astype(LOW), ref[...])
    out[...] = total.astype(LOW)


def combine(after, plan, middle, results, frozen_result):
    return ordered(
        combine_kernel, 4, after,
        name="combine",
        out_shape=jax.ShapeDtypeStruct(middle.shape, LOW),
        in_specs=[VMEM] * 4,
        out_specs=VMEM,
        compiler_params=params(),
        cost_estimate=cost(200e9, 4e6),
    )(plan, middle, results, frozen_result)


def gelu_pair(pre):
    area = 0.5 + 0.5 * lax.erf(pre * (0.5**0.5))
    density = jnp.exp(-0.5 * pre * pre) * (1.0 / (2.0 * math.pi) ** 0.5)
    return pre * area, area + pre * density


HBM = pl.BlockSpec(memory_space=pl.ANY)


def build_weight(after, name, home, sources, by_rows):
    rows, cols = sources[0].shape[1:]

    def kernel(home_ref, local, near, across, local_mate, near_mate, across_mate, out, sems):
        z, half = home_ref[0], home_ref[2]

        def move(blocks):
            copies = []
            for step, shard in enumerate(blocks):
                if by_rows:
                    start = pl.multiple_of(half * (rows // 2), 64)
                    place = pl.ds(pl.multiple_of(((z + step) & 3) * (rows // 2), 64), rows // 2)
                    copies.append((shard.at[0, pl.ds(start, rows // 2), :], out.at[place, :]))
                else:
                    place = pl.ds(pl.multiple_of(((z + step) & 3) * rows, 64), rows)
                    for block in range(4):
                        start = pl.multiple_of((2 * block + half) * (cols // 8), 128)
                        to = slice(block * (cols // 8), (block + 1) * (cols // 8))
                        copies.append((shard.at[0, :, pl.ds(start, cols // 8)], out.at[place, to]))
            made = [pltpu.make_async_copy(a, b, sems.at[i]) for i, (a, b) in enumerate(copies)]
            for copy in made:
                copy.start()
            for copy in made:
                copy.wait()

        pl.when(home_ref[1] == 1)(lambda: move((local, near_mate, across_mate, near)))
        pl.when(home_ref[1] == 0)(lambda: move((local_mate, near, across, near_mate)))

    shape = (2 * rows, cols) if by_rows else (4 * rows, cols // 2)
    return ordered(
        kernel, 7, after,
        name=name,
        out_shape=jax.ShapeDtypeStruct(shape, LOW),
        in_specs=[SMEM] + [HBM] * 6,
        out_specs=VMEM,
        scratch_shapes=[pltpu.SemaphoreType.DMA((16,))],
        compiler_params=params(),
        cost_estimate=cost(1e5, 8e6),
    )(home, *sources)


def expert_up_kernel(rows, weight, hidden_o, slope_o):
    pre = mm(rows[...], weight[...])
    hidden, slope = gelu_pair(pre)
    hidden_o[...] = hidden.astype(LOW)
    slope_o[...] = slope.astype(LOW)


def expert_up(after, rows, weight):
    count, width = rows.shape[0], weight.shape[0]
    hidden = weight.shape[1]
    step = 256
    wide = jax.ShapeDtypeStruct((count, hidden), LOW)
    return ordered(
        expert_up_kernel, 2, after,
        name="expert_up",
        out_shape=[wide, wide],
        grid=(count // step,),
        in_specs=[pl.BlockSpec((step, width), lambda i: (i, 0)), pl.BlockSpec((width, hidden), lambda i: (0, 0))],
        out_specs=[pl.BlockSpec((step, hidden), lambda i: (i, 0))] * 2,
        compiler_params=params(),
        cost_estimate=cost(6e9, 8e6),
    )(rows, weight)


def split_three(value):
    high = lax.reduce_precision(value, 8, 7)
    mid = lax.reduce_precision(value - high, 8, 7)
    return high, mid, value - high - mid


def extra_terms(value):
    lane = iota((value.shape[0], EXTRA), 1)
    extra = jnp.zeros((value.shape[0], EXTRA), F32)
    for i, term in enumerate(split_three(value)):
        extra = jnp.where(lane == i, term, extra)
    return extra.astype(LOW)


def reduce_first(after, low, kept, arrived):
    rows, columns = kept.shape[0] // 2, kept.shape[1]

    def kernel(low_ref, kept, arrived, mine, other):
        for out, which in ((mine, low_ref[0]), (other, 1 - low_ref[0])):
            at = pl.ds(pl.multiple_of(which * rows, 64), rows)
            out[...] = (kept[at, :] + arrived[at, :].astype(F32)).astype(out.dtype)

    return ordered(
        kernel, 3, after,
        name="reduce_first",
        out_shape=[jax.ShapeDtypeStruct((rows, columns), t) for t in (F32, LOW)],
        in_specs=[SMEM, VMEM, VMEM],
        out_specs=[VMEM] * 2,
        compiler_params=params(),
        cost_estimate=cost(1e6, 6e6),
    )(low, kept, arrived)


def reduce_second(after, same, mine, other):
    def kernel(same_ref, mine, other, stays, leaves):
        straight = same_ref[0] == 1
        near, far = mine[...], other[...].astype(F32)
        stays[...] = jnp.where(straight, near, far)
        leaves[...] = jnp.where(straight, far, near).astype(LOW)

    return ordered(
        kernel, 3, after,
        name="reduce_second",
        out_shape=[jax.ShapeDtypeStruct(mine.shape, t) for t in (F32, LOW)],
        in_specs=[SMEM, VMEM, VMEM],
        out_specs=[VMEM] * 2,
        compiler_params=params(),
        cost_estimate=cost(1e6, 6e6),
    )(same, mine, other)


def frozen_kernel(rows, grads, w_in, w_out, result_o, back_o, result_sum, back_sum, value_sum):
    step = pl.program_id(0)

    @pl.when(step == 0)
    def clear():
        result_sum[...] = jnp.zeros_like(result_sum)
        back_sum[...] = jnp.zeros_like(back_sum)
        value_sum[...] = jnp.zeros_like(value_sum)

    hidden, slope = gelu_pair(mm(rows[...], w_in[...]))
    hidden = hidden.astype(LOW)
    result_sum[...] += mm(hidden, w_out[...])
    grad_hidden = mm_nt(grads[...], w_out[...])
    value_sum[...] += jnp.sum(hidden.astype(F32) * grad_hidden, axis=1, keepdims=True)
    back_sum[...] += mm_nt((grad_hidden * slope).astype(LOW), w_in[...])

    @pl.when(step == pl.num_programs(0) - 1)
    def finish():
        result_o[...] = result_sum[...].astype(LOW)
        width = back_sum.shape[1]
        back_o[:, :width] = back_sum[...].astype(LOW)
        back_o[:, width:] = extra_terms(value_sum[:, 0:1])


def frozen_expert(after, sent, w_in, w_out):
    count, width = sent.shape[0], w_in.shape[0]
    wide = w_in.shape[1]
    step = 512
    small = pl.BlockSpec((count, width), lambda i: (0, 0))
    return ordered(
        frozen_kernel, 4, after,
        name="frozen_expert",
        out_shape=[
            jax.ShapeDtypeStruct((count, width), LOW),
            jax.ShapeDtypeStruct((count, width + EXTRA), LOW),
        ],
        grid=(wide // step,),
        in_specs=[
            small, pl.BlockSpec((count, width), lambda i: (0, 1)),
            pl.BlockSpec((width, step), lambda i: (0, i)),
            pl.BlockSpec((step, width), lambda i: (i, 0)),
        ],
        out_specs=[small, pl.BlockSpec((count, width + EXTRA), lambda i: (0, 0))],
        scratch_shapes=[
            pltpu.VMEM((count, width), F32),
            pltpu.VMEM((count, width), F32),
            pltpu.VMEM((count, EXTRA), F32),
        ],
        compiler_params=params(),
        cost_estimate=cost(4e9, 10e6),
    )(sent, sent, w_in, w_out)


def adamw_values(master, first, second, grad):
    first_new = beta_first * first + (1.0 - beta_first) * grad
    second_new = beta_second * second + (1.0 - beta_second) * grad * grad
    first_hat = first_new * (1.0 / (1.0 - beta_first**STEP))
    second_hat = second_new * (1.0 / (1.0 - beta_second**STEP))
    master_new = master - learn_rate * (
        first_hat / (jnp.sqrt(second_hat) + adam_eps) + decay_rate * master
    )
    return master_new, first_new, second_new, master_new.astype(LOW)


def dense_update_kernel(master, first, second, terms, *outs):
    rows = master.shape[0]
    grad = jnp.sum(terms[...].astype(F32), axis=0)[:rows]
    for out, value in zip(outs, adamw_values(master[...], first[...], second[...], grad)):
        out[...] = value


def dense_update(after, master, first, second, terms):
    shape = (master.shape[0] // 128, 128)
    results = ordered(
        dense_update_kernel, 4, after,
        name="dense_update",
        out_shape=[jax.ShapeDtypeStruct(shape, t) for t in (F32, F32, F32, LOW)],
        in_specs=[VMEM] * 4,
        out_specs=[VMEM] * 4,
        compiler_params=params(),
        cost_estimate=cost(1e6, 4e6),
    )(*(a.reshape(shape) for a in (master, first, second)), terms)
    return tuple(r.reshape(master.shape) for r in results)


def expert_update(after, core, master, first, second, stays, arrived, axis):
    rows, columns = master.shape[1:]
    if axis == 1:
        blocks, width = 4, columns // 4
        half = (rows, width // 2)
    else:
        blocks, width = 3, columns // 3
        half = (rows // 2, width)

    def kernel(core_ref, master, first, second, stays, arrived, *outs):
        near, far = stays[...], arrived[...].astype(F32)
        swapped = core_ref[0] == 1
        grad = jnp.concatenate(
            [jnp.where(swapped, far, near), jnp.where(swapped, near, far)], axis=axis
        )
        values = adamw_values(master[0], first[0], second[0], grad)
        for out, value in zip(outs, values):
            out[0] = value

    wide = pl.BlockSpec((1, rows, width), lambda i: (0, 0, i))
    slim = pl.BlockSpec(half, lambda i: (0, i))
    return tuple(
        ordered(
        kernel, 6, after,
            name="update_in" if axis == 1 else "update_out",
            out_shape=[jax.ShapeDtypeStruct(master.shape, t) for t in (F32, F32, F32, LOW)],
            grid=(blocks,),
            in_specs=[SMEM, wide, wide, wide, slim, slim],
            out_specs=[wide] * 4,
            compiler_params=params(),
            cost_estimate=cost(2e7, 18e6),
        )(core, master, first, second, stays, arrived)
    )


def swap_core(block):
    return lax.ppermute(block, "c", [(0, 1), (1, 0)])


KINDS = (0, 1, 1, 0)


def to_neighbours(shard):
    moves = []
    for z, kind in enumerate(KINDS):
        moves.append(((z - 1) % 4 * 2 + kind, z * 2 + kind))
        moves.append(((z + 1) % 4 * 2 + kind, z * 2 + 1 - kind))
    return lax.ppermute(shard, DEPTH + ("c",), moves)


def to_opposite(shard):
    moves = []
    for z, kind in enumerate(KINDS):
        source = kind if z % 2 else 1 - kind
        moves.append((z * 2 + source, (3 - z) * 2 + 1 - kind))
    return lax.ppermute(shard, DEPTH + ("c",), moves)


def swap_pair(block):
    return lax.ppermute(block, DEPTH, [(z, 3 - z) for z in range(4)])


def swap_low(block):
    return lax.ppermute(block, "zl", [(0, 1), (1, 0)])


def exchange(rows):
    cut = rows.reshape(-1, CAP, rows.shape[1])
    cut = lax.all_to_all(cut, PLANE, split_axis=0, concat_axis=0, tiled=True)
    return cut.reshape(rows.shape)


def tie(array, *others):
    return lax.optimization_barrier((array,) + others)[0]


def word(*values):
    return jnp.stack([jnp.asarray(v, jnp.int32) for v in values])


def body(
    tokens,
    segment_ids,
    routes,
    cotangent,
    w_qkv,
    w_attn_out,
    w_router,
    norm_gains,
    frozen_in,
    frozen_out,
    new_in,
    new_out,
    dense_master,
    dense_first,
    dense_second,
    master_in,
    first_in,
    second_in,
    master_out,
    first_out,
    second_out,
):
    core, zh, zl = (lax.axis_index(a) for a in ("c", "zh", "zl"))
    z = 2 * zh + zl
    kind = zh ^ zl
    same = jnp.where(kind == core, 1, 0)
    home = word(z, same, core)
    core_word, same_word, zl_word = word(core), word(same), word(zl)
    routes = routes.T
    w_router = w_router.T

    in_near, out_near = to_neighbours(new_in), to_neighbours(new_out)
    attn_in, qkv_low, mixed_low, lse, middle, ffn_in, plan, sent, frozen_sent = dense_forward(
        (), word(zh), tokens, segment_ids, routes, cotangent, w_qkv, w_attn_out, w_router, norm_gains
    )
    received = exchange(sent)
    frozen_result, frozen_back = frozen_expert((), frozen_sent, frozen_in, frozen_out)
    in_across = to_opposite(tie(in_near, plan))
    out_across = to_opposite(tie(out_near, frozen_back))
    in_shards = (new_in, in_near, in_across)
    in_shards = in_shards + tuple(swap_core(s) for s in (new_in, tie(in_near, plan), in_across))
    half_in = build_weight((frozen_back,), "build_in", home, in_shards, False)
    received = tie(received, half_in)
    received_mate = swap_core(received)
    width = tokens.shape[1]
    rows_own, rows_mate = received[:, :width], received_mate[:, :width]
    grads_own, grads_mate = received[:, width:], received_mate[:, width:]
    hidden_own, slope_own = expert_up((), received, half_in)
    hidden_mate, slope_mate = expert_up((hidden_own,), received_mate, half_in)

    def half_grad(lefts, rights, half):
        cut = lefts[0].shape[1] // 2
        parts = [lax.dynamic_slice(left, (0, half * cut), (left.shape[0], cut)) for left in lefts]
        return mm_tn(parts[0], rights[0]) + mm_tn(parts[1], rights[1])

    hiddens, grads, rows = (hidden_own, hidden_mate), (grads_own, grads_mate), (rows_own, rows_mate)
    out_away = half_grad(hiddens, grads, 1 - zh).astype(LOW)
    out_arrived = swap_pair(out_away)
    out_shards = (new_out, out_near, out_across)
    out_shards = out_shards + tuple(
        swap_core(s) for s in (new_out, tie(out_near, frozen_back), tie(out_across, hidden_own))
    )
    half_out = build_weight((out_away,), "build_out", home, out_shards, True)

    pre_of = lambda grads, slope: (mm_nt(grads, half_out) * slope.astype(F32)).astype(LOW)
    pre_mate = pre_of(grads_mate, slope_mate)
    back_arrived = swap_core(mm_nt(pre_mate, half_in).astype(LOW))
    result_arrived = swap_core(mm(hidden_mate, half_out).astype(LOW))
    pre_own = pre_of(grads_own, slope_own)
    pres = (pre_own, pre_mate)
    in_away = half_grad(rows, pres, 1 - zh).astype(LOW)
    in_arrived = swap_pair(in_away)
    result = (mm(hidden_own, half_out) + result_arrived.astype(F32)).astype(LOW)
    back = (mm_nt(pre_own, half_in) + back_arrived.astype(F32)).astype(LOW)
    value = jnp.sum(grads_own.astype(F32) * result.astype(F32), axis=1, keepdims=True)
    merged = jnp.concatenate([back, extra_terms(value)], axis=1)
    back = exchange(tie(merged, in_away))

    out_kept = half_grad(tuple(tie(h, merged) for h in hiddens), grads, zh)
    in_kept = half_grad(tuple(tie(r, merged) for r in rows), pres, zh)
    out_mine, out_other = reduce_first((merged,), zl_word, out_kept, out_arrived)
    in_mine, in_other = reduce_first((out_mine,), zl_word, in_kept, in_arrived)
    out_other, in_other = swap_low(out_other), swap_low(in_other)
    result_back = exchange(tie(result, in_mine))

    input_grad, kept, away = dense_backward(
        (in_mine,), core_word, dense_master.shape[0], plan, routes, segment_ids, cotangent, tokens, middle,
        mixed_low, ffn_in, lse, qkv_low, attn_in, w_qkv, w_attn_out, w_router, norm_gains, back, frozen_back,
    )
    arrived = swap_core(away)
    activations = combine((kept,), plan, middle, result_back, frozen_result)
    kept = tie(kept, activations, out_other, in_other)
    summed = (kept.astype(F32) + arrived.astype(F32)).astype(LOW)
    terms = lax.all_to_all(summed, ("zh", "zl", "x", "y"), split_axis=0, concat_axis=0, tiled=True)
    out_stays, out_leaves = reduce_second((summed,), same_word, out_mine, out_other)
    out_mate_grad = swap_core(out_leaves)
    in_stays, in_leaves = reduce_second((out_stays,), same_word, in_mine, in_other)
    in_mate_grad = swap_core(in_leaves)
    out_new = expert_update(
        (in_stays,), core_word, master_out, first_out, second_out, out_stays, out_mate_grad, 0
    )
    in_new = expert_update(
        (out_new[0],), core_word, master_in, first_in, second_in, in_stays, in_mate_grad, 1
    )
    dense_new = dense_update((in_new[0],), dense_master, dense_first, dense_second, terms)
    return (activations, input_grad) + dense_new + in_new + out_new


def solution(mesh):
    fine = Mesh(mesh.devices.reshape(2, 2, 4, 4, 2), ALL)
    tokens = P(ALL, None)
    flat = P(ALL)
    expert = P(("x", "y", "c"), DEPTH, None)
    return jax.shard_map(
        body,
        mesh=fine,
        in_specs=(tokens,) * 4 + (P(),) * 6 + (expert,) * 2 + (flat,) * 3 + (expert,) * 6,
        out_specs=(tokens,) * 2 + (flat,) * 4 + (expert,) * 8,
        check_vma=False,
    )
```

```python
import math

import jax
import jax.numpy as jnp
from jax import lax
from jax.experimental import pallas as pl
from jax.experimental.pallas import tpu as pltpu
from jax.sharding import Mesh
from jax.sharding import PartitionSpec as P

HEAD_DIM = 64
STEP = 5


norm_eps = 1e-05
learn_rate = 0.02
beta_first = 0.5
beta_second = 0.5
adam_eps = 1e-08
decay_rate = 0.1


PLANE = ("zl", "x", "y")
DEPTH = ("zh", "zl")
ALL = ("zh", "zl", "x", "y", "c")
CAP = 24
PAIRS = 6
EXTRA = 128
VMEM = pl.BlockSpec(memory_space=pltpu.VMEM)
SMEM = pl.BlockSpec(memory_space=pltpu.SMEM)
F32 = jnp.float32
LOW = jnp.bfloat16


def params(**more):
    return pltpu.CompilerParams(vmem_limit_bytes=56 * 1024 * 1024, **more)


def ordered(kernel, count, after, **call):
    extra = len(after)

    def inner(*refs):
        return kernel(*refs[:count], *refs[count + extra :])

    call["in_specs"] = list(call["in_specs"]) + [pl.BlockSpec(memory_space=pl.ANY)] * extra
    made = pl.pallas_call(inner, **call)
    return lambda *arrays: made(*arrays, *after)


def cost(flops, moved):
    return pl.CostEstimate(flops=int(flops), bytes_accessed=int(moved), transcendentals=0)


def mm(left, right):
    return jnp.dot(left, right, preferred_element_type=F32)


def mm_nt(left, right):
    return lax.dot_general(left, right, (((1,), (1,)), ((), ())), preferred_element_type=F32)


def mm_tn(left, right):
    return lax.dot_general(left, right, (((0,), (0,)), ((), ())), preferred_element_type=F32)


def iota(shape, axis):
    return lax.broadcasted_iota(jnp.int32, shape, axis)


def normed(values):
    centered = values - jnp.mean(values, axis=1, keepdims=True)
    scale = lax.rsqrt(jnp.mean(centered * centered, axis=1, keepdims=True) + norm_eps)
    return centered * scale, scale


def norm_backward(values, gain, upstream):
    hat, scale = normed(values)
    gain_grad = jnp.sum(upstream * hat, axis=0, keepdims=True)
    inner = upstream * gain
    mean_inner = jnp.mean(inner, axis=1, keepdims=True)
    mean_hat = jnp.mean(inner * hat, axis=1, keepdims=True)
    return scale * (inner - mean_inner - hat * mean_hat), gain_grad


def as_column(row, eye):
    return jnp.sum(jnp.where(eye, row, jnp.zeros_like(row)), axis=1, keepdims=True)


def as_row(column, eye):
    return jnp.sum(jnp.where(eye, column, jnp.zeros_like(column)), axis=0, keepdims=True)


def attention_mask(segment_row):
    count = segment_row.shape[1]
    down, across = iota((count, count), 0), iota((count, count), 1)
    eye = down == across
    column = jnp.sum(jnp.where(eye, segment_row, 0), axis=1, keepdims=True)
    return (down >= across) & (column == segment_row), eye


def dense_forward_kernel(
    zh_ref, tokens, segments, routes, cotangent, w_qkv, w_out, w_router, gains,
    attn_in_o, qkv_o, mixed_o, lse_o, middle_o, ffn_o, plan_o, sent_o, frozen_sent_o,
):
    width = tokens.shape[1]
    count = tokens.shape[0]
    inputs = tokens[...].astype(F32)
    hat, unused = normed(inputs)
    attn_in = (hat * gains[0:1, :]).astype(LOW)
    attn_in_o[...] = attn_in
    qkv_o[...] = mm(attn_in, w_qkv[...]).astype(LOW)
    allowed, eye = attention_mask(segments[...])
    lane = iota((count, 128), 1)
    low_lanes = lane < HEAD_DIM
    lse_all = jnp.zeros((count, 128), F32)
    for pair in range(width // 128):
        at = slice(128 * pair, 128 * pair + 128)
        queries = qkv_o[:, at] * jnp.asarray(HEAD_DIM**-0.5, LOW)
        keys = qkv_o[:, width + 128 * pair : width + 128 * pair + 128]
        values = qkv_o[:, 2 * width + 128 * pair : 2 * width + 128 * pair + 128]
        outs = []
        for half in range(2):
            mine = low_lanes if half == 0 else ~low_lanes
            scores = mm_nt(jnp.where(mine, queries, jnp.zeros_like(queries)), keys)
            scores = jnp.where(allowed, scores, -1e30)
            top = jnp.max(scores, axis=1, keepdims=True)
            raised = jnp.exp(scores - top)
            total = jnp.sum(raised, axis=1, keepdims=True)
            probs = (raised * (1.0 / total)).astype(LOW)
            outs.append(mm(probs, values))
            lse_all = jnp.where(lane == 2 * pair + half, top + jnp.log(total), lse_all)
        mixed_o[:, at] = jnp.where(low_lanes, outs[0], outs[1]).astype(LOW)
    lse_o[...] = lse_all
    middle = inputs + mm(mixed_o[...], w_out[...])
    middle_o[...] = middle
    hat, unused = normed(middle)
    ffn = (hat * gains[1:2, :]).astype(LOW)
    ffn_o[...] = ffn
    logits = mm_nt(ffn, w_router[...])
    experts = iota(logits.shape, 1)
    lists = [as_column(routes[k : k + 1, :], eye) for k in range(2)]
    picks = [experts == column for column in lists]
    chosen = [jnp.sum(jnp.where(p, logits, 0.0), axis=1, keepdims=True) for p in picks]
    top = jnp.maximum(chosen[0], chosen[1])
    raised = [jnp.exp(c - top) for c in chosen]
    gates = [r / (raised[0] + raised[1]) for r in raised]
    named = (picks[0] | picks[1]).astype(F32).astype(LOW)
    earlier = (iota((count, count), 0) > iota((count, count), 1)).astype(F32).astype(LOW)
    before = mm(earlier, named)
    zh = zh_ref[0]
    new_place, old_place = [], []
    for k in range(2):
        route = lists[k]
        slot = jnp.sum(jnp.where(picks[k], before, 0.0), axis=1, keepdims=True).astype(jnp.int32)
        fresh = route - 1
        block = 16 * ((fresh & 1) ^ zh) + lax.shift_right_arithmetic(fresh, 1)
        new_place.append(jnp.where(route > 0, block * CAP + slot, -1))
        old_place.append(jnp.where(route > 0, -1, slot))
    columns = gates + [p.astype(F32) for p in new_place + old_place]
    plan = jnp.zeros((count, 128), F32)
    for i, column in enumerate(columns):
        plan = jnp.where(lane == i, column, plan)
    plan_o[...] = plan
    up = cotangent[...].astype(F32)
    scaled = [(g * up).astype(LOW) for g in gates]
    for places, ref in ((new_place, sent_o), (old_place, frozen_sent_o)):
        slots = iota((ref.shape[0], count), 0)
        spread = [(slots == as_row(p, eye)).astype(F32).astype(LOW) for p in places]
        ref[:, :width] = mm(spread[0] + spread[1], ffn).astype(LOW)
        ref[:, width:] = (mm(spread[0], scaled[0]) + mm(spread[1], scaled[1])).astype(LOW)


def dense_forward(after, zh, tokens, segments, routes, cotangent, w_qkv, w_out, w_router, gains):
    count, width = tokens.shape
    slots = (w_router.shape[0] - 1) * CAP
    shapes = [
        ((count, width), LOW), ((count, 3 * width), LOW), ((count, width), LOW), ((count, 128), F32),
        ((count, width), F32), ((count, width), LOW), ((count, 128), F32),
        ((slots, 2 * width), LOW), ((CAP, 2 * width), LOW),
    ]
    return ordered(
        dense_forward_kernel, 9, after,
        name="dense_forward",
        out_shape=[jax.ShapeDtypeStruct(s, t) for s, t in shapes],
        in_specs=[SMEM] + [VMEM] * 8,
        out_specs=[VMEM] * len(shapes),
        compiler_params=params(),
        cost_estimate=cost(8e9, 30e6),
    )(zh, tokens, segments, routes, cotangent, w_qkv, w_out, w_router, gains)


def dense_backward_kernel(
    core_ref, plan, routes, segments, cotangent, tokens, middle, mixed, ffn, lse, qkv, attn_in,
    w_qkv, w_out, w_router, gains, back, frozen_back,
    input_grad_o, kept_o, away_o,
    flat, gqkv,
):
    count, width = tokens.shape
    expert_total = w_router.shape[0]
    up = cotangent[...].astype(F32)
    gates = [plan[:, k : k + 1] for k in range(2)]
    new_place = [plan[:, 2 + k : 3 + k].astype(jnp.int32) for k in range(2)]
    old_place = [plan[:, 4 + k : 5 + k].astype(jnp.int32) for k in range(2)]
    allowed, eye = attention_mask(segments[...])

    grad_ffn = jnp.zeros((count, width), F32)
    weighted = [jnp.zeros((count, 1), F32) for k in range(2)]
    for places, ref in ((new_place, back), (old_place, frozen_back)):
        size = ref.shape[0]
        slots = iota((count, size), 1)
        for k in range(2):
            choice = (slots == places[k]).astype(F32).astype(LOW)
            picked = mm(choice, ref[...])
            grad_ffn = grad_ffn + picked[:, :width]
            tail = picked[:, width:]
            weighted[k] = weighted[k] + jnp.sum(tail, axis=1, keepdims=True)
    both = weighted[0] + weighted[1]
    experts = iota((count, expert_total), 1)
    grad_logits = jnp.zeros((count, expert_total), F32)
    for k in range(2):
        grad_logits = jnp.where(
            experts == as_column(routes[k : k + 1, :], eye), weighted[k] - gates[k] * both, grad_logits
        )
    grad_logits = grad_logits.astype(LOW)
    grad_ffn = grad_ffn + mm(grad_logits, w_router[...])
    grad_norm, gain_ffn = norm_backward(middle[...], gains[1:2, :], grad_ffn)
    grad_middle = up + grad_norm
    grad_branch = grad_middle.astype(LOW)

    blocks = width // 128
    first_row = 3 * blocks * width
    attn_out_grad = mm_tn(mixed[...], grad_branch)
    for j in range(blocks):
        flat[pl.ds(first_row + j, width, stride=blocks), :] = attn_out_grad[:, 128 * j : 128 * j + 128]
    router_row = first_row + blocks * width
    router_rows = width * expert_total // 128
    padded_logits = jnp.concatenate(
        [grad_logits, jnp.zeros((count, 128 - expert_total), LOW)], axis=1
    )
    router_grad = mm_tn(ffn[...], padded_logits)
    feature = iota((width, 128), 0)
    lane_w = iota((width, 128), 1)
    start = feature * expert_total
    offset = start & 127
    turned = jnp.take_along_axis(router_grad, (lane_w - offset) & 127, axis=1)
    wrapped = lane_w < offset
    row_of = lax.shift_right_logical(iota((router_rows, width), 1) * expert_total, 7)
    row_here = iota((router_rows, width), 0)
    here = (row_of == row_here).astype(F32)
    after = (row_of + 1 == row_here).astype(F32)
    exact = lambda a, b: jnp.dot(a, b, precision=lax.Precision.HIGHEST, preferred_element_type=F32)
    flat[router_row : router_row + router_rows, :] = exact(
        here, jnp.where(wrapped, 0.0, turned)
    ) + exact(after, jnp.where(wrapped, turned, 0.0))
    gain_row = router_row + router_rows

    grad_mixed = mm_nt(grad_branch, w_out[...]).astype(LOW)
    lane = iota((count, 128), 1)
    low_lanes = lane < HEAD_DIM
    scale = HEAD_DIM**-0.5
    for pair in range(blocks):
        at = slice(128 * pair, 128 * pair + 128)
        queries = qkv[:, at] * jnp.asarray(scale, LOW)
        keys = qkv[:, width + 128 * pair : width + 128 * pair + 128]
        values = qkv[:, 2 * width + 128 * pair : 2 * width + 128 * pair + 128]
        grads = grad_mixed[:, at]
        grad_q = jnp.zeros((count, 128), F32)
        grad_k = jnp.zeros((count, 128), F32)
        grad_v = jnp.zeros((count, 128), F32)
        for half in range(2):
            mine = low_lanes if half == 0 else ~low_lanes
            only = lambda v: jnp.where(mine, v, jnp.zeros_like(v))
            q_half, g_half, k_half = only(queries), only(grads), only(keys)
            scores = jnp.where(allowed, mm_nt(q_half, keys), -1e30)
            head = 2 * pair + half
            probs = jnp.exp(scores - lse[:, head : head + 1])
            grad_probs = mm_nt(g_half, values)
            grad_v = grad_v + mm_tn(probs.astype(LOW), g_half)
            dots = jnp.sum(probs * grad_probs, axis=1, keepdims=True)
            grad_scores = (probs * (grad_probs - dots)).astype(LOW)
            grad_q = grad_q + mm(grad_scores, k_half)
            grad_k = grad_k + mm_tn(grad_scores, q_half)
        gqkv[:, at] = (grad_q * scale).astype(LOW)
        gqkv[:, width + 128 * pair : width + 128 * pair + 128] = grad_k.astype(LOW)
        gqkv[:, 2 * width + 128 * pair : 2 * width + 128 * pair + 128] = grad_v.astype(LOW)
    for j in range(0, 3 * blocks, 2):
        piece = mm_tn(attn_in[...], gqkv[:, 128 * j : 128 * j + 256])
        flat[pl.ds(j, width, stride=3 * blocks), :] = piece[:, :128]
        flat[pl.ds(j + 1, width, stride=3 * blocks), :] = piece[:, 128:]
    grad_attn = mm_nt(gqkv[...], w_qkv[...])
    grad_norm, gain_attn = norm_backward(tokens[...].astype(F32), gains[0:1, :], grad_attn)
    input_grad_o[...] = grad_middle + grad_norm
    for j in range(blocks):
        flat[gain_row + j : gain_row + j + 1, :] = gain_attn[:, 128 * j : 128 * j + 128]
        flat[gain_row + blocks + j : gain_row + blocks + j + 1, :] = gain_ffn[:, 128 * j : 128 * j + 128]
    last = gain_row + 2 * blocks
    flat[last:, :] = jnp.zeros((flat.shape[0] - last, 128), F32)

    core = core_ref[0]
    rows = flat.shape[0] // 128
    padded = kept_o.shape[1]

    @pl.loop(0, kept_o.shape[0])
    def move(i):
        kept_o[pl.ds(i, 1)] = flat[pl.ds((2 * i + core) * rows, padded), :].astype(LOW)[None]
        away_o[pl.ds(i, 1)] = flat[pl.ds((2 * i + 1 - core) * rows, padded), :].astype(LOW)[None]


def dense_backward(after, core, dense_rows, *arrays):
    count, width = arrays[4].shape
    rows = dense_rows // 128
    padded = (rows + 31) // 32 * 32
    return ordered(
        dense_backward_kernel, 1 + len(arrays), after,
        name="dense_backward",
        out_shape=[
            jax.ShapeDtypeStruct((count, width), F32),
            jax.ShapeDtypeStruct((64, padded, 128), LOW),
            jax.ShapeDtypeStruct((64, padded, 128), LOW),
        ],
        in_specs=[SMEM] + [VMEM] * len(arrays),
        out_specs=[VMEM] * 3,
        scratch_shapes=[
            pltpu.VMEM((rows * 128 + padded - rows, 128), F32),
            pltpu.VMEM((count, 3 * width), LOW),
        ],
        compiler_params=params(),
        cost_estimate=cost(12e9, 40e6),
    )(core, *arrays)


def combine_kernel(plan, middle, results, frozen_result, out):
    count, width = middle.shape
    total = middle[...]
    for first, ref in ((2, results), (4, frozen_result)):
        slots = iota((count, ref.shape[0]), 1)
        for k in range(2):
            place = plan[:, first + k : first + k + 1].astype(jnp.int32)
            total = total + plan[:, k : k + 1] * mm((slots == place).astype(F32).astype(LOW), ref[...])
    out[...] = total.astype(LOW)


def combine(after, plan, middle, results, frozen_result):
    return ordered(
        combine_kernel, 4, after,
        name="combine",
        out_shape=jax.ShapeDtypeStruct(middle.shape, LOW),
        in_specs=[VMEM] * 4,
        out_specs=VMEM,
        compiler_params=params(),
        cost_estimate=cost(200e9, 4e6),
    )(plan, middle, results, frozen_result)


def gelu_pair(pre):
    area = 0.5 + 0.5 * lax.erf(pre * (0.5**0.5))
    density = jnp.exp(-0.5 * pre * pre) * (1.0 / (2.0 * math.pi) ** 0.5)
    return pre * area, area + pre * density


HBM = pl.BlockSpec(memory_space=pl.ANY)


def build_weight(after, name, home, sources, by_rows):
    rows, cols = sources[0].shape[1:]

    def kernel(home_ref, local, near, across, local_mate, near_mate, across_mate, out, sems):
        z, half = home_ref[0], home_ref[2]

        def move(blocks):
            copies = []
            for step, shard in enumerate(blocks):
                if by_rows:
                    start = pl.multiple_of(half * (rows // 2), 64)
                    place = pl.ds(pl.multiple_of(((z + step) & 3) * (rows // 2), 64), rows // 2)
                    copies.append((shard.at[0, pl.ds(start, rows // 2), :], out.at[place, :]))
                else:
                    place = pl.ds(pl.multiple_of(((z + step) & 3) * rows, 64), rows)
                    for block in range(4):
                        start = pl.multiple_of((2 * block + half) * (cols // 8), 128)
                        to = slice(block * (cols // 8), (block + 1) * (cols // 8))
                        copies.append((shard.at[0, :, pl.ds(start, cols // 8)], out.at[place, to]))
            made = [pltpu.make_async_copy(a, b, sems.at[i]) for i, (a, b) in enumerate(copies)]
            for copy in made:
                copy.start()
            for copy in made:
                copy.wait()

        pl.when(home_ref[1] == 1)(lambda: move((local, near_mate, across_mate, near)))
        pl.when(home_ref[1] == 0)(lambda: move((local_mate, near, across, near_mate)))

    shape = (2 * rows, cols) if by_rows else (4 * rows, cols // 2)
    return ordered(
        kernel, 7, after,
        name=name,
        out_shape=jax.ShapeDtypeStruct(shape, LOW),
        in_specs=[SMEM] + [HBM] * 6,
        out_specs=VMEM,
        scratch_shapes=[pltpu.SemaphoreType.DMA((16,))],
        compiler_params=params(),
        cost_estimate=cost(1e5, 8e6),
    )(home, *sources)


def expert_up_kernel(rows, weight, hidden_o, slope_o):
    pre = mm(rows[...], weight[...])
    hidden, slope = gelu_pair(pre)
    hidden_o[...] = hidden.astype(LOW)
    slope_o[...] = slope.astype(LOW)


def expert_up(after, rows, weight):
    count, width = rows.shape[0], weight.shape[0]
    hidden = weight.shape[1]
    step = 256
    wide = jax.ShapeDtypeStruct((count, hidden), LOW)
    return ordered(
        expert_up_kernel, 2, after,
        name="expert_up",
        out_shape=[wide, wide],
        grid=(count // step,),
        in_specs=[pl.BlockSpec((step, width), lambda i: (i, 0)), pl.BlockSpec((width, hidden), lambda i: (0, 0))],
        out_specs=[pl.BlockSpec((step, hidden), lambda i: (i, 0))] * 2,
        compiler_params=params(),
        cost_estimate=cost(6e9, 8e6),
    )(rows, weight)


def split_three(value):
    high = lax.reduce_precision(value, 8, 7)
    mid = lax.reduce_precision(value - high, 8, 7)
    return high, mid, value - high - mid


def extra_terms(value):
    lane = iota((value.shape[0], EXTRA), 1)
    extra = jnp.zeros((value.shape[0], EXTRA), F32)
    for i, term in enumerate(split_three(value)):
        extra = jnp.where(lane == i, term, extra)
    return extra.astype(LOW)


def reduce_first(after, low, kept, arrived):
    rows, columns = kept.shape[0] // 2, kept.shape[1]

    def kernel(low_ref, kept, arrived, mine, other):
        for out, which in ((mine, low_ref[0]), (other, 1 - low_ref[0])):
            at = pl.ds(pl.multiple_of(which * rows, 64), rows)
            out[...] = (kept[at, :] + arrived[at, :].astype(F32)).astype(out.dtype)

    return ordered(
        kernel, 3, after,
        name="reduce_first",
        out_shape=[jax.ShapeDtypeStruct((rows, columns), t) for t in (F32, LOW)],
        in_specs=[SMEM, VMEM, VMEM],
        out_specs=[VMEM] * 2,
        compiler_params=params(),
        cost_estimate=cost(1e6, 6e6),
    )(low, kept, arrived)


def reduce_second(after, same, mine, other):
    def kernel(same_ref, mine, other, stays, leaves):
        straight = same_ref[0] == 1
        near, far = mine[...], other[...].astype(F32)
        stays[...] = jnp.where(straight, near, far)
        leaves[...] = jnp.where(straight, far, near).astype(LOW)

    return ordered(
        kernel, 3, after,
        name="reduce_second",
        out_shape=[jax.ShapeDtypeStruct(mine.shape, t) for t in (F32, LOW)],
        in_specs=[SMEM, VMEM, VMEM],
        out_specs=[VMEM] * 2,
        compiler_params=params(),
        cost_estimate=cost(1e6, 6e6),
    )(same, mine, other)


def frozen_kernel(rows, grads, w_in, w_out, result_o, back_o, result_sum, back_sum, value_sum):
    step = pl.program_id(0)

    @pl.when(step == 0)
    def clear():
        result_sum[...] = jnp.zeros_like(result_sum)
        back_sum[...] = jnp.zeros_like(back_sum)
        value_sum[...] = jnp.zeros_like(value_sum)

    hidden, slope = gelu_pair(mm(rows[...], w_in[...]))
    hidden = hidden.astype(LOW)
    result_sum[...] += mm(hidden, w_out[...])
    grad_hidden = mm_nt(grads[...], w_out[...])
    value_sum[...] += jnp.sum(hidden.astype(F32) * grad_hidden, axis=1, keepdims=True)
    back_sum[...] += mm_nt((grad_hidden * slope).astype(LOW), w_in[...])

    @pl.when(step == pl.num_programs(0) - 1)
    def finish():
        result_o[...] = result_sum[...].astype(LOW)
        width = back_sum.shape[1]
        back_o[:, :width] = back_sum[...].astype(LOW)
        back_o[:, width:] = extra_terms(value_sum[:, 0:1])


def frozen_expert(after, sent, w_in, w_out):
    count, width = sent.shape[0], w_in.shape[0]
    wide = w_in.shape[1]
    step = 512
    small = pl.BlockSpec((count, width), lambda i: (0, 0))
    return ordered(
        frozen_kernel, 4, after,
        name="frozen_expert",
        out_shape=[
            jax.ShapeDtypeStruct((count, width), LOW),
            jax.ShapeDtypeStruct((count, width + EXTRA), LOW),
        ],
        grid=(wide // step,),
        in_specs=[
            small, pl.BlockSpec((count, width), lambda i: (0, 1)),
            pl.BlockSpec((width, step), lambda i: (0, i)),
            pl.BlockSpec((step, width), lambda i: (i, 0)),
        ],
        out_specs=[small, pl.BlockSpec((count, width + EXTRA), lambda i: (0, 0))],
        scratch_shapes=[
            pltpu.VMEM((count, width), F32),
            pltpu.VMEM((count, width), F32),
            pltpu.VMEM((count, EXTRA), F32),
        ],
        compiler_params=params(),
        cost_estimate=cost(4e9, 10e6),
    )(sent, sent, w_in, w_out)


def adamw_values(master, first, second, grad):
    first_new = beta_first * first + (1.0 - beta_first) * grad
    second_new = beta_second * second + (1.0 - beta_second) * grad * grad
    first_hat = first_new * (1.0 / (1.0 - beta_first**STEP))
    second_hat = second_new * (1.0 / (1.0 - beta_second**STEP))
    master_new = master - learn_rate * (
        first_hat / (jnp.sqrt(second_hat) + adam_eps) + decay_rate * master
    )
    return master_new, first_new, second_new, master_new.astype(LOW)


def dense_update_kernel(master, first, second, terms, *outs):
    rows = master.shape[0]
    grad = jnp.sum(terms[...].astype(F32), axis=0)[:rows]
    for out, value in zip(outs, adamw_values(master[...], first[...], second[...], grad)):
        out[...] = value


def dense_update(after, master, first, second, terms):
    shape = (master.shape[0] // 128, 128)
    results = ordered(
        dense_update_kernel, 4, after,
        name="dense_update",
        out_shape=[jax.ShapeDtypeStruct(shape, t) for t in (F32, F32, F32, LOW)],
        in_specs=[VMEM] * 4,
        out_specs=[VMEM] * 4,
        compiler_params=params(),
        cost_estimate=cost(1e6, 4e6),
    )(*(a.reshape(shape) for a in (master, first, second)), terms)
    return tuple(r.reshape(master.shape) for r in results)


def expert_update(after, core, master, first, second, stays, arrived, axis):
    rows, columns = master.shape[1:]
    if axis == 1:
        blocks, width = 4, columns // 4
        half = (rows, width // 2)
    else:
        blocks, width = 3, columns // 3
        half = (rows // 2, width)

    def kernel(core_ref, master, first, second, stays, arrived, *outs):
        near, far = stays[...], arrived[...].astype(F32)
        swapped = core_ref[0] == 1
        grad = jnp.concatenate(
            [jnp.where(swapped, far, near), jnp.where(swapped, near, far)], axis=axis
        )
        values = adamw_values(master[0], first[0], second[0], grad)
        for out, value in zip(outs, values):
            out[0] = value

    wide = pl.BlockSpec((1, rows, width), lambda i: (0, 0, i))
    slim = pl.BlockSpec(half, lambda i: (0, i))
    return tuple(
        ordered(
        kernel, 6, after,
            name="update_in" if axis == 1 else "update_out",
            out_shape=[jax.ShapeDtypeStruct(master.shape, t) for t in (F32, F32, F32, LOW)],
            grid=(blocks,),
            in_specs=[SMEM, wide, wide, wide, slim, slim],
            out_specs=[wide] * 4,
            compiler_params=params(),
            cost_estimate=cost(2e7, 18e6),
        )(core, master, first, second, stays, arrived)
    )


def swap_core(block):
    return lax.ppermute(block, "c", [(0, 1), (1, 0)])


KINDS = (0, 1, 1, 0)


def to_neighbours(shard):
    moves = []
    for z, kind in enumerate(KINDS):
        moves.append(((z - 1) % 4 * 2 + kind, z * 2 + kind))
        moves.append(((z + 1) % 4 * 2 + kind, z * 2 + 1 - kind))
    return lax.ppermute(shard, DEPTH + ("c",), moves)


def to_opposite(shard):
    moves = []
    for z, kind in enumerate(KINDS):
        source = kind if z % 2 else 1 - kind
        moves.append((z * 2 + source, (3 - z) * 2 + 1 - kind))
    return lax.ppermute(shard, DEPTH + ("c",), moves)


def swap_pair(block):
    return lax.ppermute(block, DEPTH, [(z, 3 - z) for z in range(4)])


def swap_low(block):
    return lax.ppermute(block, "zl", [(0, 1), (1, 0)])


def exchange(rows):
    cut = rows.reshape(-1, CAP, rows.shape[1])
    cut = lax.all_to_all(cut, PLANE, split_axis=0, concat_axis=0, tiled=True)
    return cut.reshape(rows.shape)


def tie(array, *others):
    return lax.optimization_barrier((array,) + others)[0]


def word(*values):
    return jnp.stack([jnp.asarray(v, jnp.int32) for v in values])


def body(
    tokens,
    segment_ids,
    routes,
    cotangent,
    w_qkv,
    w_attn_out,
    w_router,
    norm_gains,
    frozen_in,
    frozen_out,
    new_in,
    new_out,
    dense_master,
    dense_first,
    dense_second,
    master_in,
    first_in,
    second_in,
    master_out,
    first_out,
    second_out,
):
    core, zh, zl = (lax.axis_index(a) for a in ("c", "zh", "zl"))
    z = 2 * zh + zl
    kind = zh ^ zl
    same = jnp.where(kind == core, 1, 0)
    home = word(z, same, core)
    core_word, same_word, zl_word = word(core), word(same), word(zl)
    routes = routes.T
    w_router = w_router.T

    in_near, out_near = to_neighbours(new_in), to_neighbours(new_out)
    attn_in, qkv_low, mixed_low, lse, middle, ffn_in, plan, sent, frozen_sent = dense_forward(
        (), word(zh), tokens, segment_ids, routes, cotangent, w_qkv, w_attn_out, w_router, norm_gains
    )
    received = exchange(sent)
    frozen_result, frozen_back = frozen_expert((), frozen_sent, frozen_in, frozen_out)
    in_across = to_opposite(tie(in_near, plan))
    out_across = to_opposite(tie(out_near, frozen_back))
    in_shards = (new_in, in_near, in_across)
    in_shards = in_shards + tuple(swap_core(s) for s in (new_in, tie(in_near, plan), in_across))
    half_in = build_weight((frozen_back,), "build_in", home, in_shards, False)
    received = tie(received, frozen_back, in_across)
    received_mate = swap_core(received)
    width = tokens.shape[1]
    rows_own, rows_mate = received[:, :width], received_mate[:, :width]
    grads_own, grads_mate = received[:, width:], received_mate[:, width:]
    hidden_own, slope_own = expert_up((), received, half_in)
    hidden_mate, slope_mate = expert_up((hidden_own,), received_mate, half_in)

    def half_grad(lefts, rights, half):
        cut = lefts[0].shape[1] // 2
        parts = [lax.dynamic_slice(left, (0, half * cut), (left.shape[0], cut)) for left in lefts]
        return mm_tn(parts[0], rights[0]) + mm_tn(parts[1], rights[1])

    hiddens, grads, rows = (hidden_own, hidden_mate), (grads_own, grads_mate), (rows_own, rows_mate)
    out_away = half_grad(hiddens, grads, 1 - zh).astype(LOW)
    out_arrived = swap_pair(out_away)
    out_shards = (new_out, out_near, out_across)
    out_shards = out_shards + tuple(
        swap_core(s) for s in (new_out, tie(out_near, frozen_back), tie(out_across, hidden_own))
    )
    half_out = build_weight((out_away,), "build_out", home, out_shards, True)

    pre_of = lambda grads, slope: (mm_nt(grads, half_out) * slope.astype(F32)).astype(LOW)
    pre_mate = pre_of(grads_mate, slope_mate)
    back_arrived = swap_core(mm_nt(pre_mate, half_in).astype(LOW))
    result_arrived = swap_core(mm(hidden_mate, half_out).astype(LOW))
    result = (mm(hidden_own, half_out) + result_arrived.astype(F32)).astype(LOW)
    result_back = exchange(result)
    pre_own = pre_of(tie(grads_own, result), slope_own)
    pres = (pre_own, pre_mate)
    in_away = half_grad(rows, pres, 1 - zh).astype(LOW)
    in_arrived = swap_pair(in_away)
    back = (mm_nt(pre_own, half_in) + back_arrived.astype(F32)).astype(LOW)
    value = jnp.sum(grads_own.astype(F32) * result.astype(F32), axis=1, keepdims=True)
    merged = jnp.concatenate([back, extra_terms(value)], axis=1)
    back = exchange(tie(merged, in_away, result_back))

    out_kept = half_grad(tuple(tie(h, merged) for h in hiddens), grads, zh)
    in_kept = half_grad(tuple(tie(r, merged) for r in rows), pres, zh)
    out_mine, out_other = reduce_first((merged,), zl_word, out_kept, out_arrived)
    in_mine, in_other = reduce_first((out_mine,), zl_word, in_kept, in_arrived)
    out_other, in_other = swap_low(out_other), swap_low(in_other)

    input_grad, kept, away = dense_backward(
        (in_mine,), core_word, dense_master.shape[0], plan, routes, segment_ids, cotangent, tokens, middle,
        mixed_low, ffn_in, lse, qkv_low, attn_in, w_qkv, w_attn_out, w_router, norm_gains, back, frozen_back,
    )
    arrived = swap_core(away)
    activations = combine((kept,), plan, middle, result_back, frozen_result)
    kept = tie(kept, activations, out_other, in_other)
    summed = (kept.astype(F32) + arrived.astype(F32)).astype(LOW)
    terms = lax.all_to_all(summed, ("zh", "zl", "x", "y"), split_axis=0, concat_axis=0, tiled=True)
    out_stays, out_leaves = reduce_second((summed,), same_word, out_mine, out_other)
    out_mate_grad = swap_core(out_leaves)
    in_stays, in_leaves = reduce_second((out_stays,), same_word, in_mine, in_other)
    in_mate_grad = swap_core(in_leaves)
    out_new = expert_update(
        (in_stays,), core_word, master_out, first_out, second_out, out_stays, out_mate_grad, 0
    )
    in_new = expert_update(
        (out_new[0],), core_word, master_in, first_in, second_in, in_stays, in_mate_grad, 1
    )
    dense_new = dense_update((in_new[0],), dense_master, dense_first, dense_second, terms)
    return (activations, input_grad) + dense_new + in_new + out_new


def solution(mesh):
    fine = Mesh(mesh.devices.reshape(2, 2, 4, 4, 2), ALL)
    tokens = P(ALL, None)
    flat = P(ALL)
    expert = P(("x", "y", "c"), DEPTH, None)
    return jax.shard_map(
        body,
        mesh=fine,
        in_specs=(tokens,) * 4 + (P(),) * 6 + (expert,) * 2 + (flat,) * 3 + (expert,) * 6,
        out_specs=(tokens,) * 2 + (flat,) * 4 + (expert,) * 8,
        check_vma=False,
    )
```

```python
import math

import jax
import jax.numpy as jnp
from jax import lax
from jax.experimental import pallas as pl
from jax.experimental.pallas import tpu as pltpu
from jax.sharding import Mesh
from jax.sharding import PartitionSpec as P

HEAD_DIM = 64
STEP = 5


norm_eps = 1e-05
learn_rate = 0.02
beta_first = 0.5
beta_second = 0.5
adam_eps = 1e-08
decay_rate = 0.1


PLANE = ("zl", "x", "y")
DEPTH = ("zh", "zl")
ALL = ("zh", "zl", "x", "y", "c")
CAP = 24
PAIRS = 6
EXTRA = 128
VMEM = pl.BlockSpec(memory_space=pltpu.VMEM)
SMEM = pl.BlockSpec(memory_space=pltpu.SMEM)
F32 = jnp.float32
LOW = jnp.bfloat16


def params(**more):
    return pltpu.CompilerParams(vmem_limit_bytes=56 * 1024 * 1024, **more)


def ordered(kernel, count, after, **call):
    extra = len(after)

    def inner(*refs):
        return kernel(*refs[:count], *refs[count + extra :])

    call["in_specs"] = list(call["in_specs"]) + [pl.BlockSpec(memory_space=pl.ANY)] * extra
    made = pl.pallas_call(inner, **call)
    return lambda *arrays: made(*arrays, *after)


def cost(flops, moved):
    return pl.CostEstimate(flops=int(flops), bytes_accessed=int(moved), transcendentals=0)


def mm(left, right):
    return jnp.dot(left, right, preferred_element_type=F32)


def mm_nt(left, right):
    return lax.dot_general(left, right, (((1,), (1,)), ((), ())), preferred_element_type=F32)


def mm_tn(left, right):
    return lax.dot_general(left, right, (((0,), (0,)), ((), ())), preferred_element_type=F32)


def iota(shape, axis):
    return lax.broadcasted_iota(jnp.int32, shape, axis)


def normed(values):
    centered = values - jnp.mean(values, axis=1, keepdims=True)
    scale = lax.rsqrt(jnp.mean(centered * centered, axis=1, keepdims=True) + norm_eps)
    return centered * scale, scale


def norm_backward(values, gain, upstream):
    hat, scale = normed(values)
    gain_grad = jnp.sum(upstream * hat, axis=0, keepdims=True)
    inner = upstream * gain
    mean_inner = jnp.mean(inner, axis=1, keepdims=True)
    mean_hat = jnp.mean(inner * hat, axis=1, keepdims=True)
    return scale * (inner - mean_inner - hat * mean_hat), gain_grad


def as_column(row, eye):
    return jnp.sum(jnp.where(eye, row, jnp.zeros_like(row)), axis=1, keepdims=True)


def as_row(column, eye):
    return jnp.sum(jnp.where(eye, column, jnp.zeros_like(column)), axis=0, keepdims=True)


def attention_mask(segment_row):
    count = segment_row.shape[1]
    down, across = iota((count, count), 0), iota((count, count), 1)
    eye = down == across
    column = jnp.sum(jnp.where(eye, segment_row, 0), axis=1, keepdims=True)
    return (down >= across) & (column == segment_row), eye


def dense_forward_kernel(
    zh_ref, tokens, segments, routes, cotangent, w_qkv, w_out, w_router, gains,
    attn_in_o, qkv_o, mixed_o, lse_o, middle_o, ffn_o, plan_o, sent_o, frozen_sent_o,
):
    width = tokens.shape[1]
    count = tokens.shape[0]
    inputs = tokens[...].astype(F32)
    hat, unused = normed(inputs)
    attn_in = (hat * gains[0:1, :]).astype(LOW)
    attn_in_o[...] = attn_in
    qkv_o[...] = mm(attn_in, w_qkv[...]).astype(LOW)
    allowed, eye = attention_mask(segments[...])
    lane = iota((count, 128), 1)
    low_lanes = lane < HEAD_DIM
    lse_all = jnp.zeros((count, 128), F32)
    for pair in range(width // 128):
        at = slice(128 * pair, 128 * pair + 128)
        queries = qkv_o[:, at] * jnp.asarray(HEAD_DIM**-0.5, LOW)
        keys = qkv_o[:, width + 128 * pair : width + 128 * pair + 128]
        values = qkv_o[:, 2 * width + 128 * pair : 2 * width + 128 * pair + 128]
        outs = []
        for half in range(2):
            mine = low_lanes if half == 0 else ~low_lanes
            scores = mm_nt(jnp.where(mine, queries, jnp.zeros_like(queries)), keys)
            scores = jnp.where(allowed, scores, -1e30)
            top = jnp.max(scores, axis=1, keepdims=True)
            raised = jnp.exp(scores - top)
            total = jnp.sum(raised, axis=1, keepdims=True)
            probs = (raised * (1.0 / total)).astype(LOW)
            outs.append(mm(probs, values))
            lse_all = jnp.where(lane == 2 * pair + half, top + jnp.log(total), lse_all)
        mixed_o[:, at] = jnp.where(low_lanes, outs[0], outs[1]).astype(LOW)
    lse_o[...] = lse_all
    middle = inputs + mm(mixed_o[...], w_out[...])
    middle_o[...] = middle
    hat, unused = normed(middle)
    ffn = (hat * gains[1:2, :]).astype(LOW)
    ffn_o[...] = ffn
    logits = mm_nt(ffn, w_router[...])
    experts = iota(logits.shape, 1)
    lists = [as_column(routes[k : k + 1, :], eye) for k in range(2)]
    picks = [experts == column for column in lists]
    chosen = [jnp.sum(jnp.where(p, logits, 0.0), axis=1, keepdims=True) for p in picks]
    top = jnp.maximum(chosen[0], chosen[1])
    raised = [jnp.exp(c - top) for c in chosen]
    gates = [r / (raised[0] + raised[1]) for r in raised]
    named = (picks[0] | picks[1]).astype(F32).astype(LOW)
    earlier = (iota((count, count), 0) > iota((count, count), 1)).astype(F32).astype(LOW)
    before = mm(earlier, named)
    zh = zh_ref[0]
    new_place, old_place = [], []
    for k in range(2):
        route = lists[k]
        slot = jnp.sum(jnp.where(picks[k], before, 0.0), axis=1, keepdims=True).astype(jnp.int32)
        fresh = route - 1
        block = 16 * ((fresh & 1) ^ zh) + lax.shift_right_arithmetic(fresh, 1)
        new_place.append(jnp.where(route > 0, block * CAP + slot, -1))
        old_place.append(jnp.where(route > 0, -1, slot))
    columns = gates + [p.astype(F32) for p in new_place + old_place]
    plan = jnp.zeros((count, 128), F32)
    for i, column in enumerate(columns):
        plan = jnp.where(lane == i, column, plan)
    plan_o[...] = plan
    up = cotangent[...].astype(F32)
    scaled = [(g * up).astype(LOW) for g in gates]
    for places, ref in ((new_place, sent_o), (old_place, frozen_sent_o)):
        slots = iota((ref.shape[0], count), 0)
        spread = [(slots == as_row(p, eye)).astype(F32).astype(LOW) for p in places]
        ref[:, :width] = mm(spread[0] + spread[1], ffn).astype(LOW)
        ref[:, width:] = (mm(spread[0], scaled[0]) + mm(spread[1], scaled[1])).astype(LOW)


def dense_forward(after, zh, tokens, segments, routes, cotangent, w_qkv, w_out, w_router, gains):
    count, width = tokens.shape
    slots = (w_router.shape[0] - 1) * CAP
    shapes = [
        ((count, width), LOW), ((count, 3 * width), LOW), ((count, width), LOW), ((count, 128), F32),
        ((count, width), F32), ((count, width), LOW), ((count, 128), F32),
        ((slots, 2 * width), LOW), ((CAP, 2 * width), LOW),
    ]
    return ordered(
        dense_forward_kernel, 9, after,
        name="dense_forward",
        out_shape=[jax.ShapeDtypeStruct(s, t) for s, t in shapes],
        in_specs=[SMEM] + [VMEM] * 8,
        out_specs=[VMEM] * len(shapes),
        compiler_params=params(),
        cost_estimate=cost(8e9, 30e6),
    )(zh, tokens, segments, routes, cotangent, w_qkv, w_out, w_router, gains)


def dense_backward_kernel(
    core_ref, plan, routes, segments, cotangent, tokens, middle, mixed, ffn, lse, qkv, attn_in,
    w_qkv, w_out, w_router, gains, back, frozen_back,
    input_grad_o, kept_o, away_o,
    flat, gqkv,
):
    count, width = tokens.shape
    expert_total = w_router.shape[0]
    up = cotangent[...].astype(F32)
    gates = [plan[:, k : k + 1] for k in range(2)]
    new_place = [plan[:, 2 + k : 3 + k].astype(jnp.int32) for k in range(2)]
    old_place = [plan[:, 4 + k : 5 + k].astype(jnp.int32) for k in range(2)]
    allowed, eye = attention_mask(segments[...])

    grad_ffn = jnp.zeros((count, width), F32)
    weighted = [jnp.zeros((count, 1), F32) for k in range(2)]
    for places, ref in ((new_place, back), (old_place, frozen_back)):
        size = ref.shape[0]
        slots = iota((count, size), 1)
        for k in range(2):
            choice = (slots == places[k]).astype(F32).astype(LOW)
            picked = mm(choice, ref[...])
            grad_ffn = grad_ffn + picked[:, :width]
            tail = picked[:, width:]
            weighted[k] = weighted[k] + jnp.sum(tail, axis=1, keepdims=True)
    both = weighted[0] + weighted[1]
    experts = iota((count, expert_total), 1)
    grad_logits = jnp.zeros((count, expert_total), F32)
    for k in range(2):
        grad_logits = jnp.where(
            experts == as_column(routes[k : k + 1, :], eye), weighted[k] - gates[k] * both, grad_logits
        )
    grad_logits = grad_logits.astype(LOW)
    grad_ffn = grad_ffn + mm(grad_logits, w_router[...])
    grad_norm, gain_ffn = norm_backward(middle[...], gains[1:2, :], grad_ffn)
    grad_middle = up + grad_norm
    grad_branch = grad_middle.astype(LOW)

    blocks = width // 128
    first_row = 3 * blocks * width
    attn_out_grad = mm_tn(mixed[...], grad_branch)
    for j in range(blocks):
        flat[pl.ds(first_row + j, width, stride=blocks), :] = attn_out_grad[:, 128 * j : 128 * j + 128]
    router_row = first_row + blocks * width
    router_rows = width * expert_total // 128
    padded_logits = jnp.concatenate(
        [grad_logits, jnp.zeros((count, 128 - expert_total), LOW)], axis=1
    )
    router_grad = mm_tn(ffn[...], padded_logits)
    feature = iota((width, 128), 0)
    lane_w = iota((width, 128), 1)
    start = feature * expert_total
    offset = start & 127
    turned = jnp.take_along_axis(router_grad, (lane_w - offset) & 127, axis=1)
    wrapped = lane_w < offset
    row_of = lax.shift_right_logical(iota((router_rows, width), 1) * expert_total, 7)
    row_here = iota((router_rows, width), 0)
    here = (row_of == row_here).astype(F32)
    after = (row_of + 1 == row_here).astype(F32)
    exact = lambda a, b: jnp.dot(a, b, precision=lax.Precision.HIGHEST, preferred_element_type=F32)
    flat[router_row : router_row + router_rows, :] = exact(
        here, jnp.where(wrapped, 0.0, turned)
    ) + exact(after, jnp.where(wrapped, turned, 0.0))
    gain_row = router_row + router_rows

    grad_mixed = mm_nt(grad_branch, w_out[...]).astype(LOW)
    lane = iota((count, 128), 1)
    low_lanes = lane < HEAD_DIM
    scale = HEAD_DIM**-0.5
    for pair in range(blocks):
        at = slice(128 * pair, 128 * pair + 128)
        queries = qkv[:, at] * jnp.asarray(scale, LOW)
        keys = qkv[:, width + 128 * pair : width + 128 * pair + 128]
        values = qkv[:, 2 * width + 128 * pair : 2 * width + 128 * pair + 128]
        grads = grad_mixed[:, at]
        grad_q = jnp.zeros((count, 128), F32)
        grad_k = jnp.zeros((count, 128), F32)
        grad_v = jnp.zeros((count, 128), F32)
        for half in range(2):
            mine = low_lanes if half == 0 else ~low_lanes
            only = lambda v: jnp.where(mine, v, jnp.zeros_like(v))
            q_half, g_half, k_half = only(queries), only(grads), only(keys)
            scores = jnp.where(allowed, mm_nt(q_half, keys), -1e30)
            head = 2 * pair + half
            probs = jnp.exp(scores - lse[:, head : head + 1])
            grad_probs = mm_nt(g_half, values)
            grad_v = grad_v + mm_tn(probs.astype(LOW), g_half)
            dots = jnp.sum(probs * grad_probs, axis=1, keepdims=True)
            grad_scores = (probs * (grad_probs - dots)).astype(LOW)
            grad_q = grad_q + mm(grad_scores, k_half)
            grad_k = grad_k + mm_tn(grad_scores, q_half)
        gqkv[:, at] = (grad_q * scale).astype(LOW)
        gqkv[:, width + 128 * pair : width + 128 * pair + 128] = grad_k.astype(LOW)
        gqkv[:, 2 * width + 128 * pair : 2 * width + 128 * pair + 128] = grad_v.astype(LOW)
    for j in range(0, 3 * blocks, 2):
        piece = mm_tn(attn_in[...], gqkv[:, 128 * j : 128 * j + 256])
        flat[pl.ds(j, width, stride=3 * blocks), :] = piece[:, :128]
        flat[pl.ds(j + 1, width, stride=3 * blocks), :] = piece[:, 128:]
    grad_attn = mm_nt(gqkv[...], w_qkv[...])
    grad_norm, gain_attn = norm_backward(tokens[...].astype(F32), gains[0:1, :], grad_attn)
    input_grad_o[...] = grad_middle + grad_norm
    for j in range(blocks):
        flat[gain_row + j : gain_row + j + 1, :] = gain_attn[:, 128 * j : 128 * j + 128]
        flat[gain_row + blocks + j : gain_row + blocks + j + 1, :] = gain_ffn[:, 128 * j : 128 * j + 128]
    last = gain_row + 2 * blocks
    flat[last:, :] = jnp.zeros((flat.shape[0] - last, 128), F32)

    core = core_ref[0]
    rows = flat.shape[0] // 128
    padded = kept_o.shape[1]

    @pl.loop(0, kept_o.shape[0])
    def move(i):
        kept_o[pl.ds(i, 1)] = flat[pl.ds((2 * i + core) * rows, padded), :].astype(LOW)[None]
        away_o[pl.ds(i, 1)] = flat[pl.ds((2 * i + 1 - core) * rows, padded), :].astype(LOW)[None]


def dense_backward(after, core, dense_rows, *arrays):
    count, width = arrays[4].shape
    rows = dense_rows // 128
    padded = (rows + 31) // 32 * 32
    return ordered(
        dense_backward_kernel, 1 + len(arrays), after,
        name="dense_backward",
        out_shape=[
            jax.ShapeDtypeStruct((count, width), F32),
            jax.ShapeDtypeStruct((64, padded, 128), LOW),
            jax.ShapeDtypeStruct((64, padded, 128), LOW),
        ],
        in_specs=[SMEM] + [VMEM] * len(arrays),
        out_specs=[VMEM] * 3,
        scratch_shapes=[
            pltpu.VMEM((rows * 128 + padded - rows, 128), F32),
            pltpu.VMEM((count, 3 * width), LOW),
        ],
        compiler_params=params(),
        cost_estimate=cost(12e9, 40e6),
    )(core, *arrays)


def combine_kernel(plan, middle, results, frozen_result, out):
    count, width = middle.shape
    total = middle[...]
    for first, ref in ((2, results), (4, frozen_result)):
        slots = iota((count, ref.shape[0]), 1)
        for k in range(2):
            place = plan[:, first + k : first + k + 1].astype(jnp.int32)
            total = total + plan[:, k : k + 1] * mm((slots == place).astype(F32).astype(LOW), ref[...])
    out[...] = total.astype(LOW)


def combine(after, plan, middle, results, frozen_result):
    return ordered(
        combine_kernel, 4, after,
        name="combine",
        out_shape=jax.ShapeDtypeStruct(middle.shape, LOW),
        in_specs=[VMEM] * 4,
        out_specs=VMEM,
        compiler_params=params(),
        cost_estimate=cost(200e9, 4e6),
    )(plan, middle, results, frozen_result)


def gelu_pair(pre):
    area = 0.5 + 0.5 * lax.erf(pre * (0.5**0.5))
    density = jnp.exp(-0.5 * pre * pre) * (1.0 / (2.0 * math.pi) ** 0.5)
    return pre * area, area + pre * density


HBM = pl.BlockSpec(memory_space=pl.ANY)


def build_weight(after, name, home, sources, by_rows):
    rows, cols = sources[0].shape[1:]

    def kernel(home_ref, local, near, across, local_mate, near_mate, across_mate, out, sems):
        z, half = home_ref[0], home_ref[2]

        def move(blocks):
            copies = []
            for step, shard in enumerate(blocks):
                if by_rows:
                    start = pl.multiple_of(half * (rows // 2), 64)
                    place = pl.ds(pl.multiple_of(((z + step) & 3) * (rows // 2), 64), rows // 2)
                    copies.append((shard.at[0, pl.ds(start, rows // 2), :], out.at[place, :]))
                else:
                    place = pl.ds(pl.multiple_of(((z + step) & 3) * rows, 64), rows)
                    for block in range(4):
                        start = pl.multiple_of((2 * block + half) * (cols // 8), 128)
                        to = slice(block * (cols // 8), (block + 1) * (cols // 8))
                        copies.append((shard.at[0, :, pl.ds(start, cols // 8)], out.at[place, to]))
            made = [pltpu.make_async_copy(a, b, sems.at[i]) for i, (a, b) in enumerate(copies)]
            for copy in made:
                copy.start()
            for copy in made:
                copy.wait()

        pl.when(home_ref[1] == 1)(lambda: move((local, near_mate, across_mate, near)))
        pl.when(home_ref[1] == 0)(lambda: move((local_mate, near, across, near_mate)))

    shape = (2 * rows, cols) if by_rows else (4 * rows, cols // 2)
    return ordered(
        kernel, 7, after,
        name=name,
        out_shape=jax.ShapeDtypeStruct(shape, LOW),
        in_specs=[SMEM] + [HBM] * 6,
        out_specs=VMEM,
        scratch_shapes=[pltpu.SemaphoreType.DMA((16,))],
        compiler_params=params(),
        cost_estimate=cost(1e5 if by_rows else 19e9, 8e6),
    )(home, *sources)


def expert_up_kernel(own, mate, weight, hidden_o, slope_o, rows_o, grads_o):
    width = weight.shape[0]
    both = jnp.where(pl.program_id(0) < pl.num_programs(0) // 2, own[...], mate[...])
    rows = both[:, :width]
    rows_o[...] = rows
    grads_o[...] = both[:, width:]
    hidden, slope = gelu_pair(mm(rows, weight[...]))
    hidden_o[...] = hidden.astype(LOW)
    slope_o[...] = slope.astype(LOW)


def expert_up(after, own, mate, weight):
    count, width = own.shape[0], weight.shape[0]
    hidden = weight.shape[1]
    step = 256
    half = count // step
    block = lambda cols: pl.BlockSpec((step, cols), lambda i: (i, 0))
    return ordered(
        expert_up_kernel, 3, after,
        name="expert_up",
        out_shape=[jax.ShapeDtypeStruct((2 * count, n), LOW) for n in (hidden, hidden, width, width)],
        grid=(2 * half,),
        in_specs=[
            pl.BlockSpec((step, 2 * width), lambda i: (jnp.minimum(i, half - 1), 0)),
            pl.BlockSpec((step, 2 * width), lambda i: (jnp.maximum(i - half, 0), 0)),
            pl.BlockSpec((width, hidden), lambda i: (0, 0)),
        ],
        out_specs=[block(n) for n in (hidden, hidden, width, width)],
        compiler_params=params(),
        cost_estimate=cost(12e9, 20e6),
    )(own, mate, weight)


def split_three(value):
    high = lax.reduce_precision(value, 8, 7)
    mid = lax.reduce_precision(value - high, 8, 7)
    return high, mid, value - high - mid


def extra_terms(value):
    lane = iota((value.shape[0], EXTRA), 1)
    extra = jnp.zeros((value.shape[0], EXTRA), F32)
    for i, term in enumerate(split_three(value)):
        extra = jnp.where(lane == i, term, extra)
    return extra.astype(LOW)


def reduce_first(after, low, kept, arrived):
    rows, columns = kept.shape[0] // 2, kept.shape[1]

    def kernel(low_ref, kept, arrived, mine, other):
        for out, which in ((mine, low_ref[0]), (other, 1 - low_ref[0])):
            at = pl.ds(pl.multiple_of(which * rows, 64), rows)
            out[...] = (kept[at, :] + arrived[at, :].astype(F32)).astype(out.dtype)

    return ordered(
        kernel, 3, after,
        name="reduce_first",
        out_shape=[jax.ShapeDtypeStruct((rows, columns), t) for t in (F32, LOW)],
        in_specs=[SMEM, VMEM, VMEM],
        out_specs=[VMEM] * 2,
        compiler_params=params(),
        cost_estimate=cost(1e6, 6e6),
    )(low, kept, arrived)


def reduce_second(after, same, mine, other):
    def kernel(same_ref, mine, other, stays, leaves):
        straight = same_ref[0] == 1
        near, far = mine[...], other[...].astype(F32)
        stays[...] = jnp.where(straight, near, far)
        leaves[...] = jnp.where(straight, far, near).astype(LOW)

    return ordered(
        kernel, 3, after,
        name="reduce_second",
        out_shape=[jax.ShapeDtypeStruct(mine.shape, t) for t in (F32, LOW)],
        in_specs=[SMEM, VMEM, VMEM],
        out_specs=[VMEM] * 2,
        compiler_params=params(),
        cost_estimate=cost(1e6, 6e6),
    )(same, mine, other)


def frozen_kernel(rows, grads, w_in, w_out, result_o, back_o, result_sum, back_sum, value_sum):
    step = pl.program_id(0)

    @pl.when(step == 0)
    def clear():
        result_sum[...] = jnp.zeros_like(result_sum)
        back_sum[...] = jnp.zeros_like(back_sum)
        value_sum[...] = jnp.zeros_like(value_sum)

    hidden, slope = gelu_pair(mm(rows[...], w_in[...]))
    hidden = hidden.astype(LOW)
    result_sum[...] += mm(hidden, w_out[...])
    grad_hidden = mm_nt(grads[...], w_out[...])
    value_sum[...] += jnp.sum(hidden.astype(F32) * grad_hidden, axis=1, keepdims=True)
    back_sum[...] += mm_nt((grad_hidden * slope).astype(LOW), w_in[...])

    @pl.when(step == pl.num_programs(0) - 1)
    def finish():
        result_o[...] = result_sum[...].astype(LOW)
        width = back_sum.shape[1]
        back_o[:, :width] = back_sum[...].astype(LOW)
        back_o[:, width:] = extra_terms(value_sum[:, 0:1])


def frozen_expert(after, sent, w_in, w_out):
    count, width = sent.shape[0], w_in.shape[0]
    wide = w_in.shape[1]
    step = 512
    small = pl.BlockSpec((count, width), lambda i: (0, 0))
    return ordered(
        frozen_kernel, 4, after,
        name="frozen_expert",
        out_shape=[
            jax.ShapeDtypeStruct((count, width), LOW),
            jax.ShapeDtypeStruct((count, width + EXTRA), LOW),
        ],
        grid=(wide // step,),
        in_specs=[
            small, pl.BlockSpec((count, width), lambda i: (0, 1)),
            pl.BlockSpec((width, step), lambda i: (0, i)),
            pl.BlockSpec((step, width), lambda i: (i, 0)),
        ],
        out_specs=[small, pl.BlockSpec((count, width + EXTRA), lambda i: (0, 0))],
        scratch_shapes=[
            pltpu.VMEM((count, width), F32),
            pltpu.VMEM((count, width), F32),
            pltpu.VMEM((count, EXTRA), F32),
        ],
        compiler_params=params(),
        cost_estimate=cost(4e9, 10e6),
    )(sent, sent, w_in, w_out)


def adamw_values(master, first, second, grad):
    first_new = beta_first * first + (1.0 - beta_first) * grad
    second_new = beta_second * second + (1.0 - beta_second) * grad * grad
    first_hat = first_new * (1.0 / (1.0 - beta_first**STEP))
    second_hat = second_new * (1.0 / (1.0 - beta_second**STEP))
    master_new = master - learn_rate * (
        first_hat / (jnp.sqrt(second_hat) + adam_eps) + decay_rate * master
    )
    return master_new, first_new, second_new, master_new.astype(LOW)


def dense_update_kernel(master, first, second, terms, *outs):
    rows = master.shape[0]
    grad = jnp.sum(terms[...].astype(F32), axis=0)[:rows]
    for out, value in zip(outs, adamw_values(master[...], first[...], second[...], grad)):
        out[...] = value


def dense_update(after, master, first, second, terms):
    shape = (master.shape[0] // 128, 128)
    results = ordered(
        dense_update_kernel, 4, after,
        name="dense_update",
        out_shape=[jax.ShapeDtypeStruct(shape, t) for t in (F32, F32, F32, LOW)],
        in_specs=[VMEM] * 4,
        out_specs=[VMEM] * 4,
        compiler_params=params(),
        cost_estimate=cost(1e6, 4e6),
    )(*(a.reshape(shape) for a in (master, first, second)), terms)
    return tuple(r.reshape(master.shape) for r in results)


def expert_update(after, core, master, first, second, stays, arrived, axis):
    rows, columns = master.shape[1:]
    if axis == 1:
        blocks, width = 4, columns // 4
        half = (rows, width // 2)
    else:
        blocks, width = 3, columns // 3
        half = (rows // 2, width)

    def kernel(core_ref, master, first, second, stays, arrived, *outs):
        near, far = stays[...], arrived[...].astype(F32)
        swapped = core_ref[0] == 1
        grad = jnp.concatenate(
            [jnp.where(swapped, far, near), jnp.where(swapped, near, far)], axis=axis
        )
        values = adamw_values(master[0], first[0], second[0], grad)
        for out, value in zip(outs, values):
            out[0] = value

    wide = pl.BlockSpec((1, rows, width), lambda i: (0, 0, i))
    slim = pl.BlockSpec(half, lambda i: (0, i))
    return tuple(
        ordered(
        kernel, 6, after,
            name="update_in" if axis == 1 else "update_out",
            out_shape=[jax.ShapeDtypeStruct(master.shape, t) for t in (F32, F32, F32, LOW)],
            grid=(blocks,),
            in_specs=[SMEM, wide, wide, wide, slim, slim],
            out_specs=[wide] * 4,
            compiler_params=params(),
            cost_estimate=cost(2e7, 18e6),
        )(core, master, first, second, stays, arrived)
    )


def swap_core(block):
    return lax.ppermute(block, "c", [(0, 1), (1, 0)])


KINDS = (0, 1, 1, 0)


def to_neighbours(shard):
    moves = []
    for z, kind in enumerate(KINDS):
        moves.append(((z - 1) % 4 * 2 + kind, z * 2 + kind))
        moves.append(((z + 1) % 4 * 2 + kind, z * 2 + 1 - kind))
    return lax.ppermute(shard, DEPTH + ("c",), moves)


def to_opposite(shard):
    moves = []
    for z, kind in enumerate(KINDS):
        source = kind if z % 2 else 1 - kind
        moves.append((z * 2 + source, (3 - z) * 2 + 1 - kind))
    return lax.ppermute(shard, DEPTH + ("c",), moves)


def swap_pair(block):
    return lax.ppermute(block, DEPTH, [(z, 3 - z) for z in range(4)])


def swap_low(block):
    return lax.ppermute(block, "zl", [(0, 1), (1, 0)])


def exchange(rows):
    cut = rows.reshape(-1, CAP, rows.shape[1])
    cut = lax.all_to_all(cut, PLANE, split_axis=0, concat_axis=0, tiled=True)
    return cut.reshape(rows.shape)


def tie(array, *others):
    return lax.optimization_barrier((array,) + others)[0]


def word(*values):
    return jnp.stack([jnp.asarray(v, jnp.int32) for v in values])


def body(
    tokens,
    segment_ids,
    routes,
    cotangent,
    w_qkv,
    w_attn_out,
    w_router,
    norm_gains,
    frozen_in,
    frozen_out,
    new_in,
    new_out,
    dense_master,
    dense_first,
    dense_second,
    master_in,
    first_in,
    second_in,
    master_out,
    first_out,
    second_out,
):
    core, zh, zl = (lax.axis_index(a) for a in ("c", "zh", "zl"))
    z = 2 * zh + zl
    kind = zh ^ zl
    same = jnp.where(kind == core, 1, 0)
    home = word(z, same, core)
    core_word, same_word, zl_word = word(core), word(same), word(zl)
    routes = routes.T
    w_router = w_router.T

    in_near, out_near = to_neighbours(new_in), to_neighbours(new_out)
    in_mates, out_mates = [swap_core(new_in)], [swap_core(new_out)]
    attn_in, qkv_low, mixed_low, lse, middle, ffn_in, plan, sent, frozen_sent = dense_forward(
        (), word(zh), tokens, segment_ids, routes, cotangent, w_qkv, w_attn_out, w_router, norm_gains
    )
    received = exchange(sent)
    in_across = to_opposite(tie(in_near, plan))
    in_mates.append(swap_core(tie(in_near, plan)))
    frozen_result, frozen_back = frozen_expert(
        (in_mates[0], out_mates[0], in_mates[1]), frozen_sent, frozen_in, frozen_out
    )
    in_mates.append(swap_core(in_across))
    half_in = build_weight(
        (frozen_back,), "build_in", home, (new_in, in_near, in_across, *in_mates), False
    )
    out_across = to_opposite(tie(out_near, frozen_back))
    out_mates.append(swap_core(tie(out_near, frozen_back)))
    received = tie(received, frozen_back, in_across)
    hidden, slope, rows, grads = expert_up((), received, swap_core(received), half_in)
    out_mates.append(swap_core(tie(out_across, hidden)))
    count = received.shape[0]

    def half_grad(left, right, half):
        cut = left.shape[1] // 2
        return mm_tn(lax.dynamic_slice(left, (0, half * cut), (left.shape[0], cut)), right)

    out_away = half_grad(hidden, grads, 1 - zh).astype(LOW)
    out_arrived = swap_pair(out_away)
    half_out = build_weight(
        (out_away,), "build_out", home, (new_out, out_near, out_across, *out_mates), True
    )

    result_arrived = swap_core(mm(hidden[count:], half_out).astype(LOW))
    pre = (mm_nt(grads, half_out) * slope.astype(F32)).astype(LOW)
    result = (mm(hidden[:count], half_out) + result_arrived.astype(F32)).astype(LOW)
    result_back = exchange(result)
    back_arrived = swap_core(mm_nt(pre[count:], half_in).astype(LOW))
    in_away = half_grad(rows, pre, 1 - zh).astype(LOW)
    in_arrived = swap_pair(in_away)
    back = (mm_nt(pre[:count], half_in) + back_arrived.astype(F32)).astype(LOW)
    value = jnp.sum(grads[:count].astype(F32) * result.astype(F32), axis=1, keepdims=True)
    merged = jnp.concatenate([back, extra_terms(value)], axis=1)
    back = exchange(tie(merged, in_away, result_back))

    out_kept = half_grad(tie(hidden, merged), grads, zh)
    in_kept = half_grad(tie(rows, merged), pre, zh)
    out_mine, out_other = reduce_first((merged,), zl_word, out_kept, out_arrived)
    in_mine, in_other = reduce_first((out_mine,), zl_word, in_kept, in_arrived)
    out_other, in_other = swap_low(out_other), swap_low(in_other)

    input_grad, kept, away = dense_backward(
        (in_mine,), core_word, dense_master.shape[0], plan, routes, segment_ids, cotangent, tokens, middle,
        mixed_low, ffn_in, lse, qkv_low, attn_in, w_qkv, w_attn_out, w_router, norm_gains, back, frozen_back,
    )
    arrived = swap_core(away)
    activations = combine((kept,), plan, middle, result_back, frozen_result)
    kept = tie(kept, activations, out_other, in_other)
    summed = (kept.astype(F32) + arrived.astype(F32)).astype(LOW)
    terms = lax.all_to_all(summed, ("zh", "zl", "x", "y"), split_axis=0, concat_axis=0, tiled=True)
    out_stays, out_leaves = reduce_second((summed,), same_word, out_mine, out_other)
    out_mate_grad = swap_core(out_leaves)
    in_stays, in_leaves = reduce_second((out_stays,), same_word, in_mine, in_other)
    in_mate_grad = swap_core(in_leaves)
    out_new = expert_update(
        (in_stays,), core_word, master_out, first_out, second_out, out_stays, out_mate_grad, 0
    )
    in_new = expert_update(
        (out_new[0],), core_word, master_in, first_in, second_in, in_stays, in_mate_grad, 1
    )
    dense_new = dense_update((in_new[0],), dense_master, dense_first, dense_second, terms)
    return (activations, input_grad) + dense_new + in_new + out_new


def solution(mesh):
    fine = Mesh(mesh.devices.reshape(2, 2, 4, 4, 2), ALL)
    tokens = P(ALL, None)
    flat = P(ALL)
    expert = P(("x", "y", "c"), DEPTH, None)
    return jax.shard_map(
        body,
        mesh=fine,
        in_specs=(tokens,) * 4 + (P(),) * 6 + (expert,) * 2 + (flat,) * 3 + (expert,) * 6,
        out_specs=(tokens,) * 2 + (flat,) * 4 + (expert,) * 8,
        check_vma=False,
    )
```

```python
import math

import jax
import jax.numpy as jnp
from jax import lax
from jax.experimental import pallas as pl
from jax.experimental.pallas import tpu as pltpu
from jax.sharding import Mesh
from jax.sharding import PartitionSpec as P

HEAD_DIM = 64
STEP = 5


norm_eps = 1e-05
learn_rate = 0.02
beta_first = 0.5
beta_second = 0.5
adam_eps = 1e-08
decay_rate = 0.1


PLANE = ("zl", "x", "y")
DEPTH = ("zh", "zl")
ALL = ("zh", "zl", "x", "y", "c")
CAP = 24
PAIRS = 6
EXTRA = 128
VMEM = pl.BlockSpec(memory_space=pltpu.VMEM)
SMEM = pl.BlockSpec(memory_space=pltpu.SMEM)
F32 = jnp.float32
LOW = jnp.bfloat16


def params(**more):
    return pltpu.CompilerParams(vmem_limit_bytes=56 * 1024 * 1024, **more)


def ordered(kernel, count, after, **call):
    extra = len(after)

    def inner(*refs):
        return kernel(*refs[:count], *refs[count + extra :])

    call["in_specs"] = list(call["in_specs"]) + [pl.BlockSpec(memory_space=pl.ANY)] * extra
    made = pl.pallas_call(inner, **call)
    return lambda *arrays: made(*arrays, *after)


def cost(flops, moved):
    return pl.CostEstimate(flops=int(flops), bytes_accessed=int(moved), transcendentals=0)


def mm(left, right):
    return jnp.dot(left, right, preferred_element_type=F32)


def mm_nt(left, right):
    return lax.dot_general(left, right, (((1,), (1,)), ((), ())), preferred_element_type=F32)


def mm_tn(left, right):
    return lax.dot_general(left, right, (((0,), (0,)), ((), ())), preferred_element_type=F32)


def iota(shape, axis):
    return lax.broadcasted_iota(jnp.int32, shape, axis)


def normed(values):
    centered = values - jnp.mean(values, axis=1, keepdims=True)
    scale = lax.rsqrt(jnp.mean(centered * centered, axis=1, keepdims=True) + norm_eps)
    return centered * scale, scale


def norm_backward(values, gain, upstream):
    hat, scale = normed(values)
    gain_grad = jnp.sum(upstream * hat, axis=0, keepdims=True)
    inner = upstream * gain
    mean_inner = jnp.mean(inner, axis=1, keepdims=True)
    mean_hat = jnp.mean(inner * hat, axis=1, keepdims=True)
    return scale * (inner - mean_inner - hat * mean_hat), gain_grad


def as_column(row, eye):
    return jnp.sum(jnp.where(eye, row, jnp.zeros_like(row)), axis=1, keepdims=True)


def as_row(column, eye):
    return jnp.sum(jnp.where(eye, column, jnp.zeros_like(column)), axis=0, keepdims=True)


def attention_mask(segment_row):
    count = segment_row.shape[1]
    down, across = iota((count, count), 0), iota((count, count), 1)
    eye = down == across
    column = jnp.sum(jnp.where(eye, segment_row, 0), axis=1, keepdims=True)
    return (down >= across) & (column == segment_row), eye


def dense_forward_kernel(
    zh_ref, tokens, segments, routes, cotangent, w_qkv, w_out, w_router, gains,
    attn_in_o, qkv_o, mixed_o, lse_o, middle_o, ffn_o, plan_o, sent_o, frozen_sent_o,
):
    width = tokens.shape[1]
    count = tokens.shape[0]
    inputs = tokens[...].astype(F32)
    hat, unused = normed(inputs)
    attn_in = (hat * gains[0:1, :]).astype(LOW)
    attn_in_o[...] = attn_in
    qkv_o[...] = mm(attn_in, w_qkv[...]).astype(LOW)
    allowed, eye = attention_mask(segments[...])
    lane = iota((count, 128), 1)
    low_lanes = lane < HEAD_DIM
    lse_all = jnp.zeros((count, 128), F32)
    for pair in range(width // 128):
        at = slice(128 * pair, 128 * pair + 128)
        queries = qkv_o[:, at] * jnp.asarray(HEAD_DIM**-0.5, LOW)
        keys = qkv_o[:, width + 128 * pair : width + 128 * pair + 128]
        values = qkv_o[:, 2 * width + 128 * pair : 2 * width + 128 * pair + 128]
        outs = []
        for half in range(2):
            mine = low_lanes if half == 0 else ~low_lanes
            scores = mm_nt(jnp.where(mine, queries, jnp.zeros_like(queries)), keys)
            scores = jnp.where(allowed, scores, -1e30)
            top = jnp.max(scores, axis=1, keepdims=True)
            raised = jnp.exp(scores - top)
            total = jnp.sum(raised, axis=1, keepdims=True)
            probs = (raised * (1.0 / total)).astype(LOW)
            outs.append(mm(probs, values))
            lse_all = jnp.where(lane == 2 * pair + half, top + jnp.log(total), lse_all)
        mixed_o[:, at] = jnp.where(low_lanes, outs[0], outs[1]).astype(LOW)
    lse_o[...] = lse_all
    middle = inputs + mm(mixed_o[...], w_out[...])
    middle_o[...] = middle
    hat, unused = normed(middle)
    ffn = (hat * gains[1:2, :]).astype(LOW)
    ffn_o[...] = ffn
    logits = mm_nt(ffn, w_router[...])
    experts = iota(logits.shape, 1)
    lists = [as_column(routes[k : k + 1, :], eye) for k in range(2)]
    picks = [experts == column for column in lists]
    chosen = [jnp.sum(jnp.where(p, logits, 0.0), axis=1, keepdims=True) for p in picks]
    top = jnp.maximum(chosen[0], chosen[1])
    raised = [jnp.exp(c - top) for c in chosen]
    gates = [r / (raised[0] + raised[1]) for r in raised]
    named = (picks[0] | picks[1]).astype(F32).astype(LOW)
    earlier = (iota((count, count), 0) > iota((count, count), 1)).astype(F32).astype(LOW)
    before = mm(earlier, named)
    zh = zh_ref[0]
    new_place, old_place = [], []
    for k in range(2):
        route = lists[k]
        slot = jnp.sum(jnp.where(picks[k], before, 0.0), axis=1, keepdims=True).astype(jnp.int32)
        fresh = route - 1
        block = 16 * ((fresh & 1) ^ zh) + lax.shift_right_arithmetic(fresh, 1)
        new_place.append(jnp.where(route > 0, block * CAP + slot, -1))
        old_place.append(jnp.where(route > 0, -1, slot))
    columns = gates + [p.astype(F32) for p in new_place + old_place]
    plan = jnp.zeros((count, 128), F32)
    for i, column in enumerate(columns):
        plan = jnp.where(lane == i, column, plan)
    plan_o[...] = plan
    up = cotangent[...].astype(F32)
    scaled = [(g * up).astype(LOW) for g in gates]
    for places, ref in ((new_place, sent_o), (old_place, frozen_sent_o)):
        slots = iota((ref.shape[0], count), 0)
        spread = [(slots == as_row(p, eye)).astype(F32).astype(LOW) for p in places]
        ref[:, :width] = mm(spread[0] + spread[1], ffn).astype(LOW)
        ref[:, width:] = (mm(spread[0], scaled[0]) + mm(spread[1], scaled[1])).astype(LOW)


def dense_forward(after, zh, tokens, segments, routes, cotangent, w_qkv, w_out, w_router, gains):
    count, width = tokens.shape
    slots = (w_router.shape[0] - 1) * CAP
    shapes = [
        ((count, width), LOW), ((count, 3 * width), LOW), ((count, width), LOW), ((count, 128), F32),
        ((count, width), F32), ((count, width), LOW), ((count, 128), F32),
        ((slots, 2 * width), LOW), ((CAP, 2 * width), LOW),
    ]
    return ordered(
        dense_forward_kernel, 9, after,
        name="dense_forward",
        out_shape=[jax.ShapeDtypeStruct(s, t) for s, t in shapes],
        in_specs=[SMEM] + [VMEM] * 8,
        out_specs=[VMEM] * len(shapes),
        compiler_params=params(),
        cost_estimate=cost(8e9, 30e6),
    )(zh, tokens, segments, routes, cotangent, w_qkv, w_out, w_router, gains)


def dense_backward_kernel(
    core_ref, plan, routes, segments, cotangent, tokens, middle, mixed, ffn, lse, qkv, attn_in,
    w_qkv, w_out, w_router, gains, back, frozen_back,
    input_grad_o, kept_o, away_o, active_o,
    flat, gqkv,
):
    count, width = tokens.shape
    expert_total = w_router.shape[0]
    up = cotangent[...].astype(F32)
    gates = [plan[:, k : k + 1] for k in range(2)]
    new_place = [plan[:, 2 + k : 3 + k].astype(jnp.int32) for k in range(2)]
    old_place = [plan[:, 4 + k : 5 + k].astype(jnp.int32) for k in range(2)]
    allowed, eye = attention_mask(segments[...])

    grad_ffn = jnp.zeros((count, width), F32)
    weighted = [jnp.zeros((count, 1), F32) for k in range(2)]
    active = middle[...]
    for places, ref in ((new_place, back), (old_place, frozen_back)):
        size = ref.shape[0]
        slots = iota((count, size), 1)
        for k in range(2):
            choice = (slots == places[k]).astype(F32).astype(LOW)
            picked = mm(choice, ref[...])
            grad_ffn = grad_ffn + picked[:, :width]
            tail = picked[:, width : width + EXTRA]
            weighted[k] = weighted[k] + jnp.sum(tail, axis=1, keepdims=True)
            active = active + gates[k] * picked[:, width + EXTRA :]
    active_o[...] = active.astype(LOW)
    both = weighted[0] + weighted[1]
    experts = iota((count, expert_total), 1)
    grad_logits = jnp.zeros((count, expert_total), F32)
    for k in range(2):
        grad_logits = jnp.where(
            experts == as_column(routes[k : k + 1, :], eye), weighted[k] - gates[k] * both, grad_logits
        )
    grad_logits = grad_logits.astype(LOW)
    grad_ffn = grad_ffn + mm(grad_logits, w_router[...])
    grad_norm, gain_ffn = norm_backward(middle[...], gains[1:2, :], grad_ffn)
    grad_middle = up + grad_norm
    grad_branch = grad_middle.astype(LOW)

    blocks = width // 128
    first_row = 3 * blocks * width
    attn_out_grad = mm_tn(mixed[...], grad_branch)
    for j in range(blocks):
        flat[pl.ds(first_row + j, width, stride=blocks), :] = attn_out_grad[:, 128 * j : 128 * j + 128]
    router_row = first_row + blocks * width
    router_rows = width * expert_total // 128
    padded_logits = jnp.concatenate(
        [grad_logits, jnp.zeros((count, 128 - expert_total), LOW)], axis=1
    )
    router_grad = mm_tn(ffn[...], padded_logits)
    feature = iota((width, 128), 0)
    lane_w = iota((width, 128), 1)
    start = feature * expert_total
    offset = start & 127
    turned = jnp.take_along_axis(router_grad, (lane_w - offset) & 127, axis=1)
    wrapped = lane_w < offset
    row_of = lax.shift_right_logical(iota((router_rows, width), 1) * expert_total, 7)
    row_here = iota((router_rows, width), 0)
    here = (row_of == row_here).astype(F32)
    after = (row_of + 1 == row_here).astype(F32)
    exact = lambda a, b: jnp.dot(a, b, precision=lax.Precision.HIGHEST, preferred_element_type=F32)
    flat[router_row : router_row + router_rows, :] = exact(
        here, jnp.where(wrapped, 0.0, turned)
    ) + exact(after, jnp.where(wrapped, turned, 0.0))
    gain_row = router_row + router_rows

    grad_mixed = mm_nt(grad_branch, w_out[...]).astype(LOW)
    lane = iota((count, 128), 1)
    low_lanes = lane < HEAD_DIM
    scale = HEAD_DIM**-0.5
    for pair in range(blocks):
        at = slice(128 * pair, 128 * pair + 128)
        queries = qkv[:, at] * jnp.asarray(scale, LOW)
        keys = qkv[:, width + 128 * pair : width + 128 * pair + 128]
        values = qkv[:, 2 * width + 128 * pair : 2 * width + 128 * pair + 128]
        grads = grad_mixed[:, at]
        grad_q = jnp.zeros((count, 128), F32)
        grad_k = jnp.zeros((count, 128), F32)
        grad_v = jnp.zeros((count, 128), F32)
        for half in range(2):
            mine = low_lanes if half == 0 else ~low_lanes
            only = lambda v: jnp.where(mine, v, jnp.zeros_like(v))
            q_half, g_half, k_half = only(queries), only(grads), only(keys)
            scores = jnp.where(allowed, mm_nt(q_half, keys), -1e30)
            head = 2 * pair + half
            probs = jnp.exp(scores - lse[:, head : head + 1])
            grad_probs = mm_nt(g_half, values)
            grad_v = grad_v + mm_tn(probs.astype(LOW), g_half)
            dots = jnp.sum(probs * grad_probs, axis=1, keepdims=True)
            grad_scores = (probs * (grad_probs - dots)).astype(LOW)
            grad_q = grad_q + mm(grad_scores, k_half)
            grad_k = grad_k + mm_tn(grad_scores, q_half)
        gqkv[:, at] = (grad_q * scale).astype(LOW)
        gqkv[:, width + 128 * pair : width + 128 * pair + 128] = grad_k.astype(LOW)
        gqkv[:, 2 * width + 128 * pair : 2 * width + 128 * pair + 128] = grad_v.astype(LOW)
    for j in range(0, 3 * blocks, 2):
        piece = mm_tn(attn_in[...], gqkv[:, 128 * j : 128 * j + 256])
        flat[pl.ds(j, width, stride=3 * blocks), :] = piece[:, :128]
        flat[pl.ds(j + 1, width, stride=3 * blocks), :] = piece[:, 128:]
    grad_attn = mm_nt(gqkv[...], w_qkv[...])
    grad_norm, gain_attn = norm_backward(tokens[...].astype(F32), gains[0:1, :], grad_attn)
    input_grad_o[...] = grad_middle + grad_norm
    for j in range(blocks):
        flat[gain_row + j : gain_row + j + 1, :] = gain_attn[:, 128 * j : 128 * j + 128]
        flat[gain_row + blocks + j : gain_row + blocks + j + 1, :] = gain_ffn[:, 128 * j : 128 * j + 128]
    last = gain_row + 2 * blocks
    flat[last:, :] = jnp.zeros((flat.shape[0] - last, 128), F32)

    core = core_ref[0]
    rows = flat.shape[0] // 128
    padded = kept_o.shape[1]

    @pl.loop(0, kept_o.shape[0])
    def move(i):
        kept_o[pl.ds(i, 1)] = flat[pl.ds((2 * i + core) * rows, padded), :].astype(LOW)[None]
        away_o[pl.ds(i, 1)] = flat[pl.ds((2 * i + 1 - core) * rows, padded), :].astype(LOW)[None]


def dense_backward(after, core, dense_rows, *arrays):
    count, width = arrays[4].shape
    rows = dense_rows // 128
    padded = (rows + 31) // 32 * 32
    return ordered(
        dense_backward_kernel, 1 + len(arrays), after,
        name="dense_backward",
        out_shape=[
            jax.ShapeDtypeStruct((count, width), F32),
            jax.ShapeDtypeStruct((64, padded, 128), LOW),
            jax.ShapeDtypeStruct((64, padded, 128), LOW),
            jax.ShapeDtypeStruct((count, width), LOW),
        ],
        in_specs=[SMEM] + [VMEM] * len(arrays),
        out_specs=[VMEM] * 4,
        scratch_shapes=[
            pltpu.VMEM((rows * 128 + padded - rows, 128), F32),
            pltpu.VMEM((count, 3 * width), LOW),
        ],
        compiler_params=params(),
        cost_estimate=cost(12e9, 40e6),
    )(core, *arrays)


def gelu_pair(pre):
    area = 0.5 + 0.5 * lax.erf(pre * (0.5**0.5))
    density = jnp.exp(-0.5 * pre * pre) * (1.0 / (2.0 * math.pi) ** 0.5)
    return pre * area, area + pre * density


HBM = pl.BlockSpec(memory_space=pl.ANY)


def build_weight(after, name, home, sources, by_rows):
    rows, cols = sources[0].shape[1:]

    def kernel(home_ref, local, near, across, local_mate, near_mate, across_mate, out, sems):
        z, half = home_ref[0], home_ref[2]

        def move(blocks):
            copies = []
            for step, shard in enumerate(blocks):
                if by_rows:
                    start = pl.multiple_of(half * (rows // 2), 64)
                    place = pl.ds(pl.multiple_of(((z + step) & 3) * (rows // 2), 64), rows // 2)
                    copies.append((shard.at[0, pl.ds(start, rows // 2), :], out.at[place, :]))
                else:
                    place = pl.ds(pl.multiple_of(((z + step) & 3) * rows, 64), rows)
                    for block in range(4):
                        start = pl.multiple_of((2 * block + half) * (cols // 8), 128)
                        to = slice(block * (cols // 8), (block + 1) * (cols // 8))
                        copies.append((shard.at[0, :, pl.ds(start, cols // 8)], out.at[place, to]))
            made = [pltpu.make_async_copy(a, b, sems.at[i]) for i, (a, b) in enumerate(copies)]
            for copy in made:
                copy.start()
            for copy in made:
                copy.wait()

        pl.when(home_ref[1] == 1)(lambda: move((local, near_mate, across_mate, near)))
        pl.when(home_ref[1] == 0)(lambda: move((local_mate, near, across, near_mate)))

    shape = (2 * rows, cols) if by_rows else (4 * rows, cols // 2)
    return ordered(
        kernel, 7, after,
        name=name,
        out_shape=jax.ShapeDtypeStruct(shape, LOW),
        in_specs=[SMEM] + [HBM] * 6,
        out_specs=VMEM,
        scratch_shapes=[pltpu.SemaphoreType.DMA((16,))],
        compiler_params=params(),
        cost_estimate=cost(1e5 if by_rows else 19e9, 8e6),
    )(home, *sources)


def expert_up_kernel(own, mate, weight, hidden_o, slope_o, rows_o, grads_o):
    width = weight.shape[0]
    both = jnp.where(pl.program_id(0) < pl.num_programs(0) // 2, own[...], mate[...])
    rows = both[:, :width]
    rows_o[...] = rows
    grads_o[...] = both[:, width:]
    hidden, slope = gelu_pair(mm(rows, weight[...]))
    hidden_o[...] = hidden.astype(LOW)
    slope_o[...] = slope.astype(LOW)


def expert_up(after, own, mate, weight):
    count, width = own.shape[0], weight.shape[0]
    hidden = weight.shape[1]
    step = 256
    half = count // step
    block = lambda cols: pl.BlockSpec((step, cols), lambda i: (i, 0))
    return ordered(
        expert_up_kernel, 3, after,
        name="expert_up",
        out_shape=[jax.ShapeDtypeStruct((2 * count, n), LOW) for n in (hidden, hidden, width, width)],
        grid=(2 * half,),
        in_specs=[
            pl.BlockSpec((step, 2 * width), lambda i: (jnp.minimum(i, half - 1), 0)),
            pl.BlockSpec((step, 2 * width), lambda i: (jnp.maximum(i - half, 0), 0)),
            pl.BlockSpec((width, hidden), lambda i: (0, 0)),
        ],
        out_specs=[block(n) for n in (hidden, hidden, width, width)],
        compiler_params=params(),
        cost_estimate=cost(12e9, 20e6),
    )(own, mate, weight)


def split_three(value):
    high = lax.reduce_precision(value, 8, 7)
    mid = lax.reduce_precision(value - high, 8, 7)
    return high, mid, value - high - mid


def extra_terms(value):
    lane = iota((value.shape[0], EXTRA), 1)
    extra = jnp.zeros((value.shape[0], EXTRA), F32)
    for i, term in enumerate(split_three(value)):
        extra = jnp.where(lane == i, term, extra)
    return extra.astype(LOW)


def reduce_first(after, low, kept, arrived, work=1e6):
    rows, columns = kept.shape[0] // 2, kept.shape[1]

    def kernel(low_ref, kept, arrived, mine, other):
        for out, which in ((mine, low_ref[0]), (other, 1 - low_ref[0])):
            at = pl.ds(pl.multiple_of(which * rows, 64), rows)
            out[...] = (kept[at, :] + arrived[at, :].astype(F32)).astype(out.dtype)

    return ordered(
        kernel, 3, after,
        name="reduce_first",
        out_shape=[jax.ShapeDtypeStruct((rows, columns), t) for t in (F32, LOW)],
        in_specs=[SMEM, VMEM, VMEM],
        out_specs=[VMEM] * 2,
        compiler_params=params(),
        cost_estimate=cost(work, 6e6),
    )(low, kept, arrived)


def reduce_second(after, same, mine, other):
    def kernel(same_ref, mine, other, stays, leaves):
        straight = same_ref[0] == 1
        near, far = mine[...], other[...].astype(F32)
        stays[...] = jnp.where(straight, near, far)
        leaves[...] = jnp.where(straight, far, near).astype(LOW)

    return ordered(
        kernel, 3, after,
        name="reduce_second",
        out_shape=[jax.ShapeDtypeStruct(mine.shape, t) for t in (F32, LOW)],
        in_specs=[SMEM, VMEM, VMEM],
        out_specs=[VMEM] * 2,
        compiler_params=params(),
        cost_estimate=cost(1e6, 6e6),
    )(same, mine, other)


def frozen_kernel(rows, grads, w_in, w_out, back_o, result_sum, back_sum, value_sum):
    step = pl.program_id(0)

    @pl.when(step == 0)
    def clear():
        result_sum[...] = jnp.zeros_like(result_sum)
        back_sum[...] = jnp.zeros_like(back_sum)
        value_sum[...] = jnp.zeros_like(value_sum)

    hidden, slope = gelu_pair(mm(rows[...], w_in[...]))
    hidden = hidden.astype(LOW)
    result_sum[...] += mm(hidden, w_out[...])
    grad_hidden = mm_nt(grads[...], w_out[...])
    value_sum[...] += jnp.sum(hidden.astype(F32) * grad_hidden, axis=1, keepdims=True)
    back_sum[...] += mm_nt((grad_hidden * slope).astype(LOW), w_in[...])

    @pl.when(step == pl.num_programs(0) - 1)
    def finish():
        width = back_sum.shape[1]
        back_o[:, :width] = back_sum[...].astype(LOW)
        back_o[:, width : width + EXTRA] = extra_terms(value_sum[:, 0:1])
        back_o[:, width + EXTRA :] = result_sum[...].astype(LOW)


def frozen_expert(after, sent, w_in, w_out):
    count, width = sent.shape[0], w_in.shape[0]
    wide = w_in.shape[1]
    step = 512
    small = pl.BlockSpec((count, width), lambda i: (0, 0))
    return ordered(
        frozen_kernel, 4, after,
        name="frozen_expert",
        out_shape=jax.ShapeDtypeStruct((count, 2 * width + EXTRA), LOW),
        grid=(wide // step,),
        in_specs=[
            small, pl.BlockSpec((count, width), lambda i: (0, 1)),
            pl.BlockSpec((width, step), lambda i: (0, i)),
            pl.BlockSpec((step, width), lambda i: (i, 0)),
        ],
        out_specs=pl.BlockSpec((count, 2 * width + EXTRA), lambda i: (0, 0)),
        scratch_shapes=[
            pltpu.VMEM((count, width), F32),
            pltpu.VMEM((count, width), F32),
            pltpu.VMEM((count, EXTRA), F32),
        ],
        compiler_params=params(),
        cost_estimate=cost(4e9, 10e6),
    )(sent, sent, w_in, w_out)


def marker(after):
    def kernel(out):
        out[...] = jnp.zeros_like(out)

    return ordered(
        kernel, 0, after,
        name="marker",
        out_shape=jax.ShapeDtypeStruct((8, 128), F32),
        in_specs=[],
        out_specs=VMEM,
        compiler_params=params(),
        cost_estimate=cost(200e9, 4e3),
    )()


def adamw_values(master, first, second, grad):
    first_new = beta_first * first + (1.0 - beta_first) * grad
    second_new = beta_second * second + (1.0 - beta_second) * grad * grad
    first_hat = first_new * (1.0 / (1.0 - beta_first**STEP))
    second_hat = second_new * (1.0 / (1.0 - beta_second**STEP))
    master_new = master - learn_rate * (
        first_hat / (jnp.sqrt(second_hat) + adam_eps) + decay_rate * master
    )
    return master_new, first_new, second_new, master_new.astype(LOW)


def dense_update_kernel(master, first, second, terms, *outs):
    rows = master.shape[0]
    grad = jnp.sum(terms[...].astype(F32), axis=0)[:rows]
    for out, value in zip(outs, adamw_values(master[...], first[...], second[...], grad)):
        out[...] = value


def dense_update(after, master, first, second, terms):
    shape = (master.shape[0] // 128, 128)
    results = ordered(
        dense_update_kernel, 4, after,
        name="dense_update",
        out_shape=[jax.ShapeDtypeStruct(shape, t) for t in (F32, F32, F32, LOW)],
        in_specs=[VMEM] * 4,
        out_specs=[VMEM] * 4,
        compiler_params=params(),
        cost_estimate=cost(1e6, 4e6),
    )(*(a.reshape(shape) for a in (master, first, second)), terms)
    return tuple(r.reshape(master.shape) for r in results)


def expert_update(after, core, master, first, second, stays, arrived, axis):
    rows, columns = master.shape[1:]
    if axis == 1:
        blocks, width = 4, columns // 4
        half = (rows, width // 2)
    else:
        blocks, width = 3, columns // 3
        half = (rows // 2, width)

    def kernel(core_ref, master, first, second, stays, arrived, *outs):
        near, far = stays[...], arrived[...].astype(F32)
        swapped = core_ref[0] == 1
        grad = jnp.concatenate(
            [jnp.where(swapped, far, near), jnp.where(swapped, near, far)], axis=axis
        )
        values = adamw_values(master[0], first[0], second[0], grad)
        for out, value in zip(outs, values):
            out[0] = value

    wide = pl.BlockSpec((1, rows, width), lambda i: (0, 0, i))
    slim = pl.BlockSpec(half, lambda i: (0, i))
    return tuple(
        ordered(
        kernel, 6, after,
            name="update_in" if axis == 1 else "update_out",
            out_shape=[jax.ShapeDtypeStruct(master.shape, t) for t in (F32, F32, F32, LOW)],
            grid=(blocks,),
            in_specs=[SMEM, wide, wide, wide, slim, slim],
            out_specs=[wide] * 4,
            compiler_params=params(),
            cost_estimate=cost(2e7, 18e6),
        )(core, master, first, second, stays, arrived)
    )


def swap_core(block):
    return lax.ppermute(block, "c", [(0, 1), (1, 0)])


KINDS = (0, 1, 1, 0)


def to_neighbours(shard):
    moves = []
    for z, kind in enumerate(KINDS):
        moves.append(((z - 1) % 4 * 2 + kind, z * 2 + kind))
        moves.append(((z + 1) % 4 * 2 + kind, z * 2 + 1 - kind))
    return lax.ppermute(shard, DEPTH + ("c",), moves)


def to_opposite(shard):
    moves = []
    for z, kind in enumerate(KINDS):
        source = kind if z % 2 else 1 - kind
        moves.append((z * 2 + source, (3 - z) * 2 + 1 - kind))
    return lax.ppermute(shard, DEPTH + ("c",), moves)


def swap_pair(block):
    return lax.ppermute(block, DEPTH, [(z, 3 - z) for z in range(4)])


def swap_low(block):
    return lax.ppermute(block, "zl", [(0, 1), (1, 0)])


def exchange(rows):
    cut = rows.reshape(-1, CAP, rows.shape[1])
    cut = lax.all_to_all(cut, PLANE, split_axis=0, concat_axis=0, tiled=True)
    return cut.reshape(rows.shape)


def tie(array, *others):
    return lax.optimization_barrier((array,) + others)[0]


def word(*values):
    return jnp.stack([jnp.asarray(v, jnp.int32) for v in values])


def body(
    tokens,
    segment_ids,
    routes,
    cotangent,
    w_qkv,
    w_attn_out,
    w_router,
    norm_gains,
    frozen_in,
    frozen_out,
    new_in,
    new_out,
    dense_master,
    dense_first,
    dense_second,
    master_in,
    first_in,
    second_in,
    master_out,
    first_out,
    second_out,
):
    core, zh, zl = (lax.axis_index(a) for a in ("c", "zh", "zl"))
    z = 2 * zh + zl
    kind = zh ^ zl
    same = jnp.where(kind == core, 1, 0)
    home = word(z, same, core)
    core_word, same_word, zl_word = word(core), word(same), word(zl)
    routes = routes.T
    w_router = w_router.T

    in_near, out_near = to_neighbours(new_in), to_neighbours(new_out)
    in_mates, out_mates = [swap_core(new_in)], [swap_core(new_out)]
    attn_in, qkv_low, mixed_low, lse, middle, ffn_in, plan, sent, frozen_sent = dense_forward(
        (), word(zh), tokens, segment_ids, routes, cotangent, w_qkv, w_attn_out, w_router, norm_gains
    )
    received = exchange(sent)
    in_across = to_opposite(tie(in_near, plan))
    in_mates.append(swap_core(tie(in_near, plan)))
    frozen_back = frozen_expert(
        (in_mates[0], out_mates[0], in_mates[1]), frozen_sent, frozen_in, frozen_out
    )
    in_mates.append(swap_core(tie(in_across, frozen_back)))
    half_in = build_weight(
        (frozen_back,), "build_in", home, (new_in, in_near, in_across, *in_mates), False
    )
    out_across = to_opposite(tie(out_near, frozen_back))
    out_mates.append(swap_core(tie(out_near, frozen_back)))
    received = tie(received, frozen_back, in_across)
    hidden, slope, rows, grads = expert_up((), received, swap_core(received), half_in)
    out_mates.append(swap_core(tie(out_across, hidden)))
    count = received.shape[0]

    def half_grad(left, right, half):
        cut = left.shape[1] // 2
        return mm_tn(lax.dynamic_slice(left, (0, half * cut), (left.shape[0], cut)), right)

    out_away = half_grad(hidden, grads, 1 - zh).astype(LOW)
    out_arrived = swap_pair(out_away)
    half_out = build_weight(
        (out_away,), "build_out", home, (new_out, out_near, out_across, *out_mates), True
    )

    result_arrived = swap_core(mm(hidden[count:], half_out).astype(LOW))
    pre = (mm_nt(grads, half_out) * slope.astype(F32)).astype(LOW)
    result = (mm(hidden[:count], half_out) + result_arrived.astype(F32)).astype(LOW)
    back_arrived = swap_core(mm_nt(pre[count:], half_in).astype(LOW))
    in_away = half_grad(rows, pre, 1 - zh).astype(LOW)
    in_arrived = swap_pair(in_away)
    back = (mm_nt(pre[:count], half_in) + back_arrived.astype(F32)).astype(LOW)
    value = jnp.sum(grads[:count].astype(F32) * result.astype(F32), axis=1, keepdims=True)
    merged = jnp.concatenate([back, extra_terms(value), result], axis=1)
    back = exchange(tie(merged, in_away))

    out_kept = half_grad(tie(hidden, merged), grads, zh)
    in_kept = half_grad(tie(rows, merged), pre, zh)
    out_mine, out_other = reduce_first((merged,), zl_word, out_kept, out_arrived, 10e9)
    in_mine, in_other = reduce_first((out_mine,), zl_word, in_kept, in_arrived, 10e9)
    out_other, in_other = swap_low(out_other), swap_low(in_other)

    input_grad, kept, away, activations = dense_backward(
        (in_mine,), core_word, dense_master.shape[0], plan, routes, segment_ids, cotangent, tokens, middle,
        mixed_low, ffn_in, lse, qkv_low, attn_in, w_qkv, w_attn_out, w_router, norm_gains, back, frozen_back,
    )
    arrived = swap_core(away)
    kept_first = kept
    kept = tie(kept, out_other, in_other)
    zero = marker((kept_first,))[0, 0]
    summed = (kept.astype(F32) + arrived.astype(F32) + zero).astype(LOW)
    terms = lax.all_to_all(summed, ("zh", "zl", "x", "y"), split_axis=0, concat_axis=0, tiled=True)
    out_stays, out_leaves = reduce_second((summed,), same_word, out_mine, out_other)
    out_mate_grad = swap_core(out_leaves)
    in_stays, in_leaves = reduce_second((out_stays,), same_word, in_mine, in_other)
    in_mate_grad = swap_core(in_leaves)
    out_new = expert_update(
        (in_stays,), core_word, master_out, first_out, second_out, out_stays, out_mate_grad, 0
    )
    in_new = expert_update(
        (out_new[0],), core_word, master_in, first_in, second_in, in_stays, in_mate_grad, 1
    )
    dense_new = dense_update((in_new[0],), dense_master, dense_first, dense_second, terms)
    return (activations, input_grad) + dense_new + in_new + out_new


def solution(mesh):
    fine = Mesh(mesh.devices.reshape(2, 2, 4, 4, 2), ALL)
    tokens = P(ALL, None)
    flat = P(ALL)
    expert = P(("x", "y", "c"), DEPTH, None)
    return jax.shard_map(
        body,
        mesh=fine,
        in_specs=(tokens,) * 4 + (P(),) * 6 + (expert,) * 2 + (flat,) * 3 + (expert,) * 6,
        out_specs=(tokens,) * 2 + (flat,) * 4 + (expert,) * 8,
        check_vma=False,
    )
```

```python
import math

import jax
import jax.numpy as jnp
from jax import lax
from jax.experimental import pallas as pl
from jax.experimental.pallas import tpu as pltpu
from jax.sharding import Mesh
from jax.sharding import PartitionSpec as P

HEAD_DIM = 64
STEP = 5


norm_eps = 1e-05
learn_rate = 0.02
beta_first = 0.5
beta_second = 0.5
adam_eps = 1e-08
decay_rate = 0.1


PLANE = ("zl", "x", "y")
DEPTH = ("zh", "zl")
ALL = ("zh", "zl", "x", "y", "c")
CAP = 24
PAIRS = 6
EXTRA = 128
VMEM = pl.BlockSpec(memory_space=pltpu.VMEM)
SMEM = pl.BlockSpec(memory_space=pltpu.SMEM)
F32 = jnp.float32
LOW = jnp.bfloat16


def params(**more):
    return pltpu.CompilerParams(vmem_limit_bytes=56 * 1024 * 1024, **more)


def ordered(kernel, count, after, **call):
    extra = len(after)

    def inner(*refs):
        return kernel(*refs[:count], *refs[count + extra :])

    call["in_specs"] = list(call["in_specs"]) + [pl.BlockSpec(memory_space=pl.ANY)] * extra
    made = pl.pallas_call(inner, **call)
    return lambda *arrays: made(*arrays, *after)


def cost(flops, moved):
    return pl.CostEstimate(flops=int(flops), bytes_accessed=int(moved), transcendentals=0)


def mm(left, right):
    return jnp.dot(left, right, preferred_element_type=F32)


def mm_nt(left, right):
    return lax.dot_general(left, right, (((1,), (1,)), ((), ())), preferred_element_type=F32)


def mm_tn(left, right):
    return lax.dot_general(left, right, (((0,), (0,)), ((), ())), preferred_element_type=F32)


def iota(shape, axis):
    return lax.broadcasted_iota(jnp.int32, shape, axis)


def normed(values):
    centered = values - jnp.mean(values, axis=1, keepdims=True)
    scale = lax.rsqrt(jnp.mean(centered * centered, axis=1, keepdims=True) + norm_eps)
    return centered * scale, scale


def norm_backward(values, gain, upstream):
    hat, scale = normed(values)
    gain_grad = jnp.sum(upstream * hat, axis=0, keepdims=True)
    inner = upstream * gain
    mean_inner = jnp.mean(inner, axis=1, keepdims=True)
    mean_hat = jnp.mean(inner * hat, axis=1, keepdims=True)
    return scale * (inner - mean_inner - hat * mean_hat), gain_grad


def as_column(row, eye):
    return jnp.sum(jnp.where(eye, row, jnp.zeros_like(row)), axis=1, keepdims=True)


def as_row(column, eye):
    return jnp.sum(jnp.where(eye, column, jnp.zeros_like(column)), axis=0, keepdims=True)


def attention_mask(segment_row):
    count = segment_row.shape[1]
    down, across = iota((count, count), 0), iota((count, count), 1)
    eye = down == across
    column = jnp.sum(jnp.where(eye, segment_row, 0), axis=1, keepdims=True)
    return (down >= across) & (column == segment_row), eye


def dense_forward_kernel(
    zh_ref, tokens, segments, routes, cotangent, w_qkv, w_out, w_router, gains,
    attn_in_o, qkv_o, mixed_o, lse_o, middle_o, ffn_o, plan_o, sent_o, frozen_sent_o,
):
    width = tokens.shape[1]
    count = tokens.shape[0]
    inputs = tokens[...].astype(F32)
    hat, unused = normed(inputs)
    attn_in = (hat * gains[0:1, :]).astype(LOW)
    attn_in_o[...] = attn_in
    qkv_o[...] = mm(attn_in, w_qkv[...]).astype(LOW)
    allowed, eye = attention_mask(segments[...])
    lane = iota((count, 128), 1)
    low_lanes = lane < HEAD_DIM
    lse_all = jnp.zeros((count, 128), F32)
    for pair in range(width // 128):
        at = slice(128 * pair, 128 * pair + 128)
        queries = qkv_o[:, at] * jnp.asarray(HEAD_DIM**-0.5, LOW)
        keys = qkv_o[:, width + 128 * pair : width + 128 * pair + 128]
        values = qkv_o[:, 2 * width + 128 * pair : 2 * width + 128 * pair + 128]
        outs = []
        for half in range(2):
            mine = low_lanes if half == 0 else ~low_lanes
            scores = mm_nt(jnp.where(mine, queries, jnp.zeros_like(queries)), keys)
            scores = jnp.where(allowed, scores, -1e30)
            top = jnp.max(scores, axis=1, keepdims=True)
            raised = jnp.exp(scores - top)
            total = jnp.sum(raised, axis=1, keepdims=True)
            probs = (raised * (1.0 / total)).astype(LOW)
            outs.append(mm(probs, values))
            lse_all = jnp.where(lane == 2 * pair + half, top + jnp.log(total), lse_all)
        mixed_o[:, at] = jnp.where(low_lanes, outs[0], outs[1]).astype(LOW)
    lse_o[...] = lse_all
    middle = inputs + mm(mixed_o[...], w_out[...])
    middle_o[...] = middle
    hat, unused = normed(middle)
    ffn = (hat * gains[1:2, :]).astype(LOW)
    ffn_o[...] = ffn
    logits = mm_nt(ffn, w_router[...])
    experts = iota(logits.shape, 1)
    lists = [as_column(routes[k : k + 1, :], eye) for k in range(2)]
    picks = [experts == column for column in lists]
    chosen = [jnp.sum(jnp.where(p, logits, 0.0), axis=1, keepdims=True) for p in picks]
    top = jnp.maximum(chosen[0], chosen[1])
    raised = [jnp.exp(c - top) for c in chosen]
    gates = [r / (raised[0] + raised[1]) for r in raised]
    named = (picks[0] | picks[1]).astype(F32).astype(LOW)
    earlier = (iota((count, count), 0) > iota((count, count), 1)).astype(F32).astype(LOW)
    before = mm(earlier, named)
    zh = zh_ref[0]
    new_place, old_place = [], []
    for k in range(2):
        route = lists[k]
        slot = jnp.sum(jnp.where(picks[k], before, 0.0), axis=1, keepdims=True).astype(jnp.int32)
        fresh = route - 1
        block = 16 * ((fresh & 1) ^ zh) + lax.shift_right_arithmetic(fresh, 1)
        new_place.append(jnp.where(route > 0, block * CAP + slot, -1))
        old_place.append(jnp.where(route > 0, -1, slot))
    columns = gates + [p.astype(F32) for p in new_place + old_place]
    plan = jnp.zeros((count, 128), F32)
    for i, column in enumerate(columns):
        plan = jnp.where(lane == i, column, plan)
    plan_o[...] = plan
    up = cotangent[...].astype(F32)
    scaled = [(g * up).astype(LOW) for g in gates]
    for places, ref in ((new_place, sent_o), (old_place, frozen_sent_o)):
        slots = iota((ref.shape[0], count), 0)
        spread = [(slots == as_row(p, eye)).astype(F32).astype(LOW) for p in places]
        ref[:, :width] = mm(spread[0] + spread[1], ffn).astype(LOW)
        ref[:, width:] = (mm(spread[0], scaled[0]) + mm(spread[1], scaled[1])).astype(LOW)


def dense_forward(after, zh, tokens, segments, routes, cotangent, w_qkv, w_out, w_router, gains):
    count, width = tokens.shape
    slots = (w_router.shape[0] - 1) * CAP
    shapes = [
        ((count, width), LOW), ((count, 3 * width), LOW), ((count, width), LOW), ((count, 128), F32),
        ((count, width), F32), ((count, width), LOW), ((count, 128), F32),
        ((slots, 2 * width), LOW), ((CAP, 2 * width), LOW),
    ]
    return ordered(
        dense_forward_kernel, 9, after,
        name="dense_forward",
        out_shape=[jax.ShapeDtypeStruct(s, t) for s, t in shapes],
        in_specs=[SMEM] + [VMEM] * 8,
        out_specs=[VMEM] * len(shapes),
        compiler_params=params(),
        cost_estimate=cost(8e9, 30e6),
    )(zh, tokens, segments, routes, cotangent, w_qkv, w_out, w_router, gains)


def dense_backward_kernel(
    core_ref, plan, routes, segments, cotangent, tokens, middle, mixed, ffn, lse, qkv, attn_in,
    w_qkv, w_out, w_router, gains, back, frozen_back,
    input_grad_o, kept_o, away_o, active_o,
    flat, gqkv,
):
    count, width = tokens.shape
    expert_total = w_router.shape[0]
    up = cotangent[...].astype(F32)
    gates = [plan[:, k : k + 1] for k in range(2)]
    new_place = [plan[:, 2 + k : 3 + k].astype(jnp.int32) for k in range(2)]
    old_place = [plan[:, 4 + k : 5 + k].astype(jnp.int32) for k in range(2)]
    allowed, eye = attention_mask(segments[...])

    grad_ffn = jnp.zeros((count, width), F32)
    weighted = [jnp.zeros((count, 1), F32) for k in range(2)]
    active = middle[...]
    for places, ref in ((new_place, back), (old_place, frozen_back)):
        size = ref.shape[0]
        slots = iota((count, size), 1)
        for k in range(2):
            choice = (slots == places[k]).astype(F32).astype(LOW)
            picked = mm(choice, ref[...])
            grad_ffn = grad_ffn + picked[:, :width]
            tail = picked[:, width : width + EXTRA]
            weighted[k] = weighted[k] + jnp.sum(tail, axis=1, keepdims=True)
            active = active + gates[k] * picked[:, width + EXTRA :]
    active_o[...] = active.astype(LOW)
    both = weighted[0] + weighted[1]
    experts = iota((count, expert_total), 1)
    grad_logits = jnp.zeros((count, expert_total), F32)
    for k in range(2):
        grad_logits = jnp.where(
            experts == as_column(routes[k : k + 1, :], eye), weighted[k] - gates[k] * both, grad_logits
        )
    grad_logits = grad_logits.astype(LOW)
    grad_ffn = grad_ffn + mm(grad_logits, w_router[...])
    grad_norm, gain_ffn = norm_backward(middle[...], gains[1:2, :], grad_ffn)
    grad_middle = up + grad_norm
    grad_branch = grad_middle.astype(LOW)

    blocks = width // 128
    first_row = 3 * blocks * width
    attn_out_grad = mm_tn(mixed[...], grad_branch)
    for j in range(blocks):
        flat[pl.ds(first_row + j, width, stride=blocks), :] = attn_out_grad[:, 128 * j : 128 * j + 128]
    router_row = first_row + blocks * width
    router_rows = width * expert_total // 128
    padded_logits = jnp.concatenate(
        [grad_logits, jnp.zeros((count, 128 - expert_total), LOW)], axis=1
    )
    router_grad = mm_tn(ffn[...], padded_logits)
    feature = iota((width, 128), 0)
    lane_w = iota((width, 128), 1)
    start = feature * expert_total
    offset = start & 127
    turned = jnp.take_along_axis(router_grad, (lane_w - offset) & 127, axis=1)
    wrapped = lane_w < offset
    row_of = lax.shift_right_logical(iota((router_rows, width), 1) * expert_total, 7)
    row_here = iota((router_rows, width), 0)
    here = (row_of == row_here).astype(F32)
    after = (row_of + 1 == row_here).astype(F32)
    exact = lambda a, b: jnp.dot(a, b, precision=lax.Precision.HIGHEST, preferred_element_type=F32)
    flat[router_row : router_row + router_rows, :] = exact(
        here, jnp.where(wrapped, 0.0, turned)
    ) + exact(after, jnp.where(wrapped, turned, 0.0))
    gain_row = router_row + router_rows

    grad_mixed = mm_nt(grad_branch, w_out[...]).astype(LOW)
    lane = iota((count, 128), 1)
    low_lanes = lane < HEAD_DIM
    scale = HEAD_DIM**-0.5
    for pair in range(blocks):
        at = slice(128 * pair, 128 * pair + 128)
        queries = qkv[:, at] * jnp.asarray(scale, LOW)
        keys = qkv[:, width + 128 * pair : width + 128 * pair + 128]
        values = qkv[:, 2 * width + 128 * pair : 2 * width + 128 * pair + 128]
        grads = grad_mixed[:, at]
        grad_q = jnp.zeros((count, 128), F32)
        grad_k = jnp.zeros((count, 128), F32)
        grad_v = jnp.zeros((count, 128), F32)
        for half in range(2):
            mine = low_lanes if half == 0 else ~low_lanes
            only = lambda v: jnp.where(mine, v, jnp.zeros_like(v))
            q_half, g_half, k_half = only(queries), only(grads), only(keys)
            scores = jnp.where(allowed, mm_nt(q_half, keys), -1e30)
            head = 2 * pair + half
            probs = jnp.exp(scores - lse[:, head : head + 1])
            grad_probs = mm_nt(g_half, values)
            grad_v = grad_v + mm_tn(probs.astype(LOW), g_half)
            dots = jnp.sum(probs * grad_probs, axis=1, keepdims=True)
            grad_scores = (probs * (grad_probs - dots)).astype(LOW)
            grad_q = grad_q + mm(grad_scores, k_half)
            grad_k = grad_k + mm_tn(grad_scores, q_half)
        gqkv[:, at] = (grad_q * scale).astype(LOW)
        gqkv[:, width + 128 * pair : width + 128 * pair + 128] = grad_k.astype(LOW)
        gqkv[:, 2 * width + 128 * pair : 2 * width + 128 * pair + 128] = grad_v.astype(LOW)
    for j in range(0, 3 * blocks, 2):
        piece = mm_tn(attn_in[...], gqkv[:, 128 * j : 128 * j + 256])
        flat[pl.ds(j, width, stride=3 * blocks), :] = piece[:, :128]
        flat[pl.ds(j + 1, width, stride=3 * blocks), :] = piece[:, 128:]
    grad_attn = mm_nt(gqkv[...], w_qkv[...])
    grad_norm, gain_attn = norm_backward(tokens[...].astype(F32), gains[0:1, :], grad_attn)
    input_grad_o[...] = grad_middle + grad_norm
    for j in range(blocks):
        flat[gain_row + j : gain_row + j + 1, :] = gain_attn[:, 128 * j : 128 * j + 128]
        flat[gain_row + blocks + j : gain_row + blocks + j + 1, :] = gain_ffn[:, 128 * j : 128 * j + 128]
    last = gain_row + 2 * blocks
    flat[last:, :] = jnp.zeros((flat.shape[0] - last, 128), F32)

    core = core_ref[0]
    rows = flat.shape[0] // 128
    padded = kept_o.shape[1]

    @pl.loop(0, kept_o.shape[0])
    def move(i):
        kept_o[pl.ds(i, 1)] = flat[pl.ds((2 * i + core) * rows, padded), :].astype(LOW)[None]
        away_o[pl.ds(i, 1)] = flat[pl.ds((2 * i + 1 - core) * rows, padded), :].astype(LOW)[None]


def dense_backward(after, core, dense_rows, *arrays):
    count, width = arrays[4].shape
    rows = dense_rows // 128
    padded = (rows + 31) // 32 * 32
    return ordered(
        dense_backward_kernel, 1 + len(arrays), after,
        name="dense_backward",
        out_shape=[
            jax.ShapeDtypeStruct((count, width), F32),
            jax.ShapeDtypeStruct((64, padded, 128), LOW),
            jax.ShapeDtypeStruct((64, padded, 128), LOW),
            jax.ShapeDtypeStruct((count, width), LOW),
        ],
        in_specs=[SMEM] + [VMEM] * len(arrays),
        out_specs=[VMEM] * 4,
        scratch_shapes=[
            pltpu.VMEM((rows * 128 + padded - rows, 128), F32),
            pltpu.VMEM((count, 3 * width), LOW),
        ],
        compiler_params=params(),
        cost_estimate=cost(12e9, 40e6),
    )(core, *arrays)


def gelu_pair(pre):
    area = 0.5 + 0.5 * lax.erf(pre * (0.5**0.5))
    density = jnp.exp(-0.5 * pre * pre) * (1.0 / (2.0 * math.pi) ** 0.5)
    return pre * area, area + pre * density


HBM = pl.BlockSpec(memory_space=pl.ANY)


def build_weight(after, name, home, sources, by_rows):
    rows, cols = sources[0].shape[1:]

    def kernel(home_ref, local, near, across, local_mate, near_mate, across_mate, out, sems):
        z, half = home_ref[0], home_ref[2]

        def move(blocks):
            copies = []
            for step, shard in enumerate(blocks):
                if by_rows:
                    start = pl.multiple_of(half * (rows // 2), 64)
                    place = pl.ds(pl.multiple_of(((z + step) & 3) * (rows // 2), 64), rows // 2)
                    copies.append((shard.at[0, pl.ds(start, rows // 2), :], out.at[place, :]))
                else:
                    place = pl.ds(pl.multiple_of(((z + step) & 3) * rows, 64), rows)
                    for block in range(4):
                        start = pl.multiple_of((2 * block + half) * (cols // 8), 128)
                        to = slice(block * (cols // 8), (block + 1) * (cols // 8))
                        copies.append((shard.at[0, :, pl.ds(start, cols // 8)], out.at[place, to]))
            made = [pltpu.make_async_copy(a, b, sems.at[i]) for i, (a, b) in enumerate(copies)]
            for copy in made:
                copy.start()
            for copy in made:
                copy.wait()

        pl.when(home_ref[1] == 1)(lambda: move((local, near_mate, across_mate, near)))
        pl.when(home_ref[1] == 0)(lambda: move((local_mate, near, across, near_mate)))

    shape = (2 * rows, cols) if by_rows else (4 * rows, cols // 2)
    return ordered(
        kernel, 7, after,
        name=name,
        out_shape=jax.ShapeDtypeStruct(shape, LOW),
        in_specs=[SMEM] + [HBM] * 6,
        out_specs=VMEM,
        scratch_shapes=[pltpu.SemaphoreType.DMA((16,))],
        compiler_params=params(),
        cost_estimate=cost(1e5 if by_rows else 19e9, 8e6),
    )(home, *sources)


def expert_up_kernel(own, mate, weight, hidden_o, slope_o, rows_o, grads_o):
    width = weight.shape[0]
    both = jnp.where(pl.program_id(0) < pl.num_programs(0) // 2, own[...], mate[...])
    rows = both[:, :width]
    rows_o[...] = rows
    grads_o[...] = both[:, width:]
    hidden, slope = gelu_pair(mm(rows, weight[...]))
    hidden_o[...] = hidden.astype(LOW)
    slope_o[...] = slope.astype(LOW)


def expert_up(after, own, mate, weight):
    count, width = own.shape[0], weight.shape[0]
    hidden = weight.shape[1]
    step = 256
    half = count // step
    block = lambda cols: pl.BlockSpec((step, cols), lambda i: (i, 0))
    return ordered(
        expert_up_kernel, 3, after,
        name="expert_up",
        out_shape=[jax.ShapeDtypeStruct((2 * count, n), LOW) for n in (hidden, hidden, width, width)],
        grid=(2 * half,),
        in_specs=[
            pl.BlockSpec((step, 2 * width), lambda i: (jnp.minimum(i, half - 1), 0)),
            pl.BlockSpec((step, 2 * width), lambda i: (jnp.maximum(i - half, 0), 0)),
            pl.BlockSpec((width, hidden), lambda i: (0, 0)),
        ],
        out_specs=[block(n) for n in (hidden, hidden, width, width)],
        compiler_params=params(),
        cost_estimate=cost(12e9, 20e6),
    )(own, mate, weight)


def split_three(value):
    high = lax.reduce_precision(value, 8, 7)
    mid = lax.reduce_precision(value - high, 8, 7)
    return high, mid, value - high - mid


def extra_terms(value):
    lane = iota((value.shape[0], EXTRA), 1)
    extra = jnp.zeros((value.shape[0], EXTRA), F32)
    for i, term in enumerate(split_three(value)):
        extra = jnp.where(lane == i, term, extra)
    return extra.astype(LOW)


def reduce_first(after, low, kept, arrived, work=1e6):
    rows, columns = kept.shape[0] // 2, kept.shape[1]

    def kernel(low_ref, kept, arrived, mine, other):
        for out, which in ((mine, low_ref[0]), (other, 1 - low_ref[0])):
            at = pl.ds(pl.multiple_of(which * rows, 64), rows)
            out[...] = (kept[at, :] + arrived[at, :].astype(F32)).astype(out.dtype)

    return ordered(
        kernel, 3, after,
        name="reduce_first",
        out_shape=[jax.ShapeDtypeStruct((rows, columns), t) for t in (F32, LOW)],
        in_specs=[SMEM, VMEM, VMEM],
        out_specs=[VMEM] * 2,
        compiler_params=params(),
        cost_estimate=cost(work, 6e6),
    )(low, kept, arrived)


def reduce_second(after, same, mine, other):
    def kernel(same_ref, mine, other, stays, leaves):
        straight = same_ref[0] == 1
        near, far = mine[...], other[...].astype(F32)
        stays[...] = jnp.where(straight, near, far)
        leaves[...] = jnp.where(straight, far, near).astype(LOW)

    return ordered(
        kernel, 3, after,
        name="reduce_second",
        out_shape=[jax.ShapeDtypeStruct(mine.shape, t) for t in (F32, LOW)],
        in_specs=[SMEM, VMEM, VMEM],
        out_specs=[VMEM] * 2,
        compiler_params=params(),
        cost_estimate=cost(1e6, 6e6),
    )(same, mine, other)


def frozen_kernel(rows, grads, w_in, w_out, back_o, result_sum, back_sum, value_sum):
    step = pl.program_id(0)

    @pl.when(step == 0)
    def clear():
        result_sum[...] = jnp.zeros_like(result_sum)
        back_sum[...] = jnp.zeros_like(back_sum)
        value_sum[...] = jnp.zeros_like(value_sum)

    hidden, slope = gelu_pair(mm(rows[...], w_in[...]))
    hidden = hidden.astype(LOW)
    result_sum[...] += mm(hidden, w_out[...])
    grad_hidden = mm_nt(grads[...], w_out[...])
    value_sum[...] += jnp.sum(hidden.astype(F32) * grad_hidden, axis=1, keepdims=True)
    back_sum[...] += mm_nt((grad_hidden * slope).astype(LOW), w_in[...])

    @pl.when(step == pl.num_programs(0) - 1)
    def finish():
        width = back_sum.shape[1]
        back_o[:, :width] = back_sum[...].astype(LOW)
        back_o[:, width : width + EXTRA] = extra_terms(value_sum[:, 0:1])
        back_o[:, width + EXTRA :] = result_sum[...].astype(LOW)


def frozen_expert(after, sent, w_in, w_out):
    count, width = sent.shape[0], w_in.shape[0]
    wide = w_in.shape[1]
    step = 512
    small = pl.BlockSpec((count, width), lambda i: (0, 0))
    return ordered(
        frozen_kernel, 4, after,
        name="frozen_expert",
        out_shape=jax.ShapeDtypeStruct((count, 2 * width + EXTRA), LOW),
        grid=(wide // step,),
        in_specs=[
            small, pl.BlockSpec((count, width), lambda i: (0, 1)),
            pl.BlockSpec((width, step), lambda i: (0, i)),
            pl.BlockSpec((step, width), lambda i: (i, 0)),
        ],
        out_specs=pl.BlockSpec((count, 2 * width + EXTRA), lambda i: (0, 0)),
        scratch_shapes=[
            pltpu.VMEM((count, width), F32),
            pltpu.VMEM((count, width), F32),
            pltpu.VMEM((count, EXTRA), F32),
        ],
        compiler_params=params(),
        cost_estimate=cost(4e9, 10e6),
    )(sent, sent, w_in, w_out)


def marker(after):
    def kernel(out):
        out[...] = jnp.zeros_like(out)

    return ordered(
        kernel, 0, after,
        name="marker",
        out_shape=jax.ShapeDtypeStruct((8, 128), F32),
        in_specs=[],
        out_specs=VMEM,
        compiler_params=params(),
        cost_estimate=cost(200e9, 4e3),
    )()


def adamw_values(master, first, second, grad):
    first_new = beta_first * first + (1.0 - beta_first) * grad
    second_new = beta_second * second + (1.0 - beta_second) * grad * grad
    first_hat = first_new * (1.0 / (1.0 - beta_first**STEP))
    second_hat = second_new * (1.0 / (1.0 - beta_second**STEP))
    master_new = master - learn_rate * (
        first_hat / (jnp.sqrt(second_hat) + adam_eps) + decay_rate * master
    )
    return master_new, first_new, second_new, master_new.astype(LOW)


def dense_update_kernel(master, first, second, terms, *outs):
    rows = master.shape[0]
    grad = jnp.sum(terms[...].astype(F32), axis=0)[:rows]
    for out, value in zip(outs, adamw_values(master[...], first[...], second[...], grad)):
        out[...] = value


def dense_update(after, master, first, second, terms):
    shape = (master.shape[0] // 128, 128)
    results = ordered(
        dense_update_kernel, 4, after,
        name="dense_update",
        out_shape=[jax.ShapeDtypeStruct(shape, t) for t in (F32, F32, F32, LOW)],
        in_specs=[VMEM] * 4,
        out_specs=[VMEM] * 4,
        compiler_params=params(),
        cost_estimate=cost(1e6, 4e6),
    )(*(a.reshape(shape) for a in (master, first, second)), terms)
    return tuple(r.reshape(master.shape) for r in results)


def expert_update(after, core, master, first, second, stays, arrived, axis):
    rows, columns = master.shape[1:]
    if axis == 1:
        blocks, width = 4, columns // 4
        half = (rows, width // 2)
    else:
        blocks, width = 3, columns // 3
        half = (rows // 2, width)

    def kernel(core_ref, master, first, second, stays, arrived, *outs):
        near, far = stays[...], arrived[...].astype(F32)
        swapped = core_ref[0] == 1
        grad = jnp.concatenate(
            [jnp.where(swapped, far, near), jnp.where(swapped, near, far)], axis=axis
        )
        values = adamw_values(master[0], first[0], second[0], grad)
        for out, value in zip(outs, values):
            out[0] = value

    wide = pl.BlockSpec((1, rows, width), lambda i: (0, 0, i))
    slim = pl.BlockSpec(half, lambda i: (0, i))
    return tuple(
        ordered(
        kernel, 6, after,
            name="update_in" if axis == 1 else "update_out",
            out_shape=[jax.ShapeDtypeStruct(master.shape, t) for t in (F32, F32, F32, LOW)],
            grid=(blocks,),
            in_specs=[SMEM, wide, wide, wide, slim, slim],
            out_specs=[wide] * 4,
            compiler_params=params(),
            cost_estimate=cost(2e7, 18e6),
        )(core, master, first, second, stays, arrived)
    )


def swap_core(block):
    return lax.ppermute(block, "c", [(0, 1), (1, 0)])


KINDS = (0, 1, 1, 0)


def to_neighbours(shard):
    moves = []
    for z, kind in enumerate(KINDS):
        moves.append(((z - 1) % 4 * 2 + kind, z * 2 + kind))
        moves.append(((z + 1) % 4 * 2 + kind, z * 2 + 1 - kind))
    return lax.ppermute(shard, DEPTH + ("c",), moves)


def to_opposite(shard):
    moves = []
    for z, kind in enumerate(KINDS):
        source = kind if z % 2 else 1 - kind
        moves.append((z * 2 + source, (3 - z) * 2 + 1 - kind))
    return lax.ppermute(shard, DEPTH + ("c",), moves)


def swap_pair(block):
    return lax.ppermute(block, DEPTH, [(z, 3 - z) for z in range(4)])


def swap_low(block):
    return lax.ppermute(block, "zl", [(0, 1), (1, 0)])


def exchange(rows):
    cut = rows.reshape(-1, CAP, rows.shape[1])
    cut = lax.all_to_all(cut, PLANE, split_axis=0, concat_axis=0, tiled=True)
    return cut.reshape(rows.shape)


def tie(array, *others):
    return lax.optimization_barrier((array,) + others)[0]


def word(*values):
    return jnp.stack([jnp.asarray(v, jnp.int32) for v in values])


def body(
    tokens,
    segment_ids,
    routes,
    cotangent,
    w_qkv,
    w_attn_out,
    w_router,
    norm_gains,
    frozen_in,
    frozen_out,
    new_in,
    new_out,
    dense_master,
    dense_first,
    dense_second,
    master_in,
    first_in,
    second_in,
    master_out,
    first_out,
    second_out,
):
    core, zh, zl = (lax.axis_index(a) for a in ("c", "zh", "zl"))
    z = 2 * zh + zl
    kind = zh ^ zl
    same = jnp.where(kind == core, 1, 0)
    home = word(z, same, core)
    core_word, same_word, zl_word = word(core), word(same), word(zl)
    routes = routes.T
    w_router = w_router.T

    in_near = to_neighbours(new_in)
    in_mates, out_mates = [swap_core(new_in)], [swap_core(new_out)]
    attn_in, qkv_low, mixed_low, lse, middle, ffn_in, plan, sent, frozen_sent = dense_forward(
        (), word(zh), tokens, segment_ids, routes, cotangent, w_qkv, w_attn_out, w_router, norm_gains
    )
    received = exchange(sent)
    in_across = to_opposite(tie(in_near, plan))
    in_mates.append(swap_core(tie(in_near, plan)))
    frozen_back = frozen_expert(
        (in_mates[0], out_mates[0], in_mates[1]), frozen_sent, frozen_in, frozen_out
    )
    in_mates.append(swap_core(tie(in_across, frozen_back)))
    out_near = to_neighbours(tie(new_out, in_across))
    half_in = build_weight(
        (frozen_back,), "build_in", home, (new_in, in_near, in_across, *in_mates), False
    )
    received = tie(received, frozen_back, in_across)
    hidden, slope, rows, grads = expert_up((), received, swap_core(received), half_in)
    out_across = to_opposite(tie(out_near, hidden))
    out_mates.append(swap_core(tie(out_near, hidden)))
    count = received.shape[0]

    def half_grad(left, right, half):
        cut = left.shape[1] // 2
        return mm_tn(lax.dynamic_slice(left, (0, half * cut), (left.shape[0], cut)), right)

    out_away = half_grad(hidden, grads, 1 - zh).astype(LOW)
    out_arrived = swap_pair(out_away)
    out_mates.append(swap_core(tie(out_across, out_away)))
    half_out = build_weight(
        (out_away,), "build_out", home, (new_out, out_near, out_across, *out_mates), True
    )

    result_arrived = swap_core(mm(hidden[count:], half_out).astype(LOW))
    pre = (mm_nt(grads, half_out) * slope.astype(F32)).astype(LOW)
    result = (mm(hidden[:count], half_out) + result_arrived.astype(F32)).astype(LOW)
    back_arrived = swap_core(mm_nt(pre[count:], half_in).astype(LOW))
    in_away = half_grad(rows, pre, 1 - zh).astype(LOW)
    in_arrived = swap_pair(in_away)
    back = (mm_nt(pre[:count], half_in) + back_arrived.astype(F32)).astype(LOW)
    value = jnp.sum(grads[:count].astype(F32) * result.astype(F32), axis=1, keepdims=True)
    merged = jnp.concatenate([back, extra_terms(value), result], axis=1)
    back = exchange(tie(merged, in_away))

    out_kept = half_grad(tie(hidden, merged), grads, zh)
    in_kept = half_grad(tie(rows, merged), pre, zh)
    out_mine, out_other = reduce_first((merged,), zl_word, out_kept, out_arrived, 10e9)
    in_mine, in_other = reduce_first((out_mine,), zl_word, in_kept, in_arrived, 10e9)
    out_other, in_other = swap_low(out_other), swap_low(in_other)

    input_grad, kept, away, activations = dense_backward(
        (in_mine,), core_word, dense_master.shape[0], plan, routes, segment_ids, cotangent, tokens, middle,
        mixed_low, ffn_in, lse, qkv_low, attn_in, w_qkv, w_attn_out, w_router, norm_gains, back, frozen_back,
    )
    arrived = swap_core(away)
    kept_first = kept
    kept = tie(kept, out_other, in_other)
    zero = marker((kept_first,))[0, 0]
    summed = (kept.astype(F32) + arrived.astype(F32) + zero).astype(LOW)
    terms = lax.all_to_all(summed, ("zh", "zl", "x", "y"), split_axis=0, concat_axis=0, tiled=True)
    out_stays, out_leaves = reduce_second((summed,), same_word, out_mine, out_other)
    out_mate_grad = swap_core(out_leaves)
    in_stays, in_leaves = reduce_second((out_stays,), same_word, in_mine, in_other)
    in_mate_grad = swap_core(in_leaves)
    out_new = expert_update(
        (in_stays,), core_word, master_out, first_out, second_out, out_stays, out_mate_grad, 0
    )
    in_new = expert_update(
        (out_new[0],), core_word, master_in, first_in, second_in, in_stays, in_mate_grad, 1
    )
    dense_new = dense_update((in_new[0],), dense_master, dense_first, dense_second, terms)
    return (activations, input_grad) + dense_new + in_new + out_new


def solution(mesh):
    fine = Mesh(mesh.devices.reshape(2, 2, 4, 4, 2), ALL)
    tokens = P(ALL, None)
    flat = P(ALL)
    expert = P(("x", "y", "c"), DEPTH, None)
    return jax.shard_map(
        body,
        mesh=fine,
        in_specs=(tokens,) * 4 + (P(),) * 6 + (expert,) * 2 + (flat,) * 3 + (expert,) * 6,
        out_specs=(tokens,) * 2 + (flat,) * 4 + (expert,) * 8,
        check_vma=False,
    )
```

```python
import math

import jax
import jax.numpy as jnp
from jax import lax
from jax.experimental import pallas as pl
from jax.experimental.pallas import tpu as pltpu
from jax.sharding import Mesh
from jax.sharding import PartitionSpec as P

HEAD_DIM = 64
STEP = 5


norm_eps = 1e-05
learn_rate = 0.02
beta_first = 0.5
beta_second = 0.5
adam_eps = 1e-08
decay_rate = 0.1


PLANE = ("zl", "x", "y")
DEPTH = ("zh", "zl")
ALL = ("zh", "zl", "x", "y", "c")
CAP = 24
PAIRS = 6
EXTRA = 128
VMEM = pl.BlockSpec(memory_space=pltpu.VMEM)
SMEM = pl.BlockSpec(memory_space=pltpu.SMEM)
HBM = pl.BlockSpec(memory_space=pl.ANY)
F32 = jnp.float32
LOW = jnp.bfloat16


def params(**more):
    return pltpu.CompilerParams(vmem_limit_bytes=56 * 1024 * 1024, **more)


def ordered(kernel, count, after, **call):
    extra = len(after)

    def inner(*refs):
        return kernel(*refs[:count], *refs[count + extra :])

    call["in_specs"] = list(call["in_specs"]) + [pl.BlockSpec(memory_space=pl.ANY)] * extra
    made = pl.pallas_call(inner, **call)
    return lambda *arrays: made(*arrays, *after)


def cost(flops, moved):
    return pl.CostEstimate(flops=int(flops), bytes_accessed=int(moved), transcendentals=0)


def mm(left, right):
    return jnp.dot(left, right, preferred_element_type=F32)


def mm_nt(left, right):
    return lax.dot_general(left, right, (((1,), (1,)), ((), ())), preferred_element_type=F32)


def mm_tn(left, right):
    return lax.dot_general(left, right, (((0,), (0,)), ((), ())), preferred_element_type=F32)


def iota(shape, axis):
    return lax.broadcasted_iota(jnp.int32, shape, axis)


def normed(values):
    centered = values - jnp.mean(values, axis=1, keepdims=True)
    scale = lax.rsqrt(jnp.mean(centered * centered, axis=1, keepdims=True) + norm_eps)
    return centered * scale, scale


def norm_backward(values, gain, upstream):
    hat, scale = normed(values)
    gain_grad = jnp.sum(upstream * hat, axis=0, keepdims=True)
    inner = upstream * gain
    mean_inner = jnp.mean(inner, axis=1, keepdims=True)
    mean_hat = jnp.mean(inner * hat, axis=1, keepdims=True)
    return scale * (inner - mean_inner - hat * mean_hat), gain_grad


def as_column(row, eye):
    return jnp.sum(jnp.where(eye, row, jnp.zeros_like(row)), axis=1, keepdims=True)


def as_row(column, eye):
    return jnp.sum(jnp.where(eye, column, jnp.zeros_like(column)), axis=0, keepdims=True)


def attention_mask(segment_row):
    count = segment_row.shape[1]
    down, across = iota((count, count), 0), iota((count, count), 1)
    eye = down == across
    column = jnp.sum(jnp.where(eye, segment_row, 0), axis=1, keepdims=True)
    return (down >= across) & (column == segment_row), eye


def dense_forward_kernel(
    zh_ref, tokens, segments, routes, cotangent, w_qkv, w_out, w_router, gains,
    attn_in_o, qkv_o, mixed_o, lse_o, middle_o, ffn_o, plan_o, sent_o, frozen_sent_o,
):
    width = tokens.shape[1]
    count = tokens.shape[0]
    inputs = tokens[...].astype(F32)
    hat, unused = normed(inputs)
    attn_in = (hat * gains[0:1, :]).astype(LOW)
    attn_in_o[...] = attn_in
    qkv_o[...] = mm(attn_in, w_qkv[...]).astype(LOW)
    allowed, eye = attention_mask(segments[...])
    lane = iota((count, 128), 1)
    low_lanes = lane < HEAD_DIM
    lse_all = jnp.zeros((count, 128), F32)
    for pair in range(width // 128):
        at = slice(128 * pair, 128 * pair + 128)
        queries = qkv_o[:, at] * jnp.asarray(HEAD_DIM**-0.5, LOW)
        keys = qkv_o[:, width + 128 * pair : width + 128 * pair + 128]
        values = qkv_o[:, 2 * width + 128 * pair : 2 * width + 128 * pair + 128]
        outs = []
        for half in range(2):
            mine = low_lanes if half == 0 else ~low_lanes
            scores = mm_nt(jnp.where(mine, queries, jnp.zeros_like(queries)), keys)
            scores = jnp.where(allowed, scores, -1e30)
            top = jnp.max(scores, axis=1, keepdims=True)
            raised = jnp.exp(scores - top)
            total = jnp.sum(raised, axis=1, keepdims=True)
            probs = (raised * (1.0 / total)).astype(LOW)
            outs.append(mm(probs, values))
            lse_all = jnp.where(lane == 2 * pair + half, top + jnp.log(total), lse_all)
        mixed_o[:, at] = jnp.where(low_lanes, outs[0], outs[1]).astype(LOW)
    lse_o[...] = lse_all
    middle = inputs + mm(mixed_o[...], w_out[...])
    middle_o[...] = middle
    hat, unused = normed(middle)
    ffn = (hat * gains[1:2, :]).astype(LOW)
    ffn_o[...] = ffn
    logits = mm_nt(ffn, w_router[...])
    experts = iota(logits.shape, 1)
    lists = [as_column(routes[k : k + 1, :], eye) for k in range(2)]
    picks = [experts == column for column in lists]
    chosen = [jnp.sum(jnp.where(p, logits, 0.0), axis=1, keepdims=True) for p in picks]
    top = jnp.maximum(chosen[0], chosen[1])
    raised = [jnp.exp(c - top) for c in chosen]
    gates = [r / (raised[0] + raised[1]) for r in raised]
    named = (picks[0] | picks[1]).astype(F32).astype(LOW)
    earlier = (iota((count, count), 0) > iota((count, count), 1)).astype(F32).astype(LOW)
    before = mm(earlier, named)
    zh = zh_ref[0]
    new_place, old_place = [], []
    for k in range(2):
        route = lists[k]
        slot = jnp.sum(jnp.where(picks[k], before, 0.0), axis=1, keepdims=True).astype(jnp.int32)
        fresh = route - 1
        block = 16 * ((fresh & 1) ^ zh) + lax.shift_right_arithmetic(fresh, 1)
        new_place.append(jnp.where(route > 0, block * CAP + slot, -1))
        old_place.append(jnp.where(route > 0, -1, slot))
    columns = gates + [p.astype(F32) for p in new_place + old_place]
    plan = jnp.zeros((count, 128), F32)
    for i, column in enumerate(columns):
        plan = jnp.where(lane == i, column, plan)
    plan_o[...] = plan
    up = cotangent[...].astype(F32)
    scaled = [(g * up).astype(LOW) for g in gates]
    for places, ref in ((new_place, sent_o), (old_place, frozen_sent_o)):
        slots = iota((ref.shape[0], count), 0)
        spread = [(slots == as_row(p, eye)).astype(F32).astype(LOW) for p in places]
        ref[:, :width] = mm(spread[0] + spread[1], ffn).astype(LOW)
        ref[:, width:] = (mm(spread[0], scaled[0]) + mm(spread[1], scaled[1])).astype(LOW)


def dense_forward(after, zh, tokens, segments, routes, cotangent, w_qkv, w_out, w_router, gains):
    count, width = tokens.shape
    slots = (w_router.shape[0] - 1) * CAP
    shapes = [
        ((count, width), LOW), ((count, 3 * width), LOW), ((count, width), LOW), ((count, 128), F32),
        ((count, width), F32), ((count, width), LOW), ((count, 128), F32),
        ((slots, 2 * width), LOW), ((CAP, 2 * width), LOW),
    ]
    return ordered(
        dense_forward_kernel, 9, after,
        name="dense_forward",
        out_shape=[jax.ShapeDtypeStruct(s, t) for s, t in shapes],
        in_specs=[SMEM] + [VMEM] * 8,
        out_specs=[VMEM] * len(shapes),
        compiler_params=params(),
        cost_estimate=cost(8e9, 30e6),
    )(zh, tokens, segments, routes, cotangent, w_qkv, w_out, w_router, gains)


def dense_backward_kernel(
    core_ref, plan, routes, segments, cotangent, tokens, middle, mixed, ffn, lse, qkv, attn_in,
    w_qkv, w_out, w_router, gains, back, frozen_back,
    input_grad_o, kept_o, away_o, active_o,
    flat, gqkv, weight, kept, away, sems,
):
    count, width = tokens.shape
    weight_copy = pltpu.make_async_copy(w_qkv, weight, sems.at[0])
    weight_copy.start()
    expert_total = w_router.shape[0]
    up = cotangent[...].astype(F32)
    gates = [plan[:, k : k + 1] for k in range(2)]
    new_place = [plan[:, 2 + k : 3 + k].astype(jnp.int32) for k in range(2)]
    old_place = [plan[:, 4 + k : 5 + k].astype(jnp.int32) for k in range(2)]
    allowed, eye = attention_mask(segments[...])

    grad_ffn = jnp.zeros((count, width), F32)
    weighted = [jnp.zeros((count, 1), F32) for k in range(2)]
    active = middle[...]
    for places, ref in ((new_place, back), (old_place, frozen_back)):
        size = ref.shape[0]
        slots = iota((count, size), 1)
        for k in range(2):
            choice = (slots == places[k]).astype(F32).astype(LOW)
            picked = mm(choice, ref[...])
            grad_ffn = grad_ffn + picked[:, :width]
            tail = picked[:, width : width + EXTRA]
            weighted[k] = weighted[k] + jnp.sum(tail, axis=1, keepdims=True)
            active = active + gates[k] * picked[:, width + EXTRA :]
    active_o[...] = active.astype(LOW)
    both = weighted[0] + weighted[1]
    experts = iota((count, expert_total), 1)
    grad_logits = jnp.zeros((count, expert_total), F32)
    for k in range(2):
        grad_logits = jnp.where(
            experts == as_column(routes[k : k + 1, :], eye), weighted[k] - gates[k] * both, grad_logits
        )
    grad_logits = grad_logits.astype(LOW)
    grad_ffn = grad_ffn + mm(grad_logits, w_router[...])
    grad_norm, gain_ffn = norm_backward(middle[...], gains[1:2, :], grad_ffn)
    grad_middle = up + grad_norm
    grad_branch = grad_middle.astype(LOW)

    blocks = width // 128
    first_row = 3 * blocks * width
    attn_out_grad = mm_tn(mixed[...], grad_branch)
    for j in range(blocks):
        flat[pl.ds(first_row + j, width, stride=blocks), :] = attn_out_grad[:, 128 * j : 128 * j + 128]
    router_row = first_row + blocks * width
    router_rows = width * expert_total // 128
    padded_logits = jnp.concatenate(
        [grad_logits, jnp.zeros((count, 128 - expert_total), LOW)], axis=1
    )
    router_grad = mm_tn(ffn[...], padded_logits)
    feature = iota((width, 128), 0)
    lane_w = iota((width, 128), 1)
    start = feature * expert_total
    offset = start & 127
    turned = jnp.take_along_axis(router_grad, (lane_w - offset) & 127, axis=1)
    wrapped = lane_w < offset
    row_of = lax.shift_right_logical(iota((router_rows, width), 1) * expert_total, 7)
    row_here = iota((router_rows, width), 0)
    here = (row_of == row_here).astype(F32)
    after = (row_of + 1 == row_here).astype(F32)
    exact = lambda a, b: jnp.dot(a, b, precision=lax.Precision.HIGHEST, preferred_element_type=F32)
    flat[router_row : router_row + router_rows, :] = exact(
        here, jnp.where(wrapped, 0.0, turned)
    ) + exact(after, jnp.where(wrapped, turned, 0.0))
    gain_row = router_row + router_rows

    grad_mixed = mm_nt(grad_branch, w_out[...]).astype(LOW)
    lane = iota((count, 128), 1)
    low_lanes = lane < HEAD_DIM
    scale = HEAD_DIM**-0.5
    for pair in range(blocks):
        at = slice(128 * pair, 128 * pair + 128)
        queries = qkv[:, at] * jnp.asarray(scale, LOW)
        keys = qkv[:, width + 128 * pair : width + 128 * pair + 128]
        values = qkv[:, 2 * width + 128 * pair : 2 * width + 128 * pair + 128]
        grads = grad_mixed[:, at]
        grad_q = jnp.zeros((count, 128), F32)
        grad_k = jnp.zeros((count, 128), F32)
        grad_v = jnp.zeros((count, 128), F32)
        for half in range(2):
            mine = low_lanes if half == 0 else ~low_lanes
            only = lambda v: jnp.where(mine, v, jnp.zeros_like(v))
            q_half, g_half, k_half = only(queries), only(grads), only(keys)
            scores = jnp.where(allowed, mm_nt(q_half, keys), -1e30)
            head = 2 * pair + half
            probs = jnp.exp(scores - lse[:, head : head + 1])
            grad_probs = mm_nt(g_half, values)
            grad_v = grad_v + mm_tn(probs.astype(LOW), g_half)
            dots = jnp.sum(probs * grad_probs, axis=1, keepdims=True)
            grad_scores = (probs * (grad_probs - dots)).astype(LOW)
            grad_q = grad_q + mm(grad_scores, k_half)
            grad_k = grad_k + mm_tn(grad_scores, q_half)
        gqkv[:, at] = (grad_q * scale).astype(LOW)
        gqkv[:, width + 128 * pair : width + 128 * pair + 128] = grad_k.astype(LOW)
        gqkv[:, 2 * width + 128 * pair : 2 * width + 128 * pair + 128] = grad_v.astype(LOW)
    for j in range(0, 3 * blocks, 2):
        piece = mm_tn(attn_in[...], gqkv[:, 128 * j : 128 * j + 256])
        flat[pl.ds(j, width, stride=3 * blocks), :] = piece[:, :128]
        flat[pl.ds(j + 1, width, stride=3 * blocks), :] = piece[:, 128:]
    core = core_ref[0]
    rows = flat.shape[0] // 128
    pairs, padded = kept.shape[:2]

    def move(i):
        kept[pl.ds(i, 1)] = flat[pl.ds((2 * i + core) * rows, padded), :].astype(LOW)[None]
        away[pl.ds(i, 1)] = flat[pl.ds((2 * i + 1 - core) * rows, padded), :].astype(LOW)[None]

    pl.loop(0, pairs - 1)(move)
    early, last_one = pl.ds(0, pairs - 1), pl.ds(pairs - 1, 1)
    copies = [
        pltpu.make_async_copy(a.at[part], b.at[part], sems.at[1 + i])
        for i, (a, b, part) in enumerate(
            ((away, away_o, early), (kept, kept_o, early), (away, away_o, last_one), (kept, kept_o, last_one))
        )
    ]
    copies[0].start()
    copies[1].start()
    weight_copy.wait()
    grad_attn = mm_nt(gqkv[...], weight[...])
    grad_norm, gain_attn = norm_backward(tokens[...].astype(F32), gains[0:1, :], grad_attn)
    input_grad_o[...] = grad_middle + grad_norm
    for j in range(blocks):
        flat[gain_row + j : gain_row + j + 1, :] = gain_attn[:, 128 * j : 128 * j + 128]
        flat[gain_row + blocks + j : gain_row + blocks + j + 1, :] = gain_ffn[:, 128 * j : 128 * j + 128]
    last = gain_row + 2 * blocks
    flat[last:, :] = jnp.zeros((flat.shape[0] - last, 128), F32)

    move(pairs - 1)
    copies[2].start()
    copies[3].start()
    for copy in copies:
        copy.wait()


def dense_backward(after, core, dense_rows, *arrays):
    count, width = arrays[4].shape
    rows = dense_rows // 128
    padded = (rows + 7) // 8 * 8
    return ordered(
        dense_backward_kernel, 1 + len(arrays), after,
        name="dense_backward",
        out_shape=[
            jax.ShapeDtypeStruct((count, width), F32),
            jax.ShapeDtypeStruct((64, padded, 128), LOW),
            jax.ShapeDtypeStruct((64, padded, 128), LOW),
            jax.ShapeDtypeStruct((count, width), LOW),
        ],
        in_specs=[SMEM] + [VMEM] * 11 + [HBM] + [VMEM] * (len(arrays) - 12),
        out_specs=[VMEM, HBM, HBM, VMEM],
        scratch_shapes=[
            pltpu.VMEM((rows * 128 + padded - rows, 128), F32),
            pltpu.VMEM((count, 3 * width), LOW),
            pltpu.VMEM((width, 3 * width), LOW),
            pltpu.VMEM((64, padded, 128), LOW),
            pltpu.VMEM((64, padded, 128), LOW),
            pltpu.SemaphoreType.DMA((5,)),
        ],
        compiler_params=params(),
        cost_estimate=cost(12e9, 40e6),
    )(core, *arrays)


def gelu_pair(pre):
    area = 0.5 + 0.5 * lax.erf(pre * (0.5**0.5))
    density = jnp.exp(-0.5 * pre * pre) * (1.0 / (2.0 * math.pi) ** 0.5)
    return pre * area, area + pre * density


def build_weight(after, name, home, sources, by_rows):
    rows, cols = sources[0].shape[1:]

    def kernel(home_ref, local, near, across, local_mate, near_mate, across_mate, out, sems):
        z, half = home_ref[0], home_ref[2]

        def move(blocks):
            copies = []
            for step, shard in enumerate(blocks):
                if by_rows:
                    start = pl.multiple_of(half * (rows // 2), 64)
                    place = pl.ds(pl.multiple_of(((z + step) & 3) * (rows // 2), 64), rows // 2)
                    copies.append((shard.at[0, pl.ds(start, rows // 2), :], out.at[place, :]))
                else:
                    place = pl.ds(pl.multiple_of(((z + step) & 3) * rows, 64), rows)
                    for block in range(4):
                        start = pl.multiple_of((2 * block + half) * (cols // 8), 128)
                        to = slice(block * (cols // 8), (block + 1) * (cols // 8))
                        copies.append((shard.at[0, :, pl.ds(start, cols // 8)], out.at[place, to]))
            made = [pltpu.make_async_copy(a, b, sems.at[i]) for i, (a, b) in enumerate(copies)]
            for copy in made:
                copy.start()
            for copy in made:
                copy.wait()

        pl.when(home_ref[1] == 1)(lambda: move((local, near_mate, across_mate, near)))
        pl.when(home_ref[1] == 0)(lambda: move((local_mate, near, across, near_mate)))

    shape = (2 * rows, cols) if by_rows else (4 * rows, cols // 2)
    return ordered(
        kernel, 7, after,
        name=name,
        out_shape=jax.ShapeDtypeStruct(shape, LOW),
        in_specs=[SMEM] + [HBM] * 6,
        out_specs=VMEM,
        scratch_shapes=[pltpu.SemaphoreType.DMA((16,))],
        compiler_params=params(),
        cost_estimate=cost(1e5 if by_rows else 19e9, 8e6),
    )(home, *sources)


def expert_up_kernel(own, mate, weight, hidden_o, slope_o, rows_o, grads_o):
    width = weight.shape[0]
    both = jnp.where(pl.program_id(0) < pl.num_programs(0) // 2, own[...], mate[...])
    rows = both[:, :width]
    rows_o[...] = rows
    grads_o[...] = both[:, width:]
    hidden, slope = gelu_pair(mm(rows, weight[...]))
    hidden_o[...] = hidden.astype(LOW)
    slope_o[...] = slope.astype(LOW)


def expert_up(after, own, mate, weight):
    count, width = own.shape[0], weight.shape[0]
    hidden = weight.shape[1]
    step = 256
    half = count // step
    block = lambda cols: pl.BlockSpec((step, cols), lambda i: (i, 0))
    return ordered(
        expert_up_kernel, 3, after,
        name="expert_up",
        out_shape=[jax.ShapeDtypeStruct((2 * count, n), LOW) for n in (hidden, hidden, width, width)],
        grid=(2 * half,),
        in_specs=[
            pl.BlockSpec((step, 2 * width), lambda i: (jnp.minimum(i, half - 1), 0)),
            pl.BlockSpec((step, 2 * width), lambda i: (jnp.maximum(i - half, 0), 0)),
            pl.BlockSpec((width, hidden), lambda i: (0, 0)),
        ],
        out_specs=[block(n) for n in (hidden, hidden, width, width)],
        compiler_params=params(),
        cost_estimate=cost(12e9, 20e6),
    )(own, mate, weight)


def split_three(value):
    high = lax.reduce_precision(value, 8, 7)
    mid = lax.reduce_precision(value - high, 8, 7)
    return high, mid, value - high - mid


def extra_terms(value):
    lane = iota((value.shape[0], EXTRA), 1)
    extra = jnp.zeros((value.shape[0], EXTRA), F32)
    for i, term in enumerate(split_three(value)):
        extra = jnp.where(lane == i, term, extra)
    return extra.astype(LOW)


def reduce_first(after, low, kept, arrived, work=1e6):
    rows, columns = kept.shape[0] // 2, kept.shape[1]

    def kernel(low_ref, kept, arrived, mine, other):
        for out, which in ((mine, low_ref[0]), (other, 1 - low_ref[0])):
            at = pl.ds(pl.multiple_of(which * rows, 64), rows)
            out[...] = (kept[at, :] + arrived[at, :].astype(F32)).astype(out.dtype)

    return ordered(
        kernel, 3, after,
        name="reduce_first",
        out_shape=[jax.ShapeDtypeStruct((rows, columns), t) for t in (F32, LOW)],
        in_specs=[SMEM, VMEM, VMEM],
        out_specs=[VMEM] * 2,
        compiler_params=params(),
        cost_estimate=cost(work, 6e6),
    )(low, kept, arrived)


def reduce_second(after, same, mine, other):
    def kernel(same_ref, mine, other, stays, leaves):
        straight = same_ref[0] == 1
        near, far = mine[...], other[...].astype(F32)
        stays[...] = jnp.where(straight, near, far)
        leaves[...] = jnp.where(straight, far, near).astype(LOW)

    return ordered(
        kernel, 3, after,
        name="reduce_second",
        out_shape=[jax.ShapeDtypeStruct(mine.shape, t) for t in (F32, LOW)],
        in_specs=[SMEM, VMEM, VMEM],
        out_specs=[VMEM] * 2,
        compiler_params=params(),
        cost_estimate=cost(1e6, 6e6),
    )(same, mine, other)


def frozen_kernel(rows, grads, w_in, w_out, back_o, result_sum, back_sum, value_sum):
    step = pl.program_id(0)

    @pl.when(step == 0)
    def clear():
        result_sum[...] = jnp.zeros_like(result_sum)
        back_sum[...] = jnp.zeros_like(back_sum)
        value_sum[...] = jnp.zeros_like(value_sum)

    hidden, slope = gelu_pair(mm(rows[...], w_in[...]))
    hidden = hidden.astype(LOW)
    result_sum[...] += mm(hidden, w_out[...])
    grad_hidden = mm_nt(grads[...], w_out[...])
    value_sum[...] += jnp.sum(hidden.astype(F32) * grad_hidden, axis=1, keepdims=True)
    back_sum[...] += mm_nt((grad_hidden * slope).astype(LOW), w_in[...])

    @pl.when(step == pl.num_programs(0) - 1)
    def finish():
        width = back_sum.shape[1]
        back_o[:, :width] = back_sum[...].astype(LOW)
        back_o[:, width : width + EXTRA] = extra_terms(value_sum[:, 0:1])
        back_o[:, width + EXTRA :] = result_sum[...].astype(LOW)


def frozen_expert(after, sent, w_in, w_out):
    count, width = sent.shape[0], w_in.shape[0]
    wide = w_in.shape[1]
    step = 512
    small = pl.BlockSpec((count, width), lambda i: (0, 0))
    return ordered(
        frozen_kernel, 4, after,
        name="frozen_expert",
        out_shape=jax.ShapeDtypeStruct((count, 2 * width + EXTRA), LOW),
        grid=(wide // step,),
        in_specs=[
            small, pl.BlockSpec((count, width), lambda i: (0, 1)),
            pl.BlockSpec((width, step), lambda i: (0, i)),
            pl.BlockSpec((step, width), lambda i: (i, 0)),
        ],
        out_specs=pl.BlockSpec((count, 2 * width + EXTRA), lambda i: (0, 0)),
        scratch_shapes=[
            pltpu.VMEM((count, width), F32),
            pltpu.VMEM((count, width), F32),
            pltpu.VMEM((count, EXTRA), F32),
        ],
        compiler_params=params(),
        cost_estimate=cost(4e9, 10e6),
    )(sent, sent, w_in, w_out)


def marker(after):
    def kernel(out):
        out[...] = jnp.zeros_like(out)

    return ordered(
        kernel, 0, after,
        name="marker",
        out_shape=jax.ShapeDtypeStruct((8, 128), F32),
        in_specs=[],
        out_specs=VMEM,
        compiler_params=params(),
        cost_estimate=cost(200e9, 4e3),
    )()


def adamw_values(master, first, second, grad):
    first_new = beta_first * first + (1.0 - beta_first) * grad
    second_new = beta_second * second + (1.0 - beta_second) * grad * grad
    first_hat = first_new * (1.0 / (1.0 - beta_first**STEP))
    second_hat = second_new * (1.0 / (1.0 - beta_second**STEP))
    master_new = master - learn_rate * (
        first_hat / (jnp.sqrt(second_hat) + adam_eps) + decay_rate * master
    )
    return master_new, first_new, second_new, master_new.astype(LOW)


def dense_update_kernel(master, first, second, terms, *outs):
    rows = master.shape[0]
    grad = jnp.sum(terms[...].astype(F32), axis=0)[:rows]
    for out, value in zip(outs, adamw_values(master[...], first[...], second[...], grad)):
        out[...] = value


def dense_update(after, master, first, second, terms):
    shape = (master.shape[0] // 128, 128)
    results = ordered(
        dense_update_kernel, 4, after,
        name="dense_update",
        out_shape=[jax.ShapeDtypeStruct(shape, t) for t in (F32, F32, F32, LOW)],
        in_specs=[VMEM] * 4,
        out_specs=[VMEM] * 4,
        compiler_params=params(),
        cost_estimate=cost(1e6, 4e6),
    )(*(a.reshape(shape) for a in (master, first, second)), terms)
    return tuple(r.reshape(master.shape) for r in results)


def expert_update(after, core, master, first, second, stays, arrived, axis):
    rows, columns = master.shape[1:]
    if axis == 1:
        blocks, width = 4, columns // 4
        half = (rows, width // 2)
    else:
        blocks, width = 3, columns // 3
        half = (rows // 2, width)

    def kernel(core_ref, master, first, second, stays, arrived, *outs):
        near, far = stays[...], arrived[...].astype(F32)
        swapped = core_ref[0] == 1
        grad = jnp.concatenate(
            [jnp.where(swapped, far, near), jnp.where(swapped, near, far)], axis=axis
        )
        values = adamw_values(master[0], first[0], second[0], grad)
        for out, value in zip(outs, values):
            out[0] = value

    wide = pl.BlockSpec((1, rows, width), lambda i: (0, 0, i))
    slim = pl.BlockSpec(half, lambda i: (0, i))
    return tuple(
        ordered(
        kernel, 6, after,
            name="update_in" if axis == 1 else "update_out",
            out_shape=[jax.ShapeDtypeStruct(master.shape, t) for t in (F32, F32, F32, LOW)],
            grid=(blocks,),
            in_specs=[SMEM, wide, wide, wide, slim, slim],
            out_specs=[wide] * 4,
            compiler_params=params(),
            cost_estimate=cost(2e7, 18e6),
        )(core, master, first, second, stays, arrived)
    )


def swap_core(block):
    return lax.ppermute(block, "c", [(0, 1), (1, 0)])


KINDS = (0, 1, 1, 0)


def to_neighbours(shard):
    moves = []
    for z, kind in enumerate(KINDS):
        moves.append(((z - 1) % 4 * 2 + kind, z * 2 + kind))
        moves.append(((z + 1) % 4 * 2 + kind, z * 2 + 1 - kind))
    return lax.ppermute(shard, DEPTH + ("c",), moves)


def to_opposite(shard):
    moves = []
    for z, kind in enumerate(KINDS):
        source = kind if z % 2 else 1 - kind
        moves.append((z * 2 + source, (3 - z) * 2 + 1 - kind))
    return lax.ppermute(shard, DEPTH + ("c",), moves)


def swap_pair(block):
    return lax.ppermute(block, DEPTH, [(z, 3 - z) for z in range(4)])


def swap_low(block):
    return lax.ppermute(block, "zl", [(0, 1), (1, 0)])


def exchange(rows):
    cut = rows.reshape(-1, CAP, rows.shape[1])
    cut = lax.all_to_all(cut, PLANE, split_axis=0, concat_axis=0, tiled=True)
    return cut.reshape(rows.shape)


def tie(array, *others):
    return lax.optimization_barrier((array,) + others)[0]


def word(*values):
    return jnp.stack([jnp.asarray(v, jnp.int32) for v in values])


def body(
    tokens,
    segment_ids,
    routes,
    cotangent,
    w_qkv,
    w_attn_out,
    w_router,
    norm_gains,
    frozen_in,
    frozen_out,
    new_in,
    new_out,
    dense_master,
    dense_first,
    dense_second,
    master_in,
    first_in,
    second_in,
    master_out,
    first_out,
    second_out,
):
    core, zh, zl = (lax.axis_index(a) for a in ("c", "zh", "zl"))
    z = 2 * zh + zl
    kind = zh ^ zl
    same = jnp.where(kind == core, 1, 0)
    home = word(z, same, core)
    core_word, same_word, zl_word = word(core), word(same), word(zl)
    routes = routes.T
    w_router = w_router.T

    in_near = to_neighbours(new_in)
    in_mates, out_mates = [swap_core(new_in)], [swap_core(new_out)]
    attn_in, qkv_low, mixed_low, lse, middle, ffn_in, plan, sent, frozen_sent = dense_forward(
        (), word(zh), tokens, segment_ids, routes, cotangent, w_qkv, w_attn_out, w_router, norm_gains
    )
    received = exchange(sent)
    in_across = to_opposite(tie(in_near, plan))
    in_mates.append(swap_core(tie(in_near, plan)))
    frozen_back = frozen_expert(
        (in_mates[0], out_mates[0], in_mates[1]), frozen_sent, frozen_in, frozen_out
    )
    in_mates.append(swap_core(tie(in_across, frozen_back)))
    out_near = to_neighbours(tie(new_out, in_across))
    half_in = build_weight(
        (frozen_back,), "build_in", home, (new_in, in_near, in_across, *in_mates), False
    )
    received = tie(received, frozen_back, in_across)
    received_mate = swap_core(received)
    hidden, slope, rows, grads = expert_up((out_near,), received, received_mate, half_in)
    out_across = to_opposite(tie(out_near, half_in))
    out_mates.append(swap_core(tie(out_near, half_in)))
    count = received.shape[0]

    def half_grad(left, right, half):
        cut = left.shape[1] // 2
        return mm_tn(lax.dynamic_slice(left, (0, half * cut), (left.shape[0], cut)), right)

    out_away = half_grad(hidden, grads, 1 - zh).astype(LOW)
    out_arrived = swap_pair(out_away)
    out_mates.append(swap_core(tie(out_across, out_away)))
    half_out = build_weight(
        (out_away,), "build_out", home, (new_out, out_near, out_across, *out_mates), True
    )

    result_arrived = swap_core(mm(hidden[count:], half_out).astype(LOW))
    pre = (mm_nt(grads, half_out) * slope.astype(F32)).astype(LOW)
    result = (mm(hidden[:count], half_out) + result_arrived.astype(F32)).astype(LOW)
    back_arrived = swap_core(mm_nt(pre[count:], half_in).astype(LOW))
    in_away = half_grad(rows, pre, 1 - zh).astype(LOW)
    in_arrived = swap_pair(in_away)
    back = (mm_nt(pre[:count], half_in) + back_arrived.astype(F32)).astype(LOW)
    value = jnp.sum(grads[:count].astype(F32) * result.astype(F32), axis=1, keepdims=True)
    merged = jnp.concatenate([back, extra_terms(value), result], axis=1)
    back = exchange(tie(merged, in_away))

    out_kept = half_grad(tie(hidden, merged), grads, zh)
    in_kept = half_grad(tie(rows, merged), pre, zh)
    out_mine, out_other = reduce_first((merged,), zl_word, out_kept, out_arrived, 10e9)
    in_mine, in_other = reduce_first((out_mine,), zl_word, in_kept, in_arrived, 10e9)
    out_other, in_other = swap_low(out_other), swap_low(in_other)

    input_grad, kept, away, activations = dense_backward(
        (in_mine,), core_word, dense_master.shape[0], plan, routes, segment_ids, cotangent, tokens, middle,
        mixed_low, ffn_in, lse, qkv_low, attn_in, w_qkv, w_attn_out, w_router, norm_gains, back, frozen_back,
    )
    arrived = swap_core(away)
    kept_first = kept
    kept = tie(kept, out_other, in_other)
    zero = marker((kept_first,))[0, 0]
    summed = (kept.astype(F32) + arrived.astype(F32) + zero).astype(LOW)
    terms = lax.all_to_all(summed, ("zh", "zl", "x", "y"), split_axis=0, concat_axis=0, tiled=True)
    out_stays, out_leaves = reduce_second((summed,), same_word, out_mine, out_other)
    out_mate_grad = swap_core(out_leaves)
    in_stays, in_leaves = reduce_second((out_stays,), same_word, in_mine, in_other)
    in_mate_grad = swap_core(in_leaves)
    out_new = expert_update(
        (in_stays,), core_word, master_out, first_out, second_out, out_stays, out_mate_grad, 0
    )
    in_new = expert_update(
        (out_new[0],), core_word, master_in, first_in, second_in, in_stays, in_mate_grad, 1
    )
    dense_new = dense_update((in_new[0],), dense_master, dense_first, dense_second, terms)
    return (activations, input_grad) + dense_new + in_new + out_new


def solution(mesh):
    fine = Mesh(mesh.devices.reshape(2, 2, 4, 4, 2), ALL)
    tokens = P(ALL, None)
    flat = P(ALL)
    expert = P(("x", "y", "c"), DEPTH, None)
    return jax.shard_map(
        body,
        mesh=fine,
        in_specs=(tokens,) * 4 + (P(),) * 6 + (expert,) * 2 + (flat,) * 3 + (expert,) * 6,
        out_specs=(tokens,) * 2 + (flat,) * 4 + (expert,) * 8,
        check_vma=False,
    )
```

```python
import math

import jax
import jax.numpy as jnp
from jax import lax
from jax.experimental import pallas as pl
from jax.experimental.pallas import tpu as pltpu
from jax.sharding import Mesh
from jax.sharding import PartitionSpec as P

HEAD_DIM = 64
STEP = 5


norm_eps = 1e-05
learn_rate = 0.02
beta_first = 0.5
beta_second = 0.5
adam_eps = 1e-08
decay_rate = 0.1


PLANE = ("zl", "x", "y")
DEPTH = ("zh", "zl")
ALL = ("zh", "zl", "x", "y", "c")
CAP = 24
PAIRS = 6
EXTRA = 128
VMEM = pl.BlockSpec(memory_space=pltpu.VMEM)
SMEM = pl.BlockSpec(memory_space=pltpu.SMEM)
HBM = pl.BlockSpec(memory_space=pl.ANY)
F32 = jnp.float32
LOW = jnp.bfloat16


def params(**more):
    return pltpu.CompilerParams(vmem_limit_bytes=56 * 1024 * 1024, **more)


def ordered(kernel, count, after, **call):
    extra = len(after)

    def inner(*refs):
        return kernel(*refs[:count], *refs[count + extra :])

    call["in_specs"] = list(call["in_specs"]) + [pl.BlockSpec(memory_space=pl.ANY)] * extra
    made = pl.pallas_call(inner, **call)
    return lambda *arrays: made(*arrays, *after)


def cost(flops, moved):
    return pl.CostEstimate(flops=int(flops), bytes_accessed=int(moved), transcendentals=0)


def mm(left, right):
    return jnp.dot(left, right, preferred_element_type=F32)


def mm_nt(left, right):
    return lax.dot_general(left, right, (((1,), (1,)), ((), ())), preferred_element_type=F32)


def mm_tn(left, right):
    return lax.dot_general(left, right, (((0,), (0,)), ((), ())), preferred_element_type=F32)


def iota(shape, axis):
    return lax.broadcasted_iota(jnp.int32, shape, axis)


def normed(values):
    centered = values - jnp.mean(values, axis=1, keepdims=True)
    scale = lax.rsqrt(jnp.mean(centered * centered, axis=1, keepdims=True) + norm_eps)
    return centered * scale, scale


def norm_backward(values, gain, upstream):
    hat, scale = normed(values)
    gain_grad = jnp.sum(upstream * hat, axis=0, keepdims=True)
    inner = upstream * gain
    mean_inner = jnp.mean(inner, axis=1, keepdims=True)
    mean_hat = jnp.mean(inner * hat, axis=1, keepdims=True)
    return scale * (inner - mean_inner - hat * mean_hat), gain_grad


def as_column(row, eye):
    return jnp.sum(jnp.where(eye, row, jnp.zeros_like(row)), axis=1, keepdims=True)


def as_row(column, eye):
    return jnp.sum(jnp.where(eye, column, jnp.zeros_like(column)), axis=0, keepdims=True)


def attention_mask(segment_row):
    count = segment_row.shape[1]
    down, across = iota((count, count), 0), iota((count, count), 1)
    eye = down == across
    column = jnp.sum(jnp.where(eye, segment_row, 0), axis=1, keepdims=True)
    return (down >= across) & (column == segment_row), eye


def dense_forward_kernel(
    zh_ref, tokens, segments, routes, cotangent, w_qkv, w_out, w_router, gains,
    attn_in_o, qkv_o, mixed_o, lse_o, middle_o, ffn_o, plan_o, sent_o, frozen_sent_o,
):
    width = tokens.shape[1]
    count = tokens.shape[0]
    inputs = tokens[...].astype(F32)
    hat, unused = normed(inputs)
    attn_in = (hat * gains[0:1, :]).astype(LOW)
    attn_in_o[...] = attn_in
    qkv_o[...] = mm(attn_in, w_qkv[...]).astype(LOW)
    allowed, eye = attention_mask(segments[...])
    lane = iota((count, 128), 1)
    low_lanes = lane < HEAD_DIM
    lse_all = jnp.zeros((count, 128), F32)
    for pair in range(width // 128):
        at = slice(128 * pair, 128 * pair + 128)
        queries = qkv_o[:, at] * jnp.asarray(HEAD_DIM**-0.5, LOW)
        keys = qkv_o[:, width + 128 * pair : width + 128 * pair + 128]
        values = qkv_o[:, 2 * width + 128 * pair : 2 * width + 128 * pair + 128]
        outs = []
        for half in range(2):
            mine = low_lanes if half == 0 else ~low_lanes
            scores = mm_nt(jnp.where(mine, queries, jnp.zeros_like(queries)), keys)
            scores = jnp.where(allowed, scores, -1e30)
            top = jnp.max(scores, axis=1, keepdims=True)
            raised = jnp.exp(scores - top)
            total = jnp.sum(raised, axis=1, keepdims=True)
            probs = (raised * (1.0 / total)).astype(LOW)
            outs.append(mm(probs, values))
            lse_all = jnp.where(lane == 2 * pair + half, top + jnp.log(total), lse_all)
        mixed_o[:, at] = jnp.where(low_lanes, outs[0], outs[1]).astype(LOW)
    lse_o[...] = lse_all
    middle = inputs + mm(mixed_o[...], w_out[...])
    middle_o[...] = middle
    hat, unused = normed(middle)
    ffn = (hat * gains[1:2, :]).astype(LOW)
    ffn_o[...] = ffn
    logits = mm_nt(ffn, w_router[...])
    experts = iota(logits.shape, 1)
    lists = [as_column(routes[k : k + 1, :], eye) for k in range(2)]
    picks = [experts == column for column in lists]
    chosen = [jnp.sum(jnp.where(p, logits, 0.0), axis=1, keepdims=True) for p in picks]
    top = jnp.maximum(chosen[0], chosen[1])
    raised = [jnp.exp(c - top) for c in chosen]
    gates = [r / (raised[0] + raised[1]) for r in raised]
    named = (picks[0] | picks[1]).astype(F32).astype(LOW)
    earlier = (iota((count, count), 0) > iota((count, count), 1)).astype(F32).astype(LOW)
    before = mm(earlier, named)
    zh = zh_ref[0]
    new_place, old_place = [], []
    for k in range(2):
        route = lists[k]
        slot = jnp.sum(jnp.where(picks[k], before, 0.0), axis=1, keepdims=True).astype(jnp.int32)
        fresh = route - 1
        block = 16 * ((fresh & 1) ^ zh) + lax.shift_right_arithmetic(fresh, 1)
        new_place.append(jnp.where(route > 0, block * CAP + slot, -1))
        old_place.append(jnp.where(route > 0, -1, slot))
    columns = gates + [p.astype(F32) for p in new_place + old_place]
    plan = jnp.zeros((count, 128), F32)
    for i, column in enumerate(columns):
        plan = jnp.where(lane == i, column, plan)
    plan_o[...] = plan
    up = cotangent[...].astype(F32)
    scaled = [(g * up).astype(LOW) for g in gates]
    for places, ref in ((new_place, sent_o), (old_place, frozen_sent_o)):
        slots = iota((ref.shape[0], count), 0)
        spread = [(slots == as_row(p, eye)).astype(F32).astype(LOW) for p in places]
        ref[:, :width] = mm(spread[0] + spread[1], ffn).astype(LOW)
        ref[:, width:] = (mm(spread[0], scaled[0]) + mm(spread[1], scaled[1])).astype(LOW)


def dense_forward(after, zh, tokens, segments, routes, cotangent, w_qkv, w_out, w_router, gains):
    count, width = tokens.shape
    slots = (w_router.shape[0] - 1) * CAP
    shapes = [
        ((count, width), LOW), ((count, 3 * width), LOW), ((count, width), LOW), ((count, 128), F32),
        ((count, width), F32), ((count, width), LOW), ((count, 128), F32),
        ((slots, 2 * width), LOW), ((CAP, 2 * width), LOW),
    ]
    return ordered(
        dense_forward_kernel, 9, after,
        name="dense_forward",
        out_shape=[jax.ShapeDtypeStruct(s, t) for s, t in shapes],
        in_specs=[SMEM] + [VMEM] * 8,
        out_specs=[VMEM] * len(shapes),
        compiler_params=params(),
        cost_estimate=cost(8e9, 30e6),
    )(zh, tokens, segments, routes, cotangent, w_qkv, w_out, w_router, gains)


def dense_backward_kernel(
    core_ref, plan, routes, segments, cotangent, tokens, middle, mixed, ffn, lse, qkv, attn_in,
    w_qkv, w_out, w_router, gains, back, frozen_back,
    input_grad_o, kept_o, away_o, active_o,
    flat, gqkv, weight, kept, away, sems,
):
    count, width = tokens.shape
    weight_copy = pltpu.make_async_copy(w_qkv, weight, sems.at[0])
    weight_copy.start()
    expert_total = w_router.shape[0]
    up = cotangent[...].astype(F32)
    gates = [plan[:, k : k + 1] for k in range(2)]
    new_place = [plan[:, 2 + k : 3 + k].astype(jnp.int32) for k in range(2)]
    old_place = [plan[:, 4 + k : 5 + k].astype(jnp.int32) for k in range(2)]
    allowed, eye = attention_mask(segments[...])

    grad_ffn = jnp.zeros((count, width), F32)
    weighted = [jnp.zeros((count, 1), F32) for k in range(2)]
    active = middle[...]
    for places, ref in ((new_place, back), (old_place, frozen_back)):
        size = ref.shape[0]
        slots = iota((count, size), 1)
        for k in range(2):
            choice = (slots == places[k]).astype(F32).astype(LOW)
            picked = mm(choice, ref[...])
            grad_ffn = grad_ffn + picked[:, :width]
            tail = picked[:, width : width + EXTRA]
            weighted[k] = weighted[k] + jnp.sum(tail, axis=1, keepdims=True)
            active = active + gates[k] * picked[:, width + EXTRA :]
    active_o[...] = active.astype(LOW)
    both = weighted[0] + weighted[1]
    experts = iota((count, expert_total), 1)
    grad_logits = jnp.zeros((count, expert_total), F32)
    for k in range(2):
        grad_logits = jnp.where(
            experts == as_column(routes[k : k + 1, :], eye), weighted[k] - gates[k] * both, grad_logits
        )
    grad_logits = grad_logits.astype(LOW)
    grad_ffn = grad_ffn + mm(grad_logits, w_router[...])
    grad_norm, gain_ffn = norm_backward(middle[...], gains[1:2, :], grad_ffn)
    grad_middle = up + grad_norm
    grad_branch = grad_middle.astype(LOW)

    blocks = width // 128
    first_row = 3 * blocks * width
    attn_out_grad = mm_tn(mixed[...], grad_branch)
    for j in range(blocks):
        flat[pl.ds(first_row + j, width, stride=blocks), :] = attn_out_grad[:, 128 * j : 128 * j + 128]
    router_row = first_row + blocks * width
    router_rows = width * expert_total // 128
    padded_logits = jnp.concatenate(
        [grad_logits, jnp.zeros((count, 128 - expert_total), LOW)], axis=1
    )
    router_grad = mm_tn(ffn[...], padded_logits)
    feature = iota((width, 128), 0)
    lane_w = iota((width, 128), 1)
    start = feature * expert_total
    offset = start & 127
    turned = jnp.take_along_axis(router_grad, (lane_w - offset) & 127, axis=1)
    wrapped = lane_w < offset
    row_of = lax.shift_right_logical(iota((router_rows, width), 1) * expert_total, 7)
    row_here = iota((router_rows, width), 0)
    here = (row_of == row_here).astype(F32)
    after = (row_of + 1 == row_here).astype(F32)
    exact = lambda a, b: jnp.dot(a, b, precision=lax.Precision.HIGHEST, preferred_element_type=F32)
    flat[router_row : router_row + router_rows, :] = exact(
        here, jnp.where(wrapped, 0.0, turned)
    ) + exact(after, jnp.where(wrapped, turned, 0.0))
    gain_row = router_row + router_rows

    grad_mixed = mm_nt(grad_branch, w_out[...]).astype(LOW)
    lane = iota((count, 128), 1)
    low_lanes = lane < HEAD_DIM
    scale = HEAD_DIM**-0.5
    for pair in range(blocks):
        at = slice(128 * pair, 128 * pair + 128)
        queries = qkv[:, at] * jnp.asarray(scale, LOW)
        keys = qkv[:, width + 128 * pair : width + 128 * pair + 128]
        values = qkv[:, 2 * width + 128 * pair : 2 * width + 128 * pair + 128]
        grads = grad_mixed[:, at]
        grad_q = jnp.zeros((count, 128), F32)
        grad_k = jnp.zeros((count, 128), F32)
        grad_v = jnp.zeros((count, 128), F32)
        for half in range(2):
            mine = low_lanes if half == 0 else ~low_lanes
            only = lambda v: jnp.where(mine, v, jnp.zeros_like(v))
            q_half, g_half, k_half = only(queries), only(grads), only(keys)
            scores = jnp.where(allowed, mm_nt(q_half, keys), -1e30)
            head = 2 * pair + half
            probs = jnp.exp(scores - lse[:, head : head + 1])
            grad_probs = mm_nt(g_half, values)
            grad_v = grad_v + mm_tn(probs.astype(LOW), g_half)
            dots = jnp.sum(probs * grad_probs, axis=1, keepdims=True)
            grad_scores = (probs * (grad_probs - dots)).astype(LOW)
            grad_q = grad_q + mm(grad_scores, k_half)
            grad_k = grad_k + mm_tn(grad_scores, q_half)
        gqkv[:, at] = (grad_q * scale).astype(LOW)
        gqkv[:, width + 128 * pair : width + 128 * pair + 128] = grad_k.astype(LOW)
        gqkv[:, 2 * width + 128 * pair : 2 * width + 128 * pair + 128] = grad_v.astype(LOW)
    for j in range(0, 3 * blocks, 2):
        piece = mm_tn(attn_in[...], gqkv[:, 128 * j : 128 * j + 256])
        flat[pl.ds(j, width, stride=3 * blocks), :] = piece[:, :128]
        flat[pl.ds(j + 1, width, stride=3 * blocks), :] = piece[:, 128:]
    core = core_ref[0]
    rows = flat.shape[0] // 128
    pairs, padded = kept.shape[:2]

    def move(i):
        kept[pl.ds(i, 1)] = flat[pl.ds((2 * i + core) * rows, padded), :].astype(LOW)[None]
        away[pl.ds(i, 1)] = flat[pl.ds((2 * i + 1 - core) * rows, padded), :].astype(LOW)[None]

    pl.loop(0, pairs - 1)(move)
    early, last_one = pl.ds(0, pairs - 1), pl.ds(pairs - 1, 1)
    copies = [
        pltpu.make_async_copy(a.at[part], b.at[part], sems.at[1 + i])
        for i, (a, b, part) in enumerate(
            ((away, away_o, early), (kept, kept_o, early), (away, away_o, last_one), (kept, kept_o, last_one))
        )
    ]
    copies[0].start()
    copies[1].start()
    weight_copy.wait()
    grad_attn = mm_nt(gqkv[...], weight[...])
    grad_norm, gain_attn = norm_backward(tokens[...].astype(F32), gains[0:1, :], grad_attn)
    input_grad_o[...] = grad_middle + grad_norm
    for j in range(blocks):
        flat[gain_row + j : gain_row + j + 1, :] = gain_attn[:, 128 * j : 128 * j + 128]
        flat[gain_row + blocks + j : gain_row + blocks + j + 1, :] = gain_ffn[:, 128 * j : 128 * j + 128]
    last = gain_row + 2 * blocks
    flat[last:, :] = jnp.zeros((flat.shape[0] - last, 128), F32)

    move(pairs - 1)
    copies[2].start()
    copies[3].start()
    for copy in copies:
        copy.wait()


def dense_backward(after, core, dense_rows, *arrays):
    count, width = arrays[4].shape
    rows = dense_rows // 128
    padded = (rows + 7) // 8 * 8
    return ordered(
        dense_backward_kernel, 1 + len(arrays), after,
        name="dense_backward",
        out_shape=[
            jax.ShapeDtypeStruct((count, width), F32),
            jax.ShapeDtypeStruct((64, padded, 128), LOW),
            jax.ShapeDtypeStruct((64, padded, 128), LOW),
            jax.ShapeDtypeStruct((count, width), LOW),
        ],
        in_specs=[SMEM] + [VMEM] * 11 + [HBM] + [VMEM] * (len(arrays) - 12),
        out_specs=[VMEM, HBM, HBM, VMEM],
        scratch_shapes=[
            pltpu.VMEM((rows * 128 + padded - rows, 128), F32),
            pltpu.VMEM((count, 3 * width), LOW),
            pltpu.VMEM((width, 3 * width), LOW),
            pltpu.VMEM((64, padded, 128), LOW),
            pltpu.VMEM((64, padded, 128), LOW),
            pltpu.SemaphoreType.DMA((5,)),
        ],
        compiler_params=params(),
        cost_estimate=cost(12e9, 40e6),
    )(core, *arrays)


def gelu_pair(pre):
    area = 0.5 + 0.5 * lax.erf(pre * (0.5**0.5))
    density = jnp.exp(-0.5 * pre * pre) * (1.0 / (2.0 * math.pi) ** 0.5)
    return pre * area, area + pre * density


def build_weight(after, name, home, sources, by_rows):
    rows, cols = sources[0].shape[1:]

    def kernel(home_ref, local, near, across, local_mate, near_mate, across_mate, out, sems):
        z, half = home_ref[0], home_ref[2]

        def move(blocks):
            copies = []
            for step, shard in enumerate(blocks):
                if by_rows:
                    start = pl.multiple_of(half * (rows // 2), 64)
                    place = pl.ds(pl.multiple_of(((z + step) & 3) * (rows // 2), 64), rows // 2)
                    copies.append((shard.at[0, pl.ds(start, rows // 2), :], out.at[place, :]))
                else:
                    place = pl.ds(pl.multiple_of(((z + step) & 3) * rows, 64), rows)
                    for block in range(4):
                        start = pl.multiple_of((2 * block + half) * (cols // 8), 128)
                        to = slice(block * (cols // 8), (block + 1) * (cols // 8))
                        copies.append((shard.at[0, :, pl.ds(start, cols // 8)], out.at[place, to]))
            made = [pltpu.make_async_copy(a, b, sems.at[i]) for i, (a, b) in enumerate(copies)]
            for copy in made:
                copy.start()
            for copy in made:
                copy.wait()

        pl.when(home_ref[1] == 1)(lambda: move((local, near_mate, across_mate, near)))
        pl.when(home_ref[1] == 0)(lambda: move((local_mate, near, across, near_mate)))

    shape = (2 * rows, cols) if by_rows else (4 * rows, cols // 2)
    return ordered(
        kernel, 7, after,
        name=name,
        out_shape=jax.ShapeDtypeStruct(shape, LOW),
        in_specs=[SMEM] + [HBM] * 6,
        out_specs=VMEM,
        scratch_shapes=[pltpu.SemaphoreType.DMA((16,))],
        compiler_params=params(),
        cost_estimate=cost(1e5 if by_rows else 19e9, 8e6),
    )(home, *sources)


def expert_up_kernel(own, mate, weight, hidden_o, slope_o, rows_o, grads_o):
    width = weight.shape[0]
    both = jnp.where(pl.program_id(0) < pl.num_programs(0) // 2, own[...], mate[...])
    rows = both[:, :width]
    rows_o[...] = rows
    grads_o[...] = both[:, width:]
    hidden, slope = gelu_pair(mm(rows, weight[...]))
    hidden_o[...] = hidden.astype(LOW)
    slope_o[...] = slope.astype(LOW)


def expert_up(after, own, mate, weight):
    count, width = own.shape[0], weight.shape[0]
    hidden = weight.shape[1]
    step = 256
    half = count // step
    block = lambda cols: pl.BlockSpec((step, cols), lambda i: (i, 0))
    return ordered(
        expert_up_kernel, 3, after,
        name="expert_up",
        out_shape=[jax.ShapeDtypeStruct((2 * count, n), LOW) for n in (hidden, hidden, width, width)],
        grid=(2 * half,),
        in_specs=[
            pl.BlockSpec((step, 2 * width), lambda i: (jnp.minimum(i, half - 1), 0)),
            pl.BlockSpec((step, 2 * width), lambda i: (jnp.maximum(i - half, 0), 0)),
            pl.BlockSpec((width, hidden), lambda i: (0, 0)),
        ],
        out_specs=[block(n) for n in (hidden, hidden, width, width)],
        compiler_params=params(),
        cost_estimate=cost(12e9, 20e6),
    )(own, mate, weight)


def split_three(value):
    high = lax.reduce_precision(value, 8, 7)
    mid = lax.reduce_precision(value - high, 8, 7)
    return high, mid, value - high - mid


def extra_terms(value):
    lane = iota((value.shape[0], EXTRA), 1)
    extra = jnp.zeros((value.shape[0], EXTRA), F32)
    for i, term in enumerate(split_three(value)):
        extra = jnp.where(lane == i, term, extra)
    return extra.astype(LOW)


def reduce_first(after, low, kept, arrived, work=1e6):
    rows, columns = kept.shape[0] // 2, kept.shape[1]

    def kernel(low_ref, kept, arrived, mine, other):
        for out, which in ((mine, low_ref[0]), (other, 1 - low_ref[0])):
            at = pl.ds(pl.multiple_of(which * rows, 64), rows)
            out[...] = (kept[at, :] + arrived[at, :].astype(F32)).astype(out.dtype)

    return ordered(
        kernel, 3, after,
        name="reduce_first",
        out_shape=[jax.ShapeDtypeStruct((rows, columns), t) for t in (F32, LOW)],
        in_specs=[SMEM, VMEM, VMEM],
        out_specs=[VMEM] * 2,
        compiler_params=params(),
        cost_estimate=cost(work, 6e6),
    )(low, kept, arrived)


def reduce_second(after, same, mine, other):
    def kernel(same_ref, mine, other, stays, leaves):
        straight = same_ref[0] == 1
        near, far = mine[...], other[...].astype(F32)
        stays[...] = jnp.where(straight, near, far)
        leaves[...] = jnp.where(straight, far, near).astype(LOW)

    return ordered(
        kernel, 3, after,
        name="reduce_second",
        out_shape=[jax.ShapeDtypeStruct(mine.shape, t) for t in (F32, LOW)],
        in_specs=[SMEM, VMEM, VMEM],
        out_specs=[VMEM] * 2,
        compiler_params=params(),
        cost_estimate=cost(1e6, 6e6),
    )(same, mine, other)


def frozen_kernel(rows, grads, w_in, w_out, back_o, result_sum, back_sum, value_sum):
    step = pl.program_id(0)

    @pl.when(step == 0)
    def clear():
        result_sum[...] = jnp.zeros_like(result_sum)
        back_sum[...] = jnp.zeros_like(back_sum)
        value_sum[...] = jnp.zeros_like(value_sum)

    hidden, slope = gelu_pair(mm(rows[...], w_in[...]))
    hidden = hidden.astype(LOW)
    result_sum[...] += mm(hidden, w_out[...])
    grad_hidden = mm_nt(grads[...], w_out[...])
    value_sum[...] += jnp.sum(hidden.astype(F32) * grad_hidden, axis=1, keepdims=True)
    back_sum[...] += mm_nt((grad_hidden * slope).astype(LOW), w_in[...])

    @pl.when(step == pl.num_programs(0) - 1)
    def finish():
        width = back_sum.shape[1]
        back_o[:, :width] = back_sum[...].astype(LOW)
        back_o[:, width : width + EXTRA] = extra_terms(value_sum[:, 0:1])
        back_o[:, width + EXTRA :] = result_sum[...].astype(LOW)


def frozen_expert(after, sent, w_in, w_out):
    count, width = sent.shape[0], w_in.shape[0]
    wide = w_in.shape[1]
    step = 512
    small = pl.BlockSpec((count, width), lambda i: (0, 0))
    return ordered(
        frozen_kernel, 4, after,
        name="frozen_expert",
        out_shape=jax.ShapeDtypeStruct((count, 2 * width + EXTRA), LOW),
        grid=(wide // step,),
        in_specs=[
            small, pl.BlockSpec((count, width), lambda i: (0, 1)),
            pl.BlockSpec((width, step), lambda i: (0, i)),
            pl.BlockSpec((step, width), lambda i: (i, 0)),
        ],
        out_specs=pl.BlockSpec((count, 2 * width + EXTRA), lambda i: (0, 0)),
        scratch_shapes=[
            pltpu.VMEM((count, width), F32),
            pltpu.VMEM((count, width), F32),
            pltpu.VMEM((count, EXTRA), F32),
        ],
        compiler_params=params(),
        cost_estimate=cost(4e9, 10e6),
    )(sent, sent, w_in, w_out)


def marker(after):
    def kernel(out):
        out[...] = jnp.zeros_like(out)

    return ordered(
        kernel, 0, after,
        name="marker",
        out_shape=jax.ShapeDtypeStruct((8, 128), F32),
        in_specs=[],
        out_specs=VMEM,
        compiler_params=params(),
        cost_estimate=cost(200e9, 4e3),
    )()


def adamw_values(master, first, second, grad):
    first_new = beta_first * first + (1.0 - beta_first) * grad
    second_new = beta_second * second + (1.0 - beta_second) * grad * grad
    first_hat = first_new * (1.0 / (1.0 - beta_first**STEP))
    second_hat = second_new * (1.0 / (1.0 - beta_second**STEP))
    master_new = master - learn_rate * (
        first_hat / (jnp.sqrt(second_hat) + adam_eps) + decay_rate * master
    )
    return master_new, first_new, second_new, master_new.astype(LOW)


def dense_update_kernel(master, first, second, terms, *outs):
    rows = master.shape[0]
    grad = jnp.sum(terms[...].astype(F32), axis=0)[:rows]
    for out, value in zip(outs, adamw_values(master[...], first[...], second[...], grad)):
        out[...] = value


def dense_update(after, master, first, second, terms):
    shape = (master.shape[0] // 128, 128)
    results = ordered(
        dense_update_kernel, 4, after,
        name="dense_update",
        out_shape=[jax.ShapeDtypeStruct(shape, t) for t in (F32, F32, F32, LOW)],
        in_specs=[VMEM] * 4,
        out_specs=[VMEM] * 4,
        compiler_params=params(),
        cost_estimate=cost(1e6, 4e6),
    )(*(a.reshape(shape) for a in (master, first, second)), terms)
    return tuple(r.reshape(master.shape) for r in results)


def expert_update(after, core, master, first, second, stays, arrived, axis):
    rows, columns = master.shape[1:]
    if axis == 1:
        blocks, width = 4, columns // 4
        half = (rows, width // 2)
    else:
        blocks, width = 3, columns // 3
        half = (rows // 2, width)

    def kernel(core_ref, master, first, second, stays, arrived, *outs):
        near, far = stays[...], arrived[...].astype(F32)
        swapped = core_ref[0] == 1
        grad = jnp.concatenate(
            [jnp.where(swapped, far, near), jnp.where(swapped, near, far)], axis=axis
        )
        values = adamw_values(master[0], first[0], second[0], grad)
        for out, value in zip(outs, values):
            out[0] = value

    wide = pl.BlockSpec((1, rows, width), lambda i: (0, 0, i))
    slim = pl.BlockSpec(half, lambda i: (0, i))
    return tuple(
        ordered(
        kernel, 6, after,
            name="update_in" if axis == 1 else "update_out",
            out_shape=[jax.ShapeDtypeStruct(master.shape, t) for t in (F32, F32, F32, LOW)],
            grid=(blocks,),
            in_specs=[SMEM, wide, wide, wide, slim, slim],
            out_specs=[wide] * 4,
            compiler_params=params(),
            cost_estimate=cost(2e7, 18e6),
        )(core, master, first, second, stays, arrived)
    )


def swap_core(block):
    return lax.ppermute(block, "c", [(0, 1), (1, 0)])


KINDS = (0, 1, 1, 0)


def to_neighbours(shard):
    moves = []
    for z, kind in enumerate(KINDS):
        moves.append(((z - 1) % 4 * 2 + kind, z * 2 + kind))
        moves.append(((z + 1) % 4 * 2 + kind, z * 2 + 1 - kind))
    return lax.ppermute(shard, DEPTH + ("c",), moves)


def to_opposite(shard):
    moves = []
    for z, kind in enumerate(KINDS):
        source = kind if z % 2 else 1 - kind
        moves.append((z * 2 + source, (3 - z) * 2 + 1 - kind))
    return lax.ppermute(shard, DEPTH + ("c",), moves)


def swap_pair(block):
    return lax.ppermute(block, DEPTH, [(z, 3 - z) for z in range(4)])


def swap_low(block):
    return lax.ppermute(block, "zl", [(0, 1), (1, 0)])


def exchange(rows):
    cut = rows.reshape(-1, CAP, rows.shape[1])
    cut = lax.all_to_all(cut, PLANE, split_axis=0, concat_axis=0, tiled=True)
    return cut.reshape(rows.shape)


def tie(array, *others):
    return lax.optimization_barrier((array,) + others)[0]


def word(*values):
    return jnp.stack([jnp.asarray(v, jnp.int32) for v in values])


def body(
    tokens,
    segment_ids,
    routes,
    cotangent,
    w_qkv,
    w_attn_out,
    w_router,
    norm_gains,
    frozen_in,
    frozen_out,
    new_in,
    new_out,
    dense_master,
    dense_first,
    dense_second,
    master_in,
    first_in,
    second_in,
    master_out,
    first_out,
    second_out,
):
    core, zh, zl = (lax.axis_index(a) for a in ("c", "zh", "zl"))
    z = 2 * zh + zl
    kind = zh ^ zl
    same = jnp.where(kind == core, 1, 0)
    home = word(z, same, core)
    core_word, same_word, zl_word = word(core), word(same), word(zl)
    routes = routes.T
    w_router = w_router.T

    in_near = to_neighbours(new_in)
    in_mates, out_mates = [swap_core(new_in)], [swap_core(new_out)]
    attn_in, qkv_low, mixed_low, lse, middle, ffn_in, plan, sent, frozen_sent = dense_forward(
        (), word(zh), tokens, segment_ids, routes, cotangent, w_qkv, w_attn_out, w_router, norm_gains
    )
    received = exchange(sent)
    in_across = to_opposite(tie(in_near, plan))
    in_mates.append(swap_core(tie(in_near, plan)))
    frozen_back = frozen_expert(
        (in_mates[0], out_mates[0], in_mates[1]), frozen_sent, frozen_in, frozen_out
    )
    in_mates.append(swap_core(tie(in_across, frozen_back)))
    out_near = to_neighbours(tie(new_out, in_across))
    half_in = build_weight(
        (frozen_back,), "build_in", home, (new_in, in_near, in_across, *in_mates), False
    )
    out_across = to_opposite(tie(out_near, frozen_back))
    out_mates.append(swap_core(tie(out_near, frozen_back)))
    received = tie(received, frozen_back, in_across)
    hidden, slope, rows, grads = expert_up((), received, swap_core(received), half_in)
    out_mates.append(swap_core(tie(out_across, hidden)))
    count = received.shape[0]

    def half_grad(left, right, half):
        cut = left.shape[1] // 2
        return mm_tn(lax.dynamic_slice(left, (0, half * cut), (left.shape[0], cut)), right)

    out_away = half_grad(hidden, grads, 1 - zh).astype(LOW)
    out_arrived = swap_pair(out_away)
    half_out = build_weight(
        (out_away,), "build_out", home, (new_out, out_near, out_across, *out_mates), True
    )

    result_arrived = swap_core(mm(hidden[count:], half_out).astype(LOW))
    pre = (mm_nt(grads, half_out) * slope.astype(F32)).astype(LOW)
    result = (mm(hidden[:count], half_out) + result_arrived.astype(F32)).astype(LOW)
    back_arrived = swap_core(mm_nt(pre[count:], half_in).astype(LOW))
    in_away = half_grad(rows, pre, 1 - zh).astype(LOW)
    in_arrived = swap_pair(in_away)
    back = (mm_nt(pre[:count], half_in) + back_arrived.astype(F32)).astype(LOW)
    value = jnp.sum(grads[:count].astype(F32) * result.astype(F32), axis=1, keepdims=True)
    merged = jnp.concatenate([back, extra_terms(value), result], axis=1)
    back = exchange(tie(merged, in_away))

    out_kept = half_grad(tie(hidden, merged), grads, zh)
    in_kept = half_grad(tie(rows, merged), pre, zh)
    out_mine, out_other = reduce_first((merged,), zl_word, out_kept, out_arrived, 10e9)
    in_mine, in_other = reduce_first((out_mine,), zl_word, in_kept, in_arrived, 10e9)
    out_other, in_other = swap_low(out_other), swap_low(in_other)

    input_grad, kept, away, activations = dense_backward(
        (in_mine,), core_word, dense_master.shape[0], plan, routes, segment_ids, cotangent, tokens, middle,
        mixed_low, ffn_in, lse, qkv_low, attn_in, w_qkv, w_attn_out, w_router, norm_gains, back, frozen_back,
    )
    arrived = swap_core(away)
    kept_first = kept
    kept = tie(kept, out_other, in_other)
    zero = marker((kept_first,))[0, 0]
    summed = (kept.astype(F32) + arrived.astype(F32) + zero).astype(LOW)
    terms = lax.all_to_all(summed, ("zh", "zl", "x", "y"), split_axis=0, concat_axis=0, tiled=True)
    out_stays, out_leaves = reduce_second((summed,), same_word, out_mine, out_other)
    out_mate_grad = swap_core(out_leaves)
    in_stays, in_leaves = reduce_second((out_stays,), same_word, in_mine, in_other)
    in_mate_grad = swap_core(in_leaves)
    out_new = expert_update(
        (in_stays,), core_word, master_out, first_out, second_out, out_stays, out_mate_grad, 0
    )
    in_new = expert_update(
        (out_new[0],), core_word, master_in, first_in, second_in, in_stays, in_mate_grad, 1
    )
    dense_new = dense_update((in_new[0],), dense_master, dense_first, dense_second, terms)
    return (activations, input_grad) + dense_new + in_new + out_new


def solution(mesh):
    fine = Mesh(mesh.devices.reshape(2, 2, 4, 4, 2), ALL)
    tokens = P(ALL, None)
    flat = P(ALL)
    expert = P(("x", "y", "c"), DEPTH, None)
    return jax.shard_map(
        body,
        mesh=fine,
        in_specs=(tokens,) * 4 + (P(),) * 6 + (expert,) * 2 + (flat,) * 3 + (expert,) * 6,
        out_specs=(tokens,) * 2 + (flat,) * 4 + (expert,) * 8,
        check_vma=False,
    )
```

```python
import math

import jax
import jax.numpy as jnp
from jax import lax
from jax.experimental import pallas as pl
from jax.experimental.pallas import tpu as pltpu
from jax.sharding import Mesh
from jax.sharding import PartitionSpec as P

HEAD_DIM = 64
STEP = 5


norm_eps = 1e-05
learn_rate = 0.02
beta_first = 0.5
beta_second = 0.5
adam_eps = 1e-08
decay_rate = 0.1


PLANE = ("zl", "x", "y")
DEPTH = ("zh", "zl")
ALL = ("zh", "zl", "x", "y", "c")
CAP = 24
PAIRS = 6
EXTRA = 128
VMEM = pl.BlockSpec(memory_space=pltpu.VMEM)
SMEM = pl.BlockSpec(memory_space=pltpu.SMEM)
HBM = pl.BlockSpec(memory_space=pl.ANY)
F32 = jnp.float32
LOW = jnp.bfloat16


def params(**more):
    return pltpu.CompilerParams(vmem_limit_bytes=56 * 1024 * 1024, **more)


def ordered(kernel, count, after, **call):
    extra = len(after)

    def inner(*refs):
        return kernel(*refs[:count], *refs[count + extra :])

    call["in_specs"] = list(call["in_specs"]) + [pl.BlockSpec(memory_space=pl.ANY)] * extra
    made = pl.pallas_call(inner, **call)
    return lambda *arrays: made(*arrays, *after)


def cost(flops, moved):
    return pl.CostEstimate(flops=int(flops), bytes_accessed=int(moved), transcendentals=0)


def mm(left, right):
    return jnp.dot(left, right, preferred_element_type=F32)


def mm_nt(left, right):
    return lax.dot_general(left, right, (((1,), (1,)), ((), ())), preferred_element_type=F32)


def mm_tn(left, right):
    return lax.dot_general(left, right, (((0,), (0,)), ((), ())), preferred_element_type=F32)


def iota(shape, axis):
    return lax.broadcasted_iota(jnp.int32, shape, axis)


def normed(values):
    centered = values - jnp.mean(values, axis=1, keepdims=True)
    scale = lax.rsqrt(jnp.mean(centered * centered, axis=1, keepdims=True) + norm_eps)
    return centered * scale, scale


def norm_backward(values, gain, upstream):
    hat, scale = normed(values)
    gain_grad = jnp.sum(upstream * hat, axis=0, keepdims=True)
    inner = upstream * gain
    mean_inner = jnp.mean(inner, axis=1, keepdims=True)
    mean_hat = jnp.mean(inner * hat, axis=1, keepdims=True)
    return scale * (inner - mean_inner - hat * mean_hat), gain_grad


def as_column(row, eye):
    return jnp.sum(jnp.where(eye, row, jnp.zeros_like(row)), axis=1, keepdims=True)


def as_row(column, eye):
    return jnp.sum(jnp.where(eye, column, jnp.zeros_like(column)), axis=0, keepdims=True)


def attention_mask(segment_row):
    count = segment_row.shape[1]
    down, across = iota((count, count), 0), iota((count, count), 1)
    eye = down == across
    column = jnp.sum(jnp.where(eye, segment_row, 0), axis=1, keepdims=True)
    return (down >= across) & (column == segment_row), eye


def dense_forward_kernel(
    zh_ref, tokens, segments, routes, cotangent, w_qkv, w_out, w_router, gains,
    attn_in_o, qkv_o, mixed_o, lse_o, middle_o, ffn_o, plan_o, sent_o, frozen_sent_o,
):
    width = tokens.shape[1]
    count = tokens.shape[0]
    inputs = tokens[...].astype(F32)
    hat, unused = normed(inputs)
    attn_in = (hat * gains[0:1, :]).astype(LOW)
    attn_in_o[...] = attn_in
    qkv_o[...] = mm(attn_in, w_qkv[...]).astype(LOW)
    allowed, eye = attention_mask(segments[...])
    lane = iota((count, 128), 1)
    low_lanes = lane < HEAD_DIM
    lse_all = jnp.zeros((count, 128), F32)
    for pair in range(width // 128):
        at = slice(128 * pair, 128 * pair + 128)
        queries = qkv_o[:, at] * jnp.asarray(HEAD_DIM**-0.5, LOW)
        keys = qkv_o[:, width + 128 * pair : width + 128 * pair + 128]
        values = qkv_o[:, 2 * width + 128 * pair : 2 * width + 128 * pair + 128]
        outs = []
        for half in range(2):
            mine = low_lanes if half == 0 else ~low_lanes
            scores = mm_nt(jnp.where(mine, queries, jnp.zeros_like(queries)), keys)
            scores = jnp.where(allowed, scores, -1e30)
            top = jnp.max(scores, axis=1, keepdims=True)
            raised = jnp.exp(scores - top)
            total = jnp.sum(raised, axis=1, keepdims=True)
            probs = (raised * (1.0 / total)).astype(LOW)
            outs.append(mm(probs, values))
            lse_all = jnp.where(lane == 2 * pair + half, top + jnp.log(total), lse_all)
        mixed_o[:, at] = jnp.where(low_lanes, outs[0], outs[1]).astype(LOW)
    lse_o[...] = lse_all
    middle = inputs + mm(mixed_o[...], w_out[...])
    middle_o[...] = middle
    hat, unused = normed(middle)
    ffn = (hat * gains[1:2, :]).astype(LOW)
    ffn_o[...] = ffn
    logits = mm_nt(ffn, w_router[...])
    experts = iota(logits.shape, 1)
    lists = [as_column(routes[k : k + 1, :], eye) for k in range(2)]
    picks = [experts == column for column in lists]
    chosen = [jnp.sum(jnp.where(p, logits, 0.0), axis=1, keepdims=True) for p in picks]
    top = jnp.maximum(chosen[0], chosen[1])
    raised = [jnp.exp(c - top) for c in chosen]
    gates = [r / (raised[0] + raised[1]) for r in raised]
    named = (picks[0] | picks[1]).astype(F32).astype(LOW)
    earlier = (iota((count, count), 0) > iota((count, count), 1)).astype(F32).astype(LOW)
    before = mm(earlier, named)
    zh = zh_ref[0]
    new_place, old_place = [], []
    for k in range(2):
        route = lists[k]
        slot = jnp.sum(jnp.where(picks[k], before, 0.0), axis=1, keepdims=True).astype(jnp.int32)
        fresh = route - 1
        block = 16 * ((fresh & 1) ^ zh) + lax.shift_right_arithmetic(fresh, 1)
        new_place.append(jnp.where(route > 0, block * CAP + slot, -1))
        old_place.append(jnp.where(route > 0, -1, slot))
    columns = gates + [p.astype(F32) for p in new_place + old_place]
    plan = jnp.zeros((count, 128), F32)
    for i, column in enumerate(columns):
        plan = jnp.where(lane == i, column, plan)
    plan_o[...] = plan
    up = cotangent[...].astype(F32)
    scaled = [(g * up).astype(LOW) for g in gates]
    for places, ref in ((new_place, sent_o), (old_place, frozen_sent_o)):
        slots = iota((ref.shape[0], count), 0)
        spread = [(slots == as_row(p, eye)).astype(F32).astype(LOW) for p in places]
        ref[:, :width] = mm(spread[0] + spread[1], ffn).astype(LOW)
        ref[:, width:] = (mm(spread[0], scaled[0]) + mm(spread[1], scaled[1])).astype(LOW)


def dense_forward(after, zh, tokens, segments, routes, cotangent, w_qkv, w_out, w_router, gains):
    count, width = tokens.shape
    slots = (w_router.shape[0] - 1) * CAP
    shapes = [
        ((count, width), LOW), ((count, 3 * width), LOW), ((count, width), LOW), ((count, 128), F32),
        ((count, width), F32), ((count, width), LOW), ((count, 128), F32),
        ((slots, 2 * width), LOW), ((CAP, 2 * width), LOW),
    ]
    return ordered(
        dense_forward_kernel, 9, after,
        name="dense_forward",
        out_shape=[jax.ShapeDtypeStruct(s, t) for s, t in shapes],
        in_specs=[SMEM] + [VMEM] * 8,
        out_specs=[VMEM] * len(shapes),
        compiler_params=params(),
        cost_estimate=cost(8e9, 30e6),
    )(zh, tokens, segments, routes, cotangent, w_qkv, w_out, w_router, gains)


def dense_backward_kernel(
    core_ref, plan, routes, segments, cotangent, tokens, middle, mixed, ffn, lse, qkv, attn_in,
    w_qkv, w_out, w_router, gains, back, frozen_back,
    input_grad_o, kept_o, away_o, active_o,
    flat, gqkv, weight, kept, away, sems,
):
    count, width = tokens.shape
    weight_copy = pltpu.make_async_copy(w_qkv, weight, sems.at[0])
    weight_copy.start()
    expert_total = w_router.shape[0]
    up = cotangent[...].astype(F32)
    gates = [plan[:, k : k + 1] for k in range(2)]
    new_place = [plan[:, 2 + k : 3 + k].astype(jnp.int32) for k in range(2)]
    old_place = [plan[:, 4 + k : 5 + k].astype(jnp.int32) for k in range(2)]
    allowed, eye = attention_mask(segments[...])

    grad_ffn = jnp.zeros((count, width), F32)
    weighted = [jnp.zeros((count, 1), F32) for k in range(2)]
    active = middle[...]
    for places, ref in ((new_place, back), (old_place, frozen_back)):
        size = ref.shape[0]
        slots = iota((count, size), 1)
        for k in range(2):
            choice = (slots == places[k]).astype(F32).astype(LOW)
            picked = mm(choice, ref[...])
            grad_ffn = grad_ffn + picked[:, :width]
            tail = picked[:, width : width + EXTRA]
            weighted[k] = weighted[k] + jnp.sum(tail, axis=1, keepdims=True)
            active = active + gates[k] * picked[:, width + EXTRA :]
    active_o[...] = active.astype(LOW)
    both = weighted[0] + weighted[1]
    experts = iota((count, expert_total), 1)
    grad_logits = jnp.zeros((count, expert_total), F32)
    for k in range(2):
        grad_logits = jnp.where(
            experts == as_column(routes[k : k + 1, :], eye), weighted[k] - gates[k] * both, grad_logits
        )
    grad_logits = grad_logits.astype(LOW)
    grad_ffn = grad_ffn + mm(grad_logits, w_router[...])
    grad_norm, gain_ffn = norm_backward(middle[...], gains[1:2, :], grad_ffn)
    grad_middle = up + grad_norm
    grad_branch = grad_middle.astype(LOW)

    blocks = width // 128
    first_row = 3 * blocks * width
    attn_out_grad = mm_tn(mixed[...], grad_branch)
    for j in range(blocks):
        flat[pl.ds(first_row + j, width, stride=blocks), :] = attn_out_grad[:, 128 * j : 128 * j + 128]
    router_row = first_row + blocks * width
    router_rows = width * expert_total // 128
    padded_logits = jnp.concatenate(
        [grad_logits, jnp.zeros((count, 128 - expert_total), LOW)], axis=1
    )
    router_grad = mm_tn(ffn[...], padded_logits)
    feature = iota((width, 128), 0)
    lane_w = iota((width, 128), 1)
    start = feature * expert_total
    offset = start & 127
    turned = jnp.take_along_axis(router_grad, (lane_w - offset) & 127, axis=1)
    wrapped = lane_w < offset
    row_of = lax.shift_right_logical(iota((router_rows, width), 1) * expert_total, 7)
    row_here = iota((router_rows, width), 0)
    here = (row_of == row_here).astype(F32)
    after = (row_of + 1 == row_here).astype(F32)
    exact = lambda a, b: jnp.dot(a, b, precision=lax.Precision.HIGHEST, preferred_element_type=F32)
    flat[router_row : router_row + router_rows, :] = exact(
        here, jnp.where(wrapped, 0.0, turned)
    ) + exact(after, jnp.where(wrapped, turned, 0.0))
    gain_row = router_row + router_rows

    grad_mixed = mm_nt(grad_branch, w_out[...]).astype(LOW)
    lane = iota((count, 128), 1)
    low_lanes = lane < HEAD_DIM
    scale = HEAD_DIM**-0.5
    for pair in range(blocks):
        at = slice(128 * pair, 128 * pair + 128)
        queries = qkv[:, at] * jnp.asarray(scale, LOW)
        keys = qkv[:, width + 128 * pair : width + 128 * pair + 128]
        values = qkv[:, 2 * width + 128 * pair : 2 * width + 128 * pair + 128]
        grads = grad_mixed[:, at]
        grad_q = jnp.zeros((count, 128), F32)
        grad_k = jnp.zeros((count, 128), F32)
        grad_v = jnp.zeros((count, 128), F32)
        for half in range(2):
            mine = low_lanes if half == 0 else ~low_lanes
            only = lambda v: jnp.where(mine, v, jnp.zeros_like(v))
            q_half, g_half, k_half = only(queries), only(grads), only(keys)
            scores = jnp.where(allowed, mm_nt(q_half, keys), -1e30)
            head = 2 * pair + half
            probs = jnp.exp(scores - lse[:, head : head + 1])
            grad_probs = mm_nt(g_half, values)
            grad_v = grad_v + mm_tn(probs.astype(LOW), g_half)
            dots = jnp.sum(probs * grad_probs, axis=1, keepdims=True)
            grad_scores = (probs * (grad_probs - dots)).astype(LOW)
            grad_q = grad_q + mm(grad_scores, k_half)
            grad_k = grad_k + mm_tn(grad_scores, q_half)
        gqkv[:, at] = (grad_q * scale).astype(LOW)
        gqkv[:, width + 128 * pair : width + 128 * pair + 128] = grad_k.astype(LOW)
        gqkv[:, 2 * width + 128 * pair : 2 * width + 128 * pair + 128] = grad_v.astype(LOW)
    for j in range(0, 3 * blocks, 2):
        piece = mm_tn(attn_in[...], gqkv[:, 128 * j : 128 * j + 256])
        flat[pl.ds(j, width, stride=3 * blocks), :] = piece[:, :128]
        flat[pl.ds(j + 1, width, stride=3 * blocks), :] = piece[:, 128:]
    core = core_ref[0]
    rows = flat.shape[0] // 128
    pairs, padded = kept.shape[:2]

    def move(i):
        kept[pl.ds(i, 1)] = flat[pl.ds((2 * i + core) * rows, padded), :].astype(LOW)[None]
        away[pl.ds(i, 1)] = flat[pl.ds((2 * i + 1 - core) * rows, padded), :].astype(LOW)[None]

    pl.loop(0, pairs - 1)(move)
    early, last_one = pl.ds(0, pairs - 1), pl.ds(pairs - 1, 1)
    copies = [
        pltpu.make_async_copy(a.at[part], b.at[part], sems.at[1 + i])
        for i, (a, b, part) in enumerate(
            ((away, away_o, early), (kept, kept_o, early), (away, away_o, last_one), (kept, kept_o, last_one))
        )
    ]
    copies[0].start()
    copies[1].start()
    weight_copy.wait()
    grad_attn = mm_nt(gqkv[...], weight[...])
    grad_norm, gain_attn = norm_backward(tokens[...].astype(F32), gains[0:1, :], grad_attn)
    input_grad_o[...] = grad_middle + grad_norm
    for j in range(blocks):
        flat[gain_row + j : gain_row + j + 1, :] = gain_attn[:, 128 * j : 128 * j + 128]
        flat[gain_row + blocks + j : gain_row + blocks + j + 1, :] = gain_ffn[:, 128 * j : 128 * j + 128]
    last = gain_row + 2 * blocks
    flat[last:, :] = jnp.zeros((flat.shape[0] - last, 128), F32)

    move(pairs - 1)
    copies[2].start()
    copies[3].start()
    for copy in copies:
        copy.wait()


def dense_backward(after, core, dense_rows, *arrays):
    count, width = arrays[4].shape
    rows = dense_rows // 128
    padded = (rows + 7) // 8 * 8
    return ordered(
        dense_backward_kernel, 1 + len(arrays), after,
        name="dense_backward",
        out_shape=[
            jax.ShapeDtypeStruct((count, width), F32),
            jax.ShapeDtypeStruct((64, padded, 128), LOW),
            jax.ShapeDtypeStruct((64, padded, 128), LOW),
            jax.ShapeDtypeStruct((count, width), LOW),
        ],
        in_specs=[SMEM] + [VMEM] * 11 + [HBM] + [VMEM] * (len(arrays) - 12),
        out_specs=[VMEM, HBM, HBM, VMEM],
        scratch_shapes=[
            pltpu.VMEM((rows * 128 + padded - rows, 128), F32),
            pltpu.VMEM((count, 3 * width), LOW),
            pltpu.VMEM((width, 3 * width), LOW),
            pltpu.VMEM((64, padded, 128), LOW),
            pltpu.VMEM((64, padded, 128), LOW),
            pltpu.SemaphoreType.DMA((5,)),
        ],
        compiler_params=params(),
        cost_estimate=cost(12e9, 40e6),
    )(core, *arrays)


def gelu_pair(pre):
    area = 0.5 + 0.5 * lax.erf(pre * (0.5**0.5))
    density = jnp.exp(-0.5 * pre * pre) * (1.0 / (2.0 * math.pi) ** 0.5)
    return pre * area, area + pre * density


def build_weight(after, name, home, sources, by_rows):
    rows, cols = sources[0].shape[1:]

    def kernel(home_ref, local, near, across, local_mate, near_mate, across_mate, out, sems):
        z, half = home_ref[0], home_ref[2]

        def move(blocks):
            copies = []
            for step, shard in enumerate(blocks):
                if by_rows:
                    start = pl.multiple_of(half * (rows // 2), 64)
                    place = pl.ds(pl.multiple_of(((z + step) & 3) * (rows // 2), 64), rows // 2)
                    copies.append((shard.at[0, pl.ds(start, rows // 2), :], out.at[place, :]))
                else:
                    place = pl.ds(pl.multiple_of(((z + step) & 3) * rows, 64), rows)
                    for block in range(4):
                        start = pl.multiple_of((2 * block + half) * (cols // 8), 128)
                        to = slice(block * (cols // 8), (block + 1) * (cols // 8))
                        copies.append((shard.at[0, :, pl.ds(start, cols // 8)], out.at[place, to]))
            made = [pltpu.make_async_copy(a, b, sems.at[i]) for i, (a, b) in enumerate(copies)]
            for copy in made:
                copy.start()
            for copy in made:
                copy.wait()

        pl.when(home_ref[1] == 1)(lambda: move((local, near_mate, across_mate, near)))
        pl.when(home_ref[1] == 0)(lambda: move((local_mate, near, across, near_mate)))

    shape = (2 * rows, cols) if by_rows else (4 * rows, cols // 2)
    return ordered(
        kernel, 7, after,
        name=name,
        out_shape=jax.ShapeDtypeStruct(shape, LOW),
        in_specs=[SMEM] + [HBM] * 6,
        out_specs=VMEM,
        scratch_shapes=[pltpu.SemaphoreType.DMA((16,))],
        compiler_params=params(),
        cost_estimate=cost(1e5 if by_rows else 19e9, 8e6),
    )(home, *sources)


def expert_up_kernel(own, mate, weight, hidden_o, slope_o, rows_o, grads_o):
    width = weight.shape[0]
    both = jnp.where(pl.program_id(0) < pl.num_programs(0) // 2, own[...], mate[...])
    rows = both[:, :width]
    rows_o[...] = rows
    grads_o[...] = both[:, width:]
    hidden, slope = gelu_pair(mm(rows, weight[...]))
    hidden_o[...] = hidden.astype(LOW)
    slope_o[...] = slope.astype(LOW)


def expert_up(after, own, mate, weight):
    count, width = own.shape[0], weight.shape[0]
    hidden = weight.shape[1]
    step = 256
    half = count // step
    block = lambda cols: pl.BlockSpec((step, cols), lambda i: (i, 0))
    return ordered(
        expert_up_kernel, 3, after,
        name="expert_up",
        out_shape=[jax.ShapeDtypeStruct((2 * count, n), LOW) for n in (hidden, hidden, width, width)],
        grid=(2 * half,),
        in_specs=[
            pl.BlockSpec((step, 2 * width), lambda i: (jnp.minimum(i, half - 1), 0)),
            pl.BlockSpec((step, 2 * width), lambda i: (jnp.maximum(i - half, 0), 0)),
            pl.BlockSpec((width, hidden), lambda i: (0, 0)),
        ],
        out_specs=[block(n) for n in (hidden, hidden, width, width)],
        compiler_params=params(),
        cost_estimate=cost(12e9, 20e6),
    )(own, mate, weight)


def split_three(value):
    high = lax.reduce_precision(value, 8, 7)
    mid = lax.reduce_precision(value - high, 8, 7)
    return high, mid, value - high - mid


def extra_terms(value):
    lane = iota((value.shape[0], EXTRA), 1)
    extra = jnp.zeros((value.shape[0], EXTRA), F32)
    for i, term in enumerate(split_three(value)):
        extra = jnp.where(lane == i, term, extra)
    return extra.astype(LOW)


def reduce_first(after, low, kept, arrived, work=1e6):
    rows, columns = kept.shape[0] // 2, kept.shape[1]

    def kernel(low_ref, kept, arrived, mine, other):
        for out, which in ((mine, low_ref[0]), (other, 1 - low_ref[0])):
            at = pl.ds(pl.multiple_of(which * rows, 64), rows)
            out[...] = (kept[at, :] + arrived[at, :].astype(F32)).astype(out.dtype)

    return ordered(
        kernel, 3, after,
        name="reduce_first",
        out_shape=[jax.ShapeDtypeStruct((rows, columns), t) for t in (F32, LOW)],
        in_specs=[SMEM, VMEM, VMEM],
        out_specs=[VMEM] * 2,
        compiler_params=params(),
        cost_estimate=cost(work, 6e6),
    )(low, kept, arrived)


def reduce_second(after, same, mine, other):
    def kernel(same_ref, mine, other, stays, leaves):
        straight = same_ref[0] == 1
        near, far = mine[...], other[...].astype(F32)
        stays[...] = jnp.where(straight, near, far)
        leaves[...] = jnp.where(straight, far, near).astype(LOW)

    return ordered(
        kernel, 3, after,
        name="reduce_second",
        out_shape=[jax.ShapeDtypeStruct(mine.shape, t) for t in (F32, LOW)],
        in_specs=[SMEM, VMEM, VMEM],
        out_specs=[VMEM] * 2,
        compiler_params=params(),
        cost_estimate=cost(1e6, 6e6),
    )(same, mine, other)


def frozen_kernel(rows, grads, w_in, w_out, back_o, result_sum, back_sum, value_sum):
    step = pl.program_id(0)

    @pl.when(step == 0)
    def clear():
        result_sum[...] = jnp.zeros_like(result_sum)
        back_sum[...] = jnp.zeros_like(back_sum)
        value_sum[...] = jnp.zeros_like(value_sum)

    hidden, slope = gelu_pair(mm(rows[...], w_in[...]))
    hidden = hidden.astype(LOW)
    result_sum[...] += mm(hidden, w_out[...])
    grad_hidden = mm_nt(grads[...], w_out[...])
    value_sum[...] += jnp.sum(hidden.astype(F32) * grad_hidden, axis=1, keepdims=True)
    back_sum[...] += mm_nt((grad_hidden * slope).astype(LOW), w_in[...])

    @pl.when(step == pl.num_programs(0) - 1)
    def finish():
        width = back_sum.shape[1]
        back_o[:, :width] = back_sum[...].astype(LOW)
        back_o[:, width : width + EXTRA] = extra_terms(value_sum[:, 0:1])
        back_o[:, width + EXTRA :] = result_sum[...].astype(LOW)


def frozen_expert(after, sent, w_in, w_out):
    count, width = sent.shape[0], w_in.shape[0]
    wide = w_in.shape[1]
    step = 512
    small = pl.BlockSpec((count, width), lambda i: (0, 0))
    return ordered(
        frozen_kernel, 4, after,
        name="frozen_expert",
        out_shape=jax.ShapeDtypeStruct((count, 2 * width + EXTRA), LOW),
        grid=(wide // step,),
        in_specs=[
            small, pl.BlockSpec((count, width), lambda i: (0, 1)),
            pl.BlockSpec((width, step), lambda i: (0, i)),
            pl.BlockSpec((step, width), lambda i: (i, 0)),
        ],
        out_specs=pl.BlockSpec((count, 2 * width + EXTRA), lambda i: (0, 0)),
        scratch_shapes=[
            pltpu.VMEM((count, width), F32),
            pltpu.VMEM((count, width), F32),
            pltpu.VMEM((count, EXTRA), F32),
        ],
        compiler_params=params(),
        cost_estimate=cost(4e9, 10e6),
    )(sent, sent, w_in, w_out)


def marker(after):
    def kernel(out):
        out[...] = jnp.zeros_like(out)

    return ordered(
        kernel, 0, after,
        name="marker",
        out_shape=jax.ShapeDtypeStruct((8, 128), F32),
        in_specs=[],
        out_specs=VMEM,
        compiler_params=params(),
        cost_estimate=cost(200e9, 4e3),
    )()


def adamw_values(master, first, second, grad):
    first_new = beta_first * first + (1.0 - beta_first) * grad
    second_new = beta_second * second + (1.0 - beta_second) * grad * grad
    first_hat = first_new * (1.0 / (1.0 - beta_first**STEP))
    second_hat = second_new * (1.0 / (1.0 - beta_second**STEP))
    master_new = master - learn_rate * (
        first_hat / (jnp.sqrt(second_hat) + adam_eps) + decay_rate * master
    )
    return master_new, first_new, second_new, master_new.astype(LOW)


def dense_update_kernel(master, first, second, terms, *outs):
    rows = master.shape[0]
    grad = jnp.sum(terms[...].astype(F32), axis=0)[:rows]
    for out, value in zip(outs, adamw_values(master[...], first[...], second[...], grad)):
        out[...] = value


def dense_update(after, master, first, second, terms):
    shape = (master.shape[0] // 128, 128)
    results = ordered(
        dense_update_kernel, 4, after,
        name="dense_update",
        out_shape=[jax.ShapeDtypeStruct(shape, t) for t in (F32, F32, F32, LOW)],
        in_specs=[VMEM] * 4,
        out_specs=[VMEM] * 4,
        compiler_params=params(),
        cost_estimate=cost(1e6, 4e6),
    )(*(a.reshape(shape) for a in (master, first, second)), terms)
    return tuple(r.reshape(master.shape) for r in results)


def expert_update(after, core, master, first, second, stays, arrived, axis):
    rows, columns = master.shape[1:]
    if axis == 1:
        blocks, width = 4, columns // 4
        half = (rows, width // 2)
    else:
        blocks, width = 3, columns // 3
        half = (rows // 2, width)

    def kernel(core_ref, master, first, second, stays, arrived, *outs):
        near, far = stays[...], arrived[...].astype(F32)
        swapped = core_ref[0] == 1
        grad = jnp.concatenate(
            [jnp.where(swapped, far, near), jnp.where(swapped, near, far)], axis=axis
        )
        values = adamw_values(master[0], first[0], second[0], grad)
        for out, value in zip(outs, values):
            out[0] = value

    wide = pl.BlockSpec((1, rows, width), lambda i: (0, 0, i))
    slim = pl.BlockSpec(half, lambda i: (0, i))
    return tuple(
        ordered(
        kernel, 6, after,
            name="update_in" if axis == 1 else "update_out",
            out_shape=[jax.ShapeDtypeStruct(master.shape, t) for t in (F32, F32, F32, LOW)],
            grid=(blocks,),
            in_specs=[SMEM, wide, wide, wide, slim, slim],
            out_specs=[wide] * 4,
            compiler_params=params(),
            cost_estimate=cost(2e7, 18e6),
        )(core, master, first, second, stays, arrived)
    )


def swap_core(block):
    return lax.ppermute(block, "c", [(0, 1), (1, 0)])


KINDS = (0, 1, 1, 0)


def to_neighbours(shard):
    moves = []
    for z, kind in enumerate(KINDS):
        moves.append(((z - 1) % 4 * 2 + kind, z * 2 + kind))
        moves.append(((z + 1) % 4 * 2 + kind, z * 2 + 1 - kind))
    return lax.ppermute(shard, DEPTH + ("c",), moves)


def to_opposite(shard):
    moves = []
    for z, kind in enumerate(KINDS):
        source = kind if z % 2 else 1 - kind
        moves.append((z * 2 + source, (3 - z) * 2 + 1 - kind))
    return lax.ppermute(shard, DEPTH + ("c",), moves)


def swap_pair(block):
    return lax.ppermute(block, DEPTH, [(z, 3 - z) for z in range(4)])


def swap_low(block):
    return lax.ppermute(block, "zl", [(0, 1), (1, 0)])


def exchange(rows):
    cut = rows.reshape(-1, CAP, rows.shape[1])
    cut = lax.all_to_all(cut, PLANE, split_axis=0, concat_axis=0, tiled=True)
    return cut.reshape(rows.shape)


def tie(array, *others):
    return lax.optimization_barrier((array,) + others)[0]


def word(*values):
    return jnp.stack([jnp.asarray(v, jnp.int32) for v in values])


def body(
    tokens,
    segment_ids,
    routes,
    cotangent,
    w_qkv,
    w_attn_out,
    w_router,
    norm_gains,
    frozen_in,
    frozen_out,
    new_in,
    new_out,
    dense_master,
    dense_first,
    dense_second,
    master_in,
    first_in,
    second_in,
    master_out,
    first_out,
    second_out,
):
    core, zh, zl = (lax.axis_index(a) for a in ("c", "zh", "zl"))
    z = 2 * zh + zl
    kind = zh ^ zl
    same = jnp.where(kind == core, 1, 0)
    home = word(z, same, core)
    core_word, same_word, zl_word = word(core), word(same), word(zl)
    routes = routes.T
    w_router = w_router.T

    in_near = to_neighbours(new_in)
    in_mates, out_mates = [swap_core(new_in)], [swap_core(new_out)]
    attn_in, qkv_low, mixed_low, lse, middle, ffn_in, plan, sent, frozen_sent = dense_forward(
        (), word(zh), tokens, segment_ids, routes, cotangent, w_qkv, w_attn_out, w_router, norm_gains
    )
    received = exchange(sent)
    in_across = to_opposite(tie(in_near, plan))
    in_mates.append(swap_core(tie(in_near, plan)))
    frozen_back = frozen_expert(
        (in_mates[0], out_mates[0], in_mates[1]), frozen_sent, frozen_in, frozen_out
    )
    in_mates.append(swap_core(tie(in_across, frozen_back)))
    out_near = to_neighbours(tie(new_out, in_across))
    half_in = build_weight(
        (frozen_back,), "build_in", home, (new_in, in_near, in_across, *in_mates), False
    )
    received = tie(received, frozen_back, in_across)
    hidden, slope, rows, grads = expert_up((), received, swap_core(received), half_in)
    out_across = to_opposite(tie(out_near, hidden))
    out_mates.append(swap_core(tie(out_near, hidden)))
    count = received.shape[0]

    def half_grad(left, right, half):
        cut = left.shape[1] // 2
        return mm_tn(lax.dynamic_slice(left, (0, half * cut), (left.shape[0], cut)), right)

    out_away = half_grad(hidden, grads, 1 - zh).astype(LOW)
    out_arrived = swap_pair(out_away)
    out_mates.append(swap_core(tie(out_across, out_away)))
    half_out = build_weight(
        (out_away,), "build_out", home, (new_out, out_near, out_across, *out_mates), True
    )

    result_arrived = swap_core(mm(hidden[count:], half_out).astype(LOW))
    pre = (mm_nt(grads, half_out) * slope.astype(F32)).astype(LOW)
    result = (mm(hidden[:count], half_out) + result_arrived.astype(F32)).astype(LOW)
    back_arrived = swap_core(mm_nt(pre[count:], half_in).astype(LOW))
    in_away = half_grad(rows, pre, 1 - zh).astype(LOW)
    in_arrived = swap_pair(in_away)
    back = (mm_nt(pre[:count], half_in) + back_arrived.astype(F32)).astype(LOW)
    value = jnp.sum(grads[:count].astype(F32) * result.astype(F32), axis=1, keepdims=True)
    merged = jnp.concatenate([back, extra_terms(value), result], axis=1)
    back = exchange(tie(merged, in_away))

    out_kept = half_grad(tie(hidden, merged), grads, zh)
    in_kept = half_grad(tie(rows, merged), pre, zh)
    out_mine, out_other = reduce_first((merged,), zl_word, out_kept, out_arrived, 10e9)
    in_mine, in_other = reduce_first((out_mine,), zl_word, in_kept, in_arrived, 10e9)
    out_other, in_other = swap_low(out_other), swap_low(in_other)

    input_grad, kept, away, activations = dense_backward(
        (in_mine,), core_word, dense_master.shape[0], plan, routes, segment_ids, cotangent, tokens, middle,
        mixed_low, ffn_in, lse, qkv_low, attn_in, w_qkv, w_attn_out, w_router, norm_gains, back, frozen_back,
    )
    arrived = swap_core(away)
    kept_first = kept
    kept = tie(kept, out_other, in_other)
    zero = marker((kept_first,))[0, 0]
    summed = (kept.astype(F32) + arrived.astype(F32) + zero).astype(LOW)
    terms = lax.all_to_all(summed, ("zh", "zl", "x", "y"), split_axis=0, concat_axis=0, tiled=True)
    out_stays, out_leaves = reduce_second((summed,), same_word, out_mine, out_other)
    out_mate_grad = swap_core(out_leaves)
    in_stays, in_leaves = reduce_second((out_stays,), same_word, in_mine, in_other)
    in_mate_grad = swap_core(in_leaves)
    out_new = expert_update(
        (in_stays,), core_word, master_out, first_out, second_out, out_stays, out_mate_grad, 0
    )
    in_new = expert_update(
        (out_new[0],), core_word, master_in, first_in, second_in, in_stays, in_mate_grad, 1
    )
    dense_new = dense_update((in_new[0],), dense_master, dense_first, dense_second, terms)
    return (activations, input_grad) + dense_new + in_new + out_new


def solution(mesh):
    fine = Mesh(mesh.devices.reshape(2, 2, 4, 4, 2), ALL)
    tokens = P(ALL, None)
    flat = P(ALL)
    expert = P(("x", "y", "c"), DEPTH, None)
    return jax.shard_map(
        body,
        mesh=fine,
        in_specs=(tokens,) * 4 + (P(),) * 6 + (expert,) * 2 + (flat,) * 3 + (expert,) * 6,
        out_specs=(tokens,) * 2 + (flat,) * 4 + (expert,) * 8,
        check_vma=False,
    )
```

```python
import math

import jax
import jax.numpy as jnp
from jax import lax
from jax.experimental import pallas as pl
from jax.experimental.pallas import tpu as pltpu
from jax.sharding import Mesh
from jax.sharding import PartitionSpec as P

HEAD_DIM = 64
STEP = 5


norm_eps = 1e-05
learn_rate = 0.02
beta_first = 0.5
beta_second = 0.5
adam_eps = 1e-08
decay_rate = 0.1


PLANE = ("zl", "x", "y")
DEPTH = ("zh", "zl")
ALL = ("zh", "zl", "x", "y", "c")
CAP = 24
PAIRS = 6
EXTRA = 128
VMEM = pl.BlockSpec(memory_space=pltpu.VMEM)
SMEM = pl.BlockSpec(memory_space=pltpu.SMEM)
HBM = pl.BlockSpec(memory_space=pl.ANY)
F32 = jnp.float32
LOW = jnp.bfloat16


def params(**more):
    return pltpu.CompilerParams(vmem_limit_bytes=56 * 1024 * 1024, **more)


def ordered(kernel, count, after, **call):
    extra = len(after)

    def inner(*refs):
        return kernel(*refs[:count], *refs[count + extra :])

    call["in_specs"] = list(call["in_specs"]) + [pl.BlockSpec(memory_space=pl.ANY)] * extra
    made = pl.pallas_call(inner, **call)
    return lambda *arrays: made(*arrays, *after)


def cost(flops, moved):
    return pl.CostEstimate(flops=int(flops), bytes_accessed=int(moved), transcendentals=0)


def mm(left, right):
    return jnp.dot(left, right, preferred_element_type=F32)


def mm_nt(left, right):
    return lax.dot_general(left, right, (((1,), (1,)), ((), ())), preferred_element_type=F32)


def mm_tn(left, right):
    return lax.dot_general(left, right, (((0,), (0,)), ((), ())), preferred_element_type=F32)


def iota(shape, axis):
    return lax.broadcasted_iota(jnp.int32, shape, axis)


def normed(values):
    centered = values - jnp.mean(values, axis=1, keepdims=True)
    scale = lax.rsqrt(jnp.mean(centered * centered, axis=1, keepdims=True) + norm_eps)
    return centered * scale, scale


def norm_backward(values, gain, upstream):
    hat, scale = normed(values)
    gain_grad = jnp.sum(upstream * hat, axis=0, keepdims=True)
    inner = upstream * gain
    mean_inner = jnp.mean(inner, axis=1, keepdims=True)
    mean_hat = jnp.mean(inner * hat, axis=1, keepdims=True)
    return scale * (inner - mean_inner - hat * mean_hat), gain_grad


def as_column(row, eye):
    return jnp.sum(jnp.where(eye, row, jnp.zeros_like(row)), axis=1, keepdims=True)


def as_row(column, eye):
    return jnp.sum(jnp.where(eye, column, jnp.zeros_like(column)), axis=0, keepdims=True)


def attention_mask(segment_row):
    count = segment_row.shape[1]
    down, across = iota((count, count), 0), iota((count, count), 1)
    eye = down == across
    column = jnp.sum(jnp.where(eye, segment_row, 0), axis=1, keepdims=True)
    return (down >= across) & (column == segment_row), eye


def dense_forward_kernel(
    zh_ref, tokens, segments, routes, cotangent, w_qkv, w_out, w_router, gains,
    attn_in_o, qkv_o, mixed_o, lse_o, middle_o, ffn_o, plan_o, sent_o, frozen_sent_o,
):
    width = tokens.shape[1]
    count = tokens.shape[0]
    inputs = tokens[...].astype(F32)
    hat, unused = normed(inputs)
    attn_in = (hat * gains[0:1, :]).astype(LOW)
    attn_in_o[...] = attn_in
    qkv_o[...] = mm(attn_in, w_qkv[...]).astype(LOW)
    allowed, eye = attention_mask(segments[...])
    lane = iota((count, 128), 1)
    low_lanes = lane < HEAD_DIM
    lse_all = jnp.zeros((count, 128), F32)
    for pair in range(width // 128):
        at = slice(128 * pair, 128 * pair + 128)
        queries = qkv_o[:, at] * jnp.asarray(HEAD_DIM**-0.5, LOW)
        keys = qkv_o[:, width + 128 * pair : width + 128 * pair + 128]
        values = qkv_o[:, 2 * width + 128 * pair : 2 * width + 128 * pair + 128]
        outs = []
        for half in range(2):
            mine = low_lanes if half == 0 else ~low_lanes
            scores = mm_nt(jnp.where(mine, queries, jnp.zeros_like(queries)), keys)
            scores = jnp.where(allowed, scores, -1e30)
            top = jnp.max(scores, axis=1, keepdims=True)
            raised = jnp.exp(scores - top)
            total = jnp.sum(raised, axis=1, keepdims=True)
            probs = (raised * (1.0 / total)).astype(LOW)
            outs.append(mm(probs, values))
            lse_all = jnp.where(lane == 2 * pair + half, top + jnp.log(total), lse_all)
        mixed_o[:, at] = jnp.where(low_lanes, outs[0], outs[1]).astype(LOW)
    lse_o[...] = lse_all
    middle = inputs + mm(mixed_o[...], w_out[...])
    middle_o[...] = middle
    hat, unused = normed(middle)
    ffn = (hat * gains[1:2, :]).astype(LOW)
    ffn_o[...] = ffn
    logits = mm_nt(ffn, w_router[...])
    experts = iota(logits.shape, 1)
    lists = [as_column(routes[k : k + 1, :], eye) for k in range(2)]
    picks = [experts == column for column in lists]
    chosen = [jnp.sum(jnp.where(p, logits, 0.0), axis=1, keepdims=True) for p in picks]
    top = jnp.maximum(chosen[0], chosen[1])
    raised = [jnp.exp(c - top) for c in chosen]
    gates = [r / (raised[0] + raised[1]) for r in raised]
    named = (picks[0] | picks[1]).astype(F32).astype(LOW)
    earlier = (iota((count, count), 0) > iota((count, count), 1)).astype(F32).astype(LOW)
    before = mm(earlier, named)
    zh = zh_ref[0]
    new_place, old_place = [], []
    for k in range(2):
        route = lists[k]
        slot = jnp.sum(jnp.where(picks[k], before, 0.0), axis=1, keepdims=True).astype(jnp.int32)
        fresh = route - 1
        block = 16 * ((fresh & 1) ^ zh) + lax.shift_right_arithmetic(fresh, 1)
        new_place.append(jnp.where(route > 0, block * CAP + slot, -1))
        old_place.append(jnp.where(route > 0, -1, slot))
    columns = gates + [p.astype(F32) for p in new_place + old_place]
    plan = jnp.zeros((count, 128), F32)
    for i, column in enumerate(columns):
        plan = jnp.where(lane == i, column, plan)
    plan_o[...] = plan
    up = cotangent[...].astype(F32)
    scaled = [(g * up).astype(LOW) for g in gates]
    for places, ref in ((new_place, sent_o), (old_place, frozen_sent_o)):
        slots = iota((ref.shape[0], count), 0)
        spread = [(slots == as_row(p, eye)).astype(F32).astype(LOW) for p in places]
        ref[:, :width] = mm(spread[0] + spread[1], ffn).astype(LOW)
        ref[:, width:] = (mm(spread[0], scaled[0]) + mm(spread[1], scaled[1])).astype(LOW)


def dense_forward(after, zh, tokens, segments, routes, cotangent, w_qkv, w_out, w_router, gains):
    count, width = tokens.shape
    slots = (w_router.shape[0] - 1) * CAP
    shapes = [
        ((count, width), LOW), ((count, 3 * width), LOW), ((count, width), LOW), ((count, 128), F32),
        ((count, width), F32), ((count, width), LOW), ((count, 128), F32),
        ((slots, 2 * width), LOW), ((CAP, 2 * width), LOW),
    ]
    return ordered(
        dense_forward_kernel, 9, after,
        name="dense_forward",
        out_shape=[jax.ShapeDtypeStruct(s, t) for s, t in shapes],
        in_specs=[SMEM] + [VMEM] * 8,
        out_specs=[VMEM] * len(shapes),
        compiler_params=params(),
        cost_estimate=cost(8e9, 30e6),
    )(zh, tokens, segments, routes, cotangent, w_qkv, w_out, w_router, gains)


def dense_backward_kernel(
    core_ref, plan, routes, segments, cotangent, tokens, middle, mixed, ffn, lse, qkv, attn_in,
    w_qkv, w_out, w_router, gains, back, frozen_back,
    input_grad_o, kept_o, away_o, active_o,
    flat, gqkv, weight, kept, away, sems,
):
    count, width = tokens.shape
    weight_copy = pltpu.make_async_copy(w_qkv, weight, sems.at[0])
    weight_copy.start()
    expert_total = w_router.shape[0]
    up = cotangent[...].astype(F32)
    gates = [plan[:, k : k + 1] for k in range(2)]
    new_place = [plan[:, 2 + k : 3 + k].astype(jnp.int32) for k in range(2)]
    old_place = [plan[:, 4 + k : 5 + k].astype(jnp.int32) for k in range(2)]
    allowed, eye = attention_mask(segments[...])

    grad_ffn = jnp.zeros((count, width), F32)
    weighted = [jnp.zeros((count, 1), F32) for k in range(2)]
    active = middle[...]
    for places, ref in ((new_place, back), (old_place, frozen_back)):
        size = ref.shape[0]
        slots = iota((count, size), 1)
        for k in range(2):
            choice = (slots == places[k]).astype(F32).astype(LOW)
            picked = mm(choice, ref[...])
            grad_ffn = grad_ffn + picked[:, :width]
            tail = picked[:, width : width + EXTRA]
            weighted[k] = weighted[k] + jnp.sum(tail, axis=1, keepdims=True)
            active = active + gates[k] * picked[:, width + EXTRA :]
    active_o[...] = active.astype(LOW)
    both = weighted[0] + weighted[1]
    experts = iota((count, expert_total), 1)
    grad_logits = jnp.zeros((count, expert_total), F32)
    for k in range(2):
        grad_logits = jnp.where(
            experts == as_column(routes[k : k + 1, :], eye), weighted[k] - gates[k] * both, grad_logits
        )
    grad_logits = grad_logits.astype(LOW)
    grad_ffn = grad_ffn + mm(grad_logits, w_router[...])
    grad_norm, gain_ffn = norm_backward(middle[...], gains[1:2, :], grad_ffn)
    grad_middle = up + grad_norm
    grad_branch = grad_middle.astype(LOW)

    blocks = width // 128
    first_row = 3 * blocks * width
    attn_out_grad = mm_tn(mixed[...], grad_branch)
    for j in range(blocks):
        flat[pl.ds(first_row + j, width, stride=blocks), :] = attn_out_grad[:, 128 * j : 128 * j + 128]
    router_row = first_row + blocks * width
    router_rows = width * expert_total // 128
    padded_logits = jnp.concatenate(
        [grad_logits, jnp.zeros((count, 128 - expert_total), LOW)], axis=1
    )
    router_grad = mm_tn(ffn[...], padded_logits)
    feature = iota((width, 128), 0)
    lane_w = iota((width, 128), 1)
    start = feature * expert_total
    offset = start & 127
    turned = jnp.take_along_axis(router_grad, (lane_w - offset) & 127, axis=1)
    wrapped = lane_w < offset
    row_of = lax.shift_right_logical(iota((router_rows, width), 1) * expert_total, 7)
    row_here = iota((router_rows, width), 0)
    here = (row_of == row_here).astype(F32)
    after = (row_of + 1 == row_here).astype(F32)
    exact = lambda a, b: jnp.dot(a, b, precision=lax.Precision.HIGHEST, preferred_element_type=F32)
    flat[router_row : router_row + router_rows, :] = exact(
        here, jnp.where(wrapped, 0.0, turned)
    ) + exact(after, jnp.where(wrapped, turned, 0.0))
    gain_row = router_row + router_rows

    grad_mixed = mm_nt(grad_branch, w_out[...]).astype(LOW)
    lane = iota((count, 128), 1)
    low_lanes = lane < HEAD_DIM
    scale = HEAD_DIM**-0.5
    for pair in range(blocks):
        at = slice(128 * pair, 128 * pair + 128)
        queries = qkv[:, at] * jnp.asarray(scale, LOW)
        keys = qkv[:, width + 128 * pair : width + 128 * pair + 128]
        values = qkv[:, 2 * width + 128 * pair : 2 * width + 128 * pair + 128]
        grads = grad_mixed[:, at]
        grad_q = jnp.zeros((count, 128), F32)
        grad_k = jnp.zeros((count, 128), F32)
        grad_v = jnp.zeros((count, 128), F32)
        for half in range(2):
            mine = low_lanes if half == 0 else ~low_lanes
            only = lambda v: jnp.where(mine, v, jnp.zeros_like(v))
            q_half, g_half, k_half = only(queries), only(grads), only(keys)
            scores = jnp.where(allowed, mm_nt(q_half, keys), -1e30)
            head = 2 * pair + half
            probs = jnp.exp(scores - lse[:, head : head + 1])
            grad_probs = mm_nt(g_half, values)
            grad_v = grad_v + mm_tn(probs.astype(LOW), g_half)
            dots = jnp.sum(probs * grad_probs, axis=1, keepdims=True)
            grad_scores = (probs * (grad_probs - dots)).astype(LOW)
            grad_q = grad_q + mm(grad_scores, k_half)
            grad_k = grad_k + mm_tn(grad_scores, q_half)
        gqkv[:, at] = (grad_q * scale).astype(LOW)
        gqkv[:, width + 128 * pair : width + 128 * pair + 128] = grad_k.astype(LOW)
        gqkv[:, 2 * width + 128 * pair : 2 * width + 128 * pair + 128] = grad_v.astype(LOW)
    for j in range(0, 3 * blocks, 2):
        piece = mm_tn(attn_in[...], gqkv[:, 128 * j : 128 * j + 256])
        flat[pl.ds(j, width, stride=3 * blocks), :] = piece[:, :128]
        flat[pl.ds(j + 1, width, stride=3 * blocks), :] = piece[:, 128:]
    core = core_ref[0]
    rows = flat.shape[0] // 128
    pairs, padded = kept.shape[:2]

    def move(i):
        kept[pl.ds(i, 1)] = flat[pl.ds((2 * i + core) * rows, padded), :].astype(LOW)[None]
        away[pl.ds(i, 1)] = flat[pl.ds((2 * i + 1 - core) * rows, padded), :].astype(LOW)[None]

    pl.loop(0, pairs - 1)(move)
    early, last_one = pl.ds(0, pairs - 1), pl.ds(pairs - 1, 1)
    copies = [
        pltpu.make_async_copy(a.at[part], b.at[part], sems.at[1 + i])
        for i, (a, b, part) in enumerate(
            ((away, away_o, early), (kept, kept_o, early), (away, away_o, last_one), (kept, kept_o, last_one))
        )
    ]
    copies[0].start()
    copies[1].start()
    weight_copy.wait()
    grad_attn = mm_nt(gqkv[...], weight[...])
    grad_norm, gain_attn = norm_backward(tokens[...].astype(F32), gains[0:1, :], grad_attn)
    input_grad_o[...] = grad_middle + grad_norm
    for j in range(blocks):
        flat[gain_row + j : gain_row + j + 1, :] = gain_attn[:, 128 * j : 128 * j + 128]
        flat[gain_row + blocks + j : gain_row + blocks + j + 1, :] = gain_ffn[:, 128 * j : 128 * j + 128]
    last = gain_row + 2 * blocks
    flat[last:, :] = jnp.zeros((flat.shape[0] - last, 128), F32)

    move(pairs - 1)
    copies[2].start()
    copies[3].start()
    for copy in copies:
        copy.wait()


def dense_backward(after, core, dense_rows, *arrays):
    count, width = arrays[4].shape
    rows = dense_rows // 128
    padded = (rows + 7) // 8 * 8
    return ordered(
        dense_backward_kernel, 1 + len(arrays), after,
        name="dense_backward",
        out_shape=[
            jax.ShapeDtypeStruct((count, width), F32),
            jax.ShapeDtypeStruct((64, padded, 128), LOW),
            jax.ShapeDtypeStruct((64, padded, 128), LOW),
            jax.ShapeDtypeStruct((count, width), LOW),
        ],
        in_specs=[SMEM] + [VMEM] * 11 + [HBM] + [VMEM] * (len(arrays) - 12),
        out_specs=[VMEM, HBM, HBM, VMEM],
        scratch_shapes=[
            pltpu.VMEM((rows * 128 + padded - rows, 128), F32),
            pltpu.VMEM((count, 3 * width), LOW),
            pltpu.VMEM((width, 3 * width), LOW),
            pltpu.VMEM((64, padded, 128), LOW),
            pltpu.VMEM((64, padded, 128), LOW),
            pltpu.SemaphoreType.DMA((5,)),
        ],
        compiler_params=params(),
        cost_estimate=cost(12e9, 40e6),
    )(core, *arrays)


def gelu_pair(pre):
    area = 0.5 + 0.5 * lax.erf(pre * (0.5**0.5))
    density = jnp.exp(-0.5 * pre * pre) * (1.0 / (2.0 * math.pi) ** 0.5)
    return pre * area, area + pre * density


def build_weight(after, name, home, sources, by_rows):
    rows, cols = sources[0].shape[1:]

    def kernel(home_ref, local, near, across, local_mate, near_mate, across_mate, out, sems):
        z, half = home_ref[0], home_ref[2]

        def move(blocks):
            copies = []
            for step, shard in enumerate(blocks):
                if by_rows:
                    start = pl.multiple_of(half * (rows // 2), 64)
                    place = pl.ds(pl.multiple_of(((z + step) & 3) * (rows // 2), 64), rows // 2)
                    copies.append((shard.at[0, pl.ds(start, rows // 2), :], out.at[place, :]))
                else:
                    place = pl.ds(pl.multiple_of(((z + step) & 3) * rows, 64), rows)
                    for block in range(4):
                        start = pl.multiple_of((2 * block + half) * (cols // 8), 128)
                        to = slice(block * (cols // 8), (block + 1) * (cols // 8))
                        copies.append((shard.at[0, :, pl.ds(start, cols // 8)], out.at[place, to]))
            made = [pltpu.make_async_copy(a, b, sems.at[i]) for i, (a, b) in enumerate(copies)]
            for copy in made:
                copy.start()
            for copy in made:
                copy.wait()

        pl.when(home_ref[1] == 1)(lambda: move((local, near_mate, across_mate, near)))
        pl.when(home_ref[1] == 0)(lambda: move((local_mate, near, across, near_mate)))

    shape = (2 * rows, cols) if by_rows else (4 * rows, cols // 2)
    return ordered(
        kernel, 7, after,
        name=name,
        out_shape=jax.ShapeDtypeStruct(shape, LOW),
        in_specs=[SMEM] + [HBM] * 6,
        out_specs=VMEM,
        scratch_shapes=[pltpu.SemaphoreType.DMA((16,))],
        compiler_params=params(),
        cost_estimate=cost(1e5 if by_rows else 19e9, 8e6),
    )(home, *sources)


def expert_up_kernel(own, mate, weight, hidden_o, slope_o, rows_o, grads_o):
    width = weight.shape[0]
    both = jnp.where(pl.program_id(0) < pl.num_programs(0) // 2, own[...], mate[...])
    rows = both[:, :width]
    rows_o[...] = rows
    grads_o[...] = both[:, width:]
    hidden, slope = gelu_pair(mm(rows, weight[...]))
    hidden_o[...] = hidden.astype(LOW)
    slope_o[...] = slope.astype(LOW)


def expert_up(after, own, mate, weight):
    count, width = own.shape[0], weight.shape[0]
    hidden = weight.shape[1]
    step = 256
    half = count // step
    block = lambda cols: pl.BlockSpec((step, cols), lambda i: (i, 0))
    return ordered(
        expert_up_kernel, 3, after,
        name="expert_up",
        out_shape=[jax.ShapeDtypeStruct((2 * count, n), LOW) for n in (hidden, hidden, width, width)],
        grid=(2 * half,),
        in_specs=[
            pl.BlockSpec((step, 2 * width), lambda i: (jnp.minimum(i, half - 1), 0)),
            pl.BlockSpec((step, 2 * width), lambda i: (jnp.maximum(i - half, 0), 0)),
            pl.BlockSpec((width, hidden), lambda i: (0, 0)),
        ],
        out_specs=[block(n) for n in (hidden, hidden, width, width)],
        compiler_params=params(),
        cost_estimate=cost(12e9, 20e6),
    )(own, mate, weight)


def split_three(value):
    high = lax.reduce_precision(value, 8, 7)
    mid = lax.reduce_precision(value - high, 8, 7)
    return high, mid, value - high - mid


def extra_terms(value):
    lane = iota((value.shape[0], EXTRA), 1)
    extra = jnp.zeros((value.shape[0], EXTRA), F32)
    for i, term in enumerate(split_three(value)):
        extra = jnp.where(lane == i, term, extra)
    return extra.astype(LOW)


def reduce_first(after, low, kept, arrived, work=1e6):
    rows, columns = kept.shape[0] // 2, kept.shape[1]

    def kernel(low_ref, kept, arrived, mine, other):
        for out, which in ((mine, low_ref[0]), (other, 1 - low_ref[0])):
            at = pl.ds(pl.multiple_of(which * rows, 64), rows)
            out[...] = (kept[at, :] + arrived[at, :].astype(F32)).astype(out.dtype)

    return ordered(
        kernel, 3, after,
        name="reduce_first",
        out_shape=[jax.ShapeDtypeStruct((rows, columns), t) for t in (F32, LOW)],
        in_specs=[SMEM, VMEM, VMEM],
        out_specs=[VMEM] * 2,
        compiler_params=params(),
        cost_estimate=cost(work, 6e6),
    )(low, kept, arrived)


def reduce_second(after, same, mine, other):
    def kernel(same_ref, mine, other, stays, leaves):
        straight = same_ref[0] == 1
        near, far = mine[...], other[...].astype(F32)
        stays[...] = jnp.where(straight, near, far)
        leaves[...] = jnp.where(straight, far, near).astype(LOW)

    return ordered(
        kernel, 3, after,
        name="reduce_second",
        out_shape=[jax.ShapeDtypeStruct(mine.shape, t) for t in (F32, LOW)],
        in_specs=[SMEM, VMEM, VMEM],
        out_specs=[VMEM] * 2,
        compiler_params=params(),
        cost_estimate=cost(1e6, 6e6),
    )(same, mine, other)


def frozen_kernel(rows, grads, w_in, w_out, back_o, result_sum, back_sum, value_sum):
    step = pl.program_id(0)

    @pl.when(step == 0)
    def clear():
        result_sum[...] = jnp.zeros_like(result_sum)
        back_sum[...] = jnp.zeros_like(back_sum)
        value_sum[...] = jnp.zeros_like(value_sum)

    hidden, slope = gelu_pair(mm(rows[...], w_in[...]))
    hidden = hidden.astype(LOW)
    result_sum[...] += mm(hidden, w_out[...])
    grad_hidden = mm_nt(grads[...], w_out[...])
    value_sum[...] += jnp.sum(hidden.astype(F32) * grad_hidden, axis=1, keepdims=True)
    back_sum[...] += mm_nt((grad_hidden * slope).astype(LOW), w_in[...])

    @pl.when(step == pl.num_programs(0) - 1)
    def finish():
        width = back_sum.shape[1]
        back_o[:, :width] = back_sum[...].astype(LOW)
        back_o[:, width : width + EXTRA] = extra_terms(value_sum[:, 0:1])
        back_o[:, width + EXTRA :] = result_sum[...].astype(LOW)


def frozen_expert(after, sent, w_in, w_out):
    count, width = sent.shape[0], w_in.shape[0]
    wide = w_in.shape[1]
    step = 512
    small = pl.BlockSpec((count, width), lambda i: (0, 0))
    return ordered(
        frozen_kernel, 4, after,
        name="frozen_expert",
        out_shape=jax.ShapeDtypeStruct((count, 2 * width + EXTRA), LOW),
        grid=(wide // step,),
        in_specs=[
            small, pl.BlockSpec((count, width), lambda i: (0, 1)),
            pl.BlockSpec((width, step), lambda i: (0, i)),
            pl.BlockSpec((step, width), lambda i: (i, 0)),
        ],
        out_specs=pl.BlockSpec((count, 2 * width + EXTRA), lambda i: (0, 0)),
        scratch_shapes=[
            pltpu.VMEM((count, width), F32),
            pltpu.VMEM((count, width), F32),
            pltpu.VMEM((count, EXTRA), F32),
        ],
        compiler_params=params(),
        cost_estimate=cost(4e9, 10e6),
    )(sent, sent, w_in, w_out)


def marker(after):
    def kernel(out):
        out[...] = jnp.zeros_like(out)

    return ordered(
        kernel, 0, after,
        name="marker",
        out_shape=jax.ShapeDtypeStruct((1, 1), F32),
        in_specs=[],
        out_specs=VMEM,
        compiler_params=params(),
        cost_estimate=cost(200e9, 4e3),
    )()


def adamw_values(master, first, second, grad):
    first_new = beta_first * first + (1.0 - beta_first) * grad
    second_new = beta_second * second + (1.0 - beta_second) * grad * grad
    first_hat = first_new * (1.0 / (1.0 - beta_first**STEP))
    second_hat = second_new * (1.0 / (1.0 - beta_second**STEP))
    master_new = master - learn_rate * (
        first_hat / (jnp.sqrt(second_hat) + adam_eps) + decay_rate * master
    )
    return master_new, first_new, second_new, master_new.astype(LOW)


def dense_update_kernel(master, first, second, terms, *outs):
    rows = master.shape[0]
    grad = jnp.sum(terms[...].astype(F32), axis=0)[:rows]
    for out, value in zip(outs, adamw_values(master[...], first[...], second[...], grad)):
        out[...] = value


def dense_update(after, master, first, second, terms):
    shape = (master.shape[0] // 128, 128)
    results = ordered(
        dense_update_kernel, 4, after,
        name="dense_update",
        out_shape=[jax.ShapeDtypeStruct(shape, t) for t in (F32, F32, F32, LOW)],
        in_specs=[VMEM] * 4,
        out_specs=[VMEM] * 4,
        compiler_params=params(),
        cost_estimate=cost(1e6, 4e6),
    )(*(a.reshape(shape) for a in (master, first, second)), terms)
    return tuple(r.reshape(master.shape) for r in results)


def expert_update(after, core, master, first, second, stays, arrived, axis):
    rows, columns = master.shape[1:]
    if axis == 1:
        blocks, width = 4, columns // 4
        half = (rows, width // 2)
    else:
        blocks, width = 3, columns // 3
        half = (rows // 2, width)

    def kernel(core_ref, master, first, second, stays, arrived, *outs):
        near, far = stays[...], arrived[...].astype(F32)
        swapped = core_ref[0] == 1
        grad = jnp.concatenate(
            [jnp.where(swapped, far, near), jnp.where(swapped, near, far)], axis=axis
        )
        values = adamw_values(master[0], first[0], second[0], grad)
        for out, value in zip(outs, values):
            out[0] = value

    wide = pl.BlockSpec((1, rows, width), lambda i: (0, 0, i))
    slim = pl.BlockSpec(half, lambda i: (0, i))
    return tuple(
        ordered(
        kernel, 6, after,
            name="update_in" if axis == 1 else "update_out",
            out_shape=[jax.ShapeDtypeStruct(master.shape, t) for t in (F32, F32, F32, LOW)],
            grid=(blocks,),
            in_specs=[SMEM, wide, wide, wide, slim, slim],
            out_specs=[wide] * 4,
            compiler_params=params(),
            cost_estimate=cost(2e7, 18e6),
        )(core, master, first, second, stays, arrived)
    )


def swap_core(block):
    return lax.ppermute(block, "c", [(0, 1), (1, 0)])


KINDS = (0, 1, 1, 0)


def to_neighbours(shard):
    moves = []
    for z, kind in enumerate(KINDS):
        moves.append(((z - 1) % 4 * 2 + kind, z * 2 + kind))
        moves.append(((z + 1) % 4 * 2 + kind, z * 2 + 1 - kind))
    return lax.ppermute(shard, DEPTH + ("c",), moves)


def to_opposite(shard):
    moves = []
    for z, kind in enumerate(KINDS):
        source = kind if z % 2 else 1 - kind
        moves.append((z * 2 + source, (3 - z) * 2 + 1 - kind))
    return lax.ppermute(shard, DEPTH + ("c",), moves)


def swap_pair(block):
    return lax.ppermute(block, DEPTH, [(z, 3 - z) for z in range(4)])


def swap_low(block):
    return lax.ppermute(block, "zl", [(0, 1), (1, 0)])


def exchange(rows):
    cut = rows.reshape(-1, CAP, rows.shape[1])
    cut = lax.all_to_all(cut, PLANE, split_axis=0, concat_axis=0, tiled=True)
    return cut.reshape(rows.shape)


def tie(array, *others):
    return lax.optimization_barrier((array,) + others)[0]


def word(*values):
    return jnp.stack([jnp.asarray(v, jnp.int32) for v in values])


def body(
    tokens,
    segment_ids,
    routes,
    cotangent,
    w_qkv,
    w_attn_out,
    w_router,
    norm_gains,
    frozen_in,
    frozen_out,
    new_in,
    new_out,
    dense_master,
    dense_first,
    dense_second,
    master_in,
    first_in,
    second_in,
    master_out,
    first_out,
    second_out,
):
    core, zh, zl = (lax.axis_index(a) for a in ("c", "zh", "zl"))
    z = 2 * zh + zl
    kind = zh ^ zl
    same = jnp.where(kind == core, 1, 0)
    home = word(z, same, core)
    core_word, same_word, zl_word = word(core), word(same), word(zl)
    routes = routes.T
    w_router = w_router.T

    in_near = to_neighbours(new_in)
    in_mates, out_mates = [swap_core(new_in)], [swap_core(new_out)]
    attn_in, qkv_low, mixed_low, lse, middle, ffn_in, plan, sent, frozen_sent = dense_forward(
        (), word(zh), tokens, segment_ids, routes, cotangent, w_qkv, w_attn_out, w_router, norm_gains
    )
    received = exchange(sent)
    in_across = to_opposite(tie(in_near, plan))
    in_mates.append(swap_core(tie(in_near, plan)))
    frozen_back = frozen_expert(
        (in_mates[0], out_mates[0], in_mates[1]), frozen_sent, frozen_in, frozen_out
    )
    in_mates.append(swap_core(tie(in_across, frozen_back)))
    out_near = to_neighbours(tie(new_out, in_across))
    half_in = build_weight(
        (frozen_back,), "build_in", home, (new_in, in_near, in_across, *in_mates), False
    )
    received = tie(received, frozen_back, in_across)
    hidden, slope, rows, grads = expert_up((), received, swap_core(received), half_in)
    out_across = to_opposite(tie(out_near, hidden))
    out_mates.append(swap_core(tie(out_near, hidden)))
    count = received.shape[0]

    def half_grad(left, right, half):
        cut = left.shape[1] // 2
        return mm_tn(lax.dynamic_slice(left, (0, half * cut), (left.shape[0], cut)), right)

    out_away = half_grad(hidden, grads, 1 - zh).astype(LOW)
    out_arrived = swap_pair(out_away)
    out_mates.append(swap_core(tie(out_across, out_away)))
    half_out = build_weight(
        (out_away,), "build_out", home, (new_out, out_near, out_across, *out_mates), True
    )

    result_arrived = swap_core(mm(hidden[count:], half_out).astype(LOW))
    pre = (mm_nt(grads, half_out) * slope.astype(F32)).astype(LOW)
    result = (mm(hidden[:count], half_out) + result_arrived.astype(F32)).astype(LOW)
    back_arrived = swap_core(mm_nt(pre[count:], half_in).astype(LOW))
    back = (mm_nt(pre[:count], half_in) + back_arrived.astype(F32)).astype(LOW)
    value = jnp.sum(grads[:count].astype(F32) * result.astype(F32), axis=1, keepdims=True)
    merged = jnp.concatenate([back, extra_terms(value), result], axis=1)
    back = exchange(merged)
    in_away = half_grad(tie(rows, merged), pre, 1 - zh).astype(LOW)
    in_arrived = swap_pair(in_away)

    out_kept = half_grad(tie(hidden, in_away), grads, zh)
    in_kept = half_grad(tie(rows, in_away), pre, zh)
    out_mine, out_other = reduce_first((merged,), zl_word, out_kept, out_arrived, 1e6)
    in_mine, in_other = reduce_first((out_mine,), zl_word, in_kept, in_arrived, 10e9)
    out_other, in_other = swap_low(out_other), swap_low(in_other)

    input_grad, kept, away, activations = dense_backward(
        (in_mine,), core_word, dense_master.shape[0], plan, routes, segment_ids, cotangent, tokens, middle,
        mixed_low, ffn_in, lse, qkv_low, attn_in, w_qkv, w_attn_out, w_router, norm_gains, back, frozen_back,
    )
    arrived = swap_core(away)
    kept_first = kept
    kept = tie(kept, out_other, in_other)
    zero = marker((kept_first,)).reshape(())
    summed = (kept.astype(F32) + arrived.astype(F32) + zero).astype(LOW)
    terms = lax.all_to_all(summed, ("zh", "zl", "x", "y"), split_axis=0, concat_axis=0, tiled=True)
    out_stays, out_leaves = reduce_second((summed,), same_word, out_mine, out_other)
    out_mate_grad = swap_core(out_leaves)
    in_stays, in_leaves = reduce_second((out_stays,), same_word, in_mine, in_other)
    in_mate_grad = swap_core(in_leaves)
    out_new = expert_update(
        (in_stays,), core_word, master_out, first_out, second_out, out_stays, out_mate_grad, 0
    )
    in_new = expert_update(
        (out_new[0],), core_word, master_in, first_in, second_in, in_stays, in_mate_grad, 1
    )
    dense_new = dense_update((in_new[0],), dense_master, dense_first, dense_second, terms)
    return (activations, input_grad) + dense_new + in_new + out_new


def solution(mesh):
    fine = Mesh(mesh.devices.reshape(2, 2, 4, 4, 2), ALL)
    tokens = P(ALL, None)
    flat = P(ALL)
    expert = P(("x", "y", "c"), DEPTH, None)
    return jax.shard_map(
        body,
        mesh=fine,
        in_specs=(tokens,) * 4 + (P(),) * 6 + (expert,) * 2 + (flat,) * 3 + (expert,) * 6,
        out_specs=(tokens,) * 2 + (flat,) * 4 + (expert,) * 8,
        check_vma=False,
    )
```
